32 devices in a mesh: dp: 8 (over z, x), rep: 4 (over y, core).
Axes of the slice: x: 2, y: 2, z: 4, core: 2. Of those that a mesh axis runs over, the one named last changes fastest.
Arguments:
- inputs: bfloat16 [8192, 2048], P(('dp', 'rep')), may hold values from -6 to 6
- layout: int32 [32, 3], replicated, may hold values from 1 to 16, as said below
- labels: int32 [8192], P(('dp', 'rep')), may hold values from 0 to 39
- cot_depth: bfloat16 [8192, 512], P(('dp', 'rep')), may hold values from -6 to 6
- w_reduce: bfloat16 [2048, 512], replicated, may hold values from -0.125 to 0.125
- w_spatial: bfloat16 [4608, 512], replicated, may hold values from -0.09375 to 0.09375
- w_expand: bfloat16 [512, 2048], replicated, may hold values from -0.25 to 0.25
- w_heads: bfloat16 [2048, 18432], P('rep'), may hold values from -0.046875 to 0.046875
- w_gates: bfloat16 [1024, 512], replicated, may hold values from -0.25 to 0.25
- w_messages: bfloat16 [27648, 512], P('rep'), may hold values from -0.0546875 to 0.0546875
- w_classes: bfloat16 [512, 40], replicated, may hold values from -0.5 to 0.5
- gain_mid: float32 [2, 512], replicated, may hold values from 0.5 to 2
- shift_mid: float32 [2, 512], replicated, may hold values from -3 to 3
- gain_wide: float32 [2048], replicated, may hold values from 0.5 to 2
- shift_wide: float32 [2048], replicated, may hold values from -3 to 3
- gain_head: float32 [2048], replicated, may hold values from 0.5 to 2
- shift_head: float32 [2048], replicated, may hold values from -3 to 3
Outputs:
- depth: float32 [8192, 512], P(('dp', 'rep'))
- logits: float32 [8192, 40], P(('dp', 'rep'))
- input_grad: float32 [8192, 2048], P(('dp', 'rep'))
- grad_reduce: float32 [2048, 512], P('rep')
- grad_spatial: float32 [4608, 512], P('rep')
- grad_expand: float32 [512, 2048], P('rep')
- grad_heads: float32 [2048, 18432], P('rep', 'dp')
- grad_gates: float32 [1024, 512], P('rep')
- grad_messages: float32 [27648, 512], P('rep', 'dp')
- grad_classes: float32 [512, 40], P('rep')
- grad_gain_mid: float32 [2, 512], replicated
- grad_shift_mid: float32 [2, 512], replicated
- grad_gain_wide: float32 [2048], replicated
- grad_shift_wide: float32 [2048], replicated
- grad_gain_head: float32 [2048], replicated
- grad_shift_head: float32 [2048], replicated
The draws below stay inside these ranges and needn't reach their ends.
Inputs may be any that keep to these rules, and one draw needn't show every extreme that they name: `layout`: row d describes device d (dp, then rep): its map is 16 x 16 or (8) x (8), images times map area is at most 256 and one device fills all 256 rows in every draw; rows past images times area hold no pixel.
All inputs are finite; a program needn't handle non-finite values.
Results may differ from the reference program's by a relative error of at most 0.02.
Values may be sent and summed in bfloat16 or wider, within the bound.
A program may use at most 384 MiB of HBM per device.

```python
import math
import jax
import jax.numpy as jnp
from jax import lax

WIDE = 2048
MID = 512
CLS = 40
HL = 16
WL = 16
SLOTS = 1
CAP = 256
PIX = 8192
N_DP = 8
N_REP = 4


def draw_layout(key, part):
    key = jax.random.fold_in(key, 11)
    devices = N_DP * N_REP
    key_kind, key_large, key_small, key_full = jax.random.split(key, 4)
    large = jax.random.randint(key_kind, (devices,), 0, 2)
    large_count = jax.random.randint(key_large, (devices,), 1, SLOTS + 1)
    small_count = jax.random.randint(key_small, (devices,), 1, 4 * SLOTS + 1)
    chosen = jax.random.randint(key_full, (), 0, devices)
    filled = jnp.arange(devices) == chosen
    large = jnp.where(filled, 1, large)
    large_count = jnp.where(filled, SLOTS, large_count)
    height = jnp.where(large == 1, HL, HL // 2)
    map_width = jnp.where(large == 1, WL, WL // 2)
    images = jnp.where(large == 1, large_count, small_count)
    return jnp.stack([height, map_width, images], 1).astype(jnp.int32)


def plant(drawn, key, smallest, high):
    place = [jax.random.randint(jax.random.fold_in(key, axis), (), 0, length) for axis, length in enumerate(drawn.shape)]
    longest = drawn.shape.index(max(drawn.shape))
    neighbour = place[:longest] + [(place[longest] + 1) % drawn.shape[longest]] + place[longest + 1:]
    return drawn.at[tuple(place)].set(smallest).at[tuple(neighbour)].set(high)


def block_scale(key, extent, shards, least, high):
    gain = 1.0
    for dim, parts in shards:
        steps = jax.random.uniform(jax.random.fold_in(jax.random.fold_in(key, 6), dim), (parts,), jnp.float32, least / len(shards), high / len(shards))
        gain = gain * jnp.repeat(jnp.exp(steps), extent[dim] // parts).reshape((-1,) + (1,) * (len(extent) - 1 - dim))
    return gain


def gaussian(stream_key, extent, deviation, bound, pieces=(), kind=jnp.bfloat16):
    level = block_scale(stream_key, extent, pieces, -0.22, 0.18) if pieces else 1.0
    drawn = jax.random.normal(stream_key, extent, jnp.float32) * deviation * level
    return jnp.minimum(jnp.maximum(drawn, -bound), bound).astype(kind)


def setup_inputs(seed: int = 0) -> dict:
    splits = jax.random.split(jax.random.key(seed), 18)
    return {
        "inputs": gaussian(splits[0], (PIX, WIDE), 1.0, 6.0, ((0, 32),)),
        "layout": draw_layout(jax.random.fold_in(splits[17], 71), 0),
        "labels": plant(jax.random.randint(splits[2], (PIX,), 0, CLS), jax.random.fold_in(splits[2], 1), 0, CLS - 1).astype(jnp.int32),
        "cot_depth": gaussian(splits[3], (PIX, MID), 1.0, 6.0, ((0, 32),)),
        "w_reduce": gaussian(splits[4], (WIDE, MID), WIDE ** -0.5, 0.125),
        "w_spatial": gaussian(splits[5], (9 * MID, MID), (9 * MID) ** -0.5, 0.09375),
        "w_expand": gaussian(splits[6], (MID, WIDE), MID ** -0.5, 0.25),
        "w_heads": gaussian(splits[7], (4 * MID, 9 * WIDE), (9 * WIDE) ** -0.5, 0.046875, ((0, 4),)),
        "w_gates": gaussian(splits[8], (2 * MID, MID), MID ** -0.5, 0.25),
        "w_messages": gaussian(splits[9], (54 * MID, MID), (27 * MID) ** -0.5, 0.0546875, ((0, 4),)),
        "w_classes": gaussian(splits[10], (MID, CLS), (MID // 4) ** -0.5, 0.5),
        "gain_mid": jnp.clip(jnp.exp(jax.random.uniform(splits[11], (2, MID), jnp.float32, math.log(0.5), math.log(2.0))), 0.5, 2.0),
        "shift_mid": gaussian(splits[12], (2, MID), 0.5, 3.0, (), jnp.float32),
        "gain_wide": jnp.clip(jnp.exp(jax.random.uniform(splits[13], (WIDE,), jnp.float32, math.log(0.5), math.log(2.0))), 0.5, 2.0),
        "shift_wide": gaussian(splits[14], (WIDE,), 0.5, 3.0, (), jnp.float32),
        "gain_head": jnp.clip(jnp.exp(jax.random.uniform(splits[15], (4 * MID,), jnp.float32, math.log(0.5), math.log(2.0))), 0.5, 2.0),
        "shift_head": gaussian(splits[16], (4 * MID,), 0.5, 3.0, (), jnp.float32),
    }


EPS = 1e-05
HIGH = lax.Precision.HIGHEST

@jax.custom_vjp
def low(v):
    return lax.optimization_barrier(v.astype(jnp.bfloat16)).astype(jnp.float32)

@jax.custom_vjp
def low_back(v):
    return v

def low_keep(v):
    return (low(v), None)

def low_pass(kept, grad):
    return (grad,)

def back_keep(v):
    return (v, None)

def back_low(kept, grad):
    return (low(grad),)
low.defvjp(low_keep, low_pass)
low_back.defvjp(back_keep, back_low)

def geometry(layout, span):
    position = jnp.arange(span, dtype=jnp.int32)
    height = layout[:, 0:1]
    map_width = layout[:, 1:2]
    images = layout[:, 2:3]
    map_area = height * map_width
    inside = position[None, :] % map_area
    row_of = inside // map_width
    col_of = inside % map_width
    living = position[None, :] < images * map_area
    return (row_of, col_of, living, height, map_width)

def taps(shape_info, dilation):
    row_of, col_of, living, height, map_width = shape_info
    offsets = []
    tap_marks = []
    for step_row in (-1, 0, 1):
        for step_col in (-1, 0, 1):
            target_row = row_of + dilation * step_row
            target_col = col_of + dilation * step_col
            inside = living & (target_row >= 0) & (target_row < height) & (target_col >= 0) & (target_col < map_width)
            tap_marks.append(inside.astype(jnp.float32))
            offsets.append((dilation * (step_row * map_width + step_col)).astype(jnp.int32))
    return (jnp.concatenate(offsets, 1), jnp.stack(tap_marks, 1))

def reference(inputs, layout, labels, cot_depth, w_reduce, w_spatial, w_expand, w_heads, w_gates, w_messages, w_classes, gain_mid, shift_mid, gain_wide, shift_wide, gain_head, shift_head):
    devices = N_DP * N_REP
    shape_info = geometry(layout, CAP)
    offsets_one, marks_one = taps(shape_info, 1)
    offsets_two, marks_two = taps(shape_info, 2)
    living = shape_info[2].reshape(-1, 1).astype(jnp.float32)
    pixel_count = jnp.sum(living)
    onehot_table = (labels[:, None] == jnp.arange(CLS, dtype=jnp.int32)[None, :]).astype(jnp.float32)
    cot_values = cot_depth.astype(jnp.float32)

    def columns(values, offsets, tap_marks):
        blocks = values.reshape(devices, CAP, values.shape[1])

        def one_device(block, device_offsets, device_marks):
            return jnp.concatenate([jnp.roll(block, -device_offsets[tap_number], axis=0) * device_marks[tap_number][:, None] for tap_number in range(9)], 1)
        return jax.vmap(one_device)(blocks, offsets, tap_marks).reshape(-1, 9 * values.shape[1])

    def matmul(left_side, right_side):
        return jnp.dot(left_side, right_side, precision=HIGH)

    def batchnorm(raw_value, norm_gain, norm_shift):
        center = lax.optimization_barrier(jnp.sum(living * raw_value, 0)) / pixel_count
        spread_of = lax.optimization_barrier(jnp.sum(living * raw_value * raw_value, 0)) / pixel_count - center * center
        return (raw_value - center) * lax.rsqrt(spread_of + EPS) * norm_gain + norm_shift

    def forward(source, weight_reduce, weight_spatial, weight_expand, weight_heads, weight_gates, weight_messages, weight_classes, gains_mid, shifts_mid, gains_wide, shifts_wide, gains_head, shifts_head):
        middle = MID
        reduced = low_back(matmul(low(source), weight_reduce))
        hidden_one = low(jax.nn.silu(batchnorm(reduced, gains_mid[0], shifts_mid[0])))
        spatial = low_back(matmul(columns(hidden_one, offsets_two, marks_two), weight_spatial))
        hidden_two = low(jax.nn.silu(batchnorm(spatial, gains_mid[1], shifts_mid[1])))
        expanded = low_back(matmul(hidden_two, weight_expand))
        trunk = low(jax.nn.silu(batchnorm(expanded, gains_wide, shifts_wide) + source))
        headed = low_back(matmul(columns(trunk, offsets_one, marks_one), weight_heads.T))
        features = jax.nn.silu(batchnorm(headed, gains_head, shifts_head))
        rounded = low(features)
        depth_part = rounded[:, :middle]
        seg_part = rounded[:, 3 * middle:]
        gate_depth = jax.nn.sigmoid(low_back(matmul(depth_part, weight_gates[:middle])))
        gate_seg = jax.nn.sigmoid(low_back(matmul(seg_part, weight_gates[middle:])))
        message_depth = low_back(matmul(columns(rounded[:, middle:], offsets_one, marks_one), weight_messages[:27 * middle]))
        message_seg = low_back(matmul(columns(rounded[:, :3 * middle], offsets_one, marks_one), weight_messages[27 * middle:]))
        depth_full = features[:, :middle] + gate_depth * message_depth
        seg_full = features[:, 3 * middle:] + gate_seg * message_seg
        logits_full = low_back(matmul(low(seg_full), weight_classes))
        entropy = jax.nn.logsumexp(logits_full, axis=1, keepdims=True) - lax.optimization_barrier(jnp.sum(logits_full * onehot_table, 1, keepdims=True))
        loss = jnp.sum(living * entropy) + jnp.sum(living * depth_full * cot_values)
        return (loss, (living * depth_full, living * logits_full))
    primals = (inputs.astype(jnp.float32), w_reduce.astype(jnp.float32), w_spatial.astype(jnp.float32), w_expand.astype(jnp.float32), w_heads.astype(jnp.float32), w_gates.astype(jnp.float32), w_messages.astype(jnp.float32), w_classes.astype(jnp.float32), gain_mid, shift_mid, gain_wide, shift_wide, gain_head, shift_head)
    loss, pullback, extras = jax.vjp(forward, *primals, has_aux=True)
    grads = pullback(jnp.ones_like(loss))
    return (extras[0], extras[1], grads[0], grads[1], grads[2], grads[3], grads[4], grads[5], grads[6], grads[7], grads[8], grads[9], grads[10], grads[11], grads[12], grads[13])
```

```python
import functools

import jax
import jax.numpy as jnp
from jax import lax
from jax.experimental import pallas as pl
from jax.experimental.pallas import tpu as pltpu
from jax.sharding import PartitionSpec as P

EPS = 1e-05
F32 = jnp.float32
BF16 = jnp.bfloat16
VMEM_LIMIT = 60 * 2**20


def geometry(layout, span):
    position = jnp.arange(span, dtype=jnp.int32)
    height = layout[:, 0:1]
    map_width = layout[:, 1:2]
    images = layout[:, 2:3]
    map_area = height * map_width
    inside = position[None, :] % map_area
    row_of = inside // map_width
    col_of = inside % map_width
    living = position[None, :] < images * map_area
    return (row_of, col_of, living, height, map_width)


def shift_matrices(shape_info, dilation):
    row_of, col_of, living, height, map_width = shape_info
    span = row_of.shape[1]
    position = jnp.arange(span, dtype=jnp.int32)
    every = []
    for step_row in (-1, 0, 1):
        for step_col in (-1, 0, 1):
            target_row = row_of + dilation * step_row
            target_col = col_of + dilation * step_col
            inside = (
                living
                & (target_row >= 0)
                & (target_row < height)
                & (target_col >= 0)
                & (target_col < map_width)
            )
            neighbour = position[None, :] + dilation * (step_row * map_width + step_col)
            picked = jnp.where(inside, neighbour, -1)
            every.append(picked[:, :, None] == position[None, None, :])
    return jnp.stack(every, 0).astype(BF16)


def product(left_side, right_side):
    return jnp.dot(left_side, right_side, preferred_element_type=F32)


def inner_rows(left_side, right_side):
    return lax.dot_general(
        left_side, right_side, (((0,), (0,)), ((), ())), preferred_element_type=F32
    )


def against(left_side, right_side):
    return lax.dot_general(
        left_side, right_side, (((1,), (1,)), ((), ())), preferred_element_type=F32
    )


def params():
    return pltpu.CompilerParams(vmem_limit_bytes=VMEM_LIMIT)


def cost(flops, moved):
    return pl.CostEstimate(flops=flops, bytes_accessed=moved, transcendentals=0)


def heads_forward_kernel(u_ref, w_ref, s_ref, out_ref):
    tap = pl.program_id(0)
    blocks, span = s_ref.shape[1], s_ref.shape[2]
    half = blocks // 2

    @pl.when(tap == 0)
    def _():
        out_ref[...] = jnp.zeros_like(out_ref)

    @pl.loop(0, 2)
    def _(part):
        rows = pl.ds(pl.multiple_of(part * half * span, half * span), half * span)
        y = against(u_ref[rows, :], w_ref[...]).astype(BF16)
        for k in range(half):
            at = pl.ds(pl.multiple_of((part * half + k) * span, span), span)
            out_ref[at, :] += product(s_ref[0, part * half + k], y[k * span : (k + 1) * span])


def heads_forward(u, w_heads, shifts):
    rows, wide = u.shape
    outs = w_heads.shape[0]
    taps, blocks, span, _ = shifts.shape
    return pl.pallas_call(
        heads_forward_kernel,
        grid=(taps,),
        in_specs=[
            pl.BlockSpec((rows, wide), lambda t: (0, 0)),
            pl.BlockSpec((outs, wide), lambda t: (0, t)),
            pl.BlockSpec((1, blocks, span, span), lambda t: (t, 0, 0, 0)),
        ],
        out_specs=pl.BlockSpec((rows, outs), lambda t: (0, 0)),
        out_shape=jax.ShapeDtypeStruct((rows, outs), F32),
        compiler_params=params(),
        cost_estimate=cost(2 * rows * wide * outs * taps, w_heads.size * 2 + u.size * 2),
        name="heads_forward",
    )(u, w_heads, shifts)


def shifted(g_ref, s_ref):
    blocks, span = s_ref.shape[1], s_ref.shape[2]
    return jnp.concatenate(
        [
            inner_rows(s_ref[0, k], g_ref[pl.ds(k * span, span), :]).astype(BF16)
            for k in range(blocks)
        ],
        0,
    )


def heads_data_kernel(g_ref, w_ref, s_ref, out_ref, total):
    tap = pl.program_id(0)
    taken = shifted(g_ref, s_ref)
    wide = w_ref.shape[1]
    step = 512

    @pl.when(tap == 0)
    def _():
        total[...] = jnp.zeros_like(total)

    for c in range(0, wide, step):
        total[:, c : c + step] += product(taken, w_ref[:, c : c + step])

    @pl.when(tap == pl.num_programs(0) - 1)
    def _():
        out_ref[...] = total[...].astype(out_ref.dtype)


def heads_data(g, w_heads, shifts):
    rows, outs = g.shape
    taps, blocks, span, _ = shifts.shape
    wide = w_heads.shape[1] // taps
    return pl.pallas_call(
        heads_data_kernel,
        grid=(taps,),
        in_specs=[
            pl.BlockSpec((rows, outs), lambda t: (0, 0)),
            pl.BlockSpec((outs, wide), lambda t: (0, t)),
            pl.BlockSpec((1, blocks, span, span), lambda t: (t, 0, 0, 0)),
        ],
        out_specs=pl.BlockSpec((rows, wide), lambda t: (0, 0)),
        out_shape=jax.ShapeDtypeStruct((rows, wide), BF16),
        scratch_shapes=[pltpu.VMEM((rows, wide), F32)],
        compiler_params=params(),
        cost_estimate=cost(2 * rows * wide * outs * taps, w_heads.size * 2),
        name="heads_data",
    )(g, w_heads, shifts)


def heads_weight_kernel(g_ref, u_ref, s_ref, out_ref):
    taken = shifted(g_ref, s_ref)
    step = 512
    for c in range(0, u_ref.shape[1], step):
        out_ref[:, c : c + step] = inner_rows(taken, u_ref[:, c : c + step]).astype(out_ref.dtype)


def heads_weight(g, u, shifts):
    rows, outs = g.shape
    wide = u.shape[1]
    taps, blocks, span, _ = shifts.shape
    return pl.pallas_call(
        heads_weight_kernel,
        grid=(taps,),
        in_specs=[
            pl.BlockSpec((rows, outs), lambda t: (0, 0)),
            pl.BlockSpec((rows, wide), lambda t: (0, 0)),
            pl.BlockSpec((1, blocks, span, span), lambda t: (t, 0, 0, 0)),
        ],
        out_specs=pl.BlockSpec((outs, wide), lambda t: (0, t)),
        out_shape=jax.ShapeDtypeStruct((outs, taps * wide), BF16),
        compiler_params=params(),
        cost_estimate=cost(2 * rows * wide * outs * taps, outs * taps * wide * 2),
        name="heads_weight",
    )(g, u, shifts)


def rows_forward_kernel(first_ref, u_ref, w_ref, s_ref, out_ref):
    blocks, span = s_ref.shape[1], s_ref.shape[2]

    @pl.when(pl.program_id(0) == 0)
    def _():
        out_ref[...] = jnp.zeros_like(out_ref)

    y = product(u_ref[...], w_ref[...]).astype(BF16)
    for k in range(blocks):
        at = pl.ds(k * span, span)
        out_ref[at, :] += product(s_ref[0, k], y[k * span : (k + 1) * span])


def rows_forward(first, u, w, shifts, halves):
    rows = u.shape[0]
    depth = u.shape[1] // halves
    outs = w.shape[1]
    steps = w.shape[0] // depth
    taps, blocks, span, _ = shifts.shape
    return pl.pallas_call(
        rows_forward_kernel,
        grid_spec=pltpu.PrefetchScalarGridSpec(
            num_scalar_prefetch=1,
            grid=(steps,),
            in_specs=[
                pl.BlockSpec((rows, depth), lambda b, f: (0, (b + f[0]) % halves)),
                pl.BlockSpec((depth, outs), lambda b, f: (b, 0)),
                pl.BlockSpec((1, blocks, span, span), lambda b, f: ((b + f[0]) // halves, 0, 0, 0)),
            ],
            out_specs=pl.BlockSpec((rows, outs), lambda b, f: (0, 0)),
        ),
        out_shape=jax.ShapeDtypeStruct((rows, outs), F32),
        compiler_params=params(),
        cost_estimate=cost(2 * rows * w.size, w.size * 2),
        name="rows_forward",
    )(first, u, w, shifts)


def rows_back_kernel(halves, first_ref, g_ref, u_ref, w_ref, s_ref, du_ref, dw_ref, total):
    step = pl.program_id(0)
    taken = shifted(g_ref, s_ref)
    depth = w_ref.shape[0]
    which = (step + first_ref[0]) % halves

    @pl.when(step == 0)
    def _():
        total[...] = jnp.zeros_like(total)

    total[which] += against(taken, w_ref[...])
    dw_ref[...] = inner_rows(u_ref[...], taken).astype(dw_ref.dtype)

    @pl.when(step == pl.num_programs(0) - 1)
    def _():
        for k in range(halves):
            du_ref[:, k * depth : (k + 1) * depth] = total[k].astype(du_ref.dtype)


def rows_back(first, g, u, w, shifts, halves, kind):
    rows, outs = g.shape
    depth = u.shape[1] // halves
    steps = w.shape[0] // depth
    taps, blocks, span, _ = shifts.shape
    return pl.pallas_call(
        functools.partial(rows_back_kernel, halves),
        grid_spec=pltpu.PrefetchScalarGridSpec(
            num_scalar_prefetch=1,
            grid=(steps,),
            in_specs=[
                pl.BlockSpec((rows, outs), lambda b, f: (0, 0)),
                pl.BlockSpec((rows, depth), lambda b, f: (0, (b + f[0]) % halves)),
                pl.BlockSpec((depth, outs), lambda b, f: (b, 0)),
                pl.BlockSpec((1, blocks, span, span), lambda b, f: ((b + f[0]) // halves, 0, 0, 0)),
            ],
            out_specs=[
                pl.BlockSpec((rows, halves * depth), lambda b, f: (0, 0)),
                pl.BlockSpec((depth, outs), lambda b, f: (b, 0)),
            ],
            scratch_shapes=[pltpu.VMEM((halves, rows, depth), F32)],
        ),
        out_shape=[
            jax.ShapeDtypeStruct((rows, halves * depth), kind),
            jax.ShapeDtypeStruct(w.shape, BF16),
        ],
        compiler_params=params(),
        cost_estimate=cost(4 * rows * w.size, w.size * 4),
        name="rows_back",
    )(first, g, u, w, shifts)


def silu_slope(value_in):
    sigma_of = jax.nn.sigmoid(value_in)
    return sigma_of * (1.0 + value_in * (1.0 - sigma_of))


MESH = pl.DeviceIdType.MESH


def greet(axes):
    barrier = pltpu.get_barrier_semaphore()
    count = 0
    for axis, size in axes:
        me = lax.axis_index(axis)
        for k in range(1, size):
            pl.semaphore_signal(
                barrier, inc=1, device_id={axis: lax.rem(me + k, size)}, device_id_type=MESH
            )
        count += size - 1
    pl.semaphore_wait(barrier, count)


def total_kernel(axes, x_ref, out_ref, *scratch):
    greet(axes)
    block = x_ref
    for number, (axis, size) in enumerate(axes):
        slots, stage, send_sems, recv_sems = scratch[4 * number : 4 * number + 4]
        me = lax.axis_index(axis)
        others = [lax.rem(me + k, size) for k in range(1, size)]
        for other in others:
            pltpu.make_async_remote_copy(
                src_ref=block,
                dst_ref=slots.at[me],
                send_sem=send_sems.at[other],
                recv_sem=recv_sems.at[me],
                device_id={axis: other},
                device_id_type=MESH,
            ).start()
        slots[me] = block[...]
        for other in others:
            copy = pltpu.make_async_remote_copy(
                src_ref=block,
                dst_ref=slots.at[other],
                send_sem=send_sems.at[other],
                recv_sem=recv_sems.at[other],
                device_id={axis: other},
                device_id_type=MESH,
            )
            copy.wait_recv()
            copy.wait_send()
        total = slots[0]
        for k in range(1, size):
            total = total + slots[k]
        if number == len(axes) - 1:
            out_ref[...] = total
        else:
            stage[...] = total
            block = stage


def total_of(left, right, axes):
    width = left.shape[0]
    packed = jnp.concatenate([left, right], 0).reshape(-1, 128)
    sized = tuple((axis, lax.axis_size(axis)) for axis in axes)
    scratch = []
    for _, size in sized:
        scratch += [
            pltpu.VMEM((size,) + packed.shape, F32),
            pltpu.VMEM(packed.shape, F32),
            pltpu.SemaphoreType.DMA((size,)),
            pltpu.SemaphoreType.DMA((size,)),
        ]
    number = 1 + (width != 512) + 2 * (len(axes) == 1)
    summed = pl.pallas_call(
        functools.partial(total_kernel, sized),
        out_shape=jax.ShapeDtypeStruct(packed.shape, F32),
        in_specs=[pl.BlockSpec(memory_space=pltpu.VMEM)],
        out_specs=pl.BlockSpec(memory_space=pltpu.VMEM),
        scratch_shapes=scratch,
        compiler_params=pltpu.CompilerParams(collective_id=number, has_side_effects=True),
        name="total",
    )(packed).reshape(2, width)
    return summed[0], summed[1]


def normalize(raw_value, column_sums, squares, pixel_count, norm_gain, norm_shift):
    center = column_sums / pixel_count
    spread_of = squares / pixel_count - center * center
    scaling = lax.rsqrt(spread_of + EPS)
    unit_value = (raw_value - center) * scaling
    return (unit_value * norm_gain + norm_shift, unit_value, scaling)


def moments(raw_value, living, axes):
    return total_of(
        jnp.sum(living * raw_value, 0), jnp.sum(living * raw_value * raw_value, 0), axes
    )


def norm_back(grad_out, unit_value, scaling, norm_gain, living, pixel_count, axes):
    grad_gain, grad_shift = total_of(
        jnp.sum(living * grad_out * unit_value, 0), jnp.sum(living * grad_out, 0), axes
    )
    grad_raw = (
        living
        * (norm_gain * scaling)
        * (grad_out - grad_shift / pixel_count - unit_value * grad_gain / pixel_count)
    )
    return (grad_raw, grad_gain, grad_shift)


def swap(value, bit):
    return lax.ppermute(value, "rep", [(k, k ^ bit) for k in range(4)])


def scatter_rep(value):
    return lax.psum_scatter(value.astype(BF16), "rep", scatter_dimension=0, tiled=True)


def total_dp(value):
    parts = lax.axis_size("dp")
    rows = value.shape[0]
    padded = -(-rows // (8 * parts)) * 8 * parts
    value = jnp.pad(value, ((0, padded - rows), (0, 0)))
    share = lax.psum_scatter(value, "dp", scatter_dimension=0, tiled=True)
    return lax.all_gather(share, "dp", axis=0, tiled=True)[:rows].astype(F32)


def shards(
    inputs,
    layout,
    labels,
    cot_depth,
    w_reduce,
    w_spatial,
    w_expand,
    w_heads,
    w_gates,
    w_messages,
    w_classes,
    gain_mid,
    shift_mid,
    gain_wide,
    shift_wide,
    gain_head,
    shift_head,
):
    pixels = inputs.shape[0]
    middle = w_reduce.shape[1]
    classes = w_classes.shape[1]
    group = lax.axis_size("rep")
    everyone = ("rep", "dp")
    rep = lax.axis_index("rep")
    parity = rep % 2
    upper = rep // 2
    first_row = lax.axis_index("dp") * group
    own_info = geometry(lax.dynamic_slice_in_dim(layout, first_row + rep, 1, 0), pixels)
    group_info = geometry(lax.dynamic_slice_in_dim(layout, first_row, group, 0), pixels)
    living = own_info[2][0].astype(F32)[:, None]
    group_living = group_info[2].astype(F32)
    living_all = group_living.reshape(group * pixels, 1)
    pixel_count = jnp.sum(
        jnp.minimum(layout[:, 0] * layout[:, 1] * layout[:, 2], pixels)
    ).astype(F32)
    shifts_own = shift_matrices(own_info, 2)
    shifts_all = shift_matrices(group_info, 1)
    zero = jnp.zeros((1,), jnp.int32)
    first = jnp.reshape(9 * parity, (1,)).astype(jnp.int32)

    reduced = product(inputs, w_reduce)
    sums_one, squares_one = moments(reduced, living, everyone)
    normed_one, unit_one, scale_one = normalize(
        reduced, sums_one, squares_one, pixel_count, gain_mid[0], shift_mid[0]
    )
    hidden_one = jax.nn.silu(normed_one).astype(BF16)
    spatial = rows_forward(zero, hidden_one, w_spatial, shifts_own, 1)
    sums_two, squares_two = moments(spatial, living, everyone)
    normed_two, unit_two, scale_two = normalize(
        spatial, sums_two, squares_two, pixel_count, gain_mid[1], shift_mid[1]
    )
    hidden_two = jax.nn.silu(normed_two).astype(BF16)
    expanded = product(hidden_two, w_expand)
    sums_three, squares_three = moments(expanded, living, everyone)
    normed_three, unit_three, scale_three = normalize(
        expanded, sums_three, squares_three, pixel_count, gain_wide, shift_wide
    )
    pre_act = normed_three + inputs.astype(F32)
    trunk = jax.nn.silu(pre_act).astype(BF16)
    trunk_all = lax.all_gather(trunk, "rep", axis=0, tiled=True)

    headed = heads_forward(trunk_all, w_heads, shifts_all)
    own_gain = lax.dynamic_slice_in_dim(gain_head, rep * middle, middle, 0)
    own_shift = lax.dynamic_slice_in_dim(shift_head, rep * middle, middle, 0)
    sums_head, squares_head = moments(headed, living_all, ("dp",))
    normed_head, unit_head, scale_head = normalize(
        headed, sums_head, squares_head, pixel_count, own_gain, own_shift
    )
    rounded = jax.nn.silu(normed_head).astype(BF16)
    heads_all = lax.all_gather(rounded, "rep", axis=0, tiled=False)

    is_depth = upper == 0
    source = jnp.where(
        is_depth,
        jnp.concatenate([heads_all[1], heads_all[2], heads_all[3]], 1),
        jnp.concatenate([heads_all[0], heads_all[1], heads_all[2]], 1),
    )
    partial = rows_forward(first, source, w_messages, shifts_all, 2).reshape(
        2, 2, pixels, middle
    )

    def of_parity(value, which):
        return lax.dynamic_index_in_dim(value, which, 1, keepdims=False)

    def rows_of(value):
        return value.reshape(2 * pixels, value.shape[-1])

    message = rows_of(of_parity(partial, parity) + swap(of_parity(partial, 1 - parity), 1))
    stream = rows_of(
        of_parity(
            jnp.where(is_depth, heads_all[0], heads_all[3]).reshape(2, 2, pixels, middle), parity
        )
    )
    own_gates = lax.dynamic_slice_in_dim(w_gates, upper * middle, middle, 0)
    stream_living = rows_of(of_parity(group_living.reshape(2, 2, pixels, 1), parity))
    cot_other = swap(cot_depth, 2)
    labels_other = swap(labels, 2)
    stream_cot = jnp.concatenate([cot_depth, cot_other], 0).astype(F32)
    stream_labels = jnp.concatenate([labels_other, labels], 0)
    gate = jax.nn.sigmoid(product(stream, own_gates))
    full = stream.astype(F32) + gate * message
    full_low = full.astype(BF16)
    logits_full = product(full_low, w_classes)
    probs = jax.nn.softmax(logits_full, axis=1)
    onehot_table = (
        stream_labels[:, None] == jnp.arange(classes, dtype=jnp.int32)[None, :]
    ).astype(F32)
    grad_logits = (stream_living * (probs - onehot_table)).astype(BF16)
    classes_local = inner_rows(full_low, jnp.where(is_depth, 0.0, 1.0).astype(BF16) * grad_logits)
    grad_stream = jnp.where(
        is_depth, stream_living * stream_cot, against(grad_logits, w_classes)
    )
    depth_other = swap(full[pixels:], 2)
    logits_other = swap(logits_full[:pixels], 2)
    depth = living * jnp.where(is_depth, full[:pixels], depth_other)
    logits = living * jnp.where(is_depth, logits_other, logits_full[pixels:])
    grad_gate = (grad_stream * message * gate * (1.0 - gate)).astype(BF16)
    grad_message = (grad_stream * gate).astype(BF16)
    gates_local = inner_rows(stream, grad_gate).astype(BF16)
    gates_local = gates_local.reshape(2, pixels, middle)
    gates_share = lax.dynamic_index_in_dim(gates_local, parity, 0, keepdims=False).astype(
        F32
    ) + swap(lax.dynamic_index_in_dim(gates_local, 1 - parity, 0, keepdims=False), 1).astype(F32)
    direct = (grad_stream + against(grad_gate, own_gates)).astype(BF16)

    def both_parities(value, other):
        value = value.reshape(2, pixels, middle)
        other = other.reshape(2, pixels, middle)
        even = jnp.where(parity == 0, value, other)
        odd = jnp.where(parity == 0, other, value)
        return jnp.stack([even, odd], 1).reshape(4 * pixels, middle)

    message_all = both_parities(grad_message, swap(grad_message, 1))
    direct_all = both_parities(direct, jnp.zeros_like(direct))
    source_grad, messages_local = rows_back(
        first, message_all, source, w_messages, shifts_all, 2, BF16
    )
    thirds = [source_grad[:, k * middle : (k + 1) * middle] for k in range(3)]
    by_head = jnp.stack(
        [
            jnp.where(is_depth, direct_all, thirds[0]),
            jnp.where(is_depth, thirds[0], thirds[1]),
            jnp.where(is_depth, thirds[1], thirds[2]),
            jnp.where(is_depth, thirds[2], direct_all),
        ],
        0,
    )
    feat_grad = lax.psum_scatter(by_head, "rep", scatter_dimension=0, tiled=False).astype(F32)
    grad_messages = lax.psum_scatter(messages_local, "dp", scatter_dimension=1, tiled=True)
    head_raw, gain_grad_head, shift_grad_head = norm_back(
        feat_grad * silu_slope(normed_head),
        unit_head,
        scale_head,
        own_gain,
        living_all,
        pixel_count,
        ("dp",),
    )
    head_low = head_raw.astype(BF16)
    heads_local = heads_weight(head_low, trunk_all, shifts_all)
    head_low, heads_local = lax.optimization_barrier((head_low, heads_local))
    grad_heads = lax.psum_scatter(heads_local, "dp", scatter_dimension=1, tiled=True)
    trunk_grad = lax.psum_scatter(
        heads_data(head_low, w_heads, shifts_all), "rep", scatter_dimension=0, tiled=True
    ).astype(F32)
    pre_grad = trunk_grad * silu_slope(pre_act)
    expand_raw, grad_gain_wide, grad_shift_wide = norm_back(
        pre_grad, unit_three, scale_three, gain_wide, living, pixel_count, everyone
    )
    expand_low = expand_raw.astype(BF16)
    grad_expand = scatter_rep(inner_rows(hidden_two, expand_low))
    hidden_two_grad = against(expand_low, w_expand)
    spatial_raw, gain_grad_two, shift_grad_two = norm_back(
        hidden_two_grad * silu_slope(normed_two),
        unit_two,
        scale_two,
        gain_mid[1],
        living,
        pixel_count,
        everyone,
    )
    spatial_low = spatial_raw.astype(BF16)
    hidden_one_grad, spatial_local = rows_back(
        zero, spatial_low, hidden_one, w_spatial, shifts_own, 1, F32
    )
    grad_spatial = scatter_rep(spatial_local)
    reduced_raw, gain_grad_one, shift_grad_one = norm_back(
        hidden_one_grad * silu_slope(normed_one),
        unit_one,
        scale_one,
        gain_mid[0],
        living,
        pixel_count,
        everyone,
    )
    reduced_low = reduced_raw.astype(BF16)
    grad_reduce = scatter_rep(inner_rows(inputs, reduced_low))
    input_grad = pre_grad + against(reduced_low, w_reduce)
    grad_classes = scatter_rep(classes_local)
    pieces = [
        gates_share.astype(BF16),
        grad_expand.reshape(-1, middle),
        grad_spatial,
        grad_classes.reshape(-1, middle),
    ]
    early = total_dp(jnp.concatenate(pieces, 0))
    rows = [piece.shape[0] for piece in pieces]
    starts = [sum(rows[:k]) for k in range(4)]
    grad_gates, expand_sum, grad_spatial, classes_sum = [
        early[at : at + size] for at, size in zip(starts, rows)
    ]
    grad_expand = expand_sum.reshape(grad_expand.shape)
    grad_classes = classes_sum.reshape(grad_classes.shape)
    grad_reduce = total_dp(grad_reduce)
    grad_gain_mid = jnp.stack([gain_grad_one, gain_grad_two], 0)
    grad_shift_mid = jnp.stack([shift_grad_one, shift_grad_two], 0)
    head_norms = lax.all_gather(
        jnp.stack([gain_grad_head, shift_grad_head], 0), "rep", axis=1, tiled=True
    )
    return (
        depth,
        logits,
        input_grad,
        grad_reduce,
        grad_spatial,
        grad_expand,
        grad_heads.astype(F32),
        grad_gates,
        grad_messages.astype(F32),
        grad_classes,
        grad_gain_mid,
        grad_shift_mid,
        grad_gain_wide,
        grad_shift_wide,
        head_norms[0],
        head_norms[1],
    )


def solution(mesh):
    in_specs = (
        P(("dp", "rep"), None),
        P(),
        P(("dp", "rep")),
        P(("dp", "rep"), None),
        P(),
        P(),
        P(),
        P("rep", None),
        P(),
        P("rep", None),
        P(),
        P(),
        P(),
        P(),
        P(),
        P(),
        P(),
    )
    out_specs = (
        P(("dp", "rep"), None),
        P(("dp", "rep"), None),
        P(("dp", "rep"), None),
        P("rep", None),
        P("rep", None),
        P("rep", None),
        P("rep", "dp"),
        P("rep", None),
        P("rep", "dp"),
        P("rep", None),
        P(),
        P(),
        P(),
        P(),
        P(),
        P(),
    )
    return jax.shard_map(shards, mesh=mesh, in_specs=in_specs, out_specs=out_specs, check_vma=False)
```

```python
import functools

import jax
import jax.numpy as jnp
from jax import lax
from jax.experimental import pallas as pl
from jax.experimental.pallas import tpu as pltpu
from jax.sharding import PartitionSpec as P

EPS = 1e-05
F32 = jnp.float32
BF16 = jnp.bfloat16
VMEM_LIMIT = 60 * 2**20


def geometry(layout, span):
    position = jnp.arange(span, dtype=jnp.int32)
    height = layout[:, 0:1]
    map_width = layout[:, 1:2]
    images = layout[:, 2:3]
    map_area = height * map_width
    inside = position[None, :] % map_area
    row_of = inside // map_width
    col_of = inside % map_width
    living = position[None, :] < images * map_area
    return (row_of, col_of, living, height, map_width)


def shift_matrices(shape_info, dilation):
    row_of, col_of, living, height, map_width = shape_info
    span = row_of.shape[1]
    position = jnp.arange(span, dtype=jnp.int32)
    every = []
    for step_row in (-1, 0, 1):
        for step_col in (-1, 0, 1):
            target_row = row_of + dilation * step_row
            target_col = col_of + dilation * step_col
            inside = (
                living
                & (target_row >= 0)
                & (target_row < height)
                & (target_col >= 0)
                & (target_col < map_width)
            )
            neighbour = position[None, :] + dilation * (step_row * map_width + step_col)
            picked = jnp.where(inside, neighbour, -1)
            every.append(picked[:, :, None] == position[None, None, :])
    return jnp.stack(every, 0).astype(BF16)


def product(left_side, right_side):
    return jnp.dot(left_side, right_side, preferred_element_type=F32)


def inner_rows(left_side, right_side):
    return lax.dot_general(
        left_side, right_side, (((0,), (0,)), ((), ())), preferred_element_type=F32
    )


def against(left_side, right_side):
    return lax.dot_general(
        left_side, right_side, (((1,), (1,)), ((), ())), preferred_element_type=F32
    )


def params():
    return pltpu.CompilerParams(vmem_limit_bytes=VMEM_LIMIT)


def cost(flops, moved):
    return pl.CostEstimate(flops=flops, bytes_accessed=moved, transcendentals=0)


def heads_forward_kernel(u_ref, w_ref, s_ref, out_ref):
    tap = pl.program_id(0)
    blocks, span = s_ref.shape[1], s_ref.shape[2]
    half = blocks // 2

    @pl.when(tap == 0)
    def _():
        out_ref[...] = jnp.zeros_like(out_ref)

    @pl.loop(0, 2)
    def _(part):
        rows = pl.ds(pl.multiple_of(part * half * span, half * span), half * span)
        y = against(u_ref[rows, :], w_ref[...]).astype(BF16)
        for k in range(half):
            at = pl.ds(pl.multiple_of((part * half + k) * span, span), span)
            out_ref[at, :] += product(s_ref[0, part * half + k], y[k * span : (k + 1) * span])


def heads_forward(u, w_heads, shifts):
    rows, wide = u.shape
    outs = w_heads.shape[0]
    taps, blocks, span, _ = shifts.shape
    return pl.pallas_call(
        heads_forward_kernel,
        grid=(taps,),
        in_specs=[
            pl.BlockSpec((rows, wide), lambda t: (0, 0)),
            pl.BlockSpec((outs, wide), lambda t: (0, t)),
            pl.BlockSpec((1, blocks, span, span), lambda t: (t, 0, 0, 0)),
        ],
        out_specs=pl.BlockSpec((rows, outs), lambda t: (0, 0)),
        out_shape=jax.ShapeDtypeStruct((rows, outs), F32),
        compiler_params=params(),
        cost_estimate=cost(2 * rows * wide * outs * taps, w_heads.size * 2 + u.size * 2),
        name="heads_forward",
    )(u, w_heads, shifts)


def shifted(g_ref, s_ref):
    blocks, span = s_ref.shape[1], s_ref.shape[2]
    return jnp.concatenate(
        [
            inner_rows(s_ref[0, k], g_ref[pl.ds(k * span, span), :]).astype(BF16)
            for k in range(blocks)
        ],
        0,
    )


def heads_data_kernel(g_ref, w_ref, s_ref, out_ref, total):
    tap = pl.program_id(0)
    taken = shifted(g_ref, s_ref)
    wide = w_ref.shape[1]
    step = 512

    @pl.when(tap == 0)
    def _():
        total[...] = jnp.zeros_like(total)

    for c in range(0, wide, step):
        total[:, c : c + step] += product(taken, w_ref[:, c : c + step])

    @pl.when(tap == pl.num_programs(0) - 1)
    def _():
        out_ref[...] = total[...].astype(out_ref.dtype)


def heads_data(g, w_heads, shifts):
    rows, outs = g.shape
    taps, blocks, span, _ = shifts.shape
    wide = w_heads.shape[1] // taps
    return pl.pallas_call(
        heads_data_kernel,
        grid=(taps,),
        in_specs=[
            pl.BlockSpec((rows, outs), lambda t: (0, 0)),
            pl.BlockSpec((outs, wide), lambda t: (0, t)),
            pl.BlockSpec((1, blocks, span, span), lambda t: (t, 0, 0, 0)),
        ],
        out_specs=pl.BlockSpec((rows, wide), lambda t: (0, 0)),
        out_shape=jax.ShapeDtypeStruct((rows, wide), BF16),
        scratch_shapes=[pltpu.VMEM((rows, wide), F32)],
        compiler_params=params(),
        cost_estimate=cost(2 * rows * wide * outs * taps, w_heads.size * 2),
        name="heads_data",
    )(g, w_heads, shifts)


def heads_weight_kernel(g_ref, u_ref, s_ref, out_ref):
    taken = shifted(g_ref, s_ref)
    step = 512
    for c in range(0, u_ref.shape[1], step):
        out_ref[:, c : c + step] = inner_rows(taken, u_ref[:, c : c + step]).astype(out_ref.dtype)


def heads_weight(g, u, shifts):
    rows, outs = g.shape
    wide = u.shape[1]
    taps, blocks, span, _ = shifts.shape
    return pl.pallas_call(
        heads_weight_kernel,
        grid=(taps,),
        in_specs=[
            pl.BlockSpec((rows, outs), lambda t: (0, 0)),
            pl.BlockSpec((rows, wide), lambda t: (0, 0)),
            pl.BlockSpec((1, blocks, span, span), lambda t: (t, 0, 0, 0)),
        ],
        out_specs=pl.BlockSpec((outs, wide), lambda t: (0, t)),
        out_shape=jax.ShapeDtypeStruct((outs, taps * wide), BF16),
        compiler_params=params(),
        cost_estimate=cost(2 * rows * wide * outs * taps, outs * taps * wide * 2),
        name="heads_weight",
    )(g, u, shifts)


def rows_forward_kernel(first_ref, u_ref, w_ref, s_ref, out_ref):
    blocks, span = s_ref.shape[1], s_ref.shape[2]

    @pl.when(pl.program_id(0) == 0)
    def _():
        out_ref[...] = jnp.zeros_like(out_ref)

    y = product(u_ref[...], w_ref[...]).astype(BF16)
    for k in range(blocks):
        at = pl.ds(k * span, span)
        out_ref[at, :] += product(s_ref[0, k], y[k * span : (k + 1) * span])


def rows_forward(first, u, w, shifts, halves):
    rows = u.shape[0]
    depth = u.shape[1] // halves
    outs = w.shape[1]
    steps = w.shape[0] // depth
    taps, blocks, span, _ = shifts.shape
    return pl.pallas_call(
        rows_forward_kernel,
        grid_spec=pltpu.PrefetchScalarGridSpec(
            num_scalar_prefetch=1,
            grid=(steps,),
            in_specs=[
                pl.BlockSpec((rows, depth), lambda b, f: (0, (b + f[0]) % halves)),
                pl.BlockSpec((depth, outs), lambda b, f: (b, 0)),
                pl.BlockSpec((1, blocks, span, span), lambda b, f: ((b + f[0]) // halves, 0, 0, 0)),
            ],
            out_specs=pl.BlockSpec((rows, outs), lambda b, f: (0, 0)),
        ),
        out_shape=jax.ShapeDtypeStruct((rows, outs), F32),
        compiler_params=params(),
        cost_estimate=cost(2 * rows * w.size, w.size * 2),
        name="rows_forward",
    )(first, u, w, shifts)


def rows_back_kernel(halves, first_ref, g_ref, u_ref, w_ref, s_ref, du_ref, dw_ref, total):
    step = pl.program_id(0)
    taken = shifted(g_ref, s_ref)
    depth = w_ref.shape[0]
    which = (step + first_ref[0]) % halves

    @pl.when(step == 0)
    def _():
        total[...] = jnp.zeros_like(total)

    total[which] += against(taken, w_ref[...])
    dw_ref[...] = inner_rows(u_ref[...], taken).astype(dw_ref.dtype)

    @pl.when(step == pl.num_programs(0) - 1)
    def _():
        for k in range(halves):
            du_ref[:, k * depth : (k + 1) * depth] = total[k].astype(du_ref.dtype)


def rows_back(first, g, u, w, shifts, halves, kind):
    rows, outs = g.shape
    depth = u.shape[1] // halves
    steps = w.shape[0] // depth
    taps, blocks, span, _ = shifts.shape
    return pl.pallas_call(
        functools.partial(rows_back_kernel, halves),
        grid_spec=pltpu.PrefetchScalarGridSpec(
            num_scalar_prefetch=1,
            grid=(steps,),
            in_specs=[
                pl.BlockSpec((rows, outs), lambda b, f: (0, 0)),
                pl.BlockSpec((rows, depth), lambda b, f: (0, (b + f[0]) % halves)),
                pl.BlockSpec((depth, outs), lambda b, f: (b, 0)),
                pl.BlockSpec((1, blocks, span, span), lambda b, f: ((b + f[0]) // halves, 0, 0, 0)),
            ],
            out_specs=[
                pl.BlockSpec((rows, halves * depth), lambda b, f: (0, 0)),
                pl.BlockSpec((depth, outs), lambda b, f: (b, 0)),
            ],
            scratch_shapes=[pltpu.VMEM((halves, rows, depth), F32)],
        ),
        out_shape=[
            jax.ShapeDtypeStruct((rows, halves * depth), kind),
            jax.ShapeDtypeStruct(w.shape, BF16),
        ],
        compiler_params=params(),
        cost_estimate=cost(4 * rows * w.size, w.size * 4),
        name="rows_back",
    )(first, g, u, w, shifts)


def heads_split_kernel(per_tap, units, lanes, x_ref, g_ref, h_ref, u_ref, v_ref, s_ref, r_ref, out_ref, taken):
    blocks, span = s_ref.shape[1], s_ref.shape[2]
    rows = blocks * span
    start = units * (2 * pl.program_id(0) + x_ref[0])

    @pl.loop(0, units)
    def _(unit):
        tap, chunk = (start + unit) // per_tap, (start + unit) % per_tap

        @pl.when((unit == 0) | (chunk == 0))
        def _():
            for side, (a_ref, m_ref) in enumerate(((g_ref, s_ref), (h_ref, r_ref))):
                for k in range(blocks):
                    at = (side * blocks + k) * span
                    taken[:, at : at + span] = inner_rows(
                        a_ref[k * span : (k + 1) * span, :], m_ref[tap, k]
                    ).astype(BF16)

        at = pl.ds(pl.multiple_of(chunk * lanes, lanes), lanes)
        to = pl.ds(pl.multiple_of(unit * lanes, lanes), lanes)
        out_ref[0, :, to] = (
            product(taken[:, :rows], u_ref[:, at]) + product(taken[:, rows:], v_ref[:, at])
        ).astype(BF16)


def heads_split(x, g, h, u, v, s, r, shards, lanes):
    rows, outs = g.shape
    wide = u.shape[1]
    taps, blocks, span, _ = s.shape
    units = taps * wide // (2 * shards * lanes)
    per_tap = wide // lanes
    whole = pl.BlockSpec(memory_space=pltpu.VMEM)
    return pl.pallas_call(
        functools.partial(heads_split_kernel, per_tap, units, lanes),
        grid_spec=pltpu.PrefetchScalarGridSpec(
            num_scalar_prefetch=1,
            grid=(shards,),
            in_specs=[whole] * 6,
            out_specs=pl.BlockSpec((1, outs, units * lanes), lambda i, f: (i, 0, 0)),
            scratch_shapes=[pltpu.VMEM((outs, 2 * rows), BF16)],
        ),
        out_shape=jax.ShapeDtypeStruct((shards, outs, units * lanes), BF16),
        compiler_params=params(),
        cost_estimate=cost(2 * rows * wide * outs * taps, outs * taps * wide * 2),
        name="heads_split",
    )(x, g, h, u, v, s, r)


def rows_split_kernel(first_ref, g_ref, h_ref, u_ref, v_ref, s_ref, r_ref, out_ref):
    blocks, span = s_ref.shape[1], s_ref.shape[2]
    total = 0.0
    for a_ref, b_ref, m_ref in ((g_ref, u_ref, s_ref), (h_ref, v_ref, r_ref)):
        taken = jnp.concatenate(
            [
                inner_rows(a_ref[k * span : (k + 1) * span, :], m_ref[0, k]).astype(BF16)
                for k in range(blocks)
            ],
            1,
        )
        total = total + product(taken, b_ref[...])
    out_ref[...] = total.astype(BF16)


def rows_split(first, g, h, u, v, s, r, halves, steps):
    rows, outs = g.shape
    depth = u.shape[1] // halves
    taps, blocks, span, _ = s.shape
    side = pl.BlockSpec((rows, outs), lambda b, f: (0, 0))
    values = pl.BlockSpec((rows, depth), lambda b, f: (0, (b + f[0]) % halves))
    picks = pl.BlockSpec((1, blocks, span, span), lambda b, f: ((b + f[0]) // halves, 0, 0, 0))
    return pl.pallas_call(
        rows_split_kernel,
        grid_spec=pltpu.PrefetchScalarGridSpec(
            num_scalar_prefetch=1,
            grid=(steps,),
            in_specs=[side, side, values, values, picks, picks],
            out_specs=pl.BlockSpec((outs, depth), lambda b, f: (0, b)),
        ),
        out_shape=jax.ShapeDtypeStruct((outs, steps * depth), BF16),
        compiler_params=params(),
        cost_estimate=cost(4 * rows * outs * steps * depth, outs * steps * depth * 2),
        name="rows_split",
    )(first, g, h, u, v, s, r)


def rows_data_kernel(halves, first_ref, g_ref, w_ref, s_ref, du_ref, total):
    step = pl.program_id(0)
    depth = w_ref.shape[0]
    which = (step + first_ref[0]) % halves

    @pl.when(step == 0)
    def _():
        total[...] = jnp.zeros_like(total)

    total[which] += against(shifted(g_ref, s_ref), w_ref[...])

    @pl.when(step == pl.num_programs(0) - 1)
    def _():
        for k in range(halves):
            du_ref[:, k * depth : (k + 1) * depth] = total[k].astype(du_ref.dtype)


def rows_data(first, g, w, shifts, halves, depth):
    rows, outs = g.shape
    steps = w.shape[0] // depth
    taps, blocks, span, _ = shifts.shape
    return pl.pallas_call(
        functools.partial(rows_data_kernel, halves),
        grid_spec=pltpu.PrefetchScalarGridSpec(
            num_scalar_prefetch=1,
            grid=(steps,),
            in_specs=[
                pl.BlockSpec((rows, outs), lambda b, f: (0, 0)),
                pl.BlockSpec((depth, outs), lambda b, f: (b, 0)),
                pl.BlockSpec((1, blocks, span, span), lambda b, f: ((b + f[0]) // halves, 0, 0, 0)),
            ],
            out_specs=pl.BlockSpec((rows, halves * depth), lambda b, f: (0, 0)),
            scratch_shapes=[pltpu.VMEM((halves, rows, depth), F32)],
        ),
        out_shape=jax.ShapeDtypeStruct((rows, halves * depth), BF16),
        compiler_params=params(),
        cost_estimate=cost(2 * rows * w.size, w.size * 2),
        name="rows_data",
    )(first, g, w, shifts)


CHUNKS = 4


def small_kernel(p_ref, out_ref, half_ref, core_in, core_out, y_in, x_out, x_in, z_out, z_in, send, recv):
    rep, dp = lax.axis_index("rep"), lax.axis_index("dp")
    par, upper = lax.rem(rep, 2), rep // 2
    x, z = lax.rem(dp, 2), dp // 2
    mate, far, beside = rep + 1 - 2 * par, rep + 2 - 4 * upper, dp + 1 - 2 * x
    zs = [lax.rem(z + k, 4) for k in range(1, 4)]
    barrier = pltpu.get_barrier_semaphore()
    partners = [{"rep": mate}, {"rep": far}, {"dp": beside}] + [{"dp": 2 * k + x} for k in zs]
    for partner in partners:
        pl.semaphore_signal(barrier, inc=1, device_id=partner, device_id_type=MESH)
    pl.semaphore_wait(barrier, len(partners))
    rows = p_ref.shape[1] // CHUNKS
    half, eighth = rows // 2, rows // 8

    def span(c, at=0, size=rows):
        return pl.ds(pl.multiple_of(c * rows + at, 16), size)

    def remote(src, dst, c, slot, to, slot_in=None):
        return pltpu.make_async_remote_copy(
            src_ref=src,
            dst_ref=dst,
            send_sem=send.at[c, slot],
            recv_sem=recv.at[c, slot if slot_in is None else slot_in],
            device_id=to,
            device_id_type=MESH,
        )

    def core_copy(c, hi):
        return remote(
            p_ref.at[2 * hi + 1 - par, span(c)], core_in.at[hi, span(c)], c, hi, {"rep": mate}
        )

    def y_copy(c):
        return remote(core_out.at[span(c)], y_in.at[span(c)], c, 2, {"rep": far})

    def x_copy(c):
        return remote(
            x_out.at[pl.ds(c * half, half)], x_in.at[pl.ds(c * half, half)], c, 3, {"dp": beside}
        )

    def z_copy(c, k, incoming):
        sent = pl.ds(pl.multiple_of(c * half + k * eighth, 16), eighth)
        slot = k if incoming else z
        return remote(
            z_out.at[sent], z_in.at[slot, pl.ds(c * eighth, eighth)], c, 4 + k, {"dp": 2 * k + x}, 4 + slot
        )

    def back_copy(c, k, incoming):
        place = span(c, x * half + (k if incoming else z) * eighth, eighth)
        return remote(
            half_ref.at[place], half_ref.at[place], c, 8 + k, {"dp": 2 * k + x}, 8 + (k if incoming else z)
        )

    def last_copy(c, incoming):
        place = span(c, (1 - x if incoming else x) * half, half)
        return remote(half_ref.at[place], half_ref.at[place], c, 12, {"dp": beside})

    def step(stage, c):
        if stage == 0:
            for hi in range(2):
                core_copy(c, hi).start()
        elif stage == 1:
            for hi in range(2):
                core_copy(c, hi).wait_recv()
            core_out[span(c)] = (
                p_ref[2 * (1 - upper) + par, span(c)].astype(F32)
                + core_in[1 - upper, span(c)].astype(F32)
            ).astype(BF16)
            y_copy(c).start()
        elif stage == 2:
            y_copy(c).wait_recv()

            def both(at):
                place = span(c, at, half)
                return (
                    p_ref[rep, place].astype(F32)
                    + core_in[upper, place].astype(F32)
                    + y_in[place].astype(F32)
                )

            x_out[pl.ds(c * half, half)] = both((1 - x) * half).astype(BF16)
            x_copy(c).start()
            z_out[pl.ds(c * half, half)] = both(x * half).astype(BF16)
        elif stage == 3:
            x_copy(c).wait_recv()
            at = pl.ds(c * half, half)
            z_out[at] = (z_out[at].astype(F32) + x_in[at].astype(F32)).astype(BF16)
            for k in zs:
                z_copy(c, k, False).start()
        elif stage == 4:
            for k in zs:
                z_copy(c, k, True).wait_recv()
            z_in[z, pl.ds(c * eighth, eighth)] = z_out[
                pl.ds(pl.multiple_of(c * half + z * eighth, 16), eighth)
            ]
            total = z_in[0, pl.ds(c * eighth, eighth)].astype(F32)
            for k in range(1, 4):
                total = total + z_in[k, pl.ds(c * eighth, eighth)].astype(F32)
            half_ref[span(c, x * half + z * eighth, eighth)] = total.astype(BF16)
            for k in zs:
                back_copy(c, k, False).start()
        elif stage == 5:
            for k in zs:
                back_copy(c, k, True).wait_recv()
            last_copy(c, False).start()
        else:
            last_copy(c, True).wait_recv()
            out_ref[span(c)] = half_ref[span(c)].astype(F32)
            for hi in range(2):
                core_copy(c, hi).wait_send()
            y_copy(c).wait_send()
            x_copy(c).wait_send()
            for k in zs:
                z_copy(c, k, False).wait_send()
                back_copy(c, k, False).wait_send()
            last_copy(c, False).wait_send()

    for turn in range(CHUNKS + 6):
        for c in range(CHUNKS):
            if 0 <= turn - c <= 6:
                step(turn - c, c)


def small_total(parts):
    quarters, rows, lanes = parts.shape
    return pl.pallas_call(
        small_kernel,
        out_shape=jax.ShapeDtypeStruct((rows, lanes), F32),
        in_specs=[pl.BlockSpec(memory_space=pltpu.VMEM)],
        out_specs=pl.BlockSpec(memory_space=pltpu.VMEM),
        scratch_shapes=[
            pltpu.VMEM((rows, lanes), BF16),
            pltpu.VMEM((2, rows, lanes), BF16),
            pltpu.VMEM((rows, lanes), BF16),
            pltpu.VMEM((rows, lanes), BF16),
            pltpu.VMEM((rows // 2, lanes), BF16),
            pltpu.VMEM((rows // 2, lanes), BF16),
            pltpu.VMEM((rows // 2, lanes), BF16),
            pltpu.VMEM((4, rows // 8, lanes), BF16),
            pltpu.SemaphoreType.DMA((CHUNKS, 13)),
            pltpu.SemaphoreType.DMA((CHUNKS, 13)),
        ],
        compiler_params=pltpu.CompilerParams(
            collective_id=9, has_side_effects=True, vmem_limit_bytes=VMEM_LIMIT
        ),
        name="small_total",
    )(parts)


def silu_slope(value_in):
    sigma_of = jax.nn.sigmoid(value_in)
    return sigma_of * (1.0 + value_in * (1.0 - sigma_of))


MESH = pl.DeviceIdType.MESH


def greet(axes):
    barrier = pltpu.get_barrier_semaphore()
    count = 0
    for axis, size in axes:
        me = lax.axis_index(axis)
        for k in range(1, size):
            pl.semaphore_signal(
                barrier, inc=1, device_id={axis: lax.rem(me + k, size)}, device_id_type=MESH
            )
        count += size - 1
    pl.semaphore_wait(barrier, count)


def total_kernel(axes, x_ref, out_ref, *scratch):
    greet(axes)
    block = x_ref
    for number, (axis, size) in enumerate(axes):
        slots, stage, send_sems, recv_sems = scratch[4 * number : 4 * number + 4]
        me = lax.axis_index(axis)
        others = [lax.rem(me + k, size) for k in range(1, size)]
        for other in others:
            pltpu.make_async_remote_copy(
                src_ref=block,
                dst_ref=slots.at[me],
                send_sem=send_sems.at[other],
                recv_sem=recv_sems.at[me],
                device_id={axis: other},
                device_id_type=MESH,
            ).start()
        slots[me] = block[...]
        for other in others:
            copy = pltpu.make_async_remote_copy(
                src_ref=block,
                dst_ref=slots.at[other],
                send_sem=send_sems.at[other],
                recv_sem=recv_sems.at[other],
                device_id={axis: other},
                device_id_type=MESH,
            )
            copy.wait_recv()
            copy.wait_send()
        total = slots[0]
        for k in range(1, size):
            total = total + slots[k]
        if number == len(axes) - 1:
            out_ref[...] = total
        else:
            stage[...] = total
            block = stage


def total_of(left, right, axes):
    width = left.shape[0]
    packed = jnp.concatenate([left, right], 0).reshape(-1, 128)
    sized = tuple((axis, lax.axis_size(axis)) for axis in axes)
    scratch = []
    for _, size in sized:
        scratch += [
            pltpu.VMEM((size,) + packed.shape, F32),
            pltpu.VMEM(packed.shape, F32),
            pltpu.SemaphoreType.DMA((size,)),
            pltpu.SemaphoreType.DMA((size,)),
        ]
    number = 1 + (width != 512) + 2 * (len(axes) == 1)
    summed = pl.pallas_call(
        functools.partial(total_kernel, sized),
        out_shape=jax.ShapeDtypeStruct(packed.shape, F32),
        in_specs=[pl.BlockSpec(memory_space=pltpu.VMEM)],
        out_specs=pl.BlockSpec(memory_space=pltpu.VMEM),
        scratch_shapes=scratch,
        compiler_params=pltpu.CompilerParams(collective_id=number, has_side_effects=True),
        name="total",
    )(packed).reshape(2, width)
    return summed[0], summed[1]


def normalize(raw_value, column_sums, squares, pixel_count, norm_gain, norm_shift):
    center = column_sums / pixel_count
    spread_of = squares / pixel_count - center * center
    scaling = lax.rsqrt(spread_of + EPS)
    unit_value = (raw_value - center) * scaling
    return (unit_value * norm_gain + norm_shift, unit_value, scaling)


def moments(raw_value, living, axes):
    return total_of(
        jnp.sum(living * raw_value, 0), jnp.sum(living * raw_value * raw_value, 0), axes
    )


def norm_back(grad_out, unit_value, scaling, norm_gain, living, pixel_count, axes):
    grad_gain, grad_shift = total_of(
        jnp.sum(living * grad_out * unit_value, 0), jnp.sum(living * grad_out, 0), axes
    )
    grad_raw = (
        living
        * (norm_gain * scaling)
        * (grad_out - grad_shift / pixel_count - unit_value * grad_gain / pixel_count)
    )
    return (grad_raw, grad_gain, grad_shift)


def swap(value, bit):
    return lax.ppermute(value, "rep", [(k, k ^ bit) for k in range(4)])


def scatter_rep(value):
    return lax.psum_scatter(value.astype(BF16), "rep", scatter_dimension=0, tiled=True)


def swap_x(value):
    return lax.ppermute(value, "dp", [(k, k ^ 1) for k in range(lax.axis_size("dp"))])


def own_half(value, parity):
    halves = value.reshape((2, value.shape[0] // 2) + value.shape[1:])
    return lax.dynamic_index_in_dim(halves, parity, 0, keepdims=False)


def both_halves(mine, other, parity):
    return jnp.concatenate(
        [jnp.where(parity == 0, mine, other), jnp.where(parity == 0, other, mine)], 0
    )


def total_dp(value):
    parts = lax.axis_size("dp")
    rows = value.shape[0]
    padded = -(-rows // (8 * parts)) * 8 * parts
    value = jnp.pad(value, ((0, padded - rows), (0, 0)))
    share = lax.psum_scatter(value, "dp", scatter_dimension=0, tiled=True)
    return lax.all_gather(share, "dp", axis=0, tiled=True)[:rows].astype(F32)


def shards(
    inputs,
    layout,
    labels,
    cot_depth,
    w_reduce,
    w_spatial,
    w_expand,
    w_heads,
    w_gates,
    w_messages,
    w_classes,
    gain_mid,
    shift_mid,
    gain_wide,
    shift_wide,
    gain_head,
    shift_head,
):
    pixels = inputs.shape[0]
    middle = w_reduce.shape[1]
    classes = w_classes.shape[1]
    group = lax.axis_size("rep")
    everyone = ("rep", "dp")
    rep = lax.axis_index("rep")
    parity = rep % 2
    upper = rep // 2
    first_row = lax.axis_index("dp") * group
    own_info = geometry(lax.dynamic_slice_in_dim(layout, first_row + rep, 1, 0), pixels)
    group_info = geometry(lax.dynamic_slice_in_dim(layout, first_row, group, 0), pixels)
    living = own_info[2][0].astype(F32)[:, None]
    group_living = group_info[2].astype(F32)
    living_all = group_living.reshape(group * pixels, 1)
    pixel_count = jnp.sum(
        jnp.minimum(layout[:, 0] * layout[:, 1] * layout[:, 2], pixels)
    ).astype(F32)
    shifts_own = shift_matrices(own_info, 2)
    shifts_all = shift_matrices(group_info, 1)
    split = lax.axis_size("dp") == 8
    if split:
        side = lax.axis_index("dp") % 2
        side_of = jnp.reshape(side, (1,)).astype(jnp.int32)
        beside_row = first_row + group * (1 - 2 * side)
        shifts_beside = shift_matrices(
            geometry(lax.dynamic_slice_in_dim(layout, beside_row, group, 0), pixels), 1
        )
        columns = [[z_at * 2 + k for z_at in range(4)] for k in range(2)]
    zero = jnp.zeros((1,), jnp.int32)
    first = jnp.reshape(9 * parity, (1,)).astype(jnp.int32)

    reduced = product(inputs, w_reduce)
    sums_one, squares_one = moments(reduced, living, everyone)
    normed_one, unit_one, scale_one = normalize(
        reduced, sums_one, squares_one, pixel_count, gain_mid[0], shift_mid[0]
    )
    hidden_one = jax.nn.silu(normed_one).astype(BF16)
    spatial = rows_forward(zero, hidden_one, w_spatial, shifts_own, 1)
    sums_two, squares_two = moments(spatial, living, everyone)
    normed_two, unit_two, scale_two = normalize(
        spatial, sums_two, squares_two, pixel_count, gain_mid[1], shift_mid[1]
    )
    hidden_two = jax.nn.silu(normed_two).astype(BF16)
    expanded = product(hidden_two, w_expand)
    sums_three, squares_three = moments(expanded, living, everyone)
    normed_three, unit_three, scale_three = normalize(
        expanded, sums_three, squares_three, pixel_count, gain_wide, shift_wide
    )
    pre_act = normed_three + inputs.astype(F32)
    trunk = jax.nn.silu(pre_act).astype(BF16)
    trunk_all = lax.all_gather(trunk, "rep", axis=0, tiled=True)

    if split:
        trunk_mine = swap_x(own_half(trunk_all, parity))

    headed = heads_forward(trunk_all, w_heads, shifts_all)
    own_gain = lax.dynamic_slice_in_dim(gain_head, rep * middle, middle, 0)
    own_shift = lax.dynamic_slice_in_dim(shift_head, rep * middle, middle, 0)
    sums_head, squares_head = moments(headed, living_all, ("dp",))
    normed_head, unit_head, scale_head = normalize(
        headed, sums_head, squares_head, pixel_count, own_gain, own_shift
    )
    rounded = jax.nn.silu(normed_head).astype(BF16)
    heads_all = lax.all_gather(rounded, "rep", axis=0, tiled=False)

    is_depth = upper == 0
    source = jnp.where(
        is_depth,
        jnp.concatenate([heads_all[1], heads_all[2], heads_all[3]], 1),
        jnp.concatenate([heads_all[0], heads_all[1], heads_all[2]], 1),
    )
    if split:
        source_mine = swap_x(own_half(source, parity))
    partial = rows_forward(first, source, w_messages, shifts_all, 2).reshape(
        2, 2, pixels, middle
    )

    if split:
        partial, trunk_mine = lax.optimization_barrier((partial, trunk_mine))
        trunk_other = swap(trunk_mine, 1)

    def of_parity(value, which):
        return lax.dynamic_index_in_dim(value, which, 1, keepdims=False)

    def rows_of(value):
        return value.reshape(2 * pixels, value.shape[-1])

    message = rows_of(of_parity(partial, parity) + swap(of_parity(partial, 1 - parity), 1))
    stream = rows_of(
        of_parity(
            jnp.where(is_depth, heads_all[0], heads_all[3]).reshape(2, 2, pixels, middle), parity
        )
    )
    own_gates = lax.dynamic_slice_in_dim(w_gates, upper * middle, middle, 0)
    stream_living = rows_of(of_parity(group_living.reshape(2, 2, pixels, 1), parity))
    cot_other = swap(cot_depth, 2)
    labels_other = swap(labels, 2)
    stream_cot = jnp.concatenate([cot_depth, cot_other], 0).astype(F32)
    stream_labels = jnp.concatenate([labels_other, labels], 0)
    gate = jax.nn.sigmoid(product(stream, own_gates))
    full = stream.astype(F32) + gate * message
    full_low = full.astype(BF16)
    logits_full = product(full_low, w_classes)
    probs = jax.nn.softmax(logits_full, axis=1)
    onehot_table = (
        stream_labels[:, None] == jnp.arange(classes, dtype=jnp.int32)[None, :]
    ).astype(F32)
    grad_logits = (stream_living * (probs - onehot_table)).astype(BF16)
    classes_local = inner_rows(full_low, jnp.where(is_depth, 0.0, 1.0).astype(BF16) * grad_logits)
    grad_stream = jnp.where(
        is_depth, stream_living * stream_cot, against(grad_logits, w_classes)
    )
    depth_other = swap(full[pixels:], 2)
    logits_other = swap(logits_full[:pixels], 2)
    depth = living * jnp.where(is_depth, full[:pixels], depth_other)
    logits = living * jnp.where(is_depth, logits_other, logits_full[pixels:])
    grad_gate = (grad_stream * message * gate * (1.0 - gate)).astype(BF16)
    grad_message = (grad_stream * gate).astype(BF16)
    gates_local = inner_rows(stream, grad_gate).astype(BF16)
    gates_local = gates_local.reshape(2, pixels, middle)
    if not split:
        gates_share = lax.dynamic_index_in_dim(gates_local, parity, 0, keepdims=False).astype(F32)
        gates_share += swap(
            lax.dynamic_index_in_dim(gates_local, 1 - parity, 0, keepdims=False), 1
        ).astype(F32)
    direct = (grad_stream + against(grad_gate, own_gates)).astype(BF16)

    def both_parities(value, other):
        value = value.reshape(2, pixels, middle)
        other = other.reshape(2, pixels, middle)
        even = jnp.where(parity == 0, value, other)
        odd = jnp.where(parity == 0, other, value)
        return jnp.stack([even, odd], 1).reshape(4 * pixels, middle)

    message_all = both_parities(grad_message, swap(grad_message, 1))
    direct_all = both_parities(direct, jnp.zeros_like(direct))
    if split:
        message_cut = message_all.reshape(4 * pixels, 4, 2, middle // 8)
        cut_own = lax.dynamic_index_in_dim(message_cut, side, 2, keepdims=False)
        cut_sent = lax.dynamic_index_in_dim(message_cut, 1 - side, 2, keepdims=False)
        cut_own = cut_own.reshape(4 * pixels, middle // 2)
        cut_beside = swap_x(cut_sent.reshape(4 * pixels, middle // 2))
        source_grad = rows_data(
            first, message_all, w_messages, shifts_all, 2, source.shape[1] // 2
        )
        source_grad, source_mine, cut_beside, trunk_other = lax.optimization_barrier(
            (source_grad, source_mine, cut_beside, trunk_other)
        )
        source_beside = both_halves(source_mine, swap(source_mine, 1), parity)
        trunk_beside = both_halves(trunk_mine, trunk_other, parity)
    else:
        source_grad, messages_local = rows_back(
            first, message_all, source, w_messages, shifts_all, 2, BF16
        )
    thirds = [source_grad[:, k * middle : (k + 1) * middle] for k in range(3)]
    by_head = jnp.stack(
        [
            jnp.where(is_depth, direct_all, thirds[0]),
            jnp.where(is_depth, thirds[0], thirds[1]),
            jnp.where(is_depth, thirds[1], thirds[2]),
            jnp.where(is_depth, thirds[2], direct_all),
        ],
        0,
    )
    feat_grad = lax.psum_scatter(by_head, "rep", scatter_dimension=0, tiled=False)
    if split:
        messages_local = rows_split(
            first, cut_own, cut_beside, source, source_beside, shifts_all, shifts_beside, 2, 9
        )
        feat_grad, messages_local, trunk_beside = lax.optimization_barrier(
            (feat_grad, messages_local, trunk_beside)
        )
        grad_messages = lax.psum_scatter(
            messages_local, "dp", scatter_dimension=0, tiled=True, axis_index_groups=columns
        )
    else:
        grad_messages = lax.psum_scatter(messages_local, "dp", scatter_dimension=1, tiled=True)
    head_raw, gain_grad_head, shift_grad_head = norm_back(
        feat_grad.astype(F32) * silu_slope(normed_head),
        unit_head,
        scale_head,
        own_gain,
        living_all,
        pixel_count,
        ("dp",),
    )
    head_low = head_raw.astype(BF16)
    if split:
        head_beside = swap_x(head_low)
        trunk_part = heads_data(head_low, w_heads, shifts_all)
        trunk_part, head_beside = lax.optimization_barrier((trunk_part, head_beside))
        heads_local = heads_split(
            side_of,
            head_low,
            head_beside,
            trunk_all,
            trunk_beside,
            shifts_all,
            shifts_beside,
            4,
            256,
        )
    else:
        heads_local = heads_weight(head_low, trunk_all, shifts_all)
        grad_heads = lax.psum_scatter(heads_local, "dp", scatter_dimension=1, tiled=True)
        trunk_part = heads_data(head_low, w_heads, shifts_all)
    trunk_grad = lax.psum_scatter(trunk_part, "rep", scatter_dimension=0, tiled=True)
    if split:
        trunk_grad, heads_local = lax.optimization_barrier((trunk_grad, heads_local))
        grad_heads = lax.psum_scatter(
            heads_local, "dp", scatter_dimension=0, tiled=False, axis_index_groups=columns
        )
    trunk_grad = trunk_grad.astype(F32)
    pre_grad = trunk_grad * silu_slope(pre_act)
    expand_raw, grad_gain_wide, grad_shift_wide = norm_back(
        pre_grad, unit_three, scale_three, gain_wide, living, pixel_count, everyone
    )
    expand_low = expand_raw.astype(BF16)
    expand_local = inner_rows(hidden_two, expand_low).astype(BF16)
    hidden_two_grad = against(expand_low, w_expand)
    spatial_raw, gain_grad_two, shift_grad_two = norm_back(
        hidden_two_grad * silu_slope(normed_two),
        unit_two,
        scale_two,
        gain_mid[1],
        living,
        pixel_count,
        everyone,
    )
    spatial_low = spatial_raw.astype(BF16)
    hidden_one_grad, spatial_local = rows_back(
        zero, spatial_low, hidden_one, w_spatial, shifts_own, 1, F32
    )
    reduced_raw, gain_grad_one, shift_grad_one = norm_back(
        hidden_one_grad * silu_slope(normed_one),
        unit_one,
        scale_one,
        gain_mid[0],
        living,
        pixel_count,
        everyone,
    )
    reduced_low = reduced_raw.astype(BF16)
    reduce_local = inner_rows(inputs, reduced_low).astype(BF16)
    if split:
        reduced_low, grad_messages = lax.optimization_barrier((reduced_low, grad_messages))
        grad_messages = grad_messages.T
    input_grad = pre_grad + against(reduced_low, w_reduce)
    if split:
        wide = w_expand.shape[1]
        cuts = wide // middle

        def side_by_side(value):
            value = value.reshape(4, -1, value.shape[1])
            return jnp.concatenate(
                [value[:, :, k : k + middle] for k in range(0, value.shape[2], middle)], 1
            )

        gates_zero = jnp.zeros_like(gates_local)
        gates_every = jnp.where(
            is_depth,
            jnp.concatenate([gates_local, gates_zero], 0),
            jnp.concatenate([gates_zero, gates_local], 0),
        )
        classes_wide = jnp.pad(classes_local.astype(BF16), ((0, 0), (0, 128 - classes)))
        classes_wide = classes_wide.reshape(4, 4, -1, 128)
        classes_wide = jnp.concatenate([classes_wide[:, k] for k in range(4)], 2)
        pieces = [
            reduce_local.reshape(4, -1, middle),
            spatial_local.reshape(4, -1, middle),
            side_by_side(expand_local),
            gates_every,
            classes_wide,
        ]
        rows = [piece.shape[1] for piece in pieces]
        unit = 128 * CHUNKS
        missing = -sum(rows) % unit
        pieces.append(jnp.zeros((4, missing, middle), BF16))
        summed = small_total(jnp.concatenate(pieces, 1))
        starts = [sum(rows[:k]) for k in range(5)]
        grad_reduce, grad_spatial, expand_sum, grad_gates, classes_sum = [
            summed[at : at + size] for at, size in zip(starts, rows)
        ]
        expand_sum = expand_sum.reshape(cuts, -1, middle)
        grad_expand = jnp.concatenate([expand_sum[k] for k in range(cuts)], 1)
        classes_sum = jnp.concatenate(
            [classes_sum[:, k * 128 : (k + 1) * 128] for k in range(4)], 0
        )
        grad_classes = classes_sum[:, :classes]
    else:
        grad_expand = scatter_rep(expand_local)
        grad_spatial = scatter_rep(spatial_local)
        grad_reduce = scatter_rep(reduce_local)
        grad_classes = scatter_rep(classes_local)
        pieces = [
            gates_share.astype(BF16),
            grad_expand.reshape(-1, middle),
            grad_spatial,
            grad_classes.reshape(-1, middle),
        ]
        early = total_dp(jnp.concatenate(pieces, 0))
        rows = [piece.shape[0] for piece in pieces]
        starts = [sum(rows[:k]) for k in range(4)]
        grad_gates, expand_sum, grad_spatial, classes_sum = [
            early[at : at + size] for at, size in zip(starts, rows)
        ]
        grad_expand = expand_sum.reshape(grad_expand.shape)
        grad_classes = classes_sum.reshape(grad_classes.shape)
        grad_reduce = total_dp(grad_reduce)
    grad_gain_mid = jnp.stack([gain_grad_one, gain_grad_two], 0)
    grad_shift_mid = jnp.stack([shift_grad_one, shift_grad_two], 0)
    head_norms = lax.all_gather(
        jnp.stack([gain_grad_head, shift_grad_head], 0), "rep", axis=1, tiled=True
    )
    return (
        depth,
        logits,
        input_grad,
        grad_reduce,
        grad_spatial,
        grad_expand,
        grad_heads.astype(F32),
        grad_gates,
        grad_messages.astype(F32),
        grad_classes,
        grad_gain_mid,
        grad_shift_mid,
        grad_gain_wide,
        grad_shift_wide,
        head_norms[0],
        head_norms[1],
    )


def solution(mesh):
    in_specs = (
        P(("dp", "rep"), None),
        P(),
        P(("dp", "rep")),
        P(("dp", "rep"), None),
        P(),
        P(),
        P(),
        P("rep", None),
        P(),
        P("rep", None),
        P(),
        P(),
        P(),
        P(),
        P(),
        P(),
        P(),
    )
    out_specs = (
        P(("dp", "rep"), None),
        P(("dp", "rep"), None),
        P(("dp", "rep"), None),
        P("rep", None),
        P("rep", None),
        P("rep", None),
        P("rep", "dp"),
        P("rep", None),
        P("rep", "dp"),
        P("rep", None),
        P(),
        P(),
        P(),
        P(),
        P(),
        P(),
    )
    return jax.shard_map(shards, mesh=mesh, in_specs=in_specs, out_specs=out_specs, check_vma=False)
```

```python
import functools

import jax
import jax.numpy as jnp
from jax import lax
from jax.experimental import pallas as pl
from jax.experimental.pallas import tpu as pltpu
from jax.sharding import PartitionSpec as P

EPS = 1e-05
F32 = jnp.float32
BF16 = jnp.bfloat16
VMEM_LIMIT = 60 * 2**20


def geometry(layout, span):
    position = jnp.arange(span, dtype=jnp.int32)
    height = layout[:, 0:1]
    map_width = layout[:, 1:2]
    images = layout[:, 2:3]
    map_area = height * map_width
    inside = position[None, :] % map_area
    row_of = inside // map_width
    col_of = inside % map_width
    living = position[None, :] < images * map_area
    return (row_of, col_of, living, height, map_width)


def neighbours(shape_info, dilation):
    row_of, col_of, living, height, map_width = shape_info
    span = row_of.shape[1]
    position = jnp.arange(span, dtype=jnp.int32)
    every = []
    for step_row in (-1, 0, 1):
        for step_col in (-1, 0, 1):
            target_row = row_of + dilation * step_row
            target_col = col_of + dilation * step_col
            inside = (
                living
                & (target_row >= 0)
                & (target_row < height)
                & (target_col >= 0)
                & (target_col < map_width)
            )
            neighbour = position[None, :] + dilation * (step_row * map_width + step_col)
            every.append(jnp.where(inside, neighbour, -1))
    return jnp.concatenate(every, 0).T


def shift_matrices(shape_info, dilation):
    devices, span = shape_info[0].shape
    picks = neighbours(shape_info, dilation).T.reshape(9, devices, span, 1)
    return (picks == jnp.arange(span, dtype=jnp.int32)).astype(BF16)


def product(left_side, right_side):
    return jnp.dot(left_side, right_side, preferred_element_type=F32)


def inner_rows(left_side, right_side):
    return lax.dot_general(
        left_side, right_side, (((0,), (0,)), ((), ())), preferred_element_type=F32
    )


def against(left_side, right_side):
    return lax.dot_general(
        left_side, right_side, (((1,), (1,)), ((), ())), preferred_element_type=F32
    )


def params():
    return pltpu.CompilerParams(vmem_limit_bytes=VMEM_LIMIT)


def cost(flops, moved):
    return pl.CostEstimate(flops=flops, bytes_accessed=moved, transcendentals=0)


def shifted(g_ref, s_ref):
    blocks, span = s_ref.shape[1], s_ref.shape[2]
    return jnp.concatenate(
        [
            inner_rows(s_ref[0, k], g_ref[pl.ds(k * span, span), :]).astype(BF16)
            for k in range(blocks)
        ],
        0,
    )


def heads_data_kernel(g_ref, w_ref, s_ref, out_ref, total):
    tap = pl.program_id(0)
    taken = shifted(g_ref, s_ref)
    wide = w_ref.shape[1]
    step = 512

    @pl.when(tap == 0)
    def _():
        total[...] = jnp.zeros_like(total)

    for c in range(0, wide, step):
        total[:, c : c + step] += product(taken, w_ref[:, c : c + step])

    @pl.when(tap == pl.num_programs(0) - 1)
    def _():
        out_ref[...] = total[...].astype(out_ref.dtype)


def heads_data(g, w_heads, shifts):
    rows, outs = g.shape
    taps, blocks, span, _ = shifts.shape
    wide = w_heads.shape[1] // taps
    return pl.pallas_call(
        heads_data_kernel,
        grid=(taps,),
        in_specs=[
            pl.BlockSpec((rows, outs), lambda t: (0, 0)),
            pl.BlockSpec((outs, wide), lambda t: (0, t)),
            pl.BlockSpec((1, blocks, span, span), lambda t: (t, 0, 0, 0)),
        ],
        out_specs=pl.BlockSpec((rows, wide), lambda t: (0, 0)),
        out_shape=jax.ShapeDtypeStruct((rows, wide), BF16),
        scratch_shapes=[pltpu.VMEM((rows, wide), F32)],
        compiler_params=params(),
        cost_estimate=cost(2 * rows * wide * outs * taps, w_heads.size * 2),
        name="heads_data",
    )(g, w_heads, shifts)


def heads_weight_kernel(g_ref, u_ref, s_ref, out_ref):
    taken = shifted(g_ref, s_ref)
    step = 512
    for c in range(0, u_ref.shape[1], step):
        out_ref[:, c : c + step] = inner_rows(taken, u_ref[:, c : c + step]).astype(out_ref.dtype)


def heads_weight(g, u, shifts):
    rows, outs = g.shape
    wide = u.shape[1]
    taps, blocks, span, _ = shifts.shape
    return pl.pallas_call(
        heads_weight_kernel,
        grid=(taps,),
        in_specs=[
            pl.BlockSpec((rows, outs), lambda t: (0, 0)),
            pl.BlockSpec((rows, wide), lambda t: (0, 0)),
            pl.BlockSpec((1, blocks, span, span), lambda t: (t, 0, 0, 0)),
        ],
        out_specs=pl.BlockSpec((outs, wide), lambda t: (0, t)),
        out_shape=jax.ShapeDtypeStruct((outs, taps * wide), BF16),
        compiler_params=params(),
        cost_estimate=cost(2 * rows * wide * outs * taps, outs * taps * wide * 2),
        name="heads_weight",
    )(g, u, shifts)


def rows_forward_kernel(first_ref, u_ref, w_ref, s_ref, out_ref):
    blocks, span = s_ref.shape[1], s_ref.shape[2]

    @pl.when(pl.program_id(0) == 0)
    def _():
        out_ref[...] = jnp.zeros_like(out_ref)

    y = product(u_ref[...], w_ref[...]).astype(BF16)
    for k in range(blocks):
        at = pl.ds(k * span, span)
        out_ref[at, :] += product(s_ref[0, k], y[k * span : (k + 1) * span])


def rows_forward(first, u, w, shifts, halves):
    rows = u.shape[0]
    depth = u.shape[1] // halves
    outs = w.shape[1]
    steps = w.shape[0] // depth
    taps, blocks, span, _ = shifts.shape
    return pl.pallas_call(
        rows_forward_kernel,
        grid_spec=pltpu.PrefetchScalarGridSpec(
            num_scalar_prefetch=1,
            grid=(steps,),
            in_specs=[
                pl.BlockSpec((rows, depth), lambda b, f: (0, (b + f[0]) % halves)),
                pl.BlockSpec((depth, outs), lambda b, f: (b, 0)),
                pl.BlockSpec((1, blocks, span, span), lambda b, f: ((b + f[0]) // halves, 0, 0, 0)),
            ],
            out_specs=pl.BlockSpec((rows, outs), lambda b, f: (0, 0)),
        ),
        out_shape=jax.ShapeDtypeStruct((rows, outs), F32),
        compiler_params=params(),
        cost_estimate=cost(2 * rows * w.size, w.size * 2),
        name="rows_forward",
    )(first, u, w, shifts)


def rows_back_kernel(halves, first_ref, g_ref, u_ref, w_ref, s_ref, du_ref, dw_ref, total):
    step = pl.program_id(0)
    taken = shifted(g_ref, s_ref)
    depth = w_ref.shape[0]
    which = (step + first_ref[0]) % halves

    @pl.when(step == 0)
    def _():
        total[...] = jnp.zeros_like(total)

    total[which] += against(taken, w_ref[...])
    dw_ref[...] = inner_rows(u_ref[...], taken).astype(dw_ref.dtype)

    @pl.when(step == pl.num_programs(0) - 1)
    def _():
        for k in range(halves):
            du_ref[:, k * depth : (k + 1) * depth] = total[k].astype(du_ref.dtype)


def rows_back(first, g, u, w, shifts, halves, kind):
    rows, outs = g.shape
    depth = u.shape[1] // halves
    steps = w.shape[0] // depth
    taps, blocks, span, _ = shifts.shape
    return pl.pallas_call(
        functools.partial(rows_back_kernel, halves),
        grid_spec=pltpu.PrefetchScalarGridSpec(
            num_scalar_prefetch=1,
            grid=(steps,),
            in_specs=[
                pl.BlockSpec((rows, outs), lambda b, f: (0, 0)),
                pl.BlockSpec((rows, depth), lambda b, f: (0, (b + f[0]) % halves)),
                pl.BlockSpec((depth, outs), lambda b, f: (b, 0)),
                pl.BlockSpec((1, blocks, span, span), lambda b, f: ((b + f[0]) // halves, 0, 0, 0)),
            ],
            out_specs=[
                pl.BlockSpec((rows, halves * depth), lambda b, f: (0, 0)),
                pl.BlockSpec((depth, outs), lambda b, f: (b, 0)),
            ],
            scratch_shapes=[pltpu.VMEM((halves, rows, depth), F32)],
        ),
        out_shape=[
            jax.ShapeDtypeStruct((rows, halves * depth), kind),
            jax.ShapeDtypeStruct(w.shape, BF16),
        ],
        compiler_params=params(),
        cost_estimate=cost(4 * rows * w.size, w.size * 4),
        name="rows_back",
    )(first, g, u, w, shifts)


def heads_split_kernel(per_tap, units, lanes, x_ref, g_ref, h_ref, u_ref, v_ref, s_ref, r_ref, out_ref, taken):
    blocks, span = s_ref.shape[1], s_ref.shape[2]
    rows = blocks * span
    start = units * (2 * pl.program_id(0) + x_ref[0])

    @pl.loop(0, units)
    def _(unit):
        tap, chunk = (start + unit) // per_tap, (start + unit) % per_tap

        @pl.when((unit == 0) | (chunk == 0))
        def _():
            for side, (a_ref, m_ref) in enumerate(((g_ref, s_ref), (h_ref, r_ref))):
                for k in range(blocks):
                    at = (side * blocks + k) * span
                    taken[:, at : at + span] = inner_rows(
                        a_ref[k * span : (k + 1) * span, :], m_ref[tap, k]
                    ).astype(BF16)

        at = pl.ds(pl.multiple_of(chunk * lanes, lanes), lanes)
        to = pl.ds(pl.multiple_of(unit * lanes, lanes), lanes)
        out_ref[0, :, to] = (
            product(taken[:, :rows], u_ref[:, at]) + product(taken[:, rows:], v_ref[:, at])
        ).astype(BF16)


def heads_split(x, g, h, u, v, s, r, shards, lanes):
    rows, outs = g.shape
    wide = u.shape[1]
    taps, blocks, span, _ = s.shape
    units = taps * wide // (2 * shards * lanes)
    per_tap = wide // lanes
    whole = pl.BlockSpec(memory_space=pltpu.VMEM)
    return pl.pallas_call(
        functools.partial(heads_split_kernel, per_tap, units, lanes),
        grid_spec=pltpu.PrefetchScalarGridSpec(
            num_scalar_prefetch=1,
            grid=(shards,),
            in_specs=[whole] * 6,
            out_specs=pl.BlockSpec((1, outs, units * lanes), lambda i, f: (i, 0, 0)),
            scratch_shapes=[pltpu.VMEM((outs, 2 * rows), BF16)],
        ),
        out_shape=jax.ShapeDtypeStruct((shards, outs, units * lanes), BF16),
        compiler_params=params(),
        cost_estimate=cost(2 * rows * wide * outs * taps, outs * taps * wide * 2),
        name="heads_split",
    )(x, g, h, u, v, s, r)


def rows_split_kernel(first_ref, g_ref, h_ref, u_ref, v_ref, s_ref, r_ref, out_ref):
    blocks, span = s_ref.shape[1], s_ref.shape[2]
    total = 0.0
    for a_ref, b_ref, m_ref in ((g_ref, u_ref, s_ref), (h_ref, v_ref, r_ref)):
        taken = jnp.concatenate(
            [
                inner_rows(a_ref[k * span : (k + 1) * span, :], m_ref[0, k]).astype(BF16)
                for k in range(blocks)
            ],
            1,
        )
        total = total + product(taken, b_ref[...])
    out_ref[...] = total.astype(BF16)


def rows_split(first, g, h, u, v, s, r, halves, steps):
    rows, outs = g.shape
    depth = u.shape[1] // halves
    taps, blocks, span, _ = s.shape
    side = pl.BlockSpec((rows, outs), lambda b, f: (0, 0))
    values = pl.BlockSpec((rows, depth), lambda b, f: (0, (b + f[0]) % halves))
    picks = pl.BlockSpec((1, blocks, span, span), lambda b, f: ((b + f[0]) // halves, 0, 0, 0))
    return pl.pallas_call(
        rows_split_kernel,
        grid_spec=pltpu.PrefetchScalarGridSpec(
            num_scalar_prefetch=1,
            grid=(steps,),
            in_specs=[side, side, values, values, picks, picks],
            out_specs=pl.BlockSpec((outs, depth), lambda b, f: (0, b)),
        ),
        out_shape=jax.ShapeDtypeStruct((outs, steps * depth), BF16),
        compiler_params=params(),
        cost_estimate=cost(4 * rows * outs * steps * depth, outs * steps * depth * 2),
        name="rows_split",
    )(first, g, h, u, v, s, r)


def rows_data_kernel(halves, first_ref, g_ref, w_ref, s_ref, du_ref, total):
    step = pl.program_id(0)
    depth = w_ref.shape[0]
    which = (step + first_ref[0]) % halves

    @pl.when(step == 0)
    def _():
        total[...] = jnp.zeros_like(total)

    total[which] += against(shifted(g_ref, s_ref), w_ref[...])

    @pl.when(step == pl.num_programs(0) - 1)
    def _():
        for k in range(halves):
            du_ref[:, k * depth : (k + 1) * depth] = total[k].astype(du_ref.dtype)


def rows_data(first, g, w, shifts, halves, depth):
    rows, outs = g.shape
    steps = w.shape[0] // depth
    taps, blocks, span, _ = shifts.shape
    return pl.pallas_call(
        functools.partial(rows_data_kernel, halves),
        grid_spec=pltpu.PrefetchScalarGridSpec(
            num_scalar_prefetch=1,
            grid=(steps,),
            in_specs=[
                pl.BlockSpec((rows, outs), lambda b, f: (0, 0)),
                pl.BlockSpec((depth, outs), lambda b, f: (b, 0)),
                pl.BlockSpec((1, blocks, span, span), lambda b, f: ((b + f[0]) // halves, 0, 0, 0)),
            ],
            out_specs=pl.BlockSpec((rows, halves * depth), lambda b, f: (0, 0)),
            scratch_shapes=[pltpu.VMEM((halves, rows, depth), F32)],
        ),
        out_shape=jax.ShapeDtypeStruct((rows, halves * depth), BF16),
        compiler_params=params(),
        cost_estimate=cost(2 * rows * w.size, w.size * 2),
        name="rows_data",
    )(first, g, w, shifts)


CHUNKS = 4


def small_kernel(p_ref, out_ref, half_ref, core_in, core_out, y_in, x_out, x_in, z_out, z_in, send, recv):
    rep, dp = lax.axis_index("rep"), lax.axis_index("dp")
    par, upper = lax.rem(rep, 2), rep // 2
    x, z = lax.rem(dp, 2), dp // 2
    mate, far, beside = rep + 1 - 2 * par, rep + 2 - 4 * upper, dp + 1 - 2 * x
    zs = [lax.rem(z + k, 4) for k in range(1, 4)]
    barrier = pltpu.get_barrier_semaphore()
    partners = [{"rep": mate}, {"rep": far}, {"dp": beside}] + [{"dp": 2 * k + x} for k in zs]
    for partner in partners:
        pl.semaphore_signal(barrier, inc=1, device_id=partner, device_id_type=MESH)
    pl.semaphore_wait(barrier, len(partners))
    rows = p_ref.shape[1] // CHUNKS
    half, eighth = rows // 2, rows // 8

    def span(c, at=0, size=rows):
        return pl.ds(pl.multiple_of(c * rows + at, 16), size)

    def remote(src, dst, c, slot, to, slot_in=None):
        return pltpu.make_async_remote_copy(
            src_ref=src,
            dst_ref=dst,
            send_sem=send.at[c, slot],
            recv_sem=recv.at[c, slot if slot_in is None else slot_in],
            device_id=to,
            device_id_type=MESH,
        )

    def core_copy(c, hi):
        return remote(
            p_ref.at[2 * hi + 1 - par, span(c)], core_in.at[hi, span(c)], c, hi, {"rep": mate}
        )

    def y_copy(c):
        return remote(core_out.at[span(c)], y_in.at[span(c)], c, 2, {"rep": far})

    def x_copy(c):
        return remote(
            x_out.at[pl.ds(c * half, half)], x_in.at[pl.ds(c * half, half)], c, 3, {"dp": beside}
        )

    def z_copy(c, k, incoming):
        sent = pl.ds(pl.multiple_of(c * half + k * eighth, 16), eighth)
        slot = k if incoming else z
        return remote(
            z_out.at[sent], z_in.at[slot, pl.ds(c * eighth, eighth)], c, 4 + k, {"dp": 2 * k + x}, 4 + slot
        )

    def back_copy(c, k, incoming):
        place = span(c, x * half + (k if incoming else z) * eighth, eighth)
        return remote(
            half_ref.at[place], half_ref.at[place], c, 8 + k, {"dp": 2 * k + x}, 8 + (k if incoming else z)
        )

    def last_copy(c, incoming):
        place = span(c, (1 - x if incoming else x) * half, half)
        return remote(half_ref.at[place], half_ref.at[place], c, 12, {"dp": beside})

    def step(stage, c):
        if stage == 0:
            for hi in range(2):
                core_copy(c, hi).start()
        elif stage == 1:
            for hi in range(2):
                core_copy(c, hi).wait_recv()
            core_out[span(c)] = (
                p_ref[2 * (1 - upper) + par, span(c)].astype(F32)
                + core_in[1 - upper, span(c)].astype(F32)
            ).astype(BF16)
            y_copy(c).start()
        elif stage == 2:
            y_copy(c).wait_recv()

            def both(at):
                place = span(c, at, half)
                return (
                    p_ref[rep, place].astype(F32)
                    + core_in[upper, place].astype(F32)
                    + y_in[place].astype(F32)
                )

            x_out[pl.ds(c * half, half)] = both((1 - x) * half).astype(BF16)
            x_copy(c).start()
            z_out[pl.ds(c * half, half)] = both(x * half).astype(BF16)
        elif stage == 3:
            x_copy(c).wait_recv()
            at = pl.ds(c * half, half)
            z_out[at] = (z_out[at].astype(F32) + x_in[at].astype(F32)).astype(BF16)
            for k in zs:
                z_copy(c, k, False).start()
        elif stage == 4:
            for k in zs:
                z_copy(c, k, True).wait_recv()
            z_in[z, pl.ds(c * eighth, eighth)] = z_out[
                pl.ds(pl.multiple_of(c * half + z * eighth, 16), eighth)
            ]
            total = z_in[0, pl.ds(c * eighth, eighth)].astype(F32)
            for k in range(1, 4):
                total = total + z_in[k, pl.ds(c * eighth, eighth)].astype(F32)
            half_ref[span(c, x * half + z * eighth, eighth)] = total.astype(BF16)
            for k in zs:
                back_copy(c, k, False).start()
        elif stage == 5:
            for k in zs:
                back_copy(c, k, True).wait_recv()
            last_copy(c, False).start()
        else:
            last_copy(c, True).wait_recv()
            out_ref[span(c)] = half_ref[span(c)].astype(F32)
            for hi in range(2):
                core_copy(c, hi).wait_send()
            y_copy(c).wait_send()
            x_copy(c).wait_send()
            for k in zs:
                z_copy(c, k, False).wait_send()
                back_copy(c, k, False).wait_send()
            last_copy(c, False).wait_send()

    for turn in range(CHUNKS + 6):
        for c in range(CHUNKS):
            if 0 <= turn - c <= 6:
                step(turn - c, c)


def small_total(parts):
    quarters, rows, lanes = parts.shape
    return pl.pallas_call(
        small_kernel,
        out_shape=jax.ShapeDtypeStruct((rows, lanes), F32),
        in_specs=[pl.BlockSpec(memory_space=pltpu.VMEM)],
        out_specs=pl.BlockSpec(memory_space=pltpu.VMEM),
        scratch_shapes=[
            pltpu.VMEM((rows, lanes), BF16),
            pltpu.VMEM((2, rows, lanes), BF16),
            pltpu.VMEM((rows, lanes), BF16),
            pltpu.VMEM((rows, lanes), BF16),
            pltpu.VMEM((rows // 2, lanes), BF16),
            pltpu.VMEM((rows // 2, lanes), BF16),
            pltpu.VMEM((rows // 2, lanes), BF16),
            pltpu.VMEM((4, rows // 8, lanes), BF16),
            pltpu.SemaphoreType.DMA((CHUNKS, 13)),
            pltpu.SemaphoreType.DMA((CHUNKS, 13)),
        ],
        compiler_params=pltpu.CompilerParams(
            collective_id=9, has_side_effects=True, vmem_limit_bytes=VMEM_LIMIT
        ),
        name="small_total",
    )(parts)


def send_to(axis, to, src, dst, send_sem, recv_sem):
    return pltpu.make_async_remote_copy(
        src_ref=src,
        dst_ref=dst,
        send_sem=send_sem,
        recv_sem=recv_sem,
        device_id={axis: to},
        device_id_type=MESH,
    )


def total_along(axis, size, block, slots, send_sems, recv_sems, meanwhile=None):
    me = lax.axis_index(axis)
    others = [lax.rem(me + k, size) for k in range(1, size)]
    for other in others:
        send_to(axis, other, block, slots.at[me], send_sems.at[other], recv_sems.at[me]).start()
    slots[me] = block[...]
    if meanwhile is not None:
        meanwhile()
    for other in others:
        copy = send_to(
            axis, other, block, slots.at[other], send_sems.at[other], recv_sems.at[other]
        )
        copy.wait_recv()
        copy.wait_send()
    total = slots[0]
    for k in range(1, size):
        total = total + slots[k]
    return total


def place_in_map(layout_ref, device, span):
    position = lax.broadcasted_iota(jnp.int32, (span, 1), 0)
    large = layout_ref[device, 1] == 16
    row_of = jnp.where(large, position // 16, (position % 64) // 8)
    col_of = jnp.where(large, position % 16, position % 8)
    return position, row_of, col_of


def live_mask(layout_ref, device, span):
    position = lax.broadcasted_iota(jnp.int32, (span, 1), 0)
    return position < layout_ref[device, 0] * layout_ref[device, 1] * layout_ref[device, 2]


def live_column(layout_ref, device, span):
    return jnp.where(live_mask(layout_ref, device, span), 1.0, 0.0)


def inverse_count(areas_ref, span):
    areas = areas_ref[:, 0:1] * areas_ref[:, 1:2] * areas_ref[:, 2:3]
    return 1.0 / jnp.sum(jnp.minimum(areas, span).astype(F32), 0, keepdims=True)


def shift_block(layout_ref, device, dilation, tap, span):
    position, row_of, col_of = place_in_map(layout_ref, device, span)
    height, map_width = layout_ref[device, 0], layout_ref[device, 1]
    step_row, step_col = dilation * (tap // 3 - 1), dilation * (tap % 3 - 1)
    target_row, target_col = row_of + step_row, col_of + step_col
    inside = (
        live_mask(layout_ref, device, span)
        & (target_row >= 0)
        & (target_row < height)
        & (target_col >= 0)
        & (target_col < map_width)
    )
    neighbour = jnp.where(inside, position + step_row * map_width + step_col, -1)
    lanes = lax.broadcasted_iota(jnp.int32, (span, span), 1)
    return jnp.where(neighbour == lanes, 1.0, 0.0).astype(BF16)


def trunk_kernel(
    sizes,
    in_ref,
    layout_ref,
    areas_ref,
    w_reduce_ref,
    w_spatial_hbm,
    w_expand_hbm,
    w_heads_hbm,
    gain_mid_ref,
    shift_mid_ref,
    gain_wide_ref,
    shift_wide_ref,
    reduced_ref,
    sums_one_ref,
    hidden_one_ref,
    spatial_ref,
    sums_two_ref,
    hidden_two_ref,
    expanded_ref,
    sums_three_ref,
    trunk_ref,
    headed_ref,
    own_shift_ref,
    all_shift_ref,
    w_spatial_ref,
    w_expand_ref,
    w_heads_ref,
    block_mid,
    block_wide,
    slots_mid_rep,
    slots_mid_dp,
    slots_wide_rep,
    slots_wide_dp,
    load_sems,
    rep_send,
    rep_recv,
    dp_send,
    dp_recv,
    gather_send,
    gather_recv,
):
    n_rep, n_dp = sizes
    rep = lax.axis_index("rep")
    par, upper = lax.rem(rep, 2), rep // 2
    mate, far = rep + 1 - 2 * par, rep + 2 - 4 * upper
    span, wide = in_ref.shape
    middle = w_reduce_ref.shape[1]
    taps = own_shift_ref.shape[0]
    loads = [
        pltpu.make_async_copy(w_spatial_hbm, w_spatial_ref, load_sems.at[0]),
        pltpu.make_async_copy(w_expand_hbm, w_expand_ref, load_sems.at[1]),
    ]
    heads_load = pltpu.make_async_copy(w_heads_hbm, w_heads_ref, load_sems.at[2])
    for load in loads:
        load.start()
    heads_load.start()

    barrier = pltpu.get_barrier_semaphore()
    for axis, size in (("rep", n_rep), ("dp", n_dp)):
        me = lax.axis_index(axis)
        for k in range(1, size):
            pl.semaphore_signal(
                barrier, inc=1, device_id={axis: lax.rem(me + k, size)}, device_id_type=MESH
            )
    first_row = lax.axis_index("dp") * n_rep
    live = live_column(layout_ref, first_row + rep, span)
    inverse = inverse_count(areas_ref, span)

    def make_own():
        for t in range(taps):
            own_shift_ref[t] = shift_block(layout_ref, first_row + rep, 2, t, span)

    def make_all(first, last):
        def fill():
            for t in range(first, last):
                for p in range(n_rep):
                    all_shift_ref[t, p] = shift_block(layout_ref, first_row + p, 1, t, span)

        return fill

    def everywhere(number, value_ref, blocks, rep_slots, dp_slots, meanwhile, later):
        masked = live * value_ref[...]
        blocks[0, 0:1, :] = jnp.sum(masked, 0, keepdims=True)
        blocks[0, 1:2, :] = jnp.sum(masked * value_ref[...], 0, keepdims=True)
        if number == 0:
            pl.semaphore_wait(barrier, n_rep + n_dp - 2)
        blocks[1] = total_along(
            "rep", n_rep, blocks.at[0], rep_slots, rep_send.at[number], rep_recv.at[number], meanwhile
        )
        return total_along(
            "dp", n_dp, blocks.at[1], dp_slots, dp_send.at[number], dp_recv.at[number], later
        )

    def normed(value, sums, gain, shift):
        center = sums[0:1] * inverse
        scaling = lax.rsqrt(sums[1:2] * inverse - center * center + EPS)
        return (value - center) * (scaling * gain) + shift

    def silu(value):
        return value * jax.nn.sigmoid(value)

    reduced_ref[...] = product(in_ref[...], w_reduce_ref[...])
    sums = everywhere(
        0, reduced_ref, block_mid.at[0], slots_mid_rep.at[0], slots_mid_dp.at[0], make_own, None
    )
    sums_one_ref[...] = sums
    hidden_one_ref[...] = silu(
        normed(reduced_ref[...], sums, gain_mid_ref[0:1, :], shift_mid_ref[0:1, :])
    ).astype(BF16)
    loads[0].wait()
    spatial_ref[...] = jnp.zeros_like(spatial_ref)

    @pl.loop(0, taps)
    def _(t):
        moved = product(own_shift_ref[t], hidden_one_ref[...]).astype(BF16)
        at = pl.ds(pl.multiple_of(t * middle, middle), middle)
        spatial_ref[...] += product(moved, w_spatial_ref[at, :])

    sums = everywhere(
        1, spatial_ref, block_mid.at[1], slots_mid_rep.at[1], slots_mid_dp.at[1], make_all(0, 5), None
    )
    sums_two_ref[...] = sums
    hidden_two_ref[...] = silu(
        normed(spatial_ref[...], sums, gain_mid_ref[1:2, :], shift_mid_ref[1:2, :])
    ).astype(BF16)
    loads[1].wait()
    expanded_ref[...] = product(hidden_two_ref[...], w_expand_ref[...])
    sums = everywhere(
        2, expanded_ref, block_wide, slots_wide_rep, slots_wide_dp, make_all(5, 9), None
    )
    sums_three_ref[...] = sums

    own_rows = pl.ds(pl.multiple_of(par * span, span), span)
    mate_rows = pl.ds(pl.multiple_of((1 - par) * span, span), span)
    pre = normed(expanded_ref[...], sums, gain_wide_ref[...], shift_wide_ref[...])
    trunk_ref[upper, own_rows, :] = silu(pre + in_ref[...].astype(F32)).astype(BF16)
    parts = 4
    piece = span // parts

    def rows(parity, k):
        return pl.ds(pl.multiple_of(parity * span + k * piece, piece), piece)

    def across(side, k):
        at = trunk_ref.at[side, rows(par, k)]
        return send_to("rep", far, at, at, gather_send.at[k], gather_recv.at[k])

    def own_pass(parity):
        at = trunk_ref.at[upper, pl.ds(pl.multiple_of(parity * span, span), span)]
        return send_to("rep", mate, at, at, gather_send.at[parts], gather_recv.at[parts])

    def far_pass(parity, k):
        at = trunk_ref.at[1 - upper, rows(parity, k)]
        slot = parts + 1 + k
        return send_to("rep", mate, at, at, gather_send.at[slot], gather_recv.at[slot])

    for k in range(parts):
        across(upper, k).start()
    own_pass(par).start()
    headed_ref[...] = jnp.zeros_like(headed_ref)
    own_pass(1 - par).wait_recv()
    heads_load.wait()

    def convolve(side):
        @pl.loop(0, taps)
        def _(t):
            at = pl.ds(pl.multiple_of(t * wide, wide), wide)
            y = against(trunk_ref[side], w_heads_ref[:, at]).astype(BF16)
            for k in range(2):
                place = pl.ds(k * span, span)
                headed_ref[side, place, :] += product(
                    all_shift_ref[t, 2 * side + k], y[k * span : (k + 1) * span]
                )

    convolve(upper)
    for k in range(parts):
        across(1 - upper, k).wait_recv()
        far_pass(par, k).start()
    for k in range(parts):
        far_pass(1 - par, k).wait_recv()
    convolve(1 - upper)
    for k in range(parts):
        across(upper, k).wait_send()
        far_pass(par, k).wait_send()
    own_pass(par).wait_send()


def trunk_forward(
    inputs,
    layout,
    w_reduce,
    w_spatial,
    w_expand,
    w_heads,
    gain_mid,
    shift_mid,
    gain_wide,
    shift_wide,
):
    span, wide = inputs.shape
    middle = w_reduce.shape[1]
    n_rep, n_dp = lax.axis_size("rep"), lax.axis_size("dp")
    taps = 9
    vmem = pl.BlockSpec(memory_space=pltpu.VMEM)
    hbm = pl.BlockSpec(memory_space=pl.ANY)
    smem = pl.BlockSpec(memory_space=pltpu.SMEM)
    dma = pltpu.SemaphoreType.DMA
    shape = jax.ShapeDtypeStruct
    return pl.pallas_call(
        functools.partial(trunk_kernel, (n_rep, n_dp)),
        in_specs=[vmem, smem, vmem, vmem] + [hbm] * 3 + [vmem] * 4,
        out_specs=[vmem] * 12,
        out_shape=[
            shape((span, middle), F32),
            shape((2, middle), F32),
            shape((span, middle), BF16),
            shape((span, middle), F32),
            shape((2, middle), F32),
            shape((span, middle), BF16),
            shape((span, wide), F32),
            shape((2, wide), F32),
            shape((2, 2 * span, wide), BF16),
            shape((2, 2 * span, w_heads.shape[0]), F32),
            shape((taps, span, span), BF16),
            shape((taps, n_rep, span, span), BF16),
        ],
        scratch_shapes=[
            pltpu.VMEM(w_spatial.shape, BF16),
            pltpu.VMEM(w_expand.shape, BF16),
            pltpu.VMEM(w_heads.shape, BF16),
            pltpu.VMEM((2, 2, 2, middle), F32),
            pltpu.VMEM((2, 2, wide), F32),
            pltpu.VMEM((2, n_rep, 2, middle), F32),
            pltpu.VMEM((2, n_dp, 2, middle), F32),
            pltpu.VMEM((n_rep, 2, wide), F32),
            pltpu.VMEM((n_dp, 2, wide), F32),
            dma((3,)),
            dma((3, n_rep)),
            dma((3, n_rep)),
            dma((3, n_dp)),
            dma((3, n_dp)),
            dma((9,)),
            dma((9,)),
        ],
        compiler_params=pltpu.CompilerParams(
            collective_id=10, has_side_effects=True, vmem_limit_bytes=VMEM_LIMIT
        ),
        name="trunk_forward",
    )(
        inputs,
        layout,
        layout,
        w_reduce,
        w_spatial,
        w_expand,
        w_heads,
        gain_mid,
        shift_mid,
        gain_wide[None, :],
        shift_wide[None, :],
    )


def silu_slope(value_in):
    sigma_of = jax.nn.sigmoid(value_in)
    return sigma_of * (1.0 + value_in * (1.0 - sigma_of))


MESH = pl.DeviceIdType.MESH


def greet(axes):
    barrier = pltpu.get_barrier_semaphore()
    count = 0
    for axis, size in axes:
        me = lax.axis_index(axis)
        for k in range(1, size):
            pl.semaphore_signal(
                barrier, inc=1, device_id={axis: lax.rem(me + k, size)}, device_id_type=MESH
            )
        count += size - 1
    pl.semaphore_wait(barrier, count)


def total_kernel(axes, x_ref, out_ref, *scratch):
    greet(axes)
    block = x_ref
    for number, (axis, size) in enumerate(axes):
        slots, stage, send_sems, recv_sems = scratch[4 * number : 4 * number + 4]
        me = lax.axis_index(axis)
        others = [lax.rem(me + k, size) for k in range(1, size)]
        for other in others:
            pltpu.make_async_remote_copy(
                src_ref=block,
                dst_ref=slots.at[me],
                send_sem=send_sems.at[other],
                recv_sem=recv_sems.at[me],
                device_id={axis: other},
                device_id_type=MESH,
            ).start()
        slots[me] = block[...]
        for other in others:
            copy = pltpu.make_async_remote_copy(
                src_ref=block,
                dst_ref=slots.at[other],
                send_sem=send_sems.at[other],
                recv_sem=recv_sems.at[other],
                device_id={axis: other},
                device_id_type=MESH,
            )
            copy.wait_recv()
            copy.wait_send()
        total = slots[0]
        for k in range(1, size):
            total = total + slots[k]
        if number == len(axes) - 1:
            out_ref[...] = total
        else:
            stage[...] = total
            block = stage


def total_of(left, right, axes):
    width = left.shape[0]
    packed = jnp.concatenate([left, right], 0).reshape(-1, 128)
    sized = tuple((axis, lax.axis_size(axis)) for axis in axes)
    scratch = []
    for _, size in sized:
        scratch += [
            pltpu.VMEM((size,) + packed.shape, F32),
            pltpu.VMEM(packed.shape, F32),
            pltpu.SemaphoreType.DMA((size,)),
            pltpu.SemaphoreType.DMA((size,)),
        ]
    number = 1 + (width != 512) + 2 * (len(axes) == 1)
    summed = pl.pallas_call(
        functools.partial(total_kernel, sized),
        out_shape=jax.ShapeDtypeStruct(packed.shape, F32),
        in_specs=[pl.BlockSpec(memory_space=pltpu.VMEM)],
        out_specs=pl.BlockSpec(memory_space=pltpu.VMEM),
        scratch_shapes=scratch,
        compiler_params=pltpu.CompilerParams(collective_id=number, has_side_effects=True),
        name="total",
    )(packed).reshape(2, width)
    return summed[0], summed[1]


def normalize(raw_value, column_sums, squares, pixel_count, norm_gain, norm_shift):
    center = column_sums / pixel_count
    spread_of = squares / pixel_count - center * center
    scaling = lax.rsqrt(spread_of + EPS)
    unit_value = (raw_value - center) * scaling
    return (unit_value * norm_gain + norm_shift, unit_value, scaling)


def moments(raw_value, living, axes):
    return total_of(
        jnp.sum(living * raw_value, 0), jnp.sum(living * raw_value * raw_value, 0), axes
    )


def norm_back(grad_out, unit_value, scaling, norm_gain, living, pixel_count, axes):
    grad_gain, grad_shift = total_of(
        jnp.sum(living * grad_out * unit_value, 0), jnp.sum(living * grad_out, 0), axes
    )
    grad_raw = (
        living
        * (norm_gain * scaling)
        * (grad_out - grad_shift / pixel_count - unit_value * grad_gain / pixel_count)
    )
    return (grad_raw, grad_gain, grad_shift)


def swap(value, bit):
    return lax.ppermute(value, "rep", [(k, k ^ bit) for k in range(4)])


def scatter_rep(value):
    return lax.psum_scatter(value.astype(BF16), "rep", scatter_dimension=0, tiled=True)


def swap_x(value):
    return lax.ppermute(value, "dp", [(k, k ^ 1) for k in range(lax.axis_size("dp"))])


def own_half(value, parity):
    halves = value.reshape((2, value.shape[0] // 2) + value.shape[1:])
    return lax.dynamic_index_in_dim(halves, parity, 0, keepdims=False)


def both_halves(mine, other, parity):
    return jnp.concatenate(
        [jnp.where(parity == 0, mine, other), jnp.where(parity == 0, other, mine)], 0
    )


def total_dp(value):
    parts = lax.axis_size("dp")
    rows = value.shape[0]
    padded = -(-rows // (8 * parts)) * 8 * parts
    value = jnp.pad(value, ((0, padded - rows), (0, 0)))
    share = lax.psum_scatter(value, "dp", scatter_dimension=0, tiled=True)
    return lax.all_gather(share, "dp", axis=0, tiled=True)[:rows].astype(F32)


def shards(
    inputs,
    layout,
    labels,
    cot_depth,
    w_reduce,
    w_spatial,
    w_expand,
    w_heads,
    w_gates,
    w_messages,
    w_classes,
    gain_mid,
    shift_mid,
    gain_wide,
    shift_wide,
    gain_head,
    shift_head,
):
    pixels = inputs.shape[0]
    middle = w_reduce.shape[1]
    classes = w_classes.shape[1]
    group = lax.axis_size("rep")
    everyone = ("rep", "dp")
    rep = lax.axis_index("rep")
    parity = rep % 2
    upper = rep // 2
    first_row = lax.axis_index("dp") * group
    own_info = geometry(lax.dynamic_slice_in_dim(layout, first_row + rep, 1, 0), pixels)
    group_info = geometry(lax.dynamic_slice_in_dim(layout, first_row, group, 0), pixels)
    living = own_info[2][0].astype(F32)[:, None]
    group_living = group_info[2].astype(F32)
    living_all = group_living.reshape(group * pixels, 1)
    pixel_count = jnp.sum(
        jnp.minimum(layout[:, 0] * layout[:, 1] * layout[:, 2], pixels)
    ).astype(F32)
    split = lax.axis_size("dp") == 8
    if split:
        side = lax.axis_index("dp") % 2
        side_of = jnp.reshape(side, (1,)).astype(jnp.int32)
        beside_row = first_row + group * (1 - 2 * side)
        shifts_beside = shift_matrices(
            geometry(lax.dynamic_slice_in_dim(layout, beside_row, group, 0), pixels), 1
        )
        columns = [[z_at * 2 + k for z_at in range(4)] for k in range(2)]
    zero = jnp.zeros((1,), jnp.int32)
    first = jnp.reshape(9 * parity, (1,)).astype(jnp.int32)

    (
        reduced,
        sums_one,
        hidden_one,
        spatial,
        sums_two,
        hidden_two,
        expanded,
        sums_three,
        trunk_all,
        headed,
        shifts_own,
        shifts_all,
    ) = trunk_forward(
        inputs,
        layout,
        w_reduce,
        w_spatial,
        w_expand,
        w_heads,
        gain_mid,
        shift_mid,
        gain_wide,
        shift_wide,
    )
    shifts_own = shifts_own[:, None]
    trunk_all = trunk_all.reshape(group * pixels, -1)
    headed = headed.reshape(group * pixels, middle)
    normed_one, unit_one, scale_one = normalize(
        reduced, sums_one[0], sums_one[1], pixel_count, gain_mid[0], shift_mid[0]
    )
    normed_two, unit_two, scale_two = normalize(
        spatial, sums_two[0], sums_two[1], pixel_count, gain_mid[1], shift_mid[1]
    )
    normed_three, unit_three, scale_three = normalize(
        expanded, sums_three[0], sums_three[1], pixel_count, gain_wide, shift_wide
    )
    pre_act = normed_three + inputs.astype(F32)
    if split:
        trunk_mine = swap_x(own_half(trunk_all, parity))

    own_gain = lax.dynamic_slice_in_dim(gain_head, rep * middle, middle, 0)
    own_shift = lax.dynamic_slice_in_dim(shift_head, rep * middle, middle, 0)
    sums_head, squares_head = moments(headed, living_all, ("dp",))
    normed_head, unit_head, scale_head = normalize(
        headed, sums_head, squares_head, pixel_count, own_gain, own_shift
    )
    rounded = jax.nn.silu(normed_head).astype(BF16)
    heads_all = lax.all_gather(rounded, "rep", axis=0, tiled=False)

    is_depth = upper == 0
    source = jnp.where(
        is_depth,
        jnp.concatenate([heads_all[1], heads_all[2], heads_all[3]], 1),
        jnp.concatenate([heads_all[0], heads_all[1], heads_all[2]], 1),
    )
    if split:
        source_mine = swap_x(own_half(source, parity))
    partial = rows_forward(first, source, w_messages, shifts_all, 2).reshape(
        2, 2, pixels, middle
    )

    if split:
        partial, trunk_mine = lax.optimization_barrier((partial, trunk_mine))
        trunk_other = swap(trunk_mine, 1)

    def of_parity(value, which):
        return lax.dynamic_index_in_dim(value, which, 1, keepdims=False)

    def rows_of(value):
        return value.reshape(2 * pixels, value.shape[-1])

    message = rows_of(of_parity(partial, parity) + swap(of_parity(partial, 1 - parity), 1))
    stream = rows_of(
        of_parity(
            jnp.where(is_depth, heads_all[0], heads_all[3]).reshape(2, 2, pixels, middle), parity
        )
    )
    own_gates = lax.dynamic_slice_in_dim(w_gates, upper * middle, middle, 0)
    stream_living = rows_of(of_parity(group_living.reshape(2, 2, pixels, 1), parity))
    cot_other = swap(cot_depth, 2)
    labels_other = swap(labels, 2)
    stream_cot = jnp.concatenate([cot_depth, cot_other], 0).astype(F32)
    stream_labels = jnp.concatenate([labels_other, labels], 0)
    gate = jax.nn.sigmoid(product(stream, own_gates))
    full = stream.astype(F32) + gate * message
    full_low = full.astype(BF16)
    logits_full = product(full_low, w_classes)
    probs = jax.nn.softmax(logits_full, axis=1)
    onehot_table = (
        stream_labels[:, None] == jnp.arange(classes, dtype=jnp.int32)[None, :]
    ).astype(F32)
    grad_logits = (stream_living * (probs - onehot_table)).astype(BF16)
    classes_local = inner_rows(full_low, jnp.where(is_depth, 0.0, 1.0).astype(BF16) * grad_logits)
    grad_stream = jnp.where(
        is_depth, stream_living * stream_cot, against(grad_logits, w_classes)
    )
    depth_other = swap(full[pixels:], 2)
    logits_other = swap(logits_full[:pixels], 2)
    depth = living * jnp.where(is_depth, full[:pixels], depth_other)
    logits = living * jnp.where(is_depth, logits_other, logits_full[pixels:])
    grad_gate = (grad_stream * message * gate * (1.0 - gate)).astype(BF16)
    grad_message = (grad_stream * gate).astype(BF16)
    gates_local = inner_rows(stream, grad_gate).astype(BF16)
    gates_local = gates_local.reshape(2, pixels, middle)
    if not split:
        gates_share = lax.dynamic_index_in_dim(gates_local, parity, 0, keepdims=False).astype(F32)
        gates_share += swap(
            lax.dynamic_index_in_dim(gates_local, 1 - parity, 0, keepdims=False), 1
        ).astype(F32)
    direct = (grad_stream + against(grad_gate, own_gates)).astype(BF16)

    def both_parities(value, other):
        value = value.reshape(2, pixels, middle)
        other = other.reshape(2, pixels, middle)
        even = jnp.where(parity == 0, value, other)
        odd = jnp.where(parity == 0, other, value)
        return jnp.stack([even, odd], 1).reshape(4 * pixels, middle)

    message_all = both_parities(grad_message, swap(grad_message, 1))
    direct_all = both_parities(direct, jnp.zeros_like(direct))
    if split:
        message_cut = message_all.reshape(4 * pixels, 4, 2, middle // 8)
        cut_own = lax.dynamic_index_in_dim(message_cut, side, 2, keepdims=False)
        cut_sent = lax.dynamic_index_in_dim(message_cut, 1 - side, 2, keepdims=False)
        cut_own = cut_own.reshape(4 * pixels, middle // 2)
        cut_beside = swap_x(cut_sent.reshape(4 * pixels, middle // 2))
        source_grad = rows_data(
            first, message_all, w_messages, shifts_all, 2, source.shape[1] // 2
        )
        source_grad, source_mine, cut_beside, trunk_other = lax.optimization_barrier(
            (source_grad, source_mine, cut_beside, trunk_other)
        )
        source_beside = both_halves(source_mine, swap(source_mine, 1), parity)
        trunk_beside = both_halves(trunk_mine, trunk_other, parity)
    else:
        source_grad, messages_local = rows_back(
            first, message_all, source, w_messages, shifts_all, 2, BF16
        )
    thirds = [source_grad[:, k * middle : (k + 1) * middle] for k in range(3)]
    by_head = jnp.stack(
        [
            jnp.where(is_depth, direct_all, thirds[0]),
            jnp.where(is_depth, thirds[0], thirds[1]),
            jnp.where(is_depth, thirds[1], thirds[2]),
            jnp.where(is_depth, thirds[2], direct_all),
        ],
        0,
    )
    feat_grad = lax.psum_scatter(by_head, "rep", scatter_dimension=0, tiled=False)
    if split:
        messages_local = rows_split(
            first, cut_own, cut_beside, source, source_beside, shifts_all, shifts_beside, 2, 9
        )
        feat_grad, messages_local, trunk_beside = lax.optimization_barrier(
            (feat_grad, messages_local, trunk_beside)
        )
        grad_messages = lax.psum_scatter(
            messages_local, "dp", scatter_dimension=0, tiled=True, axis_index_groups=columns
        )
    else:
        grad_messages = lax.psum_scatter(messages_local, "dp", scatter_dimension=1, tiled=True)
    head_raw, gain_grad_head, shift_grad_head = norm_back(
        feat_grad.astype(F32) * silu_slope(normed_head),
        unit_head,
        scale_head,
        own_gain,
        living_all,
        pixel_count,
        ("dp",),
    )
    head_low = head_raw.astype(BF16)
    if split:
        head_beside = swap_x(head_low)
        trunk_part = heads_data(head_low, w_heads, shifts_all)
        trunk_part, head_beside = lax.optimization_barrier((trunk_part, head_beside))
        heads_local = heads_split(
            side_of,
            head_low,
            head_beside,
            trunk_all,
            trunk_beside,
            shifts_all,
            shifts_beside,
            4,
            256,
        )
    else:
        heads_local = heads_weight(head_low, trunk_all, shifts_all)
        grad_heads = lax.psum_scatter(heads_local, "dp", scatter_dimension=1, tiled=True)
        trunk_part = heads_data(head_low, w_heads, shifts_all)
    trunk_grad = lax.psum_scatter(trunk_part, "rep", scatter_dimension=0, tiled=True)
    if split:
        trunk_grad, heads_local = lax.optimization_barrier((trunk_grad, heads_local))
        grad_heads = lax.psum_scatter(
            heads_local, "dp", scatter_dimension=0, tiled=False, axis_index_groups=columns
        )
    trunk_grad = trunk_grad.astype(F32)
    pre_grad = trunk_grad * silu_slope(pre_act)
    expand_raw, grad_gain_wide, grad_shift_wide = norm_back(
        pre_grad, unit_three, scale_three, gain_wide, living, pixel_count, everyone
    )
    expand_low = expand_raw.astype(BF16)
    expand_local = inner_rows(hidden_two, expand_low).astype(BF16)
    hidden_two_grad = against(expand_low, w_expand)
    spatial_raw, gain_grad_two, shift_grad_two = norm_back(
        hidden_two_grad * silu_slope(normed_two),
        unit_two,
        scale_two,
        gain_mid[1],
        living,
        pixel_count,
        everyone,
    )
    spatial_low = spatial_raw.astype(BF16)
    hidden_one_grad, spatial_local = rows_back(
        zero, spatial_low, hidden_one, w_spatial, shifts_own, 1, F32
    )
    reduced_raw, gain_grad_one, shift_grad_one = norm_back(
        hidden_one_grad * silu_slope(normed_one),
        unit_one,
        scale_one,
        gain_mid[0],
        living,
        pixel_count,
        everyone,
    )
    reduced_low = reduced_raw.astype(BF16)
    reduce_local = inner_rows(inputs, reduced_low).astype(BF16)
    if split:
        reduced_low, grad_messages = lax.optimization_barrier((reduced_low, grad_messages))
        grad_messages = grad_messages.T
    input_grad = pre_grad + against(reduced_low, w_reduce)
    if split:
        wide = w_expand.shape[1]
        cuts = wide // middle

        def side_by_side(value):
            value = value.reshape(4, -1, value.shape[1])
            return jnp.concatenate(
                [value[:, :, k : k + middle] for k in range(0, value.shape[2], middle)], 1
            )

        gates_zero = jnp.zeros_like(gates_local)
        gates_every = jnp.where(
            is_depth,
            jnp.concatenate([gates_local, gates_zero], 0),
            jnp.concatenate([gates_zero, gates_local], 0),
        )
        classes_wide = jnp.pad(classes_local.astype(BF16), ((0, 0), (0, 128 - classes)))
        classes_wide = classes_wide.reshape(4, 4, -1, 128)
        classes_wide = jnp.concatenate([classes_wide[:, k] for k in range(4)], 2)
        pieces = [
            reduce_local.reshape(4, -1, middle),
            spatial_local.reshape(4, -1, middle),
            side_by_side(expand_local),
            gates_every,
            classes_wide,
        ]
        rows = [piece.shape[1] for piece in pieces]
        unit = 128 * CHUNKS
        missing = -sum(rows) % unit
        pieces.append(jnp.zeros((4, missing, middle), BF16))
        summed = small_total(jnp.concatenate(pieces, 1))
        starts = [sum(rows[:k]) for k in range(5)]
        grad_reduce, grad_spatial, expand_sum, grad_gates, classes_sum = [
            summed[at : at + size] for at, size in zip(starts, rows)
        ]
        expand_sum = expand_sum.reshape(cuts, -1, middle)
        grad_expand = jnp.concatenate([expand_sum[k] for k in range(cuts)], 1)
        classes_sum = jnp.concatenate(
            [classes_sum[:, k * 128 : (k + 1) * 128] for k in range(4)], 0
        )
        grad_classes = classes_sum[:, :classes]
    else:
        grad_expand = scatter_rep(expand_local)
        grad_spatial = scatter_rep(spatial_local)
        grad_reduce = scatter_rep(reduce_local)
        grad_classes = scatter_rep(classes_local)
        pieces = [
            gates_share.astype(BF16),
            grad_expand.reshape(-1, middle),
            grad_spatial,
            grad_classes.reshape(-1, middle),
        ]
        early = total_dp(jnp.concatenate(pieces, 0))
        rows = [piece.shape[0] for piece in pieces]
        starts = [sum(rows[:k]) for k in range(4)]
        grad_gates, expand_sum, grad_spatial, classes_sum = [
            early[at : at + size] for at, size in zip(starts, rows)
        ]
        grad_expand = expand_sum.reshape(grad_expand.shape)
        grad_classes = classes_sum.reshape(grad_classes.shape)
        grad_reduce = total_dp(grad_reduce)
    grad_gain_mid = jnp.stack([gain_grad_one, gain_grad_two], 0)
    grad_shift_mid = jnp.stack([shift_grad_one, shift_grad_two], 0)
    head_norms = lax.all_gather(
        jnp.stack([gain_grad_head, shift_grad_head], 0), "rep", axis=1, tiled=True
    )
    return (
        depth,
        logits,
        input_grad,
        grad_reduce,
        grad_spatial,
        grad_expand,
        grad_heads.astype(F32),
        grad_gates,
        grad_messages.astype(F32),
        grad_classes,
        grad_gain_mid,
        grad_shift_mid,
        grad_gain_wide,
        grad_shift_wide,
        head_norms[0],
        head_norms[1],
    )


def solution(mesh):
    in_specs = (
        P(("dp", "rep"), None),
        P(),
        P(("dp", "rep")),
        P(("dp", "rep"), None),
        P(),
        P(),
        P(),
        P("rep", None),
        P(),
        P("rep", None),
        P(),
        P(),
        P(),
        P(),
        P(),
        P(),
        P(),
    )
    out_specs = (
        P(("dp", "rep"), None),
        P(("dp", "rep"), None),
        P(("dp", "rep"), None),
        P("rep", None),
        P("rep", None),
        P("rep", None),
        P("rep", "dp"),
        P("rep", None),
        P("rep", "dp"),
        P("rep", None),
        P(),
        P(),
        P(),
        P(),
        P(),
        P(),
    )
    return jax.shard_map(shards, mesh=mesh, in_specs=in_specs, out_specs=out_specs, check_vma=False)
```

```python
import functools

import jax
import jax.numpy as jnp
from jax import lax
from jax.experimental import pallas as pl
from jax.experimental.pallas import tpu as pltpu
from jax.sharding import PartitionSpec as P

EPS = 1e-05
F32 = jnp.float32
BF16 = jnp.bfloat16
VMEM_LIMIT = 60 * 2**20


def geometry(layout, span):
    position = jnp.arange(span, dtype=jnp.int32)
    height = layout[:, 0:1]
    map_width = layout[:, 1:2]
    images = layout[:, 2:3]
    map_area = height * map_width
    inside = position[None, :] % map_area
    row_of = inside // map_width
    col_of = inside % map_width
    living = position[None, :] < images * map_area
    return (row_of, col_of, living, height, map_width)


def neighbours(shape_info, dilation):
    row_of, col_of, living, height, map_width = shape_info
    span = row_of.shape[1]
    position = jnp.arange(span, dtype=jnp.int32)
    every = []
    for step_row in (-1, 0, 1):
        for step_col in (-1, 0, 1):
            target_row = row_of + dilation * step_row
            target_col = col_of + dilation * step_col
            inside = (
                living
                & (target_row >= 0)
                & (target_row < height)
                & (target_col >= 0)
                & (target_col < map_width)
            )
            neighbour = position[None, :] + dilation * (step_row * map_width + step_col)
            every.append(jnp.where(inside, neighbour, -1))
    return jnp.concatenate(every, 0).T


def shift_matrices(shape_info, dilation):
    devices, span = shape_info[0].shape
    picks = neighbours(shape_info, dilation).T.reshape(9, devices, span, 1)
    return (picks == jnp.arange(span, dtype=jnp.int32)).astype(BF16)


def product(left_side, right_side):
    return jnp.dot(left_side, right_side, preferred_element_type=F32)


def inner_rows(left_side, right_side):
    return lax.dot_general(
        left_side, right_side, (((0,), (0,)), ((), ())), preferred_element_type=F32
    )


def against(left_side, right_side):
    return lax.dot_general(
        left_side, right_side, (((1,), (1,)), ((), ())), preferred_element_type=F32
    )


def params():
    return pltpu.CompilerParams(vmem_limit_bytes=VMEM_LIMIT)


def cost(flops, moved):
    return pl.CostEstimate(flops=flops, bytes_accessed=moved, transcendentals=0)


def shifted(g_ref, s_ref):
    blocks, span = s_ref.shape[1], s_ref.shape[2]
    return jnp.concatenate(
        [
            inner_rows(s_ref[0, k], g_ref[pl.ds(k * span, span), :]).astype(BF16)
            for k in range(blocks)
        ],
        0,
    )


def heads_data_kernel(g_ref, w_ref, s_ref, out_ref, total):
    tap = pl.program_id(0)
    taken = shifted(g_ref, s_ref)
    wide = w_ref.shape[1]
    step = 512

    @pl.when(tap == 0)
    def _():
        total[...] = jnp.zeros_like(total)

    for c in range(0, wide, step):
        total[:, c : c + step] += product(taken, w_ref[:, c : c + step])

    @pl.when(tap == pl.num_programs(0) - 1)
    def _():
        out_ref[...] = total[...].astype(out_ref.dtype)


def heads_data(g, w_heads, shifts):
    rows, outs = g.shape
    taps, blocks, span, _ = shifts.shape
    wide = w_heads.shape[1] // taps
    return pl.pallas_call(
        heads_data_kernel,
        grid=(taps,),
        in_specs=[
            pl.BlockSpec((rows, outs), lambda t: (0, 0)),
            pl.BlockSpec((outs, wide), lambda t: (0, t)),
            pl.BlockSpec((1, blocks, span, span), lambda t: (t, 0, 0, 0)),
        ],
        out_specs=pl.BlockSpec((rows, wide), lambda t: (0, 0)),
        out_shape=jax.ShapeDtypeStruct((rows, wide), BF16),
        scratch_shapes=[pltpu.VMEM((rows, wide), F32)],
        compiler_params=params(),
        cost_estimate=cost(2 * rows * wide * outs * taps, w_heads.size * 2),
        name="heads_data",
    )(g, w_heads, shifts)


def heads_weight_kernel(g_ref, u_ref, s_ref, out_ref):
    taken = shifted(g_ref, s_ref)
    step = 512
    for c in range(0, u_ref.shape[1], step):
        out_ref[:, c : c + step] = inner_rows(taken, u_ref[:, c : c + step]).astype(out_ref.dtype)


def heads_weight(g, u, shifts):
    rows, outs = g.shape
    wide = u.shape[1]
    taps, blocks, span, _ = shifts.shape
    return pl.pallas_call(
        heads_weight_kernel,
        grid=(taps,),
        in_specs=[
            pl.BlockSpec((rows, outs), lambda t: (0, 0)),
            pl.BlockSpec((rows, wide), lambda t: (0, 0)),
            pl.BlockSpec((1, blocks, span, span), lambda t: (t, 0, 0, 0)),
        ],
        out_specs=pl.BlockSpec((outs, wide), lambda t: (0, t)),
        out_shape=jax.ShapeDtypeStruct((outs, taps * wide), BF16),
        compiler_params=params(),
        cost_estimate=cost(2 * rows * wide * outs * taps, outs * taps * wide * 2),
        name="heads_weight",
    )(g, u, shifts)


def rows_back_kernel(halves, first_ref, g_ref, u_ref, w_ref, s_ref, du_ref, dw_ref, total):
    step = pl.program_id(0)
    taken = shifted(g_ref, s_ref)
    depth = w_ref.shape[0]
    which = (step + first_ref[0]) % halves

    @pl.when(step == 0)
    def _():
        total[...] = jnp.zeros_like(total)

    total[which] += against(taken, w_ref[...])
    dw_ref[...] = inner_rows(u_ref[...], taken).astype(dw_ref.dtype)

    @pl.when(step == pl.num_programs(0) - 1)
    def _():
        for k in range(halves):
            du_ref[:, k * depth : (k + 1) * depth] = total[k].astype(du_ref.dtype)


def rows_back(first, g, u, w, shifts, halves, kind):
    rows, outs = g.shape
    depth = u.shape[1] // halves
    steps = w.shape[0] // depth
    taps, blocks, span, _ = shifts.shape
    return pl.pallas_call(
        functools.partial(rows_back_kernel, halves),
        grid_spec=pltpu.PrefetchScalarGridSpec(
            num_scalar_prefetch=1,
            grid=(steps,),
            in_specs=[
                pl.BlockSpec((rows, outs), lambda b, f: (0, 0)),
                pl.BlockSpec((rows, depth), lambda b, f: (0, (b + f[0]) % halves)),
                pl.BlockSpec((depth, outs), lambda b, f: (b, 0)),
                pl.BlockSpec((1, blocks, span, span), lambda b, f: ((b + f[0]) // halves, 0, 0, 0)),
            ],
            out_specs=[
                pl.BlockSpec((rows, halves * depth), lambda b, f: (0, 0)),
                pl.BlockSpec((depth, outs), lambda b, f: (b, 0)),
            ],
            scratch_shapes=[pltpu.VMEM((halves, rows, depth), F32)],
        ),
        out_shape=[
            jax.ShapeDtypeStruct((rows, halves * depth), kind),
            jax.ShapeDtypeStruct(w.shape, BF16),
        ],
        compiler_params=params(),
        cost_estimate=cost(4 * rows * w.size, w.size * 4),
        name="rows_back",
    )(first, g, u, w, shifts)


def heads_split_kernel(per_tap, units, lanes, x_ref, g_ref, h_ref, u_ref, v_ref, s_ref, r_ref, out_ref, taken):
    blocks, span = s_ref.shape[1], s_ref.shape[2]
    rows = blocks * span
    start = units * (2 * pl.program_id(0) + x_ref[0])

    @pl.loop(0, units)
    def _(unit):
        tap, chunk = (start + unit) // per_tap, (start + unit) % per_tap

        @pl.when((unit == 0) | (chunk == 0))
        def _():
            for side, (a_ref, m_ref) in enumerate(((g_ref, s_ref), (h_ref, r_ref))):
                for k in range(blocks):
                    at = (side * blocks + k) * span
                    taken[:, at : at + span] = inner_rows(
                        a_ref[k * span : (k + 1) * span, :], m_ref[tap, k]
                    ).astype(BF16)

        at = pl.ds(pl.multiple_of(chunk * lanes, lanes), lanes)
        to = pl.ds(pl.multiple_of(unit * lanes, lanes), lanes)
        out_ref[0, :, to] = (
            product(taken[:, :rows], u_ref[:, at]) + product(taken[:, rows:], v_ref[:, at])
        ).astype(BF16)


def heads_split(x, g, h, u, v, s, r, shards, lanes):
    rows, outs = g.shape
    wide = u.shape[1]
    taps, blocks, span, _ = s.shape
    units = taps * wide // (2 * shards * lanes)
    per_tap = wide // lanes
    whole = pl.BlockSpec(memory_space=pltpu.VMEM)
    return pl.pallas_call(
        functools.partial(heads_split_kernel, per_tap, units, lanes),
        grid_spec=pltpu.PrefetchScalarGridSpec(
            num_scalar_prefetch=1,
            grid=(shards,),
            in_specs=[whole] * 6,
            out_specs=pl.BlockSpec((1, outs, units * lanes), lambda i, f: (i, 0, 0)),
            scratch_shapes=[pltpu.VMEM((outs, 2 * rows), BF16)],
        ),
        out_shape=jax.ShapeDtypeStruct((shards, outs, units * lanes), BF16),
        compiler_params=params(),
        cost_estimate=cost(2 * rows * wide * outs * taps, outs * taps * wide * 2),
        name="heads_split",
    )(x, g, h, u, v, s, r)


CHUNKS = 4


def small_kernel(p_ref, out_ref, half_ref, core_in, core_out, y_in, x_out, x_in, z_out, z_in, send, recv):
    rep, dp = lax.axis_index("rep"), lax.axis_index("dp")
    par, upper = lax.rem(rep, 2), rep // 2
    x, z = lax.rem(dp, 2), dp // 2
    mate, far, beside = rep + 1 - 2 * par, rep + 2 - 4 * upper, dp + 1 - 2 * x
    zs = [lax.rem(z + k, 4) for k in range(1, 4)]
    barrier = pltpu.get_barrier_semaphore()
    partners = [{"rep": mate}, {"rep": far}, {"dp": beside}] + [{"dp": 2 * k + x} for k in zs]
    for partner in partners:
        pl.semaphore_signal(barrier, inc=1, device_id=partner, device_id_type=MESH)
    pl.semaphore_wait(barrier, len(partners))
    rows = p_ref.shape[1] // CHUNKS
    half, eighth = rows // 2, rows // 8

    def span(c, at=0, size=rows):
        return pl.ds(pl.multiple_of(c * rows + at, 16), size)

    def remote(src, dst, c, slot, to, slot_in=None):
        return pltpu.make_async_remote_copy(
            src_ref=src,
            dst_ref=dst,
            send_sem=send.at[c, slot],
            recv_sem=recv.at[c, slot if slot_in is None else slot_in],
            device_id=to,
            device_id_type=MESH,
        )

    def core_copy(c, hi):
        return remote(
            p_ref.at[2 * hi + 1 - par, span(c)], core_in.at[hi, span(c)], c, hi, {"rep": mate}
        )

    def y_copy(c):
        return remote(core_out.at[span(c)], y_in.at[span(c)], c, 2, {"rep": far})

    def x_copy(c):
        return remote(
            x_out.at[pl.ds(c * half, half)], x_in.at[pl.ds(c * half, half)], c, 3, {"dp": beside}
        )

    def z_copy(c, k, incoming):
        sent = pl.ds(pl.multiple_of(c * half + k * eighth, 16), eighth)
        slot = k if incoming else z
        return remote(
            z_out.at[sent], z_in.at[slot, pl.ds(c * eighth, eighth)], c, 4 + k, {"dp": 2 * k + x}, 4 + slot
        )

    def back_copy(c, k, incoming):
        place = span(c, x * half + (k if incoming else z) * eighth, eighth)
        return remote(
            half_ref.at[place], half_ref.at[place], c, 8 + k, {"dp": 2 * k + x}, 8 + (k if incoming else z)
        )

    def last_copy(c, incoming):
        place = span(c, (1 - x if incoming else x) * half, half)
        return remote(half_ref.at[place], half_ref.at[place], c, 12, {"dp": beside})

    def step(stage, c):
        if stage == 0:
            for hi in range(2):
                core_copy(c, hi).start()
        elif stage == 1:
            for hi in range(2):
                core_copy(c, hi).wait_recv()
            core_out[span(c)] = (
                p_ref[2 * (1 - upper) + par, span(c)].astype(F32)
                + core_in[1 - upper, span(c)].astype(F32)
            ).astype(BF16)
            y_copy(c).start()
        elif stage == 2:
            y_copy(c).wait_recv()

            def both(at):
                place = span(c, at, half)
                return (
                    p_ref[rep, place].astype(F32)
                    + core_in[upper, place].astype(F32)
                    + y_in[place].astype(F32)
                )

            x_out[pl.ds(c * half, half)] = both((1 - x) * half).astype(BF16)
            x_copy(c).start()
            z_out[pl.ds(c * half, half)] = both(x * half).astype(BF16)
        elif stage == 3:
            x_copy(c).wait_recv()
            at = pl.ds(c * half, half)
            z_out[at] = (z_out[at].astype(F32) + x_in[at].astype(F32)).astype(BF16)
            for k in zs:
                z_copy(c, k, False).start()
        elif stage == 4:
            for k in zs:
                z_copy(c, k, True).wait_recv()
            z_in[z, pl.ds(c * eighth, eighth)] = z_out[
                pl.ds(pl.multiple_of(c * half + z * eighth, 16), eighth)
            ]
            total = z_in[0, pl.ds(c * eighth, eighth)].astype(F32)
            for k in range(1, 4):
                total = total + z_in[k, pl.ds(c * eighth, eighth)].astype(F32)
            half_ref[span(c, x * half + z * eighth, eighth)] = total.astype(BF16)
            for k in zs:
                back_copy(c, k, False).start()
        elif stage == 5:
            for k in zs:
                back_copy(c, k, True).wait_recv()
            last_copy(c, False).start()
        else:
            last_copy(c, True).wait_recv()
            out_ref[span(c)] = half_ref[span(c)].astype(F32)
            for hi in range(2):
                core_copy(c, hi).wait_send()
            y_copy(c).wait_send()
            x_copy(c).wait_send()
            for k in zs:
                z_copy(c, k, False).wait_send()
                back_copy(c, k, False).wait_send()
            last_copy(c, False).wait_send()

    for turn in range(CHUNKS + 6):
        for c in range(CHUNKS):
            if 0 <= turn - c <= 6:
                step(turn - c, c)


def small_total(parts):
    quarters, rows, lanes = parts.shape
    return pl.pallas_call(
        small_kernel,
        out_shape=jax.ShapeDtypeStruct((rows, lanes), F32),
        in_specs=[pl.BlockSpec(memory_space=pltpu.VMEM)],
        out_specs=pl.BlockSpec(memory_space=pltpu.VMEM),
        scratch_shapes=[
            pltpu.VMEM((rows, lanes), BF16),
            pltpu.VMEM((2, rows, lanes), BF16),
            pltpu.VMEM((rows, lanes), BF16),
            pltpu.VMEM((rows, lanes), BF16),
            pltpu.VMEM((rows // 2, lanes), BF16),
            pltpu.VMEM((rows // 2, lanes), BF16),
            pltpu.VMEM((rows // 2, lanes), BF16),
            pltpu.VMEM((4, rows // 8, lanes), BF16),
            pltpu.SemaphoreType.DMA((CHUNKS, 13)),
            pltpu.SemaphoreType.DMA((CHUNKS, 13)),
        ],
        compiler_params=pltpu.CompilerParams(
            collective_id=9, has_side_effects=True, vmem_limit_bytes=VMEM_LIMIT
        ),
        name="small_total",
    )(parts)


def send_to(axis, to, src, dst, send_sem, recv_sem):
    return pltpu.make_async_remote_copy(
        src_ref=src,
        dst_ref=dst,
        send_sem=send_sem,
        recv_sem=recv_sem,
        device_id={axis: to},
        device_id_type=MESH,
    )


def total_along(axis, size, block, slots, send_sems, recv_sems, meanwhile=None):
    me = lax.axis_index(axis)
    others = [lax.rem(me + k, size) for k in range(1, size)]
    for other in others:
        send_to(axis, other, block, slots.at[me], send_sems.at[other], recv_sems.at[me]).start()
    slots[me] = block[...]
    if meanwhile is not None:
        meanwhile()
    for other in others:
        copy = send_to(
            axis, other, block, slots.at[other], send_sems.at[other], recv_sems.at[other]
        )
        copy.wait_recv()
        copy.wait_send()
    total = slots[0]
    for k in range(1, size):
        total = total + slots[k]
    return total


def place_in_map(layout_ref, device, span):
    position = lax.broadcasted_iota(jnp.int32, (span, 1), 0)
    large = layout_ref[device, 1] == 16
    row_of = jnp.where(large, position // 16, (position % 64) // 8)
    col_of = jnp.where(large, position % 16, position % 8)
    return position, row_of, col_of


def live_mask(layout_ref, device, span):
    position = lax.broadcasted_iota(jnp.int32, (span, 1), 0)
    return position < layout_ref[device, 0] * layout_ref[device, 1] * layout_ref[device, 2]


def live_column(layout_ref, device, span):
    return jnp.where(live_mask(layout_ref, device, span), 1.0, 0.0)


def inverse_count(areas_ref, span):
    areas = areas_ref[:, 0:1] * areas_ref[:, 1:2] * areas_ref[:, 2:3]
    return 1.0 / jnp.sum(jnp.minimum(areas, span).astype(F32), 0, keepdims=True)


def shift_block(layout_ref, device, dilation, tap, span):
    position, row_of, col_of = place_in_map(layout_ref, device, span)
    height, map_width = layout_ref[device, 0], layout_ref[device, 1]
    step_row, step_col = dilation * (tap // 3 - 1), dilation * (tap % 3 - 1)
    target_row, target_col = row_of + step_row, col_of + step_col
    inside = (
        live_mask(layout_ref, device, span)
        & (target_row >= 0)
        & (target_row < height)
        & (target_col >= 0)
        & (target_col < map_width)
    )
    neighbour = jnp.where(inside, position + step_row * map_width + step_col, -1)
    lanes = lax.broadcasted_iota(jnp.int32, (span, span), 1)
    return jnp.where(neighbour == lanes, 1.0, 0.0).astype(BF16)


def trunk_kernel(
    sizes,
    in_ref,
    layout_ref,
    areas_ref,
    w_reduce_ref,
    w_spatial_hbm,
    w_expand_hbm,
    w_heads_hbm,
    gain_mid_ref,
    shift_mid_ref,
    gain_wide_ref,
    shift_wide_ref,
    reduced_ref,
    sums_one_ref,
    hidden_one_ref,
    spatial_ref,
    sums_two_ref,
    hidden_two_ref,
    expanded_ref,
    sums_three_ref,
    trunk_ref,
    headed_ref,
    own_shift_ref,
    all_shift_ref,
    w_spatial_ref,
    w_expand_ref,
    w_heads_ref,
    block_mid,
    block_wide,
    slots_mid_rep,
    slots_mid_dp,
    slots_wide_rep,
    slots_wide_dp,
    load_sems,
    rep_send,
    rep_recv,
    dp_send,
    dp_recv,
    gather_send,
    gather_recv,
):
    n_rep, n_dp = sizes
    rep = lax.axis_index("rep")
    par, upper = lax.rem(rep, 2), rep // 2
    mate, far = rep + 1 - 2 * par, rep + 2 - 4 * upper
    span, wide = in_ref.shape
    middle = w_reduce_ref.shape[1]
    taps = own_shift_ref.shape[0]
    loads = [
        pltpu.make_async_copy(w_spatial_hbm, w_spatial_ref, load_sems.at[0]),
        pltpu.make_async_copy(w_expand_hbm, w_expand_ref, load_sems.at[1]),
    ]
    heads_load = pltpu.make_async_copy(w_heads_hbm, w_heads_ref, load_sems.at[2])
    for load in loads:
        load.start()
    heads_load.start()

    barrier = pltpu.get_barrier_semaphore()
    for axis, size in (("rep", n_rep), ("dp", n_dp)):
        me = lax.axis_index(axis)
        for k in range(1, size):
            pl.semaphore_signal(
                barrier, inc=1, device_id={axis: lax.rem(me + k, size)}, device_id_type=MESH
            )
    first_row = lax.axis_index("dp") * n_rep
    live = live_column(layout_ref, first_row + rep, span)
    inverse = inverse_count(areas_ref, span)

    def make_own():
        for t in range(taps):
            own_shift_ref[t] = shift_block(layout_ref, first_row + rep, 2, t, span)

    def make_all(first, last):
        def fill():
            for t in range(first, last):
                for p in range(n_rep):
                    all_shift_ref[t, p] = shift_block(layout_ref, first_row + p, 1, t, span)

        return fill

    def everywhere(number, value_ref, blocks, rep_slots, dp_slots, meanwhile, later):
        masked = live * value_ref[...]
        blocks[0, 0:1, :] = jnp.sum(masked, 0, keepdims=True)
        blocks[0, 1:2, :] = jnp.sum(masked * value_ref[...], 0, keepdims=True)
        if number == 0:
            pl.semaphore_wait(barrier, n_rep + n_dp - 2)
        blocks[1] = total_along(
            "rep", n_rep, blocks.at[0], rep_slots, rep_send.at[number], rep_recv.at[number], meanwhile
        )
        return total_along(
            "dp", n_dp, blocks.at[1], dp_slots, dp_send.at[number], dp_recv.at[number], later
        )

    def normed(value, sums, gain, shift):
        center = sums[0:1] * inverse
        scaling = lax.rsqrt(sums[1:2] * inverse - center * center + EPS)
        return (value - center) * (scaling * gain) + shift

    def silu(value):
        return value * jax.nn.sigmoid(value)

    reduced_ref[...] = product(in_ref[...], w_reduce_ref[...])
    sums = everywhere(
        0, reduced_ref, block_mid.at[0], slots_mid_rep.at[0], slots_mid_dp.at[0], make_own, None
    )
    sums_one_ref[...] = sums
    hidden_one_ref[...] = silu(
        normed(reduced_ref[...], sums, gain_mid_ref[0:1, :], shift_mid_ref[0:1, :])
    ).astype(BF16)
    loads[0].wait()
    spatial_ref[...] = jnp.zeros_like(spatial_ref)

    @pl.loop(0, taps)
    def _(t):
        moved = product(own_shift_ref[t], hidden_one_ref[...]).astype(BF16)
        at = pl.ds(pl.multiple_of(t * middle, middle), middle)
        spatial_ref[...] += product(moved, w_spatial_ref[at, :])

    sums = everywhere(
        1, spatial_ref, block_mid.at[1], slots_mid_rep.at[1], slots_mid_dp.at[1], make_all(0, 5), None
    )
    sums_two_ref[...] = sums
    hidden_two_ref[...] = silu(
        normed(spatial_ref[...], sums, gain_mid_ref[1:2, :], shift_mid_ref[1:2, :])
    ).astype(BF16)
    loads[1].wait()
    expanded_ref[...] = product(hidden_two_ref[...], w_expand_ref[...])
    sums = everywhere(
        2, expanded_ref, block_wide, slots_wide_rep, slots_wide_dp, make_all(5, 9), None
    )
    sums_three_ref[...] = sums

    own_rows = pl.ds(pl.multiple_of(par * span, span), span)
    mate_rows = pl.ds(pl.multiple_of((1 - par) * span, span), span)
    pre = normed(expanded_ref[...], sums, gain_wide_ref[...], shift_wide_ref[...])
    trunk_ref[upper, own_rows, :] = silu(pre + in_ref[...].astype(F32)).astype(BF16)
    parts = 4
    piece = span // parts

    def rows(parity, k):
        return pl.ds(pl.multiple_of(parity * span + k * piece, piece), piece)

    def across(side, k):
        at = trunk_ref.at[side, rows(par, k)]
        return send_to("rep", far, at, at, gather_send.at[k], gather_recv.at[k])

    def own_pass(parity):
        at = trunk_ref.at[upper, pl.ds(pl.multiple_of(parity * span, span), span)]
        return send_to("rep", mate, at, at, gather_send.at[parts], gather_recv.at[parts])

    def far_pass(parity, k):
        at = trunk_ref.at[1 - upper, rows(parity, k)]
        slot = parts + 1 + k
        return send_to("rep", mate, at, at, gather_send.at[slot], gather_recv.at[slot])

    for k in range(parts):
        across(upper, k).start()
    own_pass(par).start()
    headed_ref[...] = jnp.zeros_like(headed_ref)
    own_pass(1 - par).wait_recv()
    heads_load.wait()

    def convolve(side):
        @pl.loop(0, taps)
        def _(t):
            at = pl.ds(pl.multiple_of(t * wide, wide), wide)
            y = against(trunk_ref[side], w_heads_ref[:, at]).astype(BF16)
            for k in range(2):
                place = pl.ds(k * span, span)
                headed_ref[side, place, :] += product(
                    all_shift_ref[t, 2 * side + k], y[k * span : (k + 1) * span]
                )

    convolve(upper)
    for k in range(parts):
        across(1 - upper, k).wait_recv()
        far_pass(par, k).start()
    for k in range(parts):
        far_pass(1 - par, k).wait_recv()
    convolve(1 - upper)
    for k in range(parts):
        across(upper, k).wait_send()
        far_pass(par, k).wait_send()
    own_pass(par).wait_send()


def trunk_forward(
    inputs,
    layout,
    w_reduce,
    w_spatial,
    w_expand,
    w_heads,
    gain_mid,
    shift_mid,
    gain_wide,
    shift_wide,
):
    span, wide = inputs.shape
    middle = w_reduce.shape[1]
    n_rep, n_dp = lax.axis_size("rep"), lax.axis_size("dp")
    taps = 9
    vmem = pl.BlockSpec(memory_space=pltpu.VMEM)
    hbm = pl.BlockSpec(memory_space=pl.ANY)
    smem = pl.BlockSpec(memory_space=pltpu.SMEM)
    dma = pltpu.SemaphoreType.DMA
    shape = jax.ShapeDtypeStruct
    return pl.pallas_call(
        functools.partial(trunk_kernel, (n_rep, n_dp)),
        in_specs=[vmem, smem, vmem, vmem] + [hbm] * 3 + [vmem] * 4,
        out_specs=[vmem] * 12,
        out_shape=[
            shape((span, middle), F32),
            shape((2, middle), F32),
            shape((span, middle), BF16),
            shape((span, middle), F32),
            shape((2, middle), F32),
            shape((span, middle), BF16),
            shape((span, wide), F32),
            shape((2, wide), F32),
            shape((2, 2 * span, wide), BF16),
            shape((2, 2 * span, w_heads.shape[0]), F32),
            shape((taps, span, span), BF16),
            shape((taps, n_rep, span, span), BF16),
        ],
        scratch_shapes=[
            pltpu.VMEM(w_spatial.shape, BF16),
            pltpu.VMEM(w_expand.shape, BF16),
            pltpu.VMEM(w_heads.shape, BF16),
            pltpu.VMEM((2, 2, 2, middle), F32),
            pltpu.VMEM((2, 2, wide), F32),
            pltpu.VMEM((2, n_rep, 2, middle), F32),
            pltpu.VMEM((2, n_dp, 2, middle), F32),
            pltpu.VMEM((n_rep, 2, wide), F32),
            pltpu.VMEM((n_dp, 2, wide), F32),
            dma((3,)),
            dma((3, n_rep)),
            dma((3, n_rep)),
            dma((3, n_dp)),
            dma((3, n_dp)),
            dma((9,)),
            dma((9,)),
        ],
        compiler_params=pltpu.CompilerParams(
            collective_id=10, has_side_effects=True, vmem_limit_bytes=VMEM_LIMIT
        ),
        name="trunk_forward",
    )(
        inputs,
        layout,
        layout,
        w_reduce,
        w_spatial,
        w_expand,
        w_heads,
        gain_mid,
        shift_mid,
        gain_wide[None, :],
        shift_wide[None, :],
    )


MOVES = 28


def message_kernel(split, n_dp, classes, *refs):
    refs = list(refs)

    def take(count):
        taken, refs[:count] = refs[:count], []
        return taken

    layout_ref, areas_ref, headed_ref, s_ref, w_hbm, gates_w_ref, classes_w_ref = take(7)
    gain_ref, shift_ref, cot_ref, labels_ref = take(4)
    depth_ref, logits_ref, gates_ref, classes_ref, low_ref, norm_ref = take(6)
    if split:
        (out_ref,) = take(1)
    else:
        heads_ref, gm_ref = take(2)
    w_ref, live_ref, acc_ref, acc_in, stream_ref, direct_ref, cot_in, labels_in = take(8)
    depth_out, logits_out, picked_ref, far_ref, near_ref = take(5)
    core_out, core_in, far_out, far_in, near_out, near_in = take(6)
    sums_ref, slots_ref, load_sem, send, recv, dp_send, dp_recv = take(7)
    if split:
        heads_ref, gm_ref, beside_ref, cut_own, cut_out, cut_in, cut_taken = take(7)

    rep = lax.axis_index("rep")
    par, upper = lax.rem(rep, 2), rep // 2
    mate, far = rep + 1 - 2 * par, rep + 2 - 4 * upper
    first_row = lax.axis_index("dp") * 4
    side_x = lax.rem(lax.axis_index("dp"), 2)
    beside = lax.axis_index("dp") + 1 - 2 * side_x
    span = s_ref.shape[2]
    middle = headed_ref.shape[2]
    small = middle // 2
    load = pltpu.make_async_copy(w_hbm, w_ref, load_sem)
    load.start()

    barrier = pltpu.get_barrier_semaphore()
    me_dp = lax.axis_index("dp")
    for to in (mate, far):
        pl.semaphore_signal(barrier, inc=1, device_id={"rep": to}, device_id_type=MESH)
    for k in range(1, n_dp):
        pl.semaphore_signal(
            barrier, inc=1, device_id={"dp": lax.rem(me_dp + k, n_dp)}, device_id_type=MESH
        )

    def move(number, src, dst, to, axis="rep"):
        return send_to(axis, to, src, dst, send.at[number], recv.at[number])

    def block(parity):
        return pl.ds(pl.multiple_of(parity * span, span), span)

    for p in range(4):
        live_ref[p // 2, (p % 2) * span : (p % 2 + 1) * span, :] = live_column(
            layout_ref, first_row + p, span
        )
    inverse = inverse_count(areas_ref, span)

    def add_up(number, left, right):
        sums_ref[number, 0:1, :] = left
        sums_ref[number, 1:2, :] = right
        return total_along(
            "dp", n_dp, sums_ref.at[number], slots_ref.at[number], dp_send.at[number], dp_recv.at[number]
        )

    def column_sum(value):
        return jnp.sum(value, 0, keepdims=True)

    left, right = 0.0, 0.0
    for side in range(2):
        masked = live_ref[side] * headed_ref[side]
        left = left + column_sum(masked)
        right = right + column_sum(masked * headed_ref[side])
    pl.semaphore_wait(barrier, n_dp + 1)
    move(9, cot_ref, cot_in, far).start()
    move(10, labels_ref, labels_in, far).start()
    sums = add_up(0, left, right)
    center = sums[0:1] * inverse
    scaling = lax.rsqrt(sums[1:2] * inverse - center * center + EPS)
    gain = gain_ref[pl.ds(rep, 1), :]
    shift = shift_ref[pl.ds(rep, 1), :]

    def across(head, part):
        at = heads_ref.at[head, part // 2, pl.ds((part % 2) * span, span)]
        return move(part, at, at, far)

    def relay(head, part):
        at = heads_ref.at[head, part // 2, pl.ds((part % 2) * span, span)]
        return move(5 + part, at, at, mate)

    def own_head(head):
        return move(4, heads_ref.at[head], heads_ref.at[head], mate)

    for side in range(2):
        normed = (headed_ref[side] - center) * (scaling * gain) + shift
        heads_ref[rep, side] = (normed * jax.nn.sigmoid(normed)).astype(BF16)
        for k in range(2):
            across(rep, 2 * side + k).start()
    own_head(rep).start()
    if split:
        x_own = move(23, heads_ref.at[rep], beside_ref.at[rep], beside, "dp")
        x_far = move(24, heads_ref.at[far], beside_ref.at[far], beside, "dp")
        x_own.start()

    def tap_of(i):
        return par * 5 + i

    def row_of(i, head_at):
        return pl.multiple_of(par * (3 * small) + i * (3 * middle) + head_at * middle, small)

    half_row = (1 - par) * (12 * middle)
    full_row = pl.multiple_of(half_row + par * small, small)
    part_row = pl.multiple_of(half_row + (1 - par) * middle, small)
    part_lanes = pl.ds(pl.multiple_of(par * small, small), small)
    local = 2 * upper
    remote = 2 * (1 - upper)
    local_head = 1 + upper
    part_head = 2 - upper
    full_head = 2 * par + 1 - upper

    def wrows(row, depth):
        return w_ref[pl.ds(row, depth), :]

    def gather_taps(tap, side, y):
        y = y.astype(BF16)
        for k in range(2):
            acc_ref[side, k * span : (k + 1) * span, :] += product(
                s_ref[tap, 2 * side + k], y[k * span : (k + 1) * span]
            )

    acc_ref[...] = jnp.zeros_like(acc_ref)
    own_head(mate).wait_recv()
    load.wait()

    @pl.loop(0, 8)
    def _(n):
        i, side = n // 2, n % 2
        gather_taps(
            tap_of(i), side, product(heads_ref[local_head, side], wrows(row_of(i, local), middle))
        )

    @pl.when(par == upper)
    def _():
        @pl.loop(0, 2)
        def _(side):
            gather_taps(4, side, product(heads_ref[full_head, side], wrows(full_row, middle)))

    for part in range(4):
        across(far, part).wait_recv()
        relay(far, part).start()
    if split:
        x_far.start()
    for part in range(4):
        relay(far + 1 - 2 * par, part).wait_recv()

    @pl.loop(0, 8)
    def _(n):
        i, side = n // 2, n % 2
        y = product(heads_ref[remote, side], wrows(row_of(i, 1 - upper), middle))
        y = y + product(heads_ref[remote + 1, side], wrows(row_of(i, 2 - upper), middle))
        gather_taps(tap_of(i), side, y)

    @pl.loop(0, 2)
    def _(side):
        gather_taps(
            4, side, product(heads_ref[part_head, side, :, part_lanes], wrows(part_row, small))
        )

    @pl.when(par != upper)
    def _():
        @pl.loop(0, 2)
        def _(side):
            gather_taps(4, side, product(heads_ref[full_head, side], wrows(full_row, middle)))

    def acc_move(side):
        return move(11 + side, acc_ref.at[side, block(1 - par)], acc_in.at[side], mate)

    for side in range(2):
        acc_move(side).start()

    own_gates = gates_w_ref[pl.ds(pl.multiple_of(upper * middle, middle), middle), :]
    classes_ref[...] = jnp.zeros_like(classes_ref)
    move(9, cot_ref, cot_in, far).wait_recv()
    move(10, labels_ref, labels_in, far).wait_recv()
    gates_total = 0.0

    def gm_move(side, parity):
        at = gm_ref.at[side, block(parity)]
        return move(13 + side, at, at, mate)

    for side in range(2):
        acc_move(side).wait_recv()
        message = acc_ref[side, block(par), :] + acc_in[side]
        stream = heads_ref[3 * upper, side, block(par), :]
        gate = jax.nn.sigmoid(product(stream, own_gates))
        full = stream.astype(F32) + gate * message
        alive = live_ref[side, block(par), :]

        @pl.when(upper == 0)
        def _():
            cot = (cot_ref if side == 0 else cot_in)[...].astype(F32)
            stream_ref[side] = alive * cot
            (depth_ref if side == 0 else depth_out)[...] = alive * full

        @pl.when(upper == 1)
        def _():
            labels = (labels_in if side == 0 else labels_ref)[...]
            full_low = full.astype(BF16)
            logits = product(full_low, classes_w_ref[...])
            (logits_out if side == 0 else logits_ref)[...] = alive * logits
            lanes = lax.broadcasted_iota(jnp.int32, logits.shape, 1)
            shown = jnp.where(lanes < classes, logits, -1e30)
            grown = jnp.exp(shown - jnp.max(shown, 1, keepdims=True))
            probs = grown / jnp.sum(grown, 1, keepdims=True)
            slope = (alive * (probs - jnp.where(lanes == labels, 1.0, 0.0))).astype(BF16)
            classes_ref[...] += inner_rows(full_low, slope)
            stream_ref[side] = against(slope, classes_w_ref[...])

        grad = stream_ref[side]
        grad_gate = (grad * message * gate * (1.0 - gate)).astype(BF16)
        gm_ref[side, block(par), :] = (grad * gate).astype(BF16)
        gm_move(side, par).start()
        gates_total = gates_total + inner_rows(stream, grad_gate)
        direct_ref[side] = grad + against(grad_gate, own_gates)

    gates_ref[...] = gates_total.astype(BF16)

    @pl.when(upper == 0)
    def _():
        move(15, depth_out, depth_ref, far).start()

    @pl.when(upper == 1)
    def _():
        move(16, logits_out, logits_ref, far).start()

    for side in range(2):
        gm_move(side, 1 - par).wait_recv()
    if split:
        lanes = lax.broadcasted_iota(jnp.int32, (middle, small), 1)
        wanted = (lanes // 64) * 128 + lanes % 64
        source = lax.broadcasted_iota(jnp.int32, (middle, small), 0)
        for cut, which in ((cut_out, 1 - side_x), (cut_own, side_x)):
            pick = jnp.where(source == wanted + 64 * which, 1.0, 0.0).astype(BF16)
            for side in range(2):
                cut[side] = product(gm_ref[side], pick).astype(BF16)
        x_cut = move(27, cut_out, cut_in, beside, "dp")
        x_cut.start()

    @pl.loop(0, 10)
    def _(n):
        i, side = n // 2, n % 2
        tap = jnp.where(i == 4, 4, tap_of(i))
        for k in range(2):
            at = pl.ds(k * span, span)
            picked_ref[i, side, at, :] = inner_rows(
                s_ref[tap, 2 * side + k], gm_ref[side, at, :]
            ).astype(BF16)

    far_ref[...] = jnp.zeros_like(far_ref)
    near_ref[...] = jnp.zeros_like(near_ref)

    @pl.loop(0, 8)
    def _(n):
        i, side = n // 2, n % 2
        for j in range(2):
            far_ref[j, side] += against(
                picked_ref[i, side], wrows(row_of(i, 1 - upper + j), middle)
            )

    @pl.loop(0, 2)
    def _(side):
        far_ref[upper, side, :, part_lanes] += against(picked_ref[4, side], wrows(part_row, small))

    @pl.when(par != upper)
    def _():
        @pl.loop(0, 2)
        def _(side):
            far_ref[2 * par - 1 + upper, side] += against(
                picked_ref[4, side], wrows(full_row, middle)
            )

    core_out[...] = far_ref[1 - par].astype(BF16)
    to_mate = move(17, core_out, core_in, mate)
    to_mate.start()

    def far_move(part):
        at = pl.ds((part % 2) * span, span)
        return move(18 + part, far_out.at[part // 2, at], far_in.at[part // 2, at], far)

    @pl.loop(0, 8)
    def _(n):
        i, side = n // 2, n % 2
        near_ref[side] += against(picked_ref[i, side], wrows(row_of(i, local), middle))

    to_mate.wait_recv()
    for part in range(4):
        at = pl.ds((part % 2) * span, span)
        far_out[part // 2, at, :] = (
            far_ref[par, part // 2, at, :] + core_in[part // 2, at, :].astype(F32)
        ).astype(BF16)
        far_move(part).start()

    @pl.when(par == upper)
    def _():
        @pl.loop(0, 2)
        def _(side):
            near_ref[side] += against(picked_ref[4, side], wrows(full_row, middle))

        near_out[...] = near_ref[...].astype(BF16)
        for side in range(2):
            near_ref[side, block(par), :] = direct_ref[side]
            near_ref[side, block(1 - par), :] = jnp.zeros((span, middle), F32)

    @pl.when(par != upper)
    def _():
        for side in range(2):
            near_out[side, block(par), :] = direct_ref[side].astype(BF16)
            near_out[side, block(1 - par), :] = jnp.zeros((span, middle), BF16)

    near_move = move(22, near_out, near_in, mate)
    near_move.start()

    if split:
        x_own.wait_recv()
        relay_own = move(25, beside_ref.at[rep], beside_ref.at[rep], mate)
        relay_own.start()
        x_far.wait_recv()
        relay_far = move(26, beside_ref.at[far], beside_ref.at[far], mate)
        relay_far.start()
        x_cut.wait_recv()
        move(25, beside_ref.at[mate], beside_ref.at[mate], mate).wait_recv()
        other = far + 1 - 2 * par
        move(26, beside_ref.at[other], beside_ref.at[other], mate).wait_recv()

        def fill(tap):
            for p in range(4):
                at = pl.ds(p * span, span)
                cut_taken[0, :, at] = inner_rows(
                    cut_own[p // 2, pl.ds((p % 2) * span, span), :], s_ref[tap, p]
                ).astype(BF16)
                cut_taken[1, :, at] = inner_rows(
                    cut_in[p // 2, pl.ds((p % 2) * span, span), :],
                    shift_block(layout_ref, beside * 4 + p, 1, tap, span),
                ).astype(BF16)

        def gradient(head, lanes):
            total = 0.0
            for number, held in enumerate((heads_ref, beside_ref)):
                for side in range(2):
                    total = total + product(
                        cut_taken[number, :, side * 2 * span : (side + 1) * 2 * span],
                        held[head, side, :, lanes],
                    )
            return total.astype(BF16)

        @pl.loop(0, 4)
        def _(i):
            fill(tap_of(i))
            for at in range(3):
                for k in range(2):
                    row = pl.multiple_of(row_of(i, at) + k * small, small)
                    out_ref[:, pl.ds(row, small)] = gradient(
                        at + 1 - upper, pl.ds(k * small, small)
                    )

        fill(4)
        for k in range(2):
            row = pl.multiple_of(full_row + k * small, small)
            out_ref[:, pl.ds(row, small)] = gradient(full_head, pl.ds(k * small, small))
        out_ref[:, pl.ds(part_row, small)] = gradient(part_head, part_lanes)

    near_move.wait_recv()
    left, right = 0.0, 0.0

    def backward(side):
        unit = (headed_ref[side] - center) * scaling
        normed = unit * gain + shift
        sigma = jax.nn.sigmoid(normed)
        return unit, sigma * (1.0 + normed * (1.0 - sigma))

    for side in range(2):
        for part in (2 * side, 2 * side + 1):
            far_move(part).wait_recv()
        unit, slope = backward(side)
        grad = near_ref[side] + near_in[side].astype(F32) + far_in[side].astype(F32)
        grad = grad * slope
        near_ref[side] = grad
        masked = live_ref[side] * grad
        left = left + column_sum(masked * unit)
        right = right + column_sum(masked)
    sums = add_up(1, left, right)
    norm_ref[...] = sums
    for side in range(2):
        unit = (headed_ref[side] - center) * scaling
        low_ref[side] = (
            live_ref[side]
            * (gain * scaling)
            * (near_ref[side] - sums[1:2] * inverse - unit * (sums[0:1] * inverse))
        ).astype(BF16)

    for part in range(4):
        across(rep, part).wait_send()
        relay(far, part).wait_send()
        far_move(part).wait_send()
    own_head(rep).wait_send()
    move(9, cot_ref, cot_in, far).wait_send()
    move(10, labels_ref, labels_in, far).wait_send()
    for side in range(2):
        acc_move(side).wait_send()
        gm_move(side, par).wait_send()
    to_mate.wait_send()
    near_move.wait_send()

    @pl.when(upper == 0)
    def _():
        move(15, depth_out, depth_ref, far).wait_send()
        move(16, logits_out, logits_ref, far).wait_recv()

    @pl.when(upper == 1)
    def _():
        move(16, logits_out, logits_ref, far).wait_send()
        move(15, depth_out, depth_ref, far).wait_recv()

    if split:
        for copy in (x_own, x_far, x_cut, relay_own, relay_far):
            copy.wait_send()


def message_streams(
    split, layout, headed, shifts, w_messages, w_gates, w_classes, gain, shift, cot, labels
):
    n_dp = lax.axis_size("dp")
    span, middle = cot.shape
    small = middle // 2
    classes = w_classes.shape[1]
    vmem = pl.BlockSpec(memory_space=pltpu.VMEM)
    dma = pltpu.SemaphoreType.DMA
    shape = jax.ShapeDtypeStruct
    halves = (2, 2 * span, middle)
    heads = (4, 2, 2 * span, middle)
    out_shape = [
        shape((span, middle), F32),
        shape((span, 128), F32),
        shape((middle, middle), BF16),
        shape((middle, 128), F32),
        shape(halves, BF16),
        shape((2, middle), F32),
    ]
    if split:
        out_shape += [shape((small, w_messages.shape[0]), BF16)]
    else:
        out_shape += [shape(heads, BF16), shape(halves, BF16)]
    scratch = [
        pltpu.VMEM(w_messages.shape, BF16),
        pltpu.VMEM((2, 2 * span, 1), F32),
        pltpu.VMEM(halves, F32),
        pltpu.VMEM((2, span, middle), F32),
        pltpu.VMEM((2, span, middle), F32),
        pltpu.VMEM((2, span, middle), F32),
        pltpu.VMEM((span, middle), BF16),
        pltpu.VMEM((span, 128), jnp.int32),
        pltpu.VMEM((span, middle), F32),
        pltpu.VMEM((span, 128), F32),
        pltpu.VMEM((5,) + halves, BF16),
        pltpu.VMEM((2,) + halves, F32),
        pltpu.VMEM(halves, F32),
        pltpu.VMEM(halves, BF16),
        pltpu.VMEM(halves, BF16),
        pltpu.VMEM(halves, BF16),
        pltpu.VMEM(halves, BF16),
        pltpu.VMEM(halves, BF16),
        pltpu.VMEM(halves, BF16),
        pltpu.VMEM((2, 2, middle), F32),
        pltpu.VMEM((2, n_dp, 2, middle), F32),
        dma,
        dma((MOVES,)),
        dma((MOVES,)),
        dma((2, n_dp)),
        dma((2, n_dp)),
    ]
    if split:
        scratch += [
            pltpu.VMEM(heads, BF16),
            pltpu.VMEM(halves, BF16),
            pltpu.VMEM(heads, BF16),
            pltpu.VMEM((2, 2 * span, small), BF16),
            pltpu.VMEM((2, 2 * span, small), BF16),
            pltpu.VMEM((2, 2 * span, small), BF16),
            pltpu.VMEM((2, small, 4 * span), BF16),
        ]
    return pl.pallas_call(
        functools.partial(message_kernel, split, n_dp, classes),
        in_specs=[pl.BlockSpec(memory_space=pltpu.SMEM)]
        + [vmem] * 3
        + [pl.BlockSpec(memory_space=pl.ANY)]
        + [vmem] * 6,
        out_specs=[vmem] * len(out_shape),
        out_shape=out_shape,
        scratch_shapes=scratch,
        compiler_params=pltpu.CompilerParams(
            collective_id=11, has_side_effects=True, vmem_limit_bytes=VMEM_LIMIT
        ),
        name="message_streams",
    )(
        layout,
        layout,
        headed,
        shifts,
        w_messages,
        w_gates,
        jnp.pad(w_classes, ((0, 0), (0, 128 - classes))),
        gain.reshape(4, middle),
        shift.reshape(4, middle),
        cot,
        jnp.broadcast_to(labels[:, None], (span, 128)),
    )


def silu_slope(value_in):
    sigma_of = jax.nn.sigmoid(value_in)
    return sigma_of * (1.0 + value_in * (1.0 - sigma_of))


MESH = pl.DeviceIdType.MESH


def greet(axes):
    barrier = pltpu.get_barrier_semaphore()
    count = 0
    for axis, size in axes:
        me = lax.axis_index(axis)
        for k in range(1, size):
            pl.semaphore_signal(
                barrier, inc=1, device_id={axis: lax.rem(me + k, size)}, device_id_type=MESH
            )
        count += size - 1
    pl.semaphore_wait(barrier, count)


def total_kernel(axes, x_ref, out_ref, *scratch):
    greet(axes)
    block = x_ref
    for number, (axis, size) in enumerate(axes):
        slots, stage, send_sems, recv_sems = scratch[4 * number : 4 * number + 4]
        me = lax.axis_index(axis)
        others = [lax.rem(me + k, size) for k in range(1, size)]
        for other in others:
            pltpu.make_async_remote_copy(
                src_ref=block,
                dst_ref=slots.at[me],
                send_sem=send_sems.at[other],
                recv_sem=recv_sems.at[me],
                device_id={axis: other},
                device_id_type=MESH,
            ).start()
        slots[me] = block[...]
        for other in others:
            copy = pltpu.make_async_remote_copy(
                src_ref=block,
                dst_ref=slots.at[other],
                send_sem=send_sems.at[other],
                recv_sem=recv_sems.at[other],
                device_id={axis: other},
                device_id_type=MESH,
            )
            copy.wait_recv()
            copy.wait_send()
        total = slots[0]
        for k in range(1, size):
            total = total + slots[k]
        if number == len(axes) - 1:
            out_ref[...] = total
        else:
            stage[...] = total
            block = stage


def total_of(left, right, axes):
    width = left.shape[0]
    packed = jnp.concatenate([left, right], 0).reshape(-1, 128)
    sized = tuple((axis, lax.axis_size(axis)) for axis in axes)
    scratch = []
    for _, size in sized:
        scratch += [
            pltpu.VMEM((size,) + packed.shape, F32),
            pltpu.VMEM(packed.shape, F32),
            pltpu.SemaphoreType.DMA((size,)),
            pltpu.SemaphoreType.DMA((size,)),
        ]
    number = 1 + (width != 512) + 2 * (len(axes) == 1)
    summed = pl.pallas_call(
        functools.partial(total_kernel, sized),
        out_shape=jax.ShapeDtypeStruct(packed.shape, F32),
        in_specs=[pl.BlockSpec(memory_space=pltpu.VMEM)],
        out_specs=pl.BlockSpec(memory_space=pltpu.VMEM),
        scratch_shapes=scratch,
        compiler_params=pltpu.CompilerParams(collective_id=number, has_side_effects=True),
        name="total",
    )(packed).reshape(2, width)
    return summed[0], summed[1]


def normalize(raw_value, column_sums, squares, pixel_count, norm_gain, norm_shift):
    center = column_sums / pixel_count
    spread_of = squares / pixel_count - center * center
    scaling = lax.rsqrt(spread_of + EPS)
    unit_value = (raw_value - center) * scaling
    return (unit_value * norm_gain + norm_shift, unit_value, scaling)


def moments(raw_value, living, axes):
    return total_of(
        jnp.sum(living * raw_value, 0), jnp.sum(living * raw_value * raw_value, 0), axes
    )


def norm_back(grad_out, unit_value, scaling, norm_gain, living, pixel_count, axes):
    grad_gain, grad_shift = total_of(
        jnp.sum(living * grad_out * unit_value, 0), jnp.sum(living * grad_out, 0), axes
    )
    grad_raw = (
        living
        * (norm_gain * scaling)
        * (grad_out - grad_shift / pixel_count - unit_value * grad_gain / pixel_count)
    )
    return (grad_raw, grad_gain, grad_shift)


def swap(value, bit):
    return lax.ppermute(value, "rep", [(k, k ^ bit) for k in range(4)])


def scatter_rep(value):
    return lax.psum_scatter(value.astype(BF16), "rep", scatter_dimension=0, tiled=True)


def swap_x(value):
    return lax.ppermute(value, "dp", [(k, k ^ 1) for k in range(lax.axis_size("dp"))])


def own_half(value, parity):
    halves = value.reshape((2, value.shape[0] // 2) + value.shape[1:])
    return lax.dynamic_index_in_dim(halves, parity, 0, keepdims=False)


def both_halves(mine, other, parity):
    return jnp.concatenate(
        [jnp.where(parity == 0, mine, other), jnp.where(parity == 0, other, mine)], 0
    )


def total_dp(value):
    parts = lax.axis_size("dp")
    rows = value.shape[0]
    padded = -(-rows // (8 * parts)) * 8 * parts
    value = jnp.pad(value, ((0, padded - rows), (0, 0)))
    share = lax.psum_scatter(value, "dp", scatter_dimension=0, tiled=True)
    return lax.all_gather(share, "dp", axis=0, tiled=True)[:rows].astype(F32)


def shards(
    inputs,
    layout,
    labels,
    cot_depth,
    w_reduce,
    w_spatial,
    w_expand,
    w_heads,
    w_gates,
    w_messages,
    w_classes,
    gain_mid,
    shift_mid,
    gain_wide,
    shift_wide,
    gain_head,
    shift_head,
):
    pixels = inputs.shape[0]
    middle = w_reduce.shape[1]
    classes = w_classes.shape[1]
    group = lax.axis_size("rep")
    everyone = ("rep", "dp")
    rep = lax.axis_index("rep")
    parity = rep % 2
    upper = rep // 2
    first_row = lax.axis_index("dp") * group
    own_info = geometry(lax.dynamic_slice_in_dim(layout, first_row + rep, 1, 0), pixels)
    group_info = geometry(lax.dynamic_slice_in_dim(layout, first_row, group, 0), pixels)
    living = own_info[2][0].astype(F32)[:, None]
    group_living = group_info[2].astype(F32)
    living_all = group_living.reshape(group * pixels, 1)
    pixel_count = jnp.sum(
        jnp.minimum(layout[:, 0] * layout[:, 1] * layout[:, 2], pixels)
    ).astype(F32)
    split = lax.axis_size("dp") == 8
    if split:
        side = lax.axis_index("dp") % 2
        side_of = jnp.reshape(side, (1,)).astype(jnp.int32)
        beside_row = first_row + group * (1 - 2 * side)
        shifts_beside = shift_matrices(
            geometry(lax.dynamic_slice_in_dim(layout, beside_row, group, 0), pixels), 1
        )
        columns = [[z_at * 2 + k for z_at in range(4)] for k in range(2)]
    zero = jnp.zeros((1,), jnp.int32)
    first = jnp.reshape(9 * parity, (1,)).astype(jnp.int32)

    (
        reduced,
        sums_one,
        hidden_one,
        spatial,
        sums_two,
        hidden_two,
        expanded,
        sums_three,
        trunk_all,
        headed,
        shifts_own,
        shifts_all,
    ) = trunk_forward(
        inputs,
        layout,
        w_reduce,
        w_spatial,
        w_expand,
        w_heads,
        gain_mid,
        shift_mid,
        gain_wide,
        shift_wide,
    )
    shifts_own = shifts_own[:, None]
    trunk_all = trunk_all.reshape(group * pixels, -1)
    normed_one, unit_one, scale_one = normalize(
        reduced, sums_one[0], sums_one[1], pixel_count, gain_mid[0], shift_mid[0]
    )
    normed_two, unit_two, scale_two = normalize(
        spatial, sums_two[0], sums_two[1], pixel_count, gain_mid[1], shift_mid[1]
    )
    normed_three, unit_three, scale_three = normalize(
        expanded, sums_three[0], sums_three[1], pixel_count, gain_wide, shift_wide
    )
    pre_act = normed_three + inputs.astype(F32)
    if split:
        trunk_mine = swap_x(own_half(trunk_all, parity))

    upper_is_depth = upper == 0
    depth, logits, gates_local, classes_local, head_low, head_norm, *rest = message_streams(
        split,
        layout,
        headed,
        shifts_all,
        w_messages,
        w_gates,
        w_classes,
        gain_head,
        shift_head,
        cot_depth,
        labels,
    )
    logits = logits[:, :classes]
    classes_local = classes_local[:, :classes]
    head_low = head_low.reshape(group * pixels, middle)
    is_depth = upper_is_depth
    if split:
        head_low, trunk_mine = lax.optimization_barrier((head_low, trunk_mine))
        trunk_beside = both_halves(trunk_mine, swap(trunk_mine, 1), parity)
        grad_messages = lax.psum_scatter(
            rest[0], "dp", scatter_dimension=0, tiled=True, axis_index_groups=columns
        )
    else:
        heads_all, message_all = rest
        heads_all = heads_all.reshape(4, group * pixels, middle)
        source = jnp.where(
            is_depth,
            jnp.concatenate([heads_all[1], heads_all[2], heads_all[3]], 1),
            jnp.concatenate([heads_all[0], heads_all[1], heads_all[2]], 1),
        )
        _, messages_local = rows_back(
            first, message_all.reshape(4 * pixels, middle), source, w_messages, shifts_all, 2, BF16
        )
        grad_messages = lax.psum_scatter(messages_local, "dp", scatter_dimension=1, tiled=True)
        gates_cut = gates_local.reshape(2, pixels, middle)
        gates_share = lax.dynamic_index_in_dim(gates_cut, parity, 0, keepdims=False).astype(F32)
        gates_share += swap(
            lax.dynamic_index_in_dim(gates_cut, 1 - parity, 0, keepdims=False), 1
        ).astype(F32)
    if split:
        head_beside = swap_x(head_low)
        trunk_part = heads_data(head_low, w_heads, shifts_all)
        trunk_part, head_beside = lax.optimization_barrier((trunk_part, head_beside))
        heads_local = heads_split(
            side_of,
            head_low,
            head_beside,
            trunk_all,
            trunk_beside,
            shifts_all,
            shifts_beside,
            4,
            256,
        )
    else:
        heads_local = heads_weight(head_low, trunk_all, shifts_all)
        grad_heads = lax.psum_scatter(heads_local, "dp", scatter_dimension=1, tiled=True)
        trunk_part = heads_data(head_low, w_heads, shifts_all)
    trunk_grad = lax.psum_scatter(trunk_part, "rep", scatter_dimension=0, tiled=True)
    if split:
        trunk_grad, heads_local = lax.optimization_barrier((trunk_grad, heads_local))
        grad_heads = lax.psum_scatter(
            heads_local, "dp", scatter_dimension=0, tiled=False, axis_index_groups=columns
        )
    trunk_grad = trunk_grad.astype(F32)
    pre_grad = trunk_grad * silu_slope(pre_act)
    expand_raw, grad_gain_wide, grad_shift_wide = norm_back(
        pre_grad, unit_three, scale_three, gain_wide, living, pixel_count, everyone
    )
    expand_low = expand_raw.astype(BF16)
    expand_local = inner_rows(hidden_two, expand_low).astype(BF16)
    hidden_two_grad = against(expand_low, w_expand)
    spatial_raw, gain_grad_two, shift_grad_two = norm_back(
        hidden_two_grad * silu_slope(normed_two),
        unit_two,
        scale_two,
        gain_mid[1],
        living,
        pixel_count,
        everyone,
    )
    spatial_low = spatial_raw.astype(BF16)
    hidden_one_grad, spatial_local = rows_back(
        zero, spatial_low, hidden_one, w_spatial, shifts_own, 1, F32
    )
    reduced_raw, gain_grad_one, shift_grad_one = norm_back(
        hidden_one_grad * silu_slope(normed_one),
        unit_one,
        scale_one,
        gain_mid[0],
        living,
        pixel_count,
        everyone,
    )
    reduced_low = reduced_raw.astype(BF16)
    reduce_local = inner_rows(inputs, reduced_low).astype(BF16)
    if split:
        reduced_low, grad_messages = lax.optimization_barrier((reduced_low, grad_messages))
        grad_messages = grad_messages.T
    input_grad = pre_grad + against(reduced_low, w_reduce)
    if split:
        wide = w_expand.shape[1]
        cuts = wide // middle

        def side_by_side(value):
            value = value.reshape(4, -1, value.shape[1])
            return jnp.concatenate(
                [value[:, :, k : k + middle] for k in range(0, value.shape[2], middle)], 1
            )

        gates_local = gates_local.reshape(2, pixels, middle)
        gates_zero = jnp.zeros_like(gates_local)
        gates_every = jnp.where(
            is_depth,
            jnp.concatenate([gates_local, gates_zero], 0),
            jnp.concatenate([gates_zero, gates_local], 0),
        )
        classes_wide = jnp.pad(classes_local.astype(BF16), ((0, 0), (0, 128 - classes)))
        classes_wide = classes_wide.reshape(4, 4, -1, 128)
        classes_wide = jnp.concatenate([classes_wide[:, k] for k in range(4)], 2)
        pieces = [
            reduce_local.reshape(4, -1, middle),
            spatial_local.reshape(4, -1, middle),
            side_by_side(expand_local),
            gates_every,
            classes_wide,
        ]
        rows = [piece.shape[1] for piece in pieces]
        unit = 128 * CHUNKS
        missing = -sum(rows) % unit
        pieces.append(jnp.zeros((4, missing, middle), BF16))
        summed = small_total(jnp.concatenate(pieces, 1))
        starts = [sum(rows[:k]) for k in range(5)]
        grad_reduce, grad_spatial, expand_sum, grad_gates, classes_sum = [
            summed[at : at + size] for at, size in zip(starts, rows)
        ]
        expand_sum = expand_sum.reshape(cuts, -1, middle)
        grad_expand = jnp.concatenate([expand_sum[k] for k in range(cuts)], 1)
        classes_sum = jnp.concatenate(
            [classes_sum[:, k * 128 : (k + 1) * 128] for k in range(4)], 0
        )
        grad_classes = classes_sum[:, :classes]
    else:
        grad_expand = scatter_rep(expand_local)
        grad_spatial = scatter_rep(spatial_local)
        grad_reduce = scatter_rep(reduce_local)
        grad_classes = scatter_rep(classes_local)
        pieces = [
            gates_share.astype(BF16),
            grad_expand.reshape(-1, middle),
            grad_spatial,
            grad_classes.reshape(-1, middle),
        ]
        early = total_dp(jnp.concatenate(pieces, 0))
        rows = [piece.shape[0] for piece in pieces]
        starts = [sum(rows[:k]) for k in range(4)]
        grad_gates, expand_sum, grad_spatial, classes_sum = [
            early[at : at + size] for at, size in zip(starts, rows)
        ]
        grad_expand = expand_sum.reshape(grad_expand.shape)
        grad_classes = classes_sum.reshape(grad_classes.shape)
        grad_reduce = total_dp(grad_reduce)
    grad_gain_mid = jnp.stack([gain_grad_one, gain_grad_two], 0)
    grad_shift_mid = jnp.stack([shift_grad_one, shift_grad_two], 0)
    head_norms = lax.all_gather(
        head_norm, "rep", axis=1, tiled=True
    )
    return (
        depth,
        logits,
        input_grad,
        grad_reduce,
        grad_spatial,
        grad_expand,
        grad_heads.astype(F32),
        grad_gates,
        grad_messages.astype(F32),
        grad_classes,
        grad_gain_mid,
        grad_shift_mid,
        grad_gain_wide,
        grad_shift_wide,
        head_norms[0],
        head_norms[1],
    )


def solution(mesh):
    in_specs = (
        P(("dp", "rep"), None),
        P(),
        P(("dp", "rep")),
        P(("dp", "rep"), None),
        P(),
        P(),
        P(),
        P("rep", None),
        P(),
        P("rep", None),
        P(),
        P(),
        P(),
        P(),
        P(),
        P(),
        P(),
    )
    out_specs = (
        P(("dp", "rep"), None),
        P(("dp", "rep"), None),
        P(("dp", "rep"), None),
        P("rep", None),
        P("rep", None),
        P("rep", None),
        P("rep", "dp"),
        P("rep", None),
        P("rep", "dp"),
        P("rep", None),
        P(),
        P(),
        P(),
        P(),
        P(),
        P(),
    )
    return jax.shard_map(shards, mesh=mesh, in_specs=in_specs, out_specs=out_specs, check_vma=False)
```

```python
import functools

import jax
import jax.numpy as jnp
from jax import lax
from jax.experimental import pallas as pl
from jax.experimental.pallas import tpu as pltpu
from jax.sharding import PartitionSpec as P

EPS = 1e-05
F32 = jnp.float32
BF16 = jnp.bfloat16
VMEM_LIMIT = 60 * 2**20


def geometry(layout, span):
    position = jnp.arange(span, dtype=jnp.int32)
    height = layout[:, 0:1]
    map_width = layout[:, 1:2]
    images = layout[:, 2:3]
    map_area = height * map_width
    inside = position[None, :] % map_area
    row_of = inside // map_width
    col_of = inside % map_width
    living = position[None, :] < images * map_area
    return (row_of, col_of, living, height, map_width)


def neighbours(shape_info, dilation):
    row_of, col_of, living, height, map_width = shape_info
    span = row_of.shape[1]
    position = jnp.arange(span, dtype=jnp.int32)
    every = []
    for step_row in (-1, 0, 1):
        for step_col in (-1, 0, 1):
            target_row = row_of + dilation * step_row
            target_col = col_of + dilation * step_col
            inside = (
                living
                & (target_row >= 0)
                & (target_row < height)
                & (target_col >= 0)
                & (target_col < map_width)
            )
            neighbour = position[None, :] + dilation * (step_row * map_width + step_col)
            every.append(jnp.where(inside, neighbour, -1))
    return jnp.concatenate(every, 0).T


def shift_matrices(shape_info, dilation):
    devices, span = shape_info[0].shape
    picks = neighbours(shape_info, dilation).T.reshape(9, devices, span, 1)
    return (picks == jnp.arange(span, dtype=jnp.int32)).astype(BF16)


def product(left_side, right_side):
    return jnp.dot(left_side, right_side, preferred_element_type=F32)


def inner_rows(left_side, right_side):
    return lax.dot_general(
        left_side, right_side, (((0,), (0,)), ((), ())), preferred_element_type=F32
    )


def against(left_side, right_side):
    return lax.dot_general(
        left_side, right_side, (((1,), (1,)), ((), ())), preferred_element_type=F32
    )


def params():
    return pltpu.CompilerParams(vmem_limit_bytes=VMEM_LIMIT)


def cost(flops, moved):
    return pl.CostEstimate(flops=flops, bytes_accessed=moved, transcendentals=0)


def shifted(g_ref, s_ref):
    blocks, span = s_ref.shape[1], s_ref.shape[2]
    return jnp.concatenate(
        [
            inner_rows(s_ref[0, k], g_ref[pl.ds(k * span, span), :]).astype(BF16)
            for k in range(blocks)
        ],
        0,
    )


def heads_weight_kernel(g_ref, u_ref, s_ref, out_ref):
    taken = shifted(g_ref, s_ref)
    step = 512
    for c in range(0, u_ref.shape[1], step):
        out_ref[:, c : c + step] = inner_rows(taken, u_ref[:, c : c + step]).astype(out_ref.dtype)


def heads_weight(g, u, shifts):
    rows, outs = g.shape
    wide = u.shape[1]
    taps, blocks, span, _ = shifts.shape
    return pl.pallas_call(
        heads_weight_kernel,
        grid=(taps,),
        in_specs=[
            pl.BlockSpec((rows, outs), lambda t: (0, 0)),
            pl.BlockSpec((rows, wide), lambda t: (0, 0)),
            pl.BlockSpec((1, blocks, span, span), lambda t: (t, 0, 0, 0)),
        ],
        out_specs=pl.BlockSpec((outs, wide), lambda t: (0, t)),
        out_shape=jax.ShapeDtypeStruct((outs, taps * wide), BF16),
        compiler_params=params(),
        cost_estimate=cost(2 * rows * wide * outs * taps, outs * taps * wide * 2),
        name="heads_weight",
    )(g, u, shifts)


def rows_back_kernel(halves, first_ref, g_ref, u_ref, w_ref, s_ref, du_ref, dw_ref, total):
    step = pl.program_id(0)
    taken = shifted(g_ref, s_ref)
    depth = w_ref.shape[0]
    which = (step + first_ref[0]) % halves

    @pl.when(step == 0)
    def _():
        total[...] = jnp.zeros_like(total)

    total[which] += against(taken, w_ref[...])
    dw_ref[...] = inner_rows(u_ref[...], taken).astype(dw_ref.dtype)

    @pl.when(step == pl.num_programs(0) - 1)
    def _():
        for k in range(halves):
            du_ref[:, k * depth : (k + 1) * depth] = total[k].astype(du_ref.dtype)


def rows_back(first, g, u, w, shifts, halves, kind):
    rows, outs = g.shape
    depth = u.shape[1] // halves
    steps = w.shape[0] // depth
    taps, blocks, span, _ = shifts.shape
    return pl.pallas_call(
        functools.partial(rows_back_kernel, halves),
        grid_spec=pltpu.PrefetchScalarGridSpec(
            num_scalar_prefetch=1,
            grid=(steps,),
            in_specs=[
                pl.BlockSpec((rows, outs), lambda b, f: (0, 0)),
                pl.BlockSpec((rows, depth), lambda b, f: (0, (b + f[0]) % halves)),
                pl.BlockSpec((depth, outs), lambda b, f: (b, 0)),
                pl.BlockSpec((1, blocks, span, span), lambda b, f: ((b + f[0]) // halves, 0, 0, 0)),
            ],
            out_specs=[
                pl.BlockSpec((rows, halves * depth), lambda b, f: (0, 0)),
                pl.BlockSpec((depth, outs), lambda b, f: (b, 0)),
            ],
            scratch_shapes=[pltpu.VMEM((halves, rows, depth), F32)],
        ),
        out_shape=[
            jax.ShapeDtypeStruct((rows, halves * depth), kind),
            jax.ShapeDtypeStruct(w.shape, BF16),
        ],
        compiler_params=params(),
        cost_estimate=cost(4 * rows * w.size, w.size * 4),
        name="rows_back",
    )(first, g, u, w, shifts)


def send_to(axis, to, src, dst, send_sem, recv_sem):
    return pltpu.make_async_remote_copy(
        src_ref=src,
        dst_ref=dst,
        send_sem=send_sem,
        recv_sem=recv_sem,
        device_id={axis: to},
        device_id_type=MESH,
    )


def total_along(axis, size, block, slots, send_sems, recv_sems, meanwhile=None):
    me = lax.axis_index(axis)
    others = [lax.rem(me + k, size) for k in range(1, size)]
    for other in others:
        send_to(axis, other, block, slots.at[me], send_sems.at[other], recv_sems.at[me]).start()
    slots[me] = block[...]
    if meanwhile is not None:
        meanwhile()
    for other in others:
        copy = send_to(
            axis, other, block, slots.at[other], send_sems.at[other], recv_sems.at[other]
        )
        copy.wait_recv()
        copy.wait_send()
    total = slots[0]
    for k in range(1, size):
        total = total + slots[k]
    return total


def place_in_map(layout_ref, device, span):
    position = lax.broadcasted_iota(jnp.int32, (span, 1), 0)
    large = layout_ref[device, 1] == 16
    row_of = jnp.where(large, position // 16, (position % 64) // 8)
    col_of = jnp.where(large, position % 16, position % 8)
    return position, row_of, col_of


def live_mask(layout_ref, device, span):
    position = lax.broadcasted_iota(jnp.int32, (span, 1), 0)
    return position < layout_ref[device, 0] * layout_ref[device, 1] * layout_ref[device, 2]


def live_column(layout_ref, device, span):
    return jnp.where(live_mask(layout_ref, device, span), 1.0, 0.0)


def inverse_count(areas_ref, span):
    areas = areas_ref[:, 0:1] * areas_ref[:, 1:2] * areas_ref[:, 2:3]
    return 1.0 / jnp.sum(jnp.minimum(areas, span).astype(F32), 0, keepdims=True)


def shift_block(layout_ref, device, dilation, tap, span):
    position, row_of, col_of = place_in_map(layout_ref, device, span)
    height, map_width = layout_ref[device, 0], layout_ref[device, 1]
    step_row, step_col = dilation * (tap // 3 - 1), dilation * (tap % 3 - 1)
    target_row, target_col = row_of + step_row, col_of + step_col
    inside = (
        live_mask(layout_ref, device, span)
        & (target_row >= 0)
        & (target_row < height)
        & (target_col >= 0)
        & (target_col < map_width)
    )
    neighbour = jnp.where(inside, position + step_row * map_width + step_col, -1)
    lanes = lax.broadcasted_iota(jnp.int32, (span, span), 1)
    return jnp.where(neighbour == lanes, 1.0, 0.0).astype(BF16)


def trunk_kernel(
    split,
    sizes,
    in_ref,
    layout_ref,
    areas_ref,
    w_reduce_ref,
    w_spatial_hbm,
    w_expand_hbm,
    w_heads_hbm,
    gain_mid_ref,
    shift_mid_ref,
    gain_wide_ref,
    shift_wide_ref,
    reduced_ref,
    sums_one_ref,
    hidden_one_ref,
    spatial_ref,
    sums_two_ref,
    hidden_two_ref,
    expanded_ref,
    sums_three_ref,
    trunk_ref,
    headed_ref,
    own_shift_ref,
    all_shift_ref,
    *rest,
):
    if split:
        trunk_x, trunk_z, *rest = rest
    trunk_rest(
        split,
        sizes,
        in_ref,
        layout_ref,
        areas_ref,
        w_reduce_ref,
        w_spatial_hbm,
        w_expand_hbm,
        w_heads_hbm,
        gain_mid_ref,
        shift_mid_ref,
        gain_wide_ref,
        shift_wide_ref,
        reduced_ref,
        sums_one_ref,
        hidden_one_ref,
        spatial_ref,
        sums_two_ref,
        hidden_two_ref,
        expanded_ref,
        sums_three_ref,
        trunk_ref,
        headed_ref,
        own_shift_ref,
        all_shift_ref,
        (trunk_x, trunk_z) if split else (),
        *rest,
    )


def trunk_rest(
    split,
    sizes,
    in_ref,
    layout_ref,
    areas_ref,
    w_reduce_ref,
    w_spatial_hbm,
    w_expand_hbm,
    w_heads_hbm,
    gain_mid_ref,
    shift_mid_ref,
    gain_wide_ref,
    shift_wide_ref,
    reduced_ref,
    sums_one_ref,
    hidden_one_ref,
    spatial_ref,
    sums_two_ref,
    hidden_two_ref,
    expanded_ref,
    sums_three_ref,
    trunk_ref,
    headed_ref,
    own_shift_ref,
    all_shift_ref,
    afar,
    w_spatial_ref,
    w_expand_ref,
    w_heads_ref,
    block_mid,
    block_wide,
    slots_mid_rep,
    slots_mid_dp,
    slots_wide_rep,
    slots_wide_dp,
    load_sems,
    rep_send,
    rep_recv,
    dp_send,
    dp_recv,
    gather_send,
    gather_recv,
    away_send,
    away_recv,
):
    n_rep, n_dp = sizes
    rep = lax.axis_index("rep")
    par, upper = lax.rem(rep, 2), rep // 2
    mate, far = rep + 1 - 2 * par, rep + 2 - 4 * upper
    span, wide = in_ref.shape
    middle = w_reduce_ref.shape[1]
    taps = own_shift_ref.shape[0]
    loads = [
        pltpu.make_async_copy(w_spatial_hbm, w_spatial_ref, load_sems.at[0]),
        pltpu.make_async_copy(w_expand_hbm, w_expand_ref, load_sems.at[1]),
    ]
    heads_load = pltpu.make_async_copy(w_heads_hbm, w_heads_ref, load_sems.at[2])
    for load in loads:
        load.start()
    heads_load.start()

    barrier = pltpu.get_barrier_semaphore()
    for axis, size in (("rep", n_rep), ("dp", n_dp)):
        me = lax.axis_index(axis)
        for k in range(1, size):
            pl.semaphore_signal(
                barrier, inc=1, device_id={axis: lax.rem(me + k, size)}, device_id_type=MESH
            )
    first_row = lax.axis_index("dp") * n_rep
    live = live_column(layout_ref, first_row + rep, span)
    inverse = inverse_count(areas_ref, span)

    def make_own():
        for t in range(taps):
            own_shift_ref[t] = shift_block(layout_ref, first_row + rep, 2, t, span)

    def make_all(first, last):
        def fill():
            for t in range(first, last):
                for p in range(n_rep):
                    all_shift_ref[t, p] = shift_block(layout_ref, first_row + p, 1, t, span)

        return fill

    def everywhere(number, value_ref, blocks, rep_slots, dp_slots, meanwhile, later):
        masked = live * value_ref[...]
        blocks[0, 0:1, :] = jnp.sum(masked, 0, keepdims=True)
        blocks[0, 1:2, :] = jnp.sum(masked * value_ref[...], 0, keepdims=True)
        if number == 0:
            pl.semaphore_wait(barrier, n_rep + n_dp - 2)
        blocks[1] = total_along(
            "rep", n_rep, blocks.at[0], rep_slots, rep_send.at[number], rep_recv.at[number], meanwhile
        )
        return total_along(
            "dp", n_dp, blocks.at[1], dp_slots, dp_send.at[number], dp_recv.at[number], later
        )

    def normed(value, sums, gain, shift):
        center = sums[0:1] * inverse
        scaling = lax.rsqrt(sums[1:2] * inverse - center * center + EPS)
        return (value - center) * (scaling * gain) + shift

    def silu(value):
        return value * jax.nn.sigmoid(value)

    reduced_ref[...] = product(in_ref[...], w_reduce_ref[...])
    sums = everywhere(
        0, reduced_ref, block_mid.at[0], slots_mid_rep.at[0], slots_mid_dp.at[0], make_own, None
    )
    sums_one_ref[...] = sums
    hidden_one_ref[...] = silu(
        normed(reduced_ref[...], sums, gain_mid_ref[0:1, :], shift_mid_ref[0:1, :])
    ).astype(BF16)
    loads[0].wait()
    spatial_ref[...] = jnp.zeros_like(spatial_ref)

    @pl.loop(0, taps)
    def _(t):
        moved = product(own_shift_ref[t], hidden_one_ref[...]).astype(BF16)
        at = pl.ds(pl.multiple_of(t * middle, middle), middle)
        spatial_ref[...] += product(moved, w_spatial_ref[at, :])

    sums = everywhere(
        1, spatial_ref, block_mid.at[1], slots_mid_rep.at[1], slots_mid_dp.at[1], make_all(0, 5), None
    )
    sums_two_ref[...] = sums
    hidden_two_ref[...] = silu(
        normed(spatial_ref[...], sums, gain_mid_ref[1:2, :], shift_mid_ref[1:2, :])
    ).astype(BF16)
    loads[1].wait()
    expanded_ref[...] = product(hidden_two_ref[...], w_expand_ref[...])
    sums = everywhere(
        2, expanded_ref, block_wide, slots_wide_rep, slots_wide_dp, make_all(5, 9), None
    )
    sums_three_ref[...] = sums

    own_rows = pl.ds(pl.multiple_of(par * span, span), span)
    mate_rows = pl.ds(pl.multiple_of((1 - par) * span, span), span)
    pre = normed(expanded_ref[...], sums, gain_wide_ref[...], shift_wide_ref[...])
    trunk_ref[upper, own_rows, :] = silu(pre + in_ref[...].astype(F32)).astype(BF16)
    parts = 4
    piece = span // parts

    def rows(parity, k):
        return pl.ds(pl.multiple_of(parity * span + k * piece, piece), piece)

    def across(side, k):
        at = trunk_ref.at[side, rows(par, k)]
        return send_to("rep", far, at, at, gather_send.at[k], gather_recv.at[k])

    def own_pass(parity):
        at = trunk_ref.at[upper, pl.ds(pl.multiple_of(parity * span, span), span)]
        return send_to("rep", mate, at, at, gather_send.at[parts], gather_recv.at[parts])

    def far_pass(parity, k):
        at = trunk_ref.at[1 - upper, rows(parity, k)]
        slot = parts + 1 + k
        return send_to("rep", mate, at, at, gather_send.at[slot], gather_recv.at[slot])

    dp = lax.axis_index("dp")
    neighbours = (dp + 1 - 2 * lax.rem(dp, 2), dp + 2 - 4 * lax.rem(dp // 2, 2))

    def away(number, side):
        return send_to(
            "dp",
            neighbours[number],
            trunk_ref.at[side, own_rows],
            afar[number].at[side],
            away_send.at[number, side],
            away_recv.at[number, side],
        )

    for k in range(parts):
        across(upper, k).start()
    own_pass(par).start()
    if split:
        for number in range(2):
            away(number, upper).start()
    headed_ref[...] = jnp.zeros_like(headed_ref)
    own_pass(1 - par).wait_recv()
    heads_load.wait()

    def convolve(side):
        @pl.loop(0, taps)
        def _(t):
            at = pl.ds(pl.multiple_of(t * wide, wide), wide)
            y = against(trunk_ref[side], w_heads_ref[:, at]).astype(BF16)
            for k in range(2):
                place = pl.ds(k * span, span)
                headed_ref[side, place, :] += product(
                    all_shift_ref[t, 2 * side + k], y[k * span : (k + 1) * span]
                )

    convolve(upper)
    for k in range(parts):
        across(1 - upper, k).wait_recv()
        far_pass(par, k).start()
    if split:
        for number in range(2):
            away(number, 1 - upper).start()
    for k in range(parts):
        far_pass(1 - par, k).wait_recv()
    convolve(1 - upper)
    for k in range(parts):
        across(upper, k).wait_send()
        far_pass(par, k).wait_send()
    own_pass(par).wait_send()
    if split:
        for number in range(2):
            for side in (upper, 1 - upper):
                away(number, side).wait_send()
                away(number, side).wait_recv()


def trunk_forward(
    split,
    inputs,
    layout,
    w_reduce,
    w_spatial,
    w_expand,
    w_heads,
    gain_mid,
    shift_mid,
    gain_wide,
    shift_wide,
):
    span, wide = inputs.shape
    middle = w_reduce.shape[1]
    n_rep, n_dp = lax.axis_size("rep"), lax.axis_size("dp")
    taps = 9
    vmem = pl.BlockSpec(memory_space=pltpu.VMEM)
    hbm = pl.BlockSpec(memory_space=pl.ANY)
    smem = pl.BlockSpec(memory_space=pltpu.SMEM)
    dma = pltpu.SemaphoreType.DMA
    shape = jax.ShapeDtypeStruct
    return pl.pallas_call(
        functools.partial(trunk_kernel, split, (n_rep, n_dp)),
        in_specs=[vmem, smem, vmem, vmem] + [hbm] * 3 + [vmem] * 4,
        out_specs=[vmem] * 12 + [hbm] * (2 * split),
        out_shape=[
            shape((span, middle), F32),
            shape((2, middle), F32),
            shape((span, middle), BF16),
            shape((span, middle), F32),
            shape((2, middle), F32),
            shape((span, middle), BF16),
            shape((span, wide), F32),
            shape((2, wide), F32),
            shape((2, 2 * span, wide), BF16),
            shape((2, 2 * span, w_heads.shape[0]), F32),
            shape((taps, span, span), BF16),
            shape((taps, n_rep, span, span), BF16),
        ]
        + [shape((2, span, wide), BF16)] * (2 * split),
        scratch_shapes=[
            pltpu.VMEM(w_spatial.shape, BF16),
            pltpu.VMEM(w_expand.shape, BF16),
            pltpu.VMEM(w_heads.shape, BF16),
            pltpu.VMEM((2, 2, 2, middle), F32),
            pltpu.VMEM((2, 2, wide), F32),
            pltpu.VMEM((2, n_rep, 2, middle), F32),
            pltpu.VMEM((2, n_dp, 2, middle), F32),
            pltpu.VMEM((n_rep, 2, wide), F32),
            pltpu.VMEM((n_dp, 2, wide), F32),
            dma((3,)),
            dma((3, n_rep)),
            dma((3, n_rep)),
            dma((3, n_dp)),
            dma((3, n_dp)),
            dma((9,)),
            dma((9,)),
            dma((2, 2)),
            dma((2, 2)),
        ],
        compiler_params=pltpu.CompilerParams(
            collective_id=10, has_side_effects=True, vmem_limit_bytes=VMEM_LIMIT
        ),
        name="trunk_forward",
    )(
        inputs,
        layout,
        layout,
        w_reduce,
        w_spatial,
        w_expand,
        w_heads,
        gain_mid,
        shift_mid,
        gain_wide[None, :],
        shift_wide[None, :],
    )


MOVES = 33


def message_kernel(split, n_dp, classes, *refs):
    refs = list(refs)

    def take(count):
        taken, refs[:count] = refs[:count], []
        return taken

    layout_ref, areas_ref, headed_ref, s_ref, w_hbm, gates_w_ref, classes_w_ref = take(7)
    gain_ref, shift_ref, cot_ref, labels_ref = take(4)
    if split:
        trunk_x, trunk_z = take(2)
    depth_ref, logits_ref, gates_ref, classes_ref, low_ref, norm_ref = take(6)
    if split:
        out_ref, mate_x, mate_z, trunk_xz, mate_xz = take(5)
    else:
        heads_ref, gm_ref = take(2)
    w_ref, live_ref, acc_ref, acc_in, stream_ref, direct_ref, cot_in, labels_in = take(8)
    depth_out, logits_out, picked_ref, far_ref, near_ref = take(5)
    core_out, core_in, far_out, far_in, near_out, near_in = take(6)
    sums_ref, slots_ref, load_sem, send, recv, dp_send, dp_recv = take(7)
    if split:
        heads_ref, gm_ref, beside_ref, cut_own, cut_out, cut_in, cut_taken = take(7)

    rep = lax.axis_index("rep")
    par, upper = lax.rem(rep, 2), rep // 2
    mate, far = rep + 1 - 2 * par, rep + 2 - 4 * upper
    first_row = lax.axis_index("dp") * 4
    side_x = lax.rem(lax.axis_index("dp"), 2)
    beside = lax.axis_index("dp") + 1 - 2 * side_x
    side_z = lax.rem(lax.axis_index("dp") // 2, 2)
    along = lax.axis_index("dp") + 2 - 4 * side_z
    span = s_ref.shape[2]
    middle = headed_ref.shape[2]
    small = middle // 2
    load = pltpu.make_async_copy(w_hbm, w_ref, load_sem)
    load.start()

    barrier = pltpu.get_barrier_semaphore()
    me_dp = lax.axis_index("dp")
    for to in (mate, far):
        pl.semaphore_signal(barrier, inc=1, device_id={"rep": to}, device_id_type=MESH)
    for k in range(1, n_dp):
        pl.semaphore_signal(
            barrier, inc=1, device_id={"dp": lax.rem(me_dp + k, n_dp)}, device_id_type=MESH
        )

    def move(number, src, dst, to, axis="rep"):
        return send_to(axis, to, src, dst, send.at[number], recv.at[number])

    def block(parity):
        return pl.ds(pl.multiple_of(parity * span, span), span)

    for p in range(4):
        live_ref[p // 2, (p % 2) * span : (p % 2 + 1) * span, :] = live_column(
            layout_ref, first_row + p, span
        )
    inverse = inverse_count(areas_ref, span)

    def add_up(number, left, right):
        sums_ref[number, 0:1, :] = left
        sums_ref[number, 1:2, :] = right
        return total_along(
            "dp", n_dp, sums_ref.at[number], slots_ref.at[number], dp_send.at[number], dp_recv.at[number]
        )

    def column_sum(value):
        return jnp.sum(value, 0, keepdims=True)

    left, right = 0.0, 0.0
    for side in range(2):
        masked = live_ref[side] * headed_ref[side]
        left = left + column_sum(masked)
        right = right + column_sum(masked * headed_ref[side])
    pl.semaphore_wait(barrier, n_dp + 1)
    move(9, cot_ref, cot_in, far).start()
    move(10, labels_ref, labels_in, far).start()
    sums = add_up(0, left, right)
    if split:
        to_mate_x = move(29, trunk_x, mate_x, mate)
        to_mate_z = move(30, trunk_z, mate_z, mate)
        copy_xz = move(31, trunk_x, trunk_xz, along, "dp")
        to_mate_xz = move(32, trunk_xz, mate_xz, mate)
        copy_xz.start()

    center = sums[0:1] * inverse
    scaling = lax.rsqrt(sums[1:2] * inverse - center * center + EPS)
    gain = gain_ref[pl.ds(rep, 1), :]
    shift = shift_ref[pl.ds(rep, 1), :]

    def across(head, part):
        at = heads_ref.at[head, part // 2, pl.ds((part % 2) * span, span)]
        return move(part, at, at, far)

    def relay(head, part):
        at = heads_ref.at[head, part // 2, pl.ds((part % 2) * span, span)]
        return move(5 + part, at, at, mate)

    def own_head(head):
        return move(4, heads_ref.at[head], heads_ref.at[head], mate)

    for side in range(2):
        normed = (headed_ref[side] - center) * (scaling * gain) + shift
        heads_ref[rep, side] = (normed * jax.nn.sigmoid(normed)).astype(BF16)
        for k in range(2):
            across(rep, 2 * side + k).start()
    own_head(rep).start()
    if split:
        x_own = move(24, heads_ref.at[rep], beside_ref.at[rep], beside, "dp")
        x_far = move(25, heads_ref.at[far], beside_ref.at[far], beside, "dp")
        x_own.start()

    def tap_of(i):
        return par * 5 + i

    def row_of(i, head_at):
        return pl.multiple_of(par * (3 * small) + i * (3 * middle) + head_at * middle, small)

    half_row = (1 - par) * (12 * middle)
    full_row = pl.multiple_of(half_row + par * small, small)
    part_row = pl.multiple_of(half_row + (1 - par) * middle, small)
    part_lanes = pl.ds(pl.multiple_of(par * small, small), small)
    local = 2 * upper
    remote = 2 * (1 - upper)
    local_head = 1 + upper
    part_head = 2 - upper
    full_head = 2 * par + 1 - upper

    def wrows(row, depth):
        return w_ref[pl.ds(row, depth), :]

    def gather_taps(tap, side, y):
        y = y.astype(BF16)
        for k in range(2):
            acc_ref[side, k * span : (k + 1) * span, :] += product(
                s_ref[tap, 2 * side + k], y[k * span : (k + 1) * span]
            )

    acc_ref[...] = jnp.zeros_like(acc_ref)
    own_head(mate).wait_recv()
    load.wait()

    @pl.loop(0, 8)
    def _(n):
        i, side = n // 2, n % 2
        gather_taps(
            tap_of(i), side, product(heads_ref[local_head, side], wrows(row_of(i, local), middle))
        )

    @pl.when(par == upper)
    def _():
        @pl.loop(0, 2)
        def _(side):
            gather_taps(4, side, product(heads_ref[full_head, side], wrows(full_row, middle)))

    for part in range(4):
        across(far, part).wait_recv()
        relay(far, part).start()
    if split:
        x_far.start()
    for part in range(4):
        relay(far + 1 - 2 * par, part).wait_recv()

    @pl.loop(0, 8)
    def _(n):
        i, side = n // 2, n % 2
        y = product(heads_ref[remote, side], wrows(row_of(i, 1 - upper), middle))
        y = y + product(heads_ref[remote + 1, side], wrows(row_of(i, 2 - upper), middle))
        gather_taps(tap_of(i), side, y)

    @pl.loop(0, 2)
    def _(side):
        gather_taps(
            4, side, product(heads_ref[part_head, side, :, part_lanes], wrows(part_row, small))
        )

    @pl.when(par != upper)
    def _():
        @pl.loop(0, 2)
        def _(side):
            gather_taps(4, side, product(heads_ref[full_head, side], wrows(full_row, middle)))

    if split:
        to_mate_x.start()
        to_mate_z.start()

    def acc_move(side):
        return move(11 + side, acc_ref.at[side, block(1 - par)], acc_in.at[side], mate)

    for side in range(2):
        acc_move(side).start()

    own_gates = gates_w_ref[pl.ds(pl.multiple_of(upper * middle, middle), middle), :]
    classes_ref[...] = jnp.zeros_like(classes_ref)
    move(9, cot_ref, cot_in, far).wait_recv()
    move(10, labels_ref, labels_in, far).wait_recv()
    gates_total = 0.0

    def gm_move(side, parity):
        at = gm_ref.at[side, block(parity)]
        return move(13 + side, at, at, mate)

    for side in range(2):
        acc_move(side).wait_recv()
        message = acc_ref[side, block(par), :] + acc_in[side]
        stream = heads_ref[3 * upper, side, block(par), :]
        gate = jax.nn.sigmoid(product(stream, own_gates))
        full = stream.astype(F32) + gate * message
        alive = live_ref[side, block(par), :]

        @pl.when(upper == 0)
        def _():
            cot = (cot_ref if side == 0 else cot_in)[...].astype(F32)
            stream_ref[side] = alive * cot
            (depth_ref if side == 0 else depth_out)[...] = alive * full

        @pl.when(upper == 1)
        def _():
            labels = (labels_in if side == 0 else labels_ref)[...]
            full_low = full.astype(BF16)
            logits = product(full_low, classes_w_ref[...])
            (logits_out if side == 0 else logits_ref)[...] = alive * logits
            lanes = lax.broadcasted_iota(jnp.int32, logits.shape, 1)
            shown = jnp.where(lanes < classes, logits, -1e30)
            grown = jnp.exp(shown - jnp.max(shown, 1, keepdims=True))
            probs = grown / jnp.sum(grown, 1, keepdims=True)
            slope = (alive * (probs - jnp.where(lanes == labels, 1.0, 0.0))).astype(BF16)
            classes_ref[...] += inner_rows(full_low, slope)
            stream_ref[side] = against(slope, classes_w_ref[...])

        grad = stream_ref[side]
        grad_gate = (grad * message * gate * (1.0 - gate)).astype(BF16)
        gm_ref[side, block(par), :] = (grad * gate).astype(BF16)
        gm_move(side, par).start()
        gates_total = gates_total + inner_rows(stream, grad_gate)
        direct_ref[side] = grad + against(grad_gate, own_gates)

    gates_ref[...] = gates_total.astype(BF16)

    @pl.when(upper == 0)
    def _():
        move(15, depth_out, depth_ref, far).start()

    @pl.when(upper == 1)
    def _():
        move(16, logits_out, logits_ref, far).start()

    for side in range(2):
        gm_move(side, 1 - par).wait_recv()
    if split:
        lanes = lax.broadcasted_iota(jnp.int32, (middle, small), 1)
        wanted = (lanes // 64) * 128 + lanes % 64
        source = lax.broadcasted_iota(jnp.int32, (middle, small), 0)
        for cut, which in ((cut_out, 1 - side_x), (cut_own, side_x)):
            pick = jnp.where(source == wanted + 64 * which, 1.0, 0.0).astype(BF16)
            for side in range(2):
                cut[side] = product(gm_ref[side], pick).astype(BF16)
        x_cut = move(28, cut_out, cut_in, beside, "dp")
        x_cut.start()

    @pl.loop(0, 10)
    def _(n):
        i, side = n // 2, n % 2
        tap = jnp.where(i == 4, 4, tap_of(i))
        for k in range(2):
            at = pl.ds(k * span, span)
            picked_ref[i, side, at, :] = inner_rows(
                s_ref[tap, 2 * side + k], gm_ref[side, at, :]
            ).astype(BF16)

    def taps_back(side, head_at):
        total = 0.0
        for i in range(4):
            total = total + against(picked_ref[i, side], wrows(row_of(i, head_at), middle))
        return total

    def core_move(side):
        return move(17 + side, core_out.at[side], core_in.at[side], mate)

    def far_move(part):
        at = pl.ds((part % 2) * span, span)
        return move(19 + part, far_out.at[part // 2, at], far_in.at[part // 2, at], far)

    @pl.loop(0, 2)
    def _(side):
        @pl.loop(0, 2)
        def _(j):
            far_ref[j, side] = taps_back(side, 1 - upper + j)

        far_ref[upper, side, :, part_lanes] += against(picked_ref[4, side], wrows(part_row, small))

        @pl.when(par != upper)
        def _():
            far_ref[2 * par - 1 + upper, side] += against(
                picked_ref[4, side], wrows(full_row, middle)
            )

        core_out[side] = far_ref[1 - par, side].astype(BF16)
        core_move(side).start()

    for side in range(2):
        core_move(side).wait_recv()
        for part in (2 * side, 2 * side + 1):
            at = pl.ds((part % 2) * span, span)
            far_out[side, at, :] = (
                far_ref[par, side, at, :] + core_in[side, at, :].astype(F32)
            ).astype(BF16)
            far_move(part).start()

    @pl.loop(0, 2)
    def _(side):
        near_ref[side] = taps_back(side, local)

    @pl.when(par == upper)
    def _():
        @pl.loop(0, 2)
        def _(side):
            near_ref[side] += against(picked_ref[4, side], wrows(full_row, middle))

        near_out[...] = near_ref[...].astype(BF16)
        for side in range(2):
            near_ref[side, block(par), :] = direct_ref[side]
            near_ref[side, block(1 - par), :] = jnp.zeros((span, middle), F32)

    @pl.when(par != upper)
    def _():
        for side in range(2):
            near_out[side, block(par), :] = direct_ref[side].astype(BF16)
            near_out[side, block(1 - par), :] = jnp.zeros((span, middle), BF16)

    near_move = move(23, near_out, near_in, mate)
    near_move.start()

    if split:
        x_own.wait_recv()
        relay_own = move(26, beside_ref.at[rep], beside_ref.at[rep], mate)
        relay_own.start()
        x_far.wait_recv()
        relay_far = move(27, beside_ref.at[far], beside_ref.at[far], mate)
        relay_far.start()
        x_cut.wait_recv()
        move(26, beside_ref.at[mate], beside_ref.at[mate], mate).wait_recv()
        other = far + 1 - 2 * par
        move(27, beside_ref.at[other], beside_ref.at[other], mate).wait_recv()

        def fill(tap):
            for p in range(4):
                at = pl.ds(p * span, span)
                cut_taken[0, :, at] = inner_rows(
                    cut_own[p // 2, pl.ds((p % 2) * span, span), :], s_ref[tap, p]
                ).astype(BF16)
                cut_taken[1, :, at] = inner_rows(
                    cut_in[p // 2, pl.ds((p % 2) * span, span), :],
                    shift_block(layout_ref, beside * 4 + p, 1, tap, span),
                ).astype(BF16)

        def gradient(head, lanes):
            total = 0.0
            for number, held in enumerate((heads_ref, beside_ref)):
                for side in range(2):
                    total = total + product(
                        cut_taken[number, :, side * 2 * span : (side + 1) * 2 * span],
                        held[head, side, :, lanes],
                    )
            return total.astype(BF16)

        @pl.loop(0, 4)
        def _(i):
            fill(tap_of(i))
            for at in range(3):
                for k in range(2):
                    row = pl.multiple_of(row_of(i, at) + k * small, small)
                    out_ref[:, pl.ds(row, small)] = gradient(
                        at + 1 - upper, pl.ds(k * small, small)
                    )

        fill(4)
        for k in range(2):
            row = pl.multiple_of(full_row + k * small, small)
            out_ref[:, pl.ds(row, small)] = gradient(full_head, pl.ds(k * small, small))
        out_ref[:, pl.ds(part_row, small)] = gradient(part_head, part_lanes)

    if split:
        copy_xz.wait_recv()
        to_mate_xz.start()

    near_move.wait_recv()
    left, right = 0.0, 0.0

    def backward(side):
        unit = (headed_ref[side] - center) * scaling
        normed = unit * gain + shift
        sigma = jax.nn.sigmoid(normed)
        return unit, sigma * (1.0 + normed * (1.0 - sigma))

    for side in range(2):
        for part in (2 * side, 2 * side + 1):
            far_move(part).wait_recv()
        unit, slope = backward(side)
        grad = near_ref[side] + near_in[side].astype(F32) + far_in[side].astype(F32)
        grad = grad * slope
        near_ref[side] = grad
        masked = live_ref[side] * grad
        left = left + column_sum(masked * unit)
        right = right + column_sum(masked)
    sums = add_up(1, left, right)
    norm_ref[...] = sums
    for side in range(2):
        unit = (headed_ref[side] - center) * scaling
        low_ref[side] = (
            live_ref[side]
            * (gain * scaling)
            * (near_ref[side] - sums[1:2] * inverse - unit * (sums[0:1] * inverse))
        ).astype(BF16)

    for part in range(4):
        across(rep, part).wait_send()
        relay(far, part).wait_send()
        far_move(part).wait_send()
    own_head(rep).wait_send()
    move(9, cot_ref, cot_in, far).wait_send()
    move(10, labels_ref, labels_in, far).wait_send()
    for side in range(2):
        acc_move(side).wait_send()
        gm_move(side, par).wait_send()
    for side in range(2):
        core_move(side).wait_send()
    near_move.wait_send()

    @pl.when(upper == 0)
    def _():
        move(15, depth_out, depth_ref, far).wait_send()
        move(16, logits_out, logits_ref, far).wait_recv()

    @pl.when(upper == 1)
    def _():
        move(16, logits_out, logits_ref, far).wait_send()
        move(15, depth_out, depth_ref, far).wait_recv()

    if split:
        for copy in (to_mate_x, to_mate_z, to_mate_xz):
            copy.wait_recv()
            copy.wait_send()
        for copy in (x_own, x_far, x_cut, relay_own, relay_far, copy_xz):
            copy.wait_send()


def message_streams(
    split, layout, headed, shifts, w_messages, w_gates, w_classes, gain, shift, cot, labels, afar
):
    n_dp = lax.axis_size("dp")
    span, middle = cot.shape
    small = middle // 2
    classes = w_classes.shape[1]
    vmem = pl.BlockSpec(memory_space=pltpu.VMEM)
    dma = pltpu.SemaphoreType.DMA
    shape = jax.ShapeDtypeStruct
    halves = (2, 2 * span, middle)
    heads = (4, 2, 2 * span, middle)
    out_shape = [
        shape((span, middle), F32),
        shape((span, 128), F32),
        shape((middle, middle), BF16),
        shape((middle, 128), F32),
        shape(halves, BF16),
        shape((2, middle), F32),
    ]
    if split:
        out_shape += [shape((small, w_messages.shape[0]), BF16)] + [shape(afar[0].shape, BF16)] * 4
    else:
        out_shape += [shape(heads, BF16), shape(halves, BF16)]
    scratch = [
        pltpu.VMEM(w_messages.shape, BF16),
        pltpu.VMEM((2, 2 * span, 1), F32),
        pltpu.VMEM(halves, F32),
        pltpu.VMEM((2, span, middle), F32),
        pltpu.VMEM((2, span, middle), F32),
        pltpu.VMEM((2, span, middle), F32),
        pltpu.VMEM((span, middle), BF16),
        pltpu.VMEM((span, 128), jnp.int32),
        pltpu.VMEM((span, middle), F32),
        pltpu.VMEM((span, 128), F32),
        pltpu.VMEM((5,) + halves, BF16),
        pltpu.VMEM((2,) + halves, F32),
        pltpu.VMEM(halves, F32),
        pltpu.VMEM(halves, BF16),
        pltpu.VMEM(halves, BF16),
        pltpu.VMEM(halves, BF16),
        pltpu.VMEM(halves, BF16),
        pltpu.VMEM(halves, BF16),
        pltpu.VMEM(halves, BF16),
        pltpu.VMEM((2, 2, middle), F32),
        pltpu.VMEM((2, n_dp, 2, middle), F32),
        dma,
        dma((MOVES,)),
        dma((MOVES,)),
        dma((2, n_dp)),
        dma((2, n_dp)),
    ]
    if split:
        scratch += [
            pltpu.VMEM(heads, BF16),
            pltpu.VMEM(halves, BF16),
            pltpu.VMEM(heads, BF16),
            pltpu.VMEM((2, 2 * span, small), BF16),
            pltpu.VMEM((2, 2 * span, small), BF16),
            pltpu.VMEM((2, 2 * span, small), BF16),
            pltpu.VMEM((2, small, 4 * span), BF16),
        ]
    return pl.pallas_call(
        functools.partial(message_kernel, split, n_dp, classes),
        in_specs=[pl.BlockSpec(memory_space=pltpu.SMEM)]
        + [vmem] * 3
        + [pl.BlockSpec(memory_space=pl.ANY)]
        + [vmem] * 6
        + [pl.BlockSpec(memory_space=pl.ANY)] * len(afar),
        out_specs=[vmem] * 7 + [pl.BlockSpec(memory_space=pl.ANY) if split else vmem] * (len(out_shape) - 7),
        out_shape=out_shape,
        scratch_shapes=scratch,
        compiler_params=pltpu.CompilerParams(
            collective_id=11, has_side_effects=True, vmem_limit_bytes=VMEM_LIMIT
        ),
        name="message_streams",
    )(
        layout,
        layout,
        headed,
        shifts,
        w_messages,
        w_gates,
        jnp.pad(w_classes, ((0, 0), (0, 128 - classes))),
        gain.reshape(4, middle),
        shift.reshape(4, middle),
        cot,
        jnp.broadcast_to(labels[:, None], (span, 128)),
        *afar,
    )


def heads_back_kernel(split, *refs):
    refs = list(refs)

    def take(count):
        taken, refs[:count] = refs[:count], []
        return taken

    low_ref, s_ref, w_hbm, out_ref = take(4)
    if split:
        low_x, low_z, low_xz = take(3)
    w_ref, taken_ref, tile_ref, far_kept, near_kept = take(5)
    core_out, core_in, far_out, far_in, near_out, near_in = take(6)
    load_sems, send, recv = take(3)
    rep, dp = lax.axis_index("rep"), lax.axis_index("dp")
    par, upper = lax.rem(rep, 2), rep // 2
    mate, far = rep + 1 - 2 * par, rep + 2 - 4 * upper
    beside, along = dp + 1 - 2 * lax.rem(dp, 2), dp + 2 - 4 * lax.rem(dp // 2, 2)
    taps, span = s_ref.shape[0], s_ref.shape[2]
    wide = out_ref.shape[1]
    step = tile_ref.shape[1]
    tiles = wide // step

    def load(t):
        at = pl.ds(pl.multiple_of(t * wide, wide), wide)
        return pltpu.make_async_copy(w_hbm.at[:, at], w_ref.at[:, at], load_sems.at[t])

    for t in range(taps):
        load(t).start()
    barrier = pltpu.get_barrier_semaphore()
    partners = [{"rep": mate}, {"rep": far}]
    if split:
        partners += [{"dp": beside}, {"dp": along}]
    for partner in partners:
        pl.semaphore_signal(barrier, inc=1, device_id=partner, device_id_type=MESH)

    def move(number, src, dst, to, axis="rep"):
        return send_to(axis, to, src, dst, send.at[number], recv.at[number])

    def block(parity):
        return pl.ds(pl.multiple_of(parity * span, span), span)

    pl.semaphore_wait(barrier, len(partners))
    if split:
        copy_x = move(0, low_ref, low_x, beside, "dp")
        copy_z = move(1, low_ref, low_z, along, "dp")
        copy_xz = move(2, low_x, low_xz, along, "dp")
        copy_x.start()
        copy_z.start()

    def core_move(c):
        return move(3 + c, core_out.at[c], core_in.at[c], mate)

    def far_move(c):
        return move(3 + tiles + c, far_out.at[c], far_in.at[c], far)

    def near_move(c):
        return move(3 + 2 * tiles + c, near_out.at[c], near_in.at[c], mate)

    def take_taps(side):
        @pl.loop(0, taps)
        def _(t):
            for k in range(2):
                at = pl.ds(k * span, span)
                taken_ref[t, at, :] = inner_rows(
                    s_ref[t, 2 * side + k], low_ref[side, at, :]
                ).astype(BF16)

    def convolve(c):
        total = 0.0
        for t in range(taps):
            at = pl.ds(pl.multiple_of(t * wide + c * step, step), step)
            total = total + product(taken_ref[t], w_ref[:, at])
        tile_ref[...] = total

    def pass_on(c):
        core_move(c).wait_recv()
        far_out[c] = (far_kept[c] + core_in[c].astype(F32)).astype(BF16)
        far_move(c).start()

    take_taps(1 - upper)
    for t in range(taps):
        load(t).wait()

    @pl.loop(0, tiles)
    def _(c):
        convolve(c)
        core_out[c] = tile_ref[block(1 - par), :].astype(BF16)
        core_move(c).start()
        far_kept[c] = tile_ref[block(par), :]

        @pl.when(c > 0)
        def _():
            pass_on(c - 1)

    take_taps(upper)
    pass_on(tiles - 1)

    @pl.loop(0, tiles)
    def _(c):
        convolve(c)
        near_out[c] = tile_ref[block(1 - par), :].astype(BF16)
        near_move(c).start()
        near_kept[c] = tile_ref[block(par), :]
        if split:

            @pl.when(c == 1)
            def _():
                copy_x.wait_recv()
                copy_xz.start()

    for c in range(tiles):
        near_move(c).wait_recv()
        far_move(c).wait_recv()
        out_ref[:, c * step : (c + 1) * step] = (
            near_kept[c] + near_in[c].astype(F32) + far_in[c].astype(F32)
        ).astype(BF16)
    for c in range(tiles):
        core_move(c).wait_send()
        far_move(c).wait_send()
        near_move(c).wait_send()
    if split:
        copy_z.wait_recv()
        copy_xz.wait_recv()
        for copy in (copy_x, copy_z, copy_xz):
            copy.wait_send()


def heads_back(split, low, shifts, w_heads):
    taps, _, span, _ = shifts.shape
    wide = w_heads.shape[1] // taps
    vmem = pl.BlockSpec(memory_space=pltpu.VMEM)
    dma = pltpu.SemaphoreType.DMA
    shape = jax.ShapeDtypeStruct
    out_shape = [shape((span, wide), BF16)]
    if split:
        out_shape += [shape(low.shape, BF16)] * 3
    return pl.pallas_call(
        functools.partial(heads_back_kernel, split),
        in_specs=[vmem, vmem, pl.BlockSpec(memory_space=pl.ANY)],
        out_specs=[vmem] * len(out_shape),
        out_shape=out_shape,
        scratch_shapes=[
            pltpu.VMEM(w_heads.shape, BF16),
            pltpu.VMEM((taps, 2 * span, low.shape[2]), BF16),
            pltpu.VMEM((2 * span, 512), F32),
            pltpu.VMEM((wide // 512, span, 512), F32),
            pltpu.VMEM((wide // 512, span, 512), F32),
        ]
        + [pltpu.VMEM((wide // 512, span, 512), BF16)] * 6
        + [dma((taps,)), dma((3 + 3 * wide // 512,)), dma((3 + 3 * wide // 512,))],
        compiler_params=pltpu.CompilerParams(
            collective_id=12, has_side_effects=True, vmem_limit_bytes=VMEM_LIMIT
        ),
        name="heads_back",
    )(low, shifts, w_heads)


def heads_shard_kernel(per_tap, at_ref, layout_ref, *refs):
    lows, trunks, out_ref, taken = refs[:4], refs[4:11], refs[11], refs[12]
    unit = pl.program_id(1)
    at = at_ref[pl.program_id(0)] + unit
    tap, chunk = at // per_tap, at % per_tap
    rows = lows[0].shape[1]
    span = rows // 2
    par = at_ref[6]

    places = [(0, side, k) for side in range(2) for k in range(2)]
    for number in range(1, 4):
        places += [(number, side, q) for q in (par, 1 - par) for side in range(2)]

    @pl.when((unit == 0) | (chunk == 0))
    def _():
        for slot, (number, side, k) in enumerate(places):
            picks = shift_block(layout_ref, at_ref[2 + number] + 2 * side + k, 1, tap, span)
            mine = pl.ds(pl.multiple_of(k * span, span), span)
            taken[:, slot * span : (slot + 1) * span] = inner_rows(
                lows[number][side, mine, :], picks
            ).astype(BF16)

    total = 0.0
    slot = 0
    for trunk in trunks:
        strip = trunk[...].reshape(-1, trunk.shape[2])
        depth = strip.shape[0]
        total = total + product(taken[:, slot : slot + depth], strip)
        slot += depth
    out_ref[0] = total.astype(BF16)


def heads_shard(at, layout, lows, trunks, units, lanes):
    _, rows, outs = lows[0].shape
    wide = trunks[0].shape[2]
    per_tap = wide // lanes
    whole = pl.BlockSpec(lows[0].shape, lambda i, j, f, g: (0, 0, 0))
    strips = [
        pl.BlockSpec(trunk.shape[:2] + (lanes,), lambda i, j, f, g: (0, 0, (f[i] + j) % per_tap))
        for trunk in trunks
    ]
    return pl.pallas_call(
        functools.partial(heads_shard_kernel, per_tap),
        grid_spec=pltpu.PrefetchScalarGridSpec(
            num_scalar_prefetch=2,
            grid=(2, units),
            in_specs=[whole] * 4 + strips,
            out_specs=pl.BlockSpec((1, outs, lanes), lambda i, j, f, g: (i, 0, j)),
            scratch_shapes=[pltpu.VMEM((outs, 8 * rows), BF16)],
        ),
        out_shape=jax.ShapeDtypeStruct((2, outs, units * lanes), BF16),
        compiler_params=params(),
        cost_estimate=cost(32 * rows * outs * units * lanes, 32 * rows * units * lanes),
        name="heads_shard",
    )(at, layout, *lows, *trunks)


CHUNK_ROWS = (384, 512, 640, 512, 256, 256)
CHUNK_BASE = (0, 384, 896, 1536, 2048, 2304)
SMALL_ROWS = 2560
SPATIAL_BASE = 896
REDUCE_BASE = 2048


def trunk_back_kernel(*refs):
    refs = list(refs)

    def take(count):
        taken, refs[:count] = refs[:count], []
        return taken

    layout_ref, areas_ref, grad_ref, expanded_ref, in_ref = take(5)
    reduced_ref, spatial_ref, sums_one_ref, sums_two_ref, sums_three_ref = take(5)
    hidden_one_ref, hidden_two_ref, shift_taps_ref = take(3)
    w_reduce_ref, w_spatial_ref, w_expand_ref = take(3)
    gain_mid_ref, shift_mid_ref, gain_wide_ref, shift_wide_ref = take(4)
    gates_ref, classes_ref = take(2)
    out_ref, norm_one_ref, norm_two_ref, norm_three_ref = take(4)
    reduce_out, spatial_out, expand_out, gates_out, classes_out = take(5)
    p_ref, half_ref, core_in, core_out, y_in, x_out, x_in, z_out, z_in = take(9)
    z_mid, zz_in = take(2)
    low_wide, moved_ref, total_ref, block_mid, block_wide = take(5)
    slots_mid_rep, slots_mid_dp, slots_wide_rep, slots_wide_dp = take(4)
    rep_send, rep_recv, dp_send, dp_recv, send, recv = take(6)

    rep, dp = lax.axis_index("rep"), lax.axis_index("dp")
    par, upper = lax.rem(rep, 2), rep // 2
    x, z = lax.rem(dp, 2), dp // 2
    mate, far, beside = rep + 1 - 2 * par, rep + 2 - 4 * upper, dp + 1 - 2 * x
    low_z, high_z = lax.rem(z, 2), z // 2
    along, over = dp + 2 - 4 * low_z, dp + 4 - 8 * high_z
    span, wide = in_ref.shape
    middle = reduced_ref.shape[1]
    taps = shift_taps_ref.shape[0]
    barrier = pltpu.get_barrier_semaphore()
    for axis, size in (("rep", 4), ("dp", 8)):
        me = lax.axis_index(axis)
        for k in range(1, size):
            pl.semaphore_signal(
                barrier, inc=1, device_id={axis: lax.rem(me + k, size)}, device_id_type=MESH
            )

    def remote(src, dst, c, slot, to):
        return pltpu.make_async_remote_copy(
            src_ref=src,
            dst_ref=dst,
            send_sem=send.at[c, slot],
            recv_sem=recv.at[c, slot],
            device_id=to,
            device_id_type=MESH,
        )

    def whole(c, at=0, size=None):
        size = CHUNK_ROWS[c] if size is None else size
        return pl.ds(pl.multiple_of(CHUNK_BASE[c] + at, 16), size)

    def halves(c):
        return pl.ds(CHUNK_BASE[c] // 2, CHUNK_ROWS[c] // 2)

    def core_copy(c, hi):
        return remote(
            p_ref.at[2 * hi + 1 - par, whole(c)], core_in.at[hi, whole(c)], c, hi, {"rep": mate}
        )

    def y_copy(c):
        return remote(core_out.at[whole(c)], y_in.at[whole(c)], c, 2, {"rep": far})

    def x_copy(c):
        return remote(x_out.at[halves(c)], x_in.at[halves(c)], c, 3, {"dp": beside})

    def piece(c, base, at, size):
        return pl.ds(pl.multiple_of(CHUNK_BASE[c] // base + at, 16), size)

    def z_copy(c):
        size = CHUNK_ROWS[c] // 4
        return remote(
            z_out.at[piece(c, 2, (1 - low_z) * size, size)],
            z_in.at[piece(c, 4, 0, size)],
            c,
            4,
            {"dp": along},
        )

    def zz_copy(c):
        size = CHUNK_ROWS[c] // 8
        return remote(
            z_mid.at[piece(c, 4, (1 - high_z) * size, size)],
            zz_in.at[piece(c, 8, 0, size)],
            c,
            5,
            {"dp": over},
        )

    def own_place(c, low, high=None):
        size = CHUNK_ROWS[c] // 4
        at = x * 2 * size + low * size
        if high is None:
            return whole(c, at, size)
        return whole(c, at + high * (size // 2), size // 2)

    def zz_back(c, incoming):
        place = own_place(c, low_z, 1 - high_z if incoming else high_z)
        return remote(half_ref.at[place], half_ref.at[place], c, 6, {"dp": over})

    def z_back(c, incoming):
        place = own_place(c, 1 - low_z if incoming else low_z)
        return remote(half_ref.at[place], half_ref.at[place], c, 7, {"dp": along})

    def last_copy(c, incoming):
        half = CHUNK_ROWS[c] // 2
        place = whole(c, (1 - x if incoming else x) * half, half)
        return remote(half_ref.at[place], half_ref.at[place], c, 8, {"dp": beside})

    def finish(c):
        base = CHUNK_BASE[c]

        def held(at, size):
            return half_ref[base + at : base + at + size, :].astype(F32)

        if c == 0:
            gates_out[...] = held(0, gates_out.shape[0])
            classes_out[...] = held(gates_out.shape[0], classes_out.shape[0])
        elif c == 1:
            rows = expand_out.shape[0]
            for k in range(wide // middle):
                expand_out[:, k * middle : (k + 1) * middle] = held(k * rows, rows)
        elif c < 4:
            at = base - SPATIAL_BASE
            spatial_out[at : at + CHUNK_ROWS[c], :] = held(0, CHUNK_ROWS[c])
        else:
            at = base - REDUCE_BASE
            reduce_out[at : at + CHUNK_ROWS[c], :] = held(0, CHUNK_ROWS[c])

    def step(c, stage):
        if stage == 0:
            for hi in range(2):
                core_copy(c, hi).start()
        elif stage == 1:
            for hi in range(2):
                core_copy(c, hi).wait_recv()
            core_out[whole(c)] = (
                p_ref[2 * (1 - upper) + par, whole(c)].astype(F32)
                + core_in[1 - upper, whole(c)].astype(F32)
            ).astype(BF16)
            y_copy(c).start()
        elif stage == 2:
            y_copy(c).wait_recv()
            half = CHUNK_ROWS[c] // 2

            def both(at):
                place = whole(c, at, half)
                return (
                    p_ref[rep, place].astype(F32)
                    + core_in[upper, place].astype(F32)
                    + y_in[place].astype(F32)
                )

            x_out[halves(c)] = both((1 - x) * half).astype(BF16)
            x_copy(c).start()
            z_out[halves(c)] = both(x * half).astype(BF16)
        elif stage == 3:
            x_copy(c).wait_recv()
            z_out[halves(c)] = (
                z_out[halves(c)].astype(F32) + x_in[halves(c)].astype(F32)
            ).astype(BF16)
            z_copy(c).start()
        elif stage == 4:
            z_copy(c).wait_recv()
            size = CHUNK_ROWS[c] // 4
            at = piece(c, 4, 0, size)
            z_mid[at] = (
                z_out[piece(c, 2, low_z * size, size)].astype(F32) + z_in[at].astype(F32)
            ).astype(BF16)
            zz_copy(c).start()
        elif stage == 5:
            zz_copy(c).wait_recv()
            size = CHUNK_ROWS[c] // 8
            half_ref[own_place(c, low_z, high_z)] = (
                z_mid[piece(c, 4, high_z * size, size)].astype(F32)
                + zz_in[piece(c, 8, 0, size)].astype(F32)
            ).astype(BF16)
            zz_back(c, False).start()
        elif stage == 6:
            zz_back(c, True).wait_recv()
            z_back(c, False).start()
        elif stage == 7:
            z_back(c, True).wait_recv()
            last_copy(c, False).start()
        else:
            last_copy(c, True).wait_recv()
            finish(c)
            for hi in range(2):
                core_copy(c, hi).wait_send()
            y_copy(c).wait_send()
            x_copy(c).wait_send()
            z_copy(c).wait_send()
            zz_copy(c).wait_send()
            zz_back(c, False).wait_send()
            z_back(c, False).wait_send()
            last_copy(c, False).wait_send()

    def steps(*which):
        def run():
            for c, stage in which:
                step(c, stage)

        return run

    live = live_column(layout_ref, dp * 4 + rep, span)
    inverse = inverse_count(areas_ref, span)

    def stats(sums_ref):
        center = sums_ref[0:1, :] * inverse
        return center, lax.rsqrt(sums_ref[1:2, :] * inverse - center * center + EPS)

    def local_sums(blocks, value, unit, at):
        masked = live * value
        blocks[0, 0:1, at] = jnp.sum(masked * unit, 0, keepdims=True)
        blocks[0, 1:2, at] = jnp.sum(masked, 0, keepdims=True)

    def everywhere(number, blocks, rep_slots, dp_slots, meanwhile, later):
        if number == 0:
            pl.semaphore_wait(barrier, 10)
        blocks[1] = total_along(
            "rep", 4, blocks.at[0], rep_slots, rep_send.at[number], rep_recv.at[number], meanwhile
        )
        return total_along(
            "dp", 8, blocks.at[1], dp_slots, dp_send.at[number], dp_recv.at[number], later
        )

    def slope(value):
        sigma = jax.nn.sigmoid(value)
        return sigma * (1.0 + value * (1.0 - sigma))

    def spread_back(grad, unit, sums, gain, scaling):
        return (
            live
            * (gain * scaling)
            * (grad - sums[1:2] * inverse - unit * (sums[0:1] * inverse))
        ).astype(BF16)

    center, scaling = stats(sums_three_ref)
    strips = [pl.ds(k, middle) for k in range(0, wide, middle)]

    def unit_at(at):
        return (expanded_ref[:, at] - center[:, at.start : at.start + middle]) * scaling[
            :, at.start : at.start + middle
        ]

    for at in strips:
        unit = unit_at(at)
        pre = unit * gain_wide_ref[:, at] + shift_wide_ref[:, at] + in_ref[:, at].astype(F32)
        grad = grad_ref[:, at].astype(F32) * slope(pre)
        out_ref[:, at] = grad
        local_sums(block_wide, grad, unit, at)

    def first_chunk():
        half = gates_out.shape[0]
        rows = classes_out.shape[0]
        for q in range(4):
            p_ref[q, half : half + rows, :] = classes_ref[q]
            p_ref[q, half + rows : CHUNK_ROWS[0], :] = jnp.zeros(
                (CHUNK_ROWS[0] - half - rows, middle), BF16
            )
        for k in range(2):
            p_ref[2 * upper + k, :half, :] = gates_ref[k * half : (k + 1) * half, :]
            p_ref[2 * (1 - upper) + k, :half, :] = jnp.zeros((half, middle), BF16)
        step(0, 0)
        step(0, 1)

    sums = everywhere(
        0,
        block_wide,
        slots_wide_rep,
        slots_wide_dp,
        first_chunk,
        steps((0, 2)),
    )
    norm_three_ref[...] = sums
    for at in strips:
        cut = slice(at.start, at.start + middle)
        low_wide[:, at] = spread_back(
            out_ref[:, at], unit_at(at), sums[:, cut], gain_wide_ref[:, at], scaling[:, cut]
        )

    center, scaling = stats(sums_two_ref)
    unit = (spatial_ref[...] - center) * scaling
    normed = unit * gain_mid_ref[1:2, :] + shift_mid_ref[1:2, :]
    total_ref[...] = against(low_wide[...], w_expand_ref[...]) * slope(normed)

    def expand_gradient():
        rows = middle // 4
        for k in range(wide // middle):
            tile = inner_rows(
                hidden_two_ref[...], low_wide[:, k * middle : (k + 1) * middle]
            ).astype(BF16)
            for q in range(4):
                at = CHUNK_BASE[1] + k * rows
                p_ref[q, at : at + rows, :] = tile[q * rows : (q + 1) * rows]
        step(1, 0)
        step(1, 1)

    local_sums(block_mid.at[0], total_ref[...], unit, slice(None))
    sums = everywhere(
        1,
        block_mid.at[0],
        slots_mid_rep.at[0],
        slots_mid_dp.at[0],
        expand_gradient,
        steps((0, 3), (1, 2)),
    )
    norm_two_ref[...] = sums
    low_mid = spread_back(total_ref[...], unit, sums, gain_mid_ref[1:2, :], scaling)

    total_ref[...] = jnp.zeros_like(total_ref)
    for t in range(taps):
        moved_ref[t] = inner_rows(shift_taps_ref[t], low_mid).astype(BF16)

    @pl.loop(0, taps)
    def _(t):
        at = pl.ds(pl.multiple_of(t * middle, middle), middle)
        total_ref[...] += against(moved_ref[t], w_spatial_ref[at, :])

    center, scaling = stats(sums_one_ref)
    unit = (reduced_ref[...] - center) * scaling
    normed = unit * gain_mid_ref[0:1, :] + shift_mid_ref[0:1, :]
    total_ref[...] = total_ref[...] * slope(normed)

    def spatial_gradient():
        quarter = spatial_out.shape[0]
        for t in range(taps):
            tile = inner_rows(hidden_one_ref[...], moved_ref[t]).astype(BF16)
            for m in range(0, middle, 128):
                q, row = (t * middle + m) // quarter, (t * middle + m) % quarter
                at = SPATIAL_BASE + row
                p_ref[q, at : at + 128, :] = tile[m : m + 128]
        step(2, 0)
        step(3, 0)
        step(2, 1)
        step(3, 1)

    local_sums(block_mid.at[1], total_ref[...], unit, slice(None))
    sums = everywhere(
        2,
        block_mid.at[1],
        slots_mid_rep.at[1],
        slots_mid_dp.at[1],
        spatial_gradient,
        steps((0, 4), (1, 3), (2, 2)),
    )
    norm_one_ref[...] = sums
    low_first = spread_back(total_ref[...], unit, sums, gain_mid_ref[0:1, :], scaling)
    quarter = wide // 4
    for q in range(4):
        p_ref[q, REDUCE_BASE : REDUCE_BASE + quarter, :] = inner_rows(
            in_ref[:, q * quarter : (q + 1) * quarter], low_first
        ).astype(BF16)
    step(4, 0)
    step(5, 0)
    step(3, 2)
    step(2, 3)
    step(1, 4)
    step(0, 5)
    step(4, 1)
    step(5, 1)
    for k in range(0, wide, middle):
        out_ref[:, k : k + middle] += against(low_first, w_reduce_ref[k : k + middle, :])
    for turn in (
        ((3, 3), (2, 4), (1, 5), (0, 6), (4, 2)),
        ((3, 4), (2, 5), (1, 6), (0, 7), (4, 3), (5, 2)),
        ((3, 5), (2, 6), (1, 7), (0, 8), (4, 4), (5, 3)),
        ((3, 6), (2, 7), (1, 8), (4, 5), (5, 4)),
        ((3, 7), (2, 8), (4, 6), (5, 5)),
        ((3, 8), (4, 7), (5, 6)),
        ((4, 8), (5, 7)),
        ((5, 8),),
    ):
        for c, stage in turn:
            step(c, stage)


def trunk_back(
    layout,
    grad,
    expanded,
    inputs,
    reduced,
    spatial,
    sums,
    hidden_one,
    hidden_two,
    shift_taps,
    w_reduce,
    w_spatial,
    w_expand,
    gain_mid,
    shift_mid,
    gain_wide,
    shift_wide,
    gates,
    classes,
):
    span, wide = inputs.shape
    middle = reduced.shape[1]
    taps = shift_taps.shape[0]
    vmem = pl.BlockSpec(memory_space=pltpu.VMEM)
    dma = pltpu.SemaphoreType.DMA
    shape = jax.ShapeDtypeStruct
    small = (SMALL_ROWS, middle)
    half = (SMALL_ROWS // 2, middle)
    chunks = len(CHUNK_ROWS)
    out_shape = [
        shape((span, wide), F32),
        shape((2, middle), F32),
        shape((2, middle), F32),
        shape((2, wide), F32),
        shape((wide // 4, middle), F32),
        shape((taps * middle // 4, middle), F32),
        shape((middle // 4, wide), F32),
        shape((middle // 2, middle), F32),
        shape(classes.shape[1:], F32),
    ]
    return pl.pallas_call(
        trunk_back_kernel,
        in_specs=[pl.BlockSpec(memory_space=pltpu.SMEM)] + [vmem] * 21,
        out_specs=[vmem] * len(out_shape),
        out_shape=out_shape,
        scratch_shapes=[
            pltpu.VMEM((4,) + small, BF16),
            pltpu.VMEM(small, BF16),
            pltpu.VMEM((2,) + small, BF16),
            pltpu.VMEM(small, BF16),
            pltpu.VMEM(small, BF16),
            pltpu.VMEM(half, BF16),
            pltpu.VMEM(half, BF16),
            pltpu.VMEM(half, BF16),
            pltpu.VMEM((SMALL_ROWS // 4, middle), BF16),
            pltpu.VMEM((SMALL_ROWS // 4, middle), BF16),
            pltpu.VMEM((SMALL_ROWS // 8, middle), BF16),
            pltpu.VMEM((span, wide), BF16),
            pltpu.VMEM((taps, span, middle), BF16),
            pltpu.VMEM((span, middle), F32),
            pltpu.VMEM((2, 2, 2, middle), F32),
            pltpu.VMEM((2, 2, wide), F32),
            pltpu.VMEM((2, 4, 2, middle), F32),
            pltpu.VMEM((2, 8, 2, middle), F32),
            pltpu.VMEM((4, 2, wide), F32),
            pltpu.VMEM((8, 2, wide), F32),
            dma((3, 4)),
            dma((3, 4)),
            dma((3, 8)),
            dma((3, 8)),
            dma((chunks, 9)),
            dma((chunks, 9)),
        ],
        compiler_params=pltpu.CompilerParams(
            collective_id=9, has_side_effects=True, vmem_limit_bytes=VMEM_LIMIT
        ),
        name="trunk_back",
    )(
        layout,
        layout,
        grad,
        expanded,
        inputs,
        reduced,
        spatial,
        *sums,
        hidden_one,
        hidden_two,
        shift_taps,
        w_reduce,
        w_spatial,
        w_expand,
        gain_mid,
        shift_mid,
        gain_wide[None, :],
        shift_wide[None, :],
        gates,
        classes,
    )


def silu_slope(value_in):
    sigma_of = jax.nn.sigmoid(value_in)
    return sigma_of * (1.0 + value_in * (1.0 - sigma_of))


MESH = pl.DeviceIdType.MESH


def greet(axes):
    barrier = pltpu.get_barrier_semaphore()
    count = 0
    for axis, size in axes:
        me = lax.axis_index(axis)
        for k in range(1, size):
            pl.semaphore_signal(
                barrier, inc=1, device_id={axis: lax.rem(me + k, size)}, device_id_type=MESH
            )
        count += size - 1
    pl.semaphore_wait(barrier, count)


def total_kernel(axes, x_ref, out_ref, *scratch):
    greet(axes)
    block = x_ref
    for number, (axis, size) in enumerate(axes):
        slots, stage, send_sems, recv_sems = scratch[4 * number : 4 * number + 4]
        me = lax.axis_index(axis)
        others = [lax.rem(me + k, size) for k in range(1, size)]
        for other in others:
            pltpu.make_async_remote_copy(
                src_ref=block,
                dst_ref=slots.at[me],
                send_sem=send_sems.at[other],
                recv_sem=recv_sems.at[me],
                device_id={axis: other},
                device_id_type=MESH,
            ).start()
        slots[me] = block[...]
        for other in others:
            copy = pltpu.make_async_remote_copy(
                src_ref=block,
                dst_ref=slots.at[other],
                send_sem=send_sems.at[other],
                recv_sem=recv_sems.at[other],
                device_id={axis: other},
                device_id_type=MESH,
            )
            copy.wait_recv()
            copy.wait_send()
        total = slots[0]
        for k in range(1, size):
            total = total + slots[k]
        if number == len(axes) - 1:
            out_ref[...] = total
        else:
            stage[...] = total
            block = stage


def total_of(left, right, axes):
    width = left.shape[0]
    packed = jnp.concatenate([left, right], 0).reshape(-1, 128)
    sized = tuple((axis, lax.axis_size(axis)) for axis in axes)
    scratch = []
    for _, size in sized:
        scratch += [
            pltpu.VMEM((size,) + packed.shape, F32),
            pltpu.VMEM(packed.shape, F32),
            pltpu.SemaphoreType.DMA((size,)),
            pltpu.SemaphoreType.DMA((size,)),
        ]
    number = 1 + (width != 512) + 2 * (len(axes) == 1)
    summed = pl.pallas_call(
        functools.partial(total_kernel, sized),
        out_shape=jax.ShapeDtypeStruct(packed.shape, F32),
        in_specs=[pl.BlockSpec(memory_space=pltpu.VMEM)],
        out_specs=pl.BlockSpec(memory_space=pltpu.VMEM),
        scratch_shapes=scratch,
        compiler_params=pltpu.CompilerParams(collective_id=number, has_side_effects=True),
        name="total",
    )(packed).reshape(2, width)
    return summed[0], summed[1]


def normalize(raw_value, column_sums, squares, pixel_count, norm_gain, norm_shift):
    center = column_sums / pixel_count
    spread_of = squares / pixel_count - center * center
    scaling = lax.rsqrt(spread_of + EPS)
    unit_value = (raw_value - center) * scaling
    return (unit_value * norm_gain + norm_shift, unit_value, scaling)


def moments(raw_value, living, axes):
    return total_of(
        jnp.sum(living * raw_value, 0), jnp.sum(living * raw_value * raw_value, 0), axes
    )


def norm_back(grad_out, unit_value, scaling, norm_gain, living, pixel_count, axes):
    grad_gain, grad_shift = total_of(
        jnp.sum(living * grad_out * unit_value, 0), jnp.sum(living * grad_out, 0), axes
    )
    grad_raw = (
        living
        * (norm_gain * scaling)
        * (grad_out - grad_shift / pixel_count - unit_value * grad_gain / pixel_count)
    )
    return (grad_raw, grad_gain, grad_shift)


def swap(value, bit):
    return lax.ppermute(value, "rep", [(k, k ^ bit) for k in range(4)])


def scatter_rep(value):
    return lax.psum_scatter(value.astype(BF16), "rep", scatter_dimension=0, tiled=True)


def total_dp(value):
    parts = lax.axis_size("dp")
    rows = value.shape[0]
    padded = -(-rows // (8 * parts)) * 8 * parts
    value = jnp.pad(value, ((0, padded - rows), (0, 0)))
    share = lax.psum_scatter(value, "dp", scatter_dimension=0, tiled=True)
    return lax.all_gather(share, "dp", axis=0, tiled=True)[:rows].astype(F32)


def shards(
    inputs,
    layout,
    labels,
    cot_depth,
    w_reduce,
    w_spatial,
    w_expand,
    w_heads,
    w_gates,
    w_messages,
    w_classes,
    gain_mid,
    shift_mid,
    gain_wide,
    shift_wide,
    gain_head,
    shift_head,
):
    pixels = inputs.shape[0]
    middle = w_reduce.shape[1]
    classes = w_classes.shape[1]
    group = lax.axis_size("rep")
    everyone = ("rep", "dp")
    rep = lax.axis_index("rep")
    parity = rep % 2
    upper = rep // 2
    first_row = lax.axis_index("dp") * group
    own_info = geometry(lax.dynamic_slice_in_dim(layout, first_row + rep, 1, 0), pixels)
    group_info = geometry(lax.dynamic_slice_in_dim(layout, first_row, group, 0), pixels)
    living = own_info[2][0].astype(F32)[:, None]
    group_living = group_info[2].astype(F32)
    living_all = group_living.reshape(group * pixels, 1)
    pixel_count = jnp.sum(
        jnp.minimum(layout[:, 0] * layout[:, 1] * layout[:, 2], pixels)
    ).astype(F32)
    split = lax.axis_size("dp") == 8
    if split:
        side = lax.axis_index("dp") % 2
        columns = [[z_at * 2 + k for z_at in range(4)] for k in range(2)]
    zero = jnp.zeros((1,), jnp.int32)
    first = jnp.reshape(9 * parity, (1,)).astype(jnp.int32)

    (
        reduced,
        sums_one,
        hidden_one,
        spatial,
        sums_two,
        hidden_two,
        expanded,
        sums_three,
        trunk_all,
        headed,
        shifts_own,
        shifts_all,
        *trunk_afar,
    ) = trunk_forward(
        split,
        inputs,
        layout,
        w_reduce,
        w_spatial,
        w_expand,
        w_heads,
        gain_mid,
        shift_mid,
        gain_wide,
        shift_wide,
    )
    upper_is_depth = upper == 0
    depth, logits, gates_local, classes_local, head_low, head_norm, *rest = message_streams(
        split,
        layout,
        headed,
        shifts_all,
        w_messages,
        w_gates,
        w_classes,
        gain_head,
        shift_head,
        cot_depth,
        labels,
        trunk_afar,
    )
    logits = logits[:, :classes]
    classes_local = classes_local[:, :classes]
    is_depth = upper_is_depth
    if split:
        messages_local = rest[0]
    else:
        heads_all, message_all = rest
        heads_all = heads_all.reshape(4, group * pixels, middle)
        source = jnp.where(
            is_depth,
            jnp.concatenate([heads_all[1], heads_all[2], heads_all[3]], 1),
            jnp.concatenate([heads_all[0], heads_all[1], heads_all[2]], 1),
        )
        _, messages_local = rows_back(
            first, message_all.reshape(4 * pixels, middle), source, w_messages, shifts_all, 2, BF16
        )
        grad_messages = lax.psum_scatter(messages_local, "dp", scatter_dimension=1, tiled=True)
        gates_cut = gates_local.reshape(2, pixels, middle)
        gates_share = lax.dynamic_index_in_dim(gates_cut, parity, 0, keepdims=False).astype(F32)
        gates_share += swap(
            lax.dynamic_index_in_dim(gates_cut, 1 - parity, 0, keepdims=False), 1
        ).astype(F32)
    trunk_grad, *lows = heads_back(split, head_low, shifts_all, w_heads)
    if split:
        messages_local, trunk_grad = lax.optimization_barrier((messages_local, trunk_grad))
        grad_messages = lax.psum_scatter(
            messages_local, "dp", scatter_dimension=0, tiled=True, axis_index_groups=columns
        )
        dp = lax.axis_index("dp")
        beside, along = dp + 1 - 2 * side, dp + 2 - 4 * ((dp // 2) % 2)
        groups = [dp, beside, along, along + 1 - 2 * side]
        units = 9

        lower = dp % 4
        at = jnp.stack(
            [units * lower, units * (lower + 4)] + [group * k for k in groups] + [parity]
        )
        mate_x, mate_z, trunk_xz, mate_xz = rest[1:]
        trunks = [trunk_all, trunk_afar[0], mate_x, trunk_afar[1], mate_z, trunk_xz, mate_xz]
        heads_local = heads_shard(
            at.astype(jnp.int32), layout, [head_low] + lows, trunks, units, 256
        )
        heads_local, trunk_grad = lax.optimization_barrier((heads_local, trunk_grad))
        grad_heads = lax.psum_scatter(
            heads_local,
            "dp",
            scatter_dimension=0,
            tiled=False,
            axis_index_groups=[[k, k + 4] for k in range(4)],
        )
    else:
        heads_local = heads_weight(
            head_low.reshape(group * pixels, middle),
            trunk_all.reshape(group * pixels, -1),
            shifts_all,
        )
        grad_heads = lax.psum_scatter(heads_local, "dp", scatter_dimension=1, tiled=True)
    if split:
        classes_wide = jnp.pad(classes_local.astype(BF16), ((0, 0), (0, 128 - classes)))
        classes_wide = classes_wide.reshape(4, 4, -1, 128)
        classes_wide = jnp.concatenate([classes_wide[:, k] for k in range(4)], 2)
        (
            input_grad,
            norm_one,
            norm_two,
            norm_three,
            grad_reduce,
            grad_spatial,
            grad_expand,
            grad_gates,
            classes_sum,
        ) = trunk_back(
            layout,
            trunk_grad,
            expanded,
            inputs,
            reduced,
            spatial,
            [sums_one, sums_two, sums_three],
            hidden_one,
            hidden_two,
            shifts_own,
            w_reduce,
            w_spatial,
            w_expand,
            gain_mid,
            shift_mid,
            gain_wide,
            shift_wide,
            gates_local,
            classes_wide,
        )
        input_grad, grad_messages, grad_heads = lax.optimization_barrier(
            (input_grad, grad_messages, grad_heads)
        )
        grad_messages = grad_messages.T
        classes_sum = jnp.concatenate(
            [classes_sum[:, k * 128 : (k + 1) * 128] for k in range(4)], 0
        )
        grad_classes = classes_sum[:, :classes]
        grad_gain_mid = jnp.stack([norm_one[0], norm_two[0]], 0)
        grad_shift_mid = jnp.stack([norm_one[1], norm_two[1]], 0)
        grad_gain_wide, grad_shift_wide = norm_three[0], norm_three[1]
    else:
        normed_one, unit_one, scale_one = normalize(
            reduced, sums_one[0], sums_one[1], pixel_count, gain_mid[0], shift_mid[0]
        )
        normed_two, unit_two, scale_two = normalize(
            spatial, sums_two[0], sums_two[1], pixel_count, gain_mid[1], shift_mid[1]
        )
        normed_three, unit_three, scale_three = normalize(
            expanded, sums_three[0], sums_three[1], pixel_count, gain_wide, shift_wide
        )
        pre_act = normed_three + inputs.astype(F32)
        pre_grad = trunk_grad.astype(F32) * silu_slope(pre_act)
        expand_raw, grad_gain_wide, grad_shift_wide = norm_back(
            pre_grad, unit_three, scale_three, gain_wide, living, pixel_count, everyone
        )
        expand_low = expand_raw.astype(BF16)
        expand_local = inner_rows(hidden_two, expand_low).astype(BF16)
        hidden_two_grad = against(expand_low, w_expand)
        spatial_raw, gain_grad_two, shift_grad_two = norm_back(
            hidden_two_grad * silu_slope(normed_two),
            unit_two,
            scale_two,
            gain_mid[1],
            living,
            pixel_count,
            everyone,
        )
        spatial_low = spatial_raw.astype(BF16)
        hidden_one_grad, spatial_local = rows_back(
            zero, spatial_low, hidden_one, w_spatial, shifts_own[:, None], 1, F32
        )
        reduced_raw, gain_grad_one, shift_grad_one = norm_back(
            hidden_one_grad * silu_slope(normed_one),
            unit_one,
            scale_one,
            gain_mid[0],
            living,
            pixel_count,
            everyone,
        )
        reduced_low = reduced_raw.astype(BF16)
        reduce_local = inner_rows(inputs, reduced_low).astype(BF16)
        input_grad = pre_grad + against(reduced_low, w_reduce)
        grad_expand = scatter_rep(expand_local)
        grad_spatial = scatter_rep(spatial_local)
        grad_reduce = scatter_rep(reduce_local)
        grad_classes = scatter_rep(classes_local)
        pieces = [
            gates_share.astype(BF16),
            grad_expand.reshape(-1, middle),
            grad_spatial,
            grad_classes.reshape(-1, middle),
        ]
        early = total_dp(jnp.concatenate(pieces, 0))
        rows = [piece.shape[0] for piece in pieces]
        starts = [sum(rows[:k]) for k in range(4)]
        grad_gates, expand_sum, grad_spatial, classes_sum = [
            early[at : at + size] for at, size in zip(starts, rows)
        ]
        grad_expand = expand_sum.reshape(grad_expand.shape)
        grad_classes = classes_sum.reshape(grad_classes.shape)
        grad_reduce = total_dp(grad_reduce)
        grad_gain_mid = jnp.stack([gain_grad_one, gain_grad_two], 0)
        grad_shift_mid = jnp.stack([shift_grad_one, shift_grad_two], 0)
    head_norms = lax.all_gather(
        head_norm, "rep", axis=1, tiled=True
    )
    return (
        depth,
        logits,
        input_grad,
        grad_reduce,
        grad_spatial,
        grad_expand,
        grad_heads.astype(F32),
        grad_gates,
        grad_messages.astype(F32),
        grad_classes,
        grad_gain_mid,
        grad_shift_mid,
        grad_gain_wide,
        grad_shift_wide,
        head_norms[0],
        head_norms[1],
    )


def solution(mesh):
    in_specs = (
        P(("dp", "rep"), None),
        P(),
        P(("dp", "rep")),
        P(("dp", "rep"), None),
        P(),
        P(),
        P(),
        P("rep", None),
        P(),
        P("rep", None),
        P(),
        P(),
        P(),
        P(),
        P(),
        P(),
        P(),
    )
    out_specs = (
        P(("dp", "rep"), None),
        P(("dp", "rep"), None),
        P(("dp", "rep"), None),
        P("rep", None),
        P("rep", None),
        P("rep", None),
        P("rep", "dp"),
        P("rep", None),
        P("rep", "dp"),
        P("rep", None),
        P(),
        P(),
        P(),
        P(),
        P(),
        P(),
    )
    return jax.shard_map(shards, mesh=mesh, in_specs=in_specs, out_specs=out_specs, check_vma=False)
```

```python
import functools

import jax
import jax.numpy as jnp
from jax import lax
from jax.experimental import pallas as pl
from jax.experimental.pallas import tpu as pltpu
from jax.sharding import PartitionSpec as P

EPS = 1e-05
F32 = jnp.float32
BF16 = jnp.bfloat16
VMEM_LIMIT = 60 * 2**20


def geometry(layout, span):
    position = jnp.arange(span, dtype=jnp.int32)
    height = layout[:, 0:1]
    map_width = layout[:, 1:2]
    images = layout[:, 2:3]
    map_area = height * map_width
    inside = position[None, :] % map_area
    row_of = inside // map_width
    col_of = inside % map_width
    living = position[None, :] < images * map_area
    return (row_of, col_of, living, height, map_width)


def neighbours(shape_info, dilation):
    row_of, col_of, living, height, map_width = shape_info
    span = row_of.shape[1]
    position = jnp.arange(span, dtype=jnp.int32)
    every = []
    for step_row in (-1, 0, 1):
        for step_col in (-1, 0, 1):
            target_row = row_of + dilation * step_row
            target_col = col_of + dilation * step_col
            inside = (
                living
                & (target_row >= 0)
                & (target_row < height)
                & (target_col >= 0)
                & (target_col < map_width)
            )
            neighbour = position[None, :] + dilation * (step_row * map_width + step_col)
            every.append(jnp.where(inside, neighbour, -1))
    return jnp.concatenate(every, 0).T


def shift_matrices(shape_info, dilation):
    devices, span = shape_info[0].shape
    picks = neighbours(shape_info, dilation).T.reshape(9, devices, span, 1)
    return (picks == jnp.arange(span, dtype=jnp.int32)).astype(BF16)


def product(left_side, right_side):
    return jnp.dot(left_side, right_side, preferred_element_type=F32)


def inner_rows(left_side, right_side):
    return lax.dot_general(
        left_side, right_side, (((0,), (0,)), ((), ())), preferred_element_type=F32
    )


def against(left_side, right_side):
    return lax.dot_general(
        left_side, right_side, (((1,), (1,)), ((), ())), preferred_element_type=F32
    )


def params():
    return pltpu.CompilerParams(vmem_limit_bytes=VMEM_LIMIT)


def cost(flops, moved):
    return pl.CostEstimate(flops=flops, bytes_accessed=moved, transcendentals=0)


def shifted(g_ref, s_ref):
    blocks, span = s_ref.shape[1], s_ref.shape[2]
    return jnp.concatenate(
        [
            inner_rows(s_ref[0, k], g_ref[pl.ds(k * span, span), :]).astype(BF16)
            for k in range(blocks)
        ],
        0,
    )


def heads_weight_kernel(g_ref, u_ref, s_ref, out_ref):
    taken = shifted(g_ref, s_ref)
    step = 512
    for c in range(0, u_ref.shape[1], step):
        out_ref[:, c : c + step] = inner_rows(taken, u_ref[:, c : c + step]).astype(out_ref.dtype)


def heads_weight(g, u, shifts):
    rows, outs = g.shape
    wide = u.shape[1]
    taps, blocks, span, _ = shifts.shape
    return pl.pallas_call(
        heads_weight_kernel,
        grid=(taps,),
        in_specs=[
            pl.BlockSpec((rows, outs), lambda t: (0, 0)),
            pl.BlockSpec((rows, wide), lambda t: (0, 0)),
            pl.BlockSpec((1, blocks, span, span), lambda t: (t, 0, 0, 0)),
        ],
        out_specs=pl.BlockSpec((outs, wide), lambda t: (0, t)),
        out_shape=jax.ShapeDtypeStruct((outs, taps * wide), BF16),
        compiler_params=params(),
        cost_estimate=cost(2 * rows * wide * outs * taps, outs * taps * wide * 2),
        name="heads_weight",
    )(g, u, shifts)


def rows_back_kernel(halves, first_ref, g_ref, u_ref, w_ref, s_ref, du_ref, dw_ref, total):
    step = pl.program_id(0)
    taken = shifted(g_ref, s_ref)
    depth = w_ref.shape[0]
    which = (step + first_ref[0]) % halves

    @pl.when(step == 0)
    def _():
        total[...] = jnp.zeros_like(total)

    total[which] += against(taken, w_ref[...])
    dw_ref[...] = inner_rows(u_ref[...], taken).astype(dw_ref.dtype)

    @pl.when(step == pl.num_programs(0) - 1)
    def _():
        for k in range(halves):
            du_ref[:, k * depth : (k + 1) * depth] = total[k].astype(du_ref.dtype)


def rows_back(first, g, u, w, shifts, halves, kind):
    rows, outs = g.shape
    depth = u.shape[1] // halves
    steps = w.shape[0] // depth
    taps, blocks, span, _ = shifts.shape
    return pl.pallas_call(
        functools.partial(rows_back_kernel, halves),
        grid_spec=pltpu.PrefetchScalarGridSpec(
            num_scalar_prefetch=1,
            grid=(steps,),
            in_specs=[
                pl.BlockSpec((rows, outs), lambda b, f: (0, 0)),
                pl.BlockSpec((rows, depth), lambda b, f: (0, (b + f[0]) % halves)),
                pl.BlockSpec((depth, outs), lambda b, f: (b, 0)),
                pl.BlockSpec((1, blocks, span, span), lambda b, f: ((b + f[0]) // halves, 0, 0, 0)),
            ],
            out_specs=[
                pl.BlockSpec((rows, halves * depth), lambda b, f: (0, 0)),
                pl.BlockSpec((depth, outs), lambda b, f: (b, 0)),
            ],
            scratch_shapes=[pltpu.VMEM((halves, rows, depth), F32)],
        ),
        out_shape=[
            jax.ShapeDtypeStruct((rows, halves * depth), kind),
            jax.ShapeDtypeStruct(w.shape, BF16),
        ],
        compiler_params=params(),
        cost_estimate=cost(4 * rows * w.size, w.size * 4),
        name="rows_back",
    )(first, g, u, w, shifts)


def send_to(axis, to, src, dst, send_sem, recv_sem):
    return pltpu.make_async_remote_copy(
        src_ref=src,
        dst_ref=dst,
        send_sem=send_sem,
        recv_sem=recv_sem,
        device_id={axis: to},
        device_id_type=MESH,
    )


def total_along(axis, size, block, slots, send_sems, recv_sems, meanwhile=None):
    me = lax.axis_index(axis)
    others = [lax.rem(me + k, size) for k in range(1, size)]
    for other in others:
        send_to(axis, other, block, slots.at[me], send_sems.at[other], recv_sems.at[me]).start()
    slots[me] = block[...]
    if meanwhile is not None:
        meanwhile()
    for other in others:
        copy = send_to(
            axis, other, block, slots.at[other], send_sems.at[other], recv_sems.at[other]
        )
        copy.wait_recv()
        copy.wait_send()
    total = slots[0]
    for k in range(1, size):
        total = total + slots[k]
    return total


def place_in_map(layout_ref, device, span):
    position = lax.broadcasted_iota(jnp.int32, (span, 1), 0)
    large = layout_ref[device, 1] == 16
    row_of = jnp.where(large, position // 16, (position % 64) // 8)
    col_of = jnp.where(large, position % 16, position % 8)
    return position, row_of, col_of


def live_mask(layout_ref, device, span):
    position = lax.broadcasted_iota(jnp.int32, (span, 1), 0)
    return position < layout_ref[device, 0] * layout_ref[device, 1] * layout_ref[device, 2]


def live_column(layout_ref, device, span):
    return jnp.where(live_mask(layout_ref, device, span), 1.0, 0.0)


def inverse_count(areas_ref, span):
    areas = areas_ref[:, 0:1] * areas_ref[:, 1:2] * areas_ref[:, 2:3]
    return 1.0 / jnp.sum(jnp.minimum(areas, span).astype(F32), 0, keepdims=True)


def shift_block(layout_ref, device, dilation, tap, span):
    position, row_of, col_of = place_in_map(layout_ref, device, span)
    height, map_width = layout_ref[device, 0], layout_ref[device, 1]
    step_row, step_col = dilation * (tap // 3 - 1), dilation * (tap % 3 - 1)
    target_row, target_col = row_of + step_row, col_of + step_col
    inside = (
        live_mask(layout_ref, device, span)
        & (target_row >= 0)
        & (target_row < height)
        & (target_col >= 0)
        & (target_col < map_width)
    )
    neighbour = jnp.where(inside, position + step_row * map_width + step_col, -1)
    lanes = lax.broadcasted_iota(jnp.int32, (span, span), 1)
    return jnp.where(neighbour == lanes, 1.0, 0.0).astype(BF16)


def shift_in_maps(extent, tap, span, dilation=1):
    position = lax.broadcasted_iota(jnp.int32, (span, 1), 0)
    row_of, col_of = (position % (extent * extent)) // extent, position % extent
    step_row, step_col = dilation * (tap // 3 - 1), dilation * (tap % 3 - 1)
    target_row, target_col = row_of + step_row, col_of + step_col
    inside = (
        (target_row >= 0) & (target_row < extent) & (target_col >= 0) & (target_col < extent)
    )
    neighbour = jnp.where(inside, position + step_row * extent + step_col, -1)
    lanes = lax.broadcasted_iota(jnp.int32, (span, span), 1)
    return jnp.where(neighbour == lanes, 1.0, 0.0).astype(BF16)


def trunk_kernel(
    split,
    sizes,
    in_ref,
    layout_ref,
    areas_ref,
    w_reduce_ref,
    w_spatial_hbm,
    w_expand_hbm,
    w_heads_hbm,
    gain_mid_ref,
    shift_mid_ref,
    gain_wide_ref,
    shift_wide_ref,
    reduced_ref,
    sums_one_ref,
    hidden_one_ref,
    spatial_ref,
    sums_two_ref,
    hidden_two_ref,
    expanded_ref,
    sums_three_ref,
    trunk_ref,
    headed_ref,
    own_shift_ref,
    all_shift_ref,
    *rest,
):
    if split:
        trunk_x, trunk_z, *rest = rest
    trunk_rest(
        split,
        sizes,
        in_ref,
        layout_ref,
        areas_ref,
        w_reduce_ref,
        w_spatial_hbm,
        w_expand_hbm,
        w_heads_hbm,
        gain_mid_ref,
        shift_mid_ref,
        gain_wide_ref,
        shift_wide_ref,
        reduced_ref,
        sums_one_ref,
        hidden_one_ref,
        spatial_ref,
        sums_two_ref,
        hidden_two_ref,
        expanded_ref,
        sums_three_ref,
        trunk_ref,
        headed_ref,
        own_shift_ref,
        all_shift_ref,
        (trunk_x, trunk_z) if split else (),
        *rest,
    )


def trunk_rest(
    split,
    sizes,
    in_ref,
    layout_ref,
    areas_ref,
    w_reduce_ref,
    w_spatial_hbm,
    w_expand_hbm,
    w_heads_hbm,
    gain_mid_ref,
    shift_mid_ref,
    gain_wide_ref,
    shift_wide_ref,
    reduced_ref,
    sums_one_ref,
    hidden_one_ref,
    spatial_ref,
    sums_two_ref,
    hidden_two_ref,
    expanded_ref,
    sums_three_ref,
    trunk_ref,
    headed_ref,
    own_shift_ref,
    all_shift_ref,
    afar,
    w_spatial_ref,
    w_expand_ref,
    w_heads_ref,
    block_mid,
    block_wide,
    slots_mid_rep,
    slots_mid_dp,
    slots_wide_rep,
    slots_wide_dp,
    load_sems,
    rep_send,
    rep_recv,
    dp_send,
    dp_recv,
    gather_send,
    gather_recv,
    away_send,
    away_recv,
):
    n_rep, n_dp = sizes
    rep = lax.axis_index("rep")
    par, upper = lax.rem(rep, 2), rep // 2
    mate, far = rep + 1 - 2 * par, rep + 2 - 4 * upper
    span, wide = in_ref.shape
    middle = w_reduce_ref.shape[1]
    taps = own_shift_ref.shape[0]
    loads = [
        pltpu.make_async_copy(w_spatial_hbm, w_spatial_ref, load_sems.at[0]),
        pltpu.make_async_copy(w_expand_hbm, w_expand_ref, load_sems.at[1]),
    ]
    heads_load = pltpu.make_async_copy(w_heads_hbm, w_heads_ref, load_sems.at[2])
    for load in loads:
        load.start()
    heads_load.start()

    barrier = pltpu.get_barrier_semaphore()
    for axis, size in (("rep", n_rep), ("dp", n_dp)):
        me = lax.axis_index(axis)
        for k in range(1, size):
            pl.semaphore_signal(
                barrier, inc=1, device_id={axis: lax.rem(me + k, size)}, device_id_type=MESH
            )
    first_row = lax.axis_index("dp") * n_rep
    live = live_column(layout_ref, first_row + rep, span)
    inverse = inverse_count(areas_ref, span)

    def make_own():
        for t in range(taps):
            own_shift_ref[t] = shift_block(layout_ref, first_row + rep, 2, t, span)

    def make_all(first, last):
        def fill():
            for t in range(first, last):
                for p in range(n_rep):
                    all_shift_ref[t, p] = shift_block(layout_ref, first_row + p, 1, t, span)

        return fill

    def everywhere(number, value_ref, blocks, rep_slots, dp_slots, meanwhile, later):
        masked = live * value_ref[...]
        blocks[0, 0:1, :] = jnp.sum(masked, 0, keepdims=True)
        blocks[0, 1:2, :] = jnp.sum(masked * value_ref[...], 0, keepdims=True)
        if number == 0:
            pl.semaphore_wait(barrier, n_rep + n_dp - 2)
        blocks[1] = total_along(
            "rep", n_rep, blocks.at[0], rep_slots, rep_send.at[number], rep_recv.at[number], meanwhile
        )
        return total_along(
            "dp", n_dp, blocks.at[1], dp_slots, dp_send.at[number], dp_recv.at[number], later
        )

    def normed(value, sums, gain, shift):
        center = sums[0:1] * inverse
        scaling = lax.rsqrt(sums[1:2] * inverse - center * center + EPS)
        return (value - center) * (scaling * gain) + shift

    def silu(value):
        return value * jax.nn.sigmoid(value)

    reduced_ref[...] = product(in_ref[...], w_reduce_ref[...])
    sums = everywhere(
        0, reduced_ref, block_mid.at[0], slots_mid_rep.at[0], slots_mid_dp.at[0], make_own, None
    )
    sums_one_ref[...] = sums
    hidden_one_ref[...] = silu(
        normed(reduced_ref[...], sums, gain_mid_ref[0:1, :], shift_mid_ref[0:1, :])
    ).astype(BF16)
    loads[0].wait()
    spatial_ref[...] = jnp.zeros_like(spatial_ref)

    @pl.loop(0, taps)
    def _(t):
        moved = product(own_shift_ref[t], hidden_one_ref[...]).astype(BF16)
        at = pl.ds(pl.multiple_of(t * middle, middle), middle)
        spatial_ref[...] += product(moved, w_spatial_ref[at, :])

    sums = everywhere(
        1, spatial_ref, block_mid.at[1], slots_mid_rep.at[1], slots_mid_dp.at[1], make_all(0, 5), None
    )
    sums_two_ref[...] = sums
    hidden_two_ref[...] = silu(
        normed(spatial_ref[...], sums, gain_mid_ref[1:2, :], shift_mid_ref[1:2, :])
    ).astype(BF16)
    loads[1].wait()
    expanded_ref[...] = product(hidden_two_ref[...], w_expand_ref[...])
    sums = everywhere(
        2, expanded_ref, block_wide, slots_wide_rep, slots_wide_dp, make_all(5, 9), None
    )
    sums_three_ref[...] = sums

    own_rows = pl.ds(pl.multiple_of(par * span, span), span)
    mate_rows = pl.ds(pl.multiple_of((1 - par) * span, span), span)
    pre = normed(expanded_ref[...], sums, gain_wide_ref[...], shift_wide_ref[...])
    trunk_ref[upper, own_rows, :] = silu(pre + in_ref[...].astype(F32)).astype(BF16)
    parts = 4
    piece = span // parts

    def rows(parity, k):
        return pl.ds(pl.multiple_of(parity * span + k * piece, piece), piece)

    def across(side, k):
        at = trunk_ref.at[side, rows(par, k)]
        return send_to("rep", far, at, at, gather_send.at[k], gather_recv.at[k])

    def own_pass(parity):
        at = trunk_ref.at[upper, pl.ds(pl.multiple_of(parity * span, span), span)]
        return send_to("rep", mate, at, at, gather_send.at[parts], gather_recv.at[parts])

    def far_pass(parity, k):
        at = trunk_ref.at[1 - upper, rows(parity, k)]
        slot = parts + 1 + k
        return send_to("rep", mate, at, at, gather_send.at[slot], gather_recv.at[slot])

    dp = lax.axis_index("dp")
    neighbours = (dp + 1 - 2 * lax.rem(dp, 2), dp + 2 - 4 * lax.rem(dp // 2, 2))

    def away(number):
        return send_to(
            "dp",
            neighbours[number],
            trunk_ref.at[upper, own_rows],
            afar[number],
            away_send.at[number],
            away_recv.at[number],
        )

    for k in range(parts):
        across(upper, k).start()
    own_pass(par).start()
    if split:
        for number in range(2):
            away(number).start()
    headed_ref[...] = jnp.zeros_like(headed_ref)
    own_pass(1 - par).wait_recv()
    heads_load.wait()

    def convolve(side):
        @pl.loop(0, taps)
        def _(t):
            at = pl.ds(pl.multiple_of(t * wide, wide), wide)
            y = against(trunk_ref[side], w_heads_ref[:, at]).astype(BF16)
            for k in range(2):
                place = pl.ds(k * span, span)
                headed_ref[side, place, :] += product(
                    all_shift_ref[t, 2 * side + k], y[k * span : (k + 1) * span]
                )

    convolve(upper)
    for k in range(parts):
        across(1 - upper, k).wait_recv()
        far_pass(par, k).start()
    for k in range(parts):
        far_pass(1 - par, k).wait_recv()
    convolve(1 - upper)
    for k in range(parts):
        across(upper, k).wait_send()
        far_pass(par, k).wait_send()
    own_pass(par).wait_send()
    if split:
        for number in range(2):
            away(number).wait_send()
            away(number).wait_recv()


def trunk_forward(
    split,
    inputs,
    layout,
    w_reduce,
    w_spatial,
    w_expand,
    w_heads,
    gain_mid,
    shift_mid,
    gain_wide,
    shift_wide,
):
    span, wide = inputs.shape
    middle = w_reduce.shape[1]
    n_rep, n_dp = lax.axis_size("rep"), lax.axis_size("dp")
    taps = 9
    vmem = pl.BlockSpec(memory_space=pltpu.VMEM)
    hbm = pl.BlockSpec(memory_space=pl.ANY)
    smem = pl.BlockSpec(memory_space=pltpu.SMEM)
    dma = pltpu.SemaphoreType.DMA
    shape = jax.ShapeDtypeStruct
    return pl.pallas_call(
        functools.partial(trunk_kernel, split, (n_rep, n_dp)),
        in_specs=[vmem, smem, vmem, vmem] + [hbm] * 3 + [vmem] * 4,
        out_specs=[vmem] * 12 + [hbm] * (2 * split),
        out_shape=[
            shape((span, middle), F32),
            shape((2, middle), F32),
            shape((span, middle), BF16),
            shape((span, middle), F32),
            shape((2, middle), F32),
            shape((span, middle), BF16),
            shape((span, wide), F32),
            shape((2, wide), F32),
            shape((2, 2 * span, wide), BF16),
            shape((2, 2 * span, w_heads.shape[0]), F32),
            shape((taps, span, span), BF16),
            shape((taps, n_rep, span, span), BF16),
        ]
        + [shape((span, wide), BF16)] * (2 * split),
        scratch_shapes=[
            pltpu.VMEM(w_spatial.shape, BF16),
            pltpu.VMEM(w_expand.shape, BF16),
            pltpu.VMEM(w_heads.shape, BF16),
            pltpu.VMEM((2, 2, 2, middle), F32),
            pltpu.VMEM((2, 2, wide), F32),
            pltpu.VMEM((2, n_rep, 2, middle), F32),
            pltpu.VMEM((2, n_dp, 2, middle), F32),
            pltpu.VMEM((n_rep, 2, wide), F32),
            pltpu.VMEM((n_dp, 2, wide), F32),
            dma((3,)),
            dma((3, n_rep)),
            dma((3, n_rep)),
            dma((3, n_dp)),
            dma((3, n_dp)),
            dma((9,)),
            dma((9,)),
            dma((2,)),
            dma((2,)),
        ],
        compiler_params=pltpu.CompilerParams(
            collective_id=10, has_side_effects=True, vmem_limit_bytes=VMEM_LIMIT
        ),
        name="trunk_forward",
    )(
        inputs,
        layout,
        layout,
        w_reduce,
        w_spatial,
        w_expand,
        w_heads,
        gain_mid,
        shift_mid,
        gain_wide[None, :],
        shift_wide[None, :],
    )


MOVES = 38


def message_kernel(split, n_dp, classes, *refs):
    refs = list(refs)

    def take(count):
        taken, refs[:count] = refs[:count], []
        return taken

    layout_ref, areas_ref, headed_ref, s_ref, w_hbm, gates_w_ref, classes_w_ref = take(7)
    gain_ref, shift_ref, cot_ref, labels_ref = take(4)
    if split:
        trunk_x, trunk_z, trunk_hbm = take(3)
    depth_ref, logits_ref, gates_ref, classes_ref, low_ref, norm_ref = take(6)
    if split:
        out_ref, far_x, far_z, mate_x, mate_z, trunk_xz, mate_xz = take(7)
    else:
        heads_ref, gm_ref = take(2)
    w_ref, live_ref, acc_ref, acc_in, stream_ref, direct_ref, cot_in, labels_in = take(8)
    depth_out, logits_out, picked_ref, far_ref, near_ref = take(5)
    core_out, core_in, far_out, far_in, near_out, near_in = take(6)
    sums_ref, slots_ref, load_sem, send, recv, dp_send, dp_recv = take(7)
    if split:
        heads_ref, gm_ref, beside_ref, cut_own, cut_out, cut_in, cut_taken = take(7)

    rep = lax.axis_index("rep")
    par, upper = lax.rem(rep, 2), rep // 2
    mate, far = rep + 1 - 2 * par, rep + 2 - 4 * upper
    first_row = lax.axis_index("dp") * 4
    side_x = lax.rem(lax.axis_index("dp"), 2)
    beside = lax.axis_index("dp") + 1 - 2 * side_x
    side_z = lax.rem(lax.axis_index("dp") // 2, 2)
    along = lax.axis_index("dp") + 2 - 4 * side_z
    span = s_ref.shape[2]
    middle = headed_ref.shape[2]
    small = middle // 2
    load = pltpu.make_async_copy(w_hbm, w_ref, load_sem)
    load.start()

    barrier = pltpu.get_barrier_semaphore()
    me_dp = lax.axis_index("dp")
    for to in (mate, far):
        pl.semaphore_signal(barrier, inc=1, device_id={"rep": to}, device_id_type=MESH)
    for k in range(1, n_dp):
        pl.semaphore_signal(
            barrier, inc=1, device_id={"dp": lax.rem(me_dp + k, n_dp)}, device_id_type=MESH
        )

    def move(number, src, dst, to, axis="rep"):
        return send_to(axis, to, src, dst, send.at[number], recv.at[number])

    def block(parity):
        return pl.ds(pl.multiple_of(parity * span, span), span)

    for p in range(4):
        live_ref[p // 2, (p % 2) * span : (p % 2 + 1) * span, :] = live_column(
            layout_ref, first_row + p, span
        )
    inverse = inverse_count(areas_ref, span)

    def add_up(number, left, right):
        sums_ref[number, 0:1, :] = left
        sums_ref[number, 1:2, :] = right
        return total_along(
            "dp", n_dp, sums_ref.at[number], slots_ref.at[number], dp_send.at[number], dp_recv.at[number]
        )

    def column_sum(value):
        return jnp.sum(value, 0, keepdims=True)

    left, right = 0.0, 0.0
    for side in range(2):
        masked = live_ref[side] * headed_ref[side]
        left = left + column_sum(masked)
        right = right + column_sum(masked * headed_ref[side])
    pl.semaphore_wait(barrier, n_dp + 1)
    move(9, cot_ref, cot_in, far).start()
    move(10, labels_ref, labels_in, far).start()
    sums = add_up(0, left, right)
    if split:
        lower_side = 1 - upper
        own_block = trunk_hbm.at[lower_side, block(par)]
        copy_x = move(29, trunk_x, far_x, far)
        copy_z = move(30, own_block, far_z, along, "dp")
        near_xz = move(31, trunk_x, trunk_xz.at[upper], along, "dp")
        far_xz = move(32, far_x, trunk_xz.at[lower_side], along, "dp")
        to_mate = [
            move(33, trunk_x, mate_x.at[upper], mate),
            move(34, trunk_z, mate_z.at[upper], mate),
            move(35, far_x, mate_x.at[lower_side], mate),
            move(36, far_z, mate_z.at[lower_side], mate),
            move(37, trunk_xz, mate_xz, mate),
        ]
        near_xz.start()
        copy_z.start()

    center = sums[0:1] * inverse
    scaling = lax.rsqrt(sums[1:2] * inverse - center * center + EPS)
    own_lanes = pl.ds(pl.multiple_of(rep * middle, middle), middle)
    gain = gain_ref[:, own_lanes]
    shift = shift_ref[:, own_lanes]

    def across(head, part):
        at = heads_ref.at[head, part // 2, pl.ds((part % 2) * span, span)]
        return move(part, at, at, far)

    def relay(head, part):
        at = heads_ref.at[head, part // 2, pl.ds((part % 2) * span, span)]
        return move(5 + part, at, at, mate)

    def own_head(head):
        return move(4, heads_ref.at[head], heads_ref.at[head], mate)

    for side in range(2):
        normed = (headed_ref[side] - center) * (scaling * gain) + shift
        heads_ref[rep, side] = (normed * jax.nn.sigmoid(normed)).astype(BF16)
        for k in range(2):
            across(rep, 2 * side + k).start()
    own_head(rep).start()
    if split:
        x_own = move(24, heads_ref.at[rep], beside_ref.at[rep], beside, "dp")
        x_far = move(25, heads_ref.at[far], beside_ref.at[far], beside, "dp")
        x_own.start()
        copy_x.start()

    def tap_of(i):
        return par * 5 + i

    def row_of(i, head_at):
        return pl.multiple_of(par * (3 * small) + i * (3 * middle) + head_at * middle, small)

    half_row = (1 - par) * (12 * middle)
    full_row = pl.multiple_of(half_row + par * small, small)
    part_row = pl.multiple_of(half_row + (1 - par) * middle, small)
    part_lanes = pl.ds(pl.multiple_of(par * small, small), small)
    local = 2 * upper
    remote = 2 * (1 - upper)
    local_head = 1 + upper
    part_head = 2 - upper
    full_head = 2 * par + 1 - upper

    def wrows(row, depth):
        return w_ref[pl.ds(row, depth), :]

    def gather_taps(tap, side, y):
        y = y.astype(BF16)
        for k in range(2):
            acc_ref[side, k * span : (k + 1) * span, :] += product(
                s_ref[tap, 2 * side + k], y[k * span : (k + 1) * span]
            )

    acc_ref[...] = jnp.zeros_like(acc_ref)
    own_head(mate).wait_recv()
    load.wait()

    @pl.loop(0, 8)
    def _(n):
        i, side = n // 2, n % 2
        gather_taps(
            tap_of(i), side, product(heads_ref[local_head, side], wrows(row_of(i, local), middle))
        )

    @pl.when(par == upper)
    def _():
        @pl.loop(0, 2)
        def _(side):
            gather_taps(4, side, product(heads_ref[full_head, side], wrows(full_row, middle)))

    for part in range(4):
        across(far, part).wait_recv()
        relay(far, part).start()
    if split:
        x_far.start()
    for part in range(4):
        relay(far + 1 - 2 * par, part).wait_recv()

    @pl.loop(0, 8)
    def _(n):
        i, side = n // 2, n % 2
        y = product(heads_ref[remote, side], wrows(row_of(i, 1 - upper), middle))
        y = y + product(heads_ref[remote + 1, side], wrows(row_of(i, 2 - upper), middle))
        gather_taps(tap_of(i), side, y)

    @pl.loop(0, 2)
    def _(side):
        gather_taps(
            4, side, product(heads_ref[part_head, side, :, part_lanes], wrows(part_row, small))
        )

    @pl.when(par != upper)
    def _():
        @pl.loop(0, 2)
        def _(side):
            gather_taps(4, side, product(heads_ref[full_head, side], wrows(full_row, middle)))

    def acc_move(side):
        return move(11 + side, acc_ref.at[side, block(1 - par)], acc_in.at[side], mate)

    for side in range(2):
        acc_move(side).start()

    own_gates = gates_w_ref[pl.ds(pl.multiple_of(upper * middle, middle), middle), :]
    classes_ref[...] = jnp.zeros_like(classes_ref)
    move(9, cot_ref, cot_in, far).wait_recv()
    move(10, labels_ref, labels_in, far).wait_recv()
    gates_total = 0.0

    def gm_move(side, parity):
        at = gm_ref.at[side, block(parity)]
        return move(13 + side, at, at, mate)

    for side in range(2):
        acc_move(side).wait_recv()
        message = acc_ref[side, block(par), :] + acc_in[side]
        stream = heads_ref[3 * upper, side, block(par), :]
        gate = jax.nn.sigmoid(product(stream, own_gates))
        full = stream.astype(F32) + gate * message
        alive = live_ref[side, block(par), :]

        @pl.when(upper == 0)
        def _():
            cot = (cot_ref if side == 0 else cot_in)[...].astype(F32)
            stream_ref[side] = alive * cot
            (depth_ref if side == 0 else depth_out)[...] = alive * full

        @pl.when(upper == 1)
        def _():
            labels = (labels_in if side == 0 else labels_ref)[...]
            full_low = full.astype(BF16)
            logits = product(full_low, classes_w_ref[...])
            (logits_out if side == 0 else logits_ref)[...] = alive * logits
            lanes = lax.broadcasted_iota(jnp.int32, logits.shape, 1)
            shown = jnp.where(lanes < classes, logits, -1e30)
            grown = jnp.exp(shown - jnp.max(shown, 1, keepdims=True))
            probs = grown / jnp.sum(grown, 1, keepdims=True)
            slope = (alive * (probs - jnp.where(lanes == labels, 1.0, 0.0))).astype(BF16)
            classes_ref[...] += inner_rows(full_low, slope)
            stream_ref[side] = against(slope, classes_w_ref[...])

        grad = stream_ref[side]
        grad_gate = (grad * message * gate * (1.0 - gate)).astype(BF16)
        gm_ref[side, block(par), :] = (grad * gate).astype(BF16)
        gm_move(side, par).start()
        gates_total = gates_total + inner_rows(stream, grad_gate)
        direct_ref[side] = grad + against(grad_gate, own_gates)

    gates_ref[...] = gates_total.astype(BF16)

    @pl.when(upper == 0)
    def _():
        move(15, depth_out, depth_ref, far).start()

    @pl.when(upper == 1)
    def _():
        move(16, logits_out, logits_ref, far).start()

    for side in range(2):
        gm_move(side, 1 - par).wait_recv()
    if split:
        lanes = lax.broadcasted_iota(jnp.int32, (middle, small), 1)
        wanted = (lanes // 64) * 128 + lanes % 64
        source = lax.broadcasted_iota(jnp.int32, (middle, small), 0)
        for cut, which in ((cut_out, 1 - side_x), (cut_own, side_x)):
            pick = jnp.where(source == wanted + 64 * which, 1.0, 0.0).astype(BF16)
            for side in range(2):
                cut[side] = product(gm_ref[side], pick).astype(BF16)
        x_cut = move(28, cut_out, cut_in, beside, "dp")
        x_cut.start()

    @pl.loop(0, 10)
    def _(n):
        i, side = n // 2, n % 2
        tap = jnp.where(i == 4, 4, tap_of(i))
        for k in range(2):
            at = pl.ds(k * span, span)
            picked_ref[i, side, at, :] = inner_rows(
                s_ref[tap, 2 * side + k], gm_ref[side, at, :]
            ).astype(BF16)

    def taps_back(side, head_at):
        total = 0.0
        for i in range(4):
            total = total + against(picked_ref[i, side], wrows(row_of(i, head_at), middle))
        return total

    def core_move(side):
        return move(17 + side, core_out.at[side], core_in.at[side], mate)

    def far_move(part):
        at = pl.ds((part % 2) * span, span)
        return move(19 + part, far_out.at[part // 2, at], far_in.at[part // 2, at], far)

    @pl.loop(0, 2)
    def _(side):
        @pl.loop(0, 2)
        def _(j):
            far_ref[j, side] = taps_back(side, 1 - upper + j)

        far_ref[upper, side, :, part_lanes] += against(picked_ref[4, side], wrows(part_row, small))

        @pl.when(par != upper)
        def _():
            far_ref[2 * par - 1 + upper, side] += against(
                picked_ref[4, side], wrows(full_row, middle)
            )

        core_out[side] = far_ref[1 - par, side].astype(BF16)
        core_move(side).start()

    for side in range(2):
        core_move(side).wait_recv()
        for part in (2 * side, 2 * side + 1):
            at = pl.ds((part % 2) * span, span)
            far_out[side, at, :] = (
                far_ref[par, side, at, :] + core_in[side, at, :].astype(F32)
            ).astype(BF16)
            far_move(part).start()

    if split:
        copy_x.wait_recv()
        far_xz.start()

    @pl.loop(0, 2)
    def _(side):
        near_ref[side] = taps_back(side, local)

    @pl.when(par == upper)
    def _():
        @pl.loop(0, 2)
        def _(side):
            near_ref[side] += against(picked_ref[4, side], wrows(full_row, middle))

        near_out[...] = near_ref[...].astype(BF16)
        for side in range(2):
            near_ref[side, block(par), :] = direct_ref[side]
            near_ref[side, block(1 - par), :] = jnp.zeros((span, middle), F32)

    @pl.when(par != upper)
    def _():
        for side in range(2):
            near_out[side, block(par), :] = direct_ref[side].astype(BF16)
            near_out[side, block(1 - par), :] = jnp.zeros((span, middle), BF16)

    near_move = move(23, near_out, near_in, mate)
    near_move.start()

    if split:
        x_own.wait_recv()
        relay_own = move(26, beside_ref.at[rep], beside_ref.at[rep], mate)
        relay_own.start()
        x_far.wait_recv()
        relay_far = move(27, beside_ref.at[far], beside_ref.at[far], mate)
        relay_far.start()
        copy_z.wait_recv()
        for copy in to_mate[:4]:
            copy.start()
        x_cut.wait_recv()
        move(26, beside_ref.at[mate], beside_ref.at[mate], mate).wait_recv()
        other = far + 1 - 2 * par
        move(27, beside_ref.at[other], beside_ref.at[other], mate).wait_recv()

        def fill(tap):
            for p in range(4):
                at = pl.ds(p * span, span)
                cut_taken[0, :, at] = inner_rows(
                    cut_own[p // 2, pl.ds((p % 2) * span, span), :], s_ref[tap, p]
                ).astype(BF16)
                cut_taken[1, :, at] = inner_rows(
                    cut_in[p // 2, pl.ds((p % 2) * span, span), :],
                    shift_block(layout_ref, beside * 4 + p, 1, tap, span),
                ).astype(BF16)

        def gradient(head, lanes):
            total = 0.0
            for number, held in enumerate((heads_ref, beside_ref)):
                for side in range(2):
                    total = total + product(
                        cut_taken[number, :, side * 2 * span : (side + 1) * 2 * span],
                        held[head, side, :, lanes],
                    )
            return total.astype(BF16)

        @pl.loop(0, 4)
        def _(i):
            fill(tap_of(i))
            for at in range(3):
                for k in range(2):
                    row = pl.multiple_of(row_of(i, at) + k * small, small)
                    out_ref[:, pl.ds(row, small)] = gradient(
                        at + 1 - upper, pl.ds(k * small, small)
                    )

        fill(4)
        for k in range(2):
            row = pl.multiple_of(full_row + k * small, small)
            out_ref[:, pl.ds(row, small)] = gradient(full_head, pl.ds(k * small, small))
        out_ref[:, pl.ds(part_row, small)] = gradient(part_head, part_lanes)

    if split:
        near_xz.wait_recv()
        far_xz.wait_recv()
        to_mate[4].start()

    near_move.wait_recv()
    left, right = 0.0, 0.0

    def backward(side):
        unit = (headed_ref[side] - center) * scaling
        normed = unit * gain + shift
        sigma = jax.nn.sigmoid(normed)
        return unit, sigma * (1.0 + normed * (1.0 - sigma))

    for side in range(2):
        for part in (2 * side, 2 * side + 1):
            far_move(part).wait_recv()
        unit, slope = backward(side)
        grad = near_ref[side] + near_in[side].astype(F32) + far_in[side].astype(F32)
        grad = grad * slope
        near_ref[side] = grad
        masked = live_ref[side] * grad
        left = left + column_sum(masked * unit)
        right = right + column_sum(masked)
    sums = add_up(1, left, right)
    norm_ref[...] = sums
    for side in range(2):
        unit = (headed_ref[side] - center) * scaling
        low_ref[side] = (
            live_ref[side]
            * (gain * scaling)
            * (near_ref[side] - sums[1:2] * inverse - unit * (sums[0:1] * inverse))
        ).astype(BF16)

    for part in range(4):
        across(rep, part).wait_send()
        relay(far, part).wait_send()
        far_move(part).wait_send()
    own_head(rep).wait_send()
    move(9, cot_ref, cot_in, far).wait_send()
    move(10, labels_ref, labels_in, far).wait_send()
    for side in range(2):
        acc_move(side).wait_send()
        gm_move(side, par).wait_send()
    for side in range(2):
        core_move(side).wait_send()
    near_move.wait_send()

    @pl.when(upper == 0)
    def _():
        move(15, depth_out, depth_ref, far).wait_send()
        move(16, logits_out, logits_ref, far).wait_recv()

    @pl.when(upper == 1)
    def _():
        move(16, logits_out, logits_ref, far).wait_send()
        move(15, depth_out, depth_ref, far).wait_recv()

    if split:
        for copy in to_mate:
            copy.wait_recv()
            copy.wait_send()
        for copy in (x_own, x_far, x_cut, relay_own, relay_far, copy_x, copy_z, near_xz, far_xz):
            copy.wait_send()


def message_streams(
    split, layout, headed, shifts, w_messages, w_gates, w_classes, gain, shift, cot, labels, afar
):
    n_dp = lax.axis_size("dp")
    span, middle = cot.shape
    small = middle // 2
    classes = w_classes.shape[1]
    vmem = pl.BlockSpec(memory_space=pltpu.VMEM)
    dma = pltpu.SemaphoreType.DMA
    shape = jax.ShapeDtypeStruct
    halves = (2, 2 * span, middle)
    heads = (4, 2, 2 * span, middle)
    out_shape = [
        shape((span, middle), F32),
        shape((span, 128), F32),
        shape((middle, middle), BF16),
        shape((middle, 128), F32),
        shape(halves, BF16),
        shape((2, middle), F32),
    ]
    if split:
        out_shape += [shape((small, w_messages.shape[0]), BF16)] + [shape(afar[0].shape, BF16)] * 2
        out_shape += [shape((2,) + afar[0].shape, BF16)] * 4
    else:
        out_shape += [shape(heads, BF16), shape(halves, BF16)]
    scratch = [
        pltpu.VMEM(w_messages.shape, BF16),
        pltpu.VMEM((2, 2 * span, 1), F32),
        pltpu.VMEM(halves, F32),
        pltpu.VMEM((2, span, middle), F32),
        pltpu.VMEM((2, span, middle), F32),
        pltpu.VMEM((2, span, middle), F32),
        pltpu.VMEM((span, middle), BF16),
        pltpu.VMEM((span, 128), jnp.int32),
        pltpu.VMEM((span, middle), F32),
        pltpu.VMEM((span, 128), F32),
        pltpu.VMEM((5,) + halves, BF16),
        pltpu.VMEM((2,) + halves, F32),
        pltpu.VMEM(halves, F32),
        pltpu.VMEM(halves, BF16),
        pltpu.VMEM(halves, BF16),
        pltpu.VMEM(halves, BF16),
        pltpu.VMEM(halves, BF16),
        pltpu.VMEM(halves, BF16),
        pltpu.VMEM(halves, BF16),
        pltpu.VMEM((2, 2, middle), F32),
        pltpu.VMEM((2, n_dp, 2, middle), F32),
        dma,
        dma((MOVES,)),
        dma((MOVES,)),
        dma((2, n_dp)),
        dma((2, n_dp)),
    ]
    if split:
        scratch += [
            pltpu.VMEM(heads, BF16),
            pltpu.VMEM(halves, BF16),
            pltpu.VMEM(heads, BF16),
            pltpu.VMEM((2, 2 * span, small), BF16),
            pltpu.VMEM((2, 2 * span, small), BF16),
            pltpu.VMEM((2, 2 * span, small), BF16),
            pltpu.VMEM((2, small, 4 * span), BF16),
        ]
    return pl.pallas_call(
        functools.partial(message_kernel, split, n_dp, classes),
        in_specs=[pl.BlockSpec(memory_space=pltpu.SMEM)]
        + [vmem] * 3
        + [pl.BlockSpec(memory_space=pl.ANY)]
        + [vmem] * 6
        + [pl.BlockSpec(memory_space=pl.ANY)] * len(afar),
        out_specs=[vmem] * 7 + [pl.BlockSpec(memory_space=pl.ANY) if split else vmem] * (len(out_shape) - 7),
        out_shape=out_shape,
        scratch_shapes=scratch,
        compiler_params=pltpu.CompilerParams(
            collective_id=11, has_side_effects=True, vmem_limit_bytes=VMEM_LIMIT
        ),
        name="message_streams",
    )(
        layout,
        layout,
        headed,
        shifts,
        w_messages,
        w_gates,
        jnp.pad(w_classes, ((0, 0), (0, 128 - classes))),
        gain[None, :],
        shift[None, :],
        cot,
        jnp.broadcast_to(labels[:, None], (span, 128)),
        *afar,
    )


def heads_taps(t_ref, low_ref, taken_ref, side):
    span = t_ref.shape[2]

    @pl.loop(0, taken_ref.shape[0])
    def _(t):
        for k in range(2):
            at = pl.ds(k * span, span)
            taken_ref[t, at, :] = inner_rows(t_ref[t, 2 * side + k], low_ref[side, at, :]).astype(
                BF16
            )


def heads_tile(c, taken_ref, w_ref, tile_ref):
    taps, _, _ = taken_ref.shape
    wide = w_ref.shape[1] // taps
    step = tile_ref.shape[1]
    total = 0.0
    for t in range(taps):
        at = pl.ds(pl.multiple_of(t * wide + c * step, step), step)
        total = total + product(taken_ref[t], w_ref[:, at])
    tile_ref[...] = total


def heads_loads(w_hbm, w_ref, sems):
    taps = sems.shape[0]
    wide = w_ref.shape[1] // taps
    spans = [pl.ds(t * wide, wide) for t in range(taps)]
    return [
        pltpu.make_async_copy(w_hbm.at[:, at], w_ref.at[:, at], sems.at[t])
        for t, at in enumerate(spans)
    ]


def meet(partners):
    barrier = pltpu.get_barrier_semaphore()
    for partner in partners:
        pl.semaphore_signal(barrier, inc=1, device_id=partner, device_id_type=MESH)
    pl.semaphore_wait(barrier, len(partners))


def heads_far_kernel(split, low_ref, s_ref, w_hbm, *refs):
    sum_ref, *refs = refs
    if split:
        low_x, low_z, *refs = refs
    w_ref, taken_ref, tile_ref, kept, core_out, core_in, load_sems, send, recv = refs
    rep, dp = lax.axis_index("rep"), lax.axis_index("dp")
    par, upper = lax.rem(rep, 2), rep // 2
    mate = rep + 1 - 2 * par
    beside, along = dp + 1 - 2 * lax.rem(dp, 2), dp + 2 - 4 * lax.rem(dp // 2, 2)
    span = s_ref.shape[2]
    tiles = sum_ref.shape[0]
    loads = heads_loads(w_hbm, w_ref, load_sems)
    for load in loads:
        load.start()
    meet([{"rep": mate}] + ([{"dp": beside}, {"dp": along}] if split else []))

    def block(parity):
        return pl.ds(pl.multiple_of(parity * span, span), span)

    if split:
        copy_x = send_to("dp", beside, low_ref, low_x, send.at[tiles], recv.at[tiles])
        copy_z = send_to("dp", along, low_ref, low_z, send.at[tiles + 1], recv.at[tiles + 1])
        copy_z.start()
        copy_x.start()

    def core_move(c):
        return send_to("rep", mate, core_out.at[c], core_in.at[c], send.at[c], recv.at[c])

    heads_taps(s_ref, low_ref, taken_ref, 1 - upper)
    for load in loads:
        load.wait()

    @pl.loop(0, tiles)
    def _(c):
        heads_tile(c, taken_ref, w_ref, tile_ref)
        core_out[c] = tile_ref[block(1 - par), :].astype(BF16)
        core_move(c).start()
        kept[c] = tile_ref[block(par), :]

    for c in range(tiles):
        core_move(c).wait_recv()
        sum_ref[c] = (kept[c] + core_in[c].astype(F32)).astype(BF16)
        core_move(c).wait_send()
    if split:
        for copy in (copy_x, copy_z):
            copy.wait_recv()
            copy.wait_send()


def heads_near_kernel(split, low_ref, s_ref, w_hbm, sum_ref, *refs):
    if split:
        low_z, *refs = refs
    out_ref, *refs = refs
    if split:
        low_xz, *refs = refs
    w_ref, taken_ref, tile_ref, kept, far_in, near_out, near_in, load_sems, send, recv = refs
    rep, dp = lax.axis_index("rep"), lax.axis_index("dp")
    par, upper = lax.rem(rep, 2), rep // 2
    mate, far = rep + 1 - 2 * par, rep + 2 - 4 * upper
    beside = dp + 1 - 2 * lax.rem(dp, 2)
    span = s_ref.shape[2]
    tiles = sum_ref.shape[0]
    step = tile_ref.shape[1]
    loads = heads_loads(w_hbm, w_ref, load_sems)
    for load in loads:
        load.start()
    meet([{"rep": mate}, {"rep": far}] + ([{"dp": beside}] if split else []))

    def block(parity):
        return pl.ds(pl.multiple_of(parity * span, span), span)

    def far_move(c):
        return send_to("rep", far, sum_ref.at[c], far_in.at[c], send.at[c], recv.at[c])

    def near_move(c):
        return send_to(
            "rep", mate, near_out.at[c], near_in.at[c], send.at[tiles + c], recv.at[tiles + c]
        )

    for c in range(tiles):
        far_move(c).start()
    if split:
        copy_xz = send_to("dp", beside, low_z, low_xz, send.at[2 * tiles], recv.at[2 * tiles])
        copy_xz.start()
    heads_taps(s_ref, low_ref, taken_ref, upper)
    for load in loads:
        load.wait()

    @pl.loop(0, tiles)
    def _(c):
        heads_tile(c, taken_ref, w_ref, tile_ref)
        near_out[c] = tile_ref[block(1 - par), :].astype(BF16)
        near_move(c).start()
        kept[c] = tile_ref[block(par), :]

    for c in range(tiles):
        near_move(c).wait_recv()
        far_move(c).wait_recv()
        out_ref[:, c * step : (c + 1) * step] = (
            kept[c] + near_in[c].astype(F32) + far_in[c].astype(F32)
        ).astype(BF16)
        near_move(c).wait_send()
        far_move(c).wait_send()
    if split:
        copy_xz.wait_recv()
        copy_xz.wait_send()


def heads_back(split, low, shifts, w_heads):
    taps, _, span, _ = shifts.shape
    wide = w_heads.shape[1] // taps
    tiles = wide // 512
    vmem = pl.BlockSpec(memory_space=pltpu.VMEM)
    hbm = pl.BlockSpec(memory_space=pl.ANY)
    dma = pltpu.SemaphoreType.DMA
    shape = jax.ShapeDtypeStruct
    cut = (tiles, span, 512)
    scratch = [
        pltpu.VMEM(w_heads.shape, BF16),
        pltpu.VMEM((taps, 2 * span, low.shape[2]), BF16),
        pltpu.VMEM((2 * span, 512), F32),
        pltpu.VMEM(cut, F32),
    ]

    def of(number):
        return pltpu.CompilerParams(
            collective_id=number, has_side_effects=True, vmem_limit_bytes=VMEM_LIMIT
        )

    lows = [shape(low.shape, BF16)] * (2 * split)
    far_sum, *lows = pl.pallas_call(
        functools.partial(heads_far_kernel, split),
        in_specs=[vmem, vmem, hbm],
        out_specs=[vmem] * (1 + len(lows)),
        out_shape=[shape(cut, BF16)] + lows,
        scratch_shapes=scratch
        + [pltpu.VMEM(cut, BF16)] * 2
        + [dma((taps,)), dma((tiles + 2,)), dma((tiles + 2,))],
        compiler_params=of(12),
        name="heads_far",
    )(low, shifts, w_heads)

    def near(far_sum, *lows):
        last = lows[1:]
        grad, *more = pl.pallas_call(
            functools.partial(heads_near_kernel, split),
            in_specs=[vmem, vmem, hbm, vmem] + [vmem] * len(last),
            out_specs=[vmem] * (1 + len(last)),
            out_shape=[shape((span, wide), BF16)] + [shape(low.shape, BF16)] * len(last),
            scratch_shapes=scratch
            + [pltpu.VMEM(cut, BF16)] * 3
            + [dma((taps,)), dma((2 * tiles + 1,)), dma((2 * tiles + 1,))],
            compiler_params=of(13),
            name="heads_near",
        )(low, shifts, w_heads, far_sum, *last)
        return [grad] + list(lows) + more

    return far_sum, lows, near


def heads_shard_kernel(per_tap, at_ref, layout_ref, *refs):
    lows, trunks = refs[:4], refs[4:13]
    out_ref, taken, turned, kinds = refs[13:]
    unit = pl.program_id(1)
    at = at_ref[pl.program_id(0)] + unit
    tap, chunk = at // per_tap, at % per_tap
    rows = lows[0].shape[1]
    span = rows // 2
    par, upper = at_ref[6], at_ref[7]

    places = [(0, side, k) for side in range(2) for k in range(2)]
    for number in (1, 2):
        places += [(number, side, par) for side in (upper, 1 - upper)]
        places += [(number, side, 1 - par) for side in range(2)]
    places += [(3, side, k) for k in (par, 1 - par) for side in range(2)]

    @pl.when((pl.program_id(0) == 0) & (unit == 0))
    def _():
        for number, low in enumerate(lows):
            for side in range(2):
                for k in range(2):
                    turned[number, side, k] = low[side, k * span : (k + 1) * span, :].T

    @pl.when((unit == 0) | (chunk == 0))
    def _():
        for kind, extent in enumerate((16, 8)):
            kinds[kind] = shift_in_maps(extent, tap, span)
        for slot, (number, side, k) in enumerate(places):
            large = layout_ref[at_ref[2 + number] + 2 * side + k, 1] == 16
            picks = kinds[jnp.where(large, 0, 1)]
            taken[:, slot * span : (slot + 1) * span] = product(
                turned[number, side, k], picks
            ).astype(BF16)

    total = 0.0
    slot = 0
    for trunk in trunks:
        strip = trunk[...].reshape(-1, trunk.shape[-1])
        depth = strip.shape[0]
        total = total + product(taken[:, slot : slot + depth], strip)
        slot += depth
    out_ref[0] = total.astype(BF16)


def heads_shard(at, layout, lows, trunks, units, lanes):
    _, rows, outs = lows[0].shape
    wide = trunks[0].shape[2]
    per_tap = wide // lanes
    whole = pl.BlockSpec(lows[0].shape, lambda i, j, f, g: (0, 0, 0))

    def strip_of(trunk):
        lead = trunk.shape[:-1]
        return pl.BlockSpec(
            lead + (lanes,), lambda i, j, f, g: (0,) * len(lead) + ((f[i] + j) % per_tap,)
        )

    strips = [strip_of(trunk) for trunk in trunks]
    return pl.pallas_call(
        functools.partial(heads_shard_kernel, per_tap),
        grid_spec=pltpu.PrefetchScalarGridSpec(
            num_scalar_prefetch=2,
            grid=(2, units),
            in_specs=[whole] * 4 + strips,
            out_specs=pl.BlockSpec((1, outs, lanes), lambda i, j, f, g: (i, 0, j)),
            scratch_shapes=[
                pltpu.VMEM((outs, 8 * rows), BF16),
                pltpu.VMEM((4, 2, 2, outs, rows // 2), BF16),
                pltpu.VMEM((2, rows // 2, rows // 2), BF16),
            ],
        ),
        out_shape=jax.ShapeDtypeStruct((2, outs, units * lanes), BF16),
        compiler_params=params(),
        cost_estimate=cost(32 * rows * outs * units * lanes, 32 * rows * units * lanes),
        name="heads_shard",
    )(at, layout, *lows, *trunks)


CHUNK_ROWS = (384, 512, 640, 512, 256, 256)
CHUNK_BASE = (0, 384, 1408, 2048, 896, 1152)
SMALL_ROWS = 2560
HELD_ROWS = 1408
SPATIAL_BASE = 1408
REDUCE_BASE = 896


def trunk_back_kernel(*refs):
    refs = list(refs)

    def take(count):
        taken, refs[:count] = refs[:count], []
        return taken

    layout_ref, areas_ref, grad_ref, expanded_ref, in_ref = take(5)
    reduced_ref, spatial_ref, sums_one_ref, sums_two_ref, sums_three_ref = take(5)
    hidden_one_ref, hidden_two_ref, shift_taps_ref = take(3)
    w_reduce_hbm, w_spatial_hbm, w_expand_ref = take(3)
    gain_mid_ref, shift_mid_ref, gain_wide_ref, shift_wide_ref = take(4)
    gates_ref, classes_ref, head_norm_ref = take(3)
    out_ref, norm_one_ref, norm_two_ref, norm_three_ref, half_ref, heads_norm_ref = take(6)
    p_ref, core_in, core_out, y_in, x_out, x_in, z_out, z_in = take(8)
    z_mid, zz_in = take(2)
    low_wide, moved_ref, total_ref, block_mid, block_wide = take(5)
    slots_mid_rep, slots_mid_dp, slots_wide_rep, slots_wide_dp = take(4)
    rep_send, rep_recv, dp_send, dp_recv, send, recv, norm_send, norm_recv = take(8)
    w_reduce_ref, w_spatial_ref, hidden_all, low_all, moved_all, spatial_own = take(6)
    load_sems, gather_send, gather_recv = take(3)

    rep, dp = lax.axis_index("rep"), lax.axis_index("dp")
    par, upper = lax.rem(rep, 2), rep // 2
    x, z = lax.rem(dp, 2), dp // 2
    mate, far, beside = rep + 1 - 2 * par, rep + 2 - 4 * upper, dp + 1 - 2 * x
    low_z, high_z = lax.rem(z, 2), z // 2
    along, over = dp + 2 - 4 * low_z, dp + 4 - 8 * high_z
    span, wide = in_ref.shape
    middle = reduced_ref.shape[1]
    taps = shift_taps_ref.shape[0]
    loads = [
        pltpu.make_async_copy(w_spatial_hbm, w_spatial_ref, load_sems.at[0]),
        pltpu.make_async_copy(w_reduce_hbm, w_reduce_ref, load_sems.at[1]),
    ]
    for load in loads:
        load.start()
    barrier = pltpu.get_barrier_semaphore()
    for axis, size in (("rep", 4), ("dp", 8)):
        me = lax.axis_index(axis)
        for k in range(1, size):
            pl.semaphore_signal(
                barrier, inc=1, device_id={axis: lax.rem(me + k, size)}, device_id_type=MESH
            )

    def remote(src, dst, c, slot, to):
        return pltpu.make_async_remote_copy(
            src_ref=src,
            dst_ref=dst,
            send_sem=send.at[c, slot],
            recv_sem=recv.at[c, slot],
            device_id=to,
            device_id_type=MESH,
        )

    def whole(c, at=0, size=None):
        size = CHUNK_ROWS[c] if size is None else size
        return pl.ds(pl.multiple_of(CHUNK_BASE[c] + at, 16), size)

    def halves(c):
        return pl.ds(CHUNK_BASE[c] // 2, CHUNK_ROWS[c] // 2)

    def core_copy(c, hi):
        return remote(
            p_ref.at[2 * hi + 1 - par, whole(c)], core_in.at[hi, whole(c)], c, hi, {"rep": mate}
        )

    def y_copy(c):
        return remote(core_out.at[whole(c)], y_in.at[whole(c)], c, 2, {"rep": far})

    def x_copy(c):
        return remote(x_out.at[halves(c)], x_in.at[halves(c)], c, 3, {"dp": beside})

    def piece(c, base, at, size):
        return pl.ds(pl.multiple_of(CHUNK_BASE[c] // base + at, 16), size)

    def z_copy(c):
        size = CHUNK_ROWS[c] // 4
        return remote(
            z_out.at[piece(c, 2, (1 - low_z) * size, size)],
            z_in.at[piece(c, 4, 0, size)],
            c,
            4,
            {"dp": along},
        )

    def zz_copy(c):
        size = CHUNK_ROWS[c] // 8
        return remote(
            z_mid.at[piece(c, 4, (1 - high_z) * size, size)],
            zz_in.at[piece(c, 8, 0, size)],
            c,
            5,
            {"dp": over},
        )

    def own_place(c, low, high=None):
        size = CHUNK_ROWS[c] // 4
        at = x * 2 * size + low * size
        if high is None:
            return whole(c, at, size)
        return whole(c, at + high * (size // 2), size // 2)

    def zz_back(c, incoming):
        place = own_place(c, low_z, 1 - high_z if incoming else high_z)
        return remote(half_ref.at[place], half_ref.at[place], c, 6, {"dp": over})

    def z_back(c, incoming):
        place = own_place(c, 1 - low_z if incoming else low_z)
        return remote(half_ref.at[place], half_ref.at[place], c, 7, {"dp": along})

    def last_copy(c, incoming):
        half = CHUNK_ROWS[c] // 2
        place = whole(c, (1 - x if incoming else x) * half, half)
        return remote(half_ref.at[place], half_ref.at[place], c, 8, {"dp": beside})

    def step(c, stage):
        if stage == 0:
            for hi in range(2):
                core_copy(c, hi).start()
        elif stage == 1:
            for hi in range(2):
                core_copy(c, hi).wait_recv()
            core_out[whole(c)] = (
                p_ref[2 * (1 - upper) + par, whole(c)].astype(F32)
                + core_in[1 - upper, whole(c)].astype(F32)
            ).astype(BF16)
            y_copy(c).start()
        elif stage == 2 and c in (2, 3):
            half = CHUNK_ROWS[c] // 2
            at = CHUNK_BASE[c] - SPATIAL_BASE

            def own(k):
                return spatial_own[pl.ds(pl.multiple_of(at + k * half, 16), half)]

            x_out[halves(c)] = own(1 - x).astype(BF16)
            x_copy(c).start()
            z_out[halves(c)] = own(x).astype(BF16)
        elif stage == 2:
            y_copy(c).wait_recv()
            half = CHUNK_ROWS[c] // 2

            def both(at):
                place = whole(c, at, half)
                return (
                    p_ref[rep, place].astype(F32)
                    + core_in[upper, place].astype(F32)
                    + y_in[place].astype(F32)
                )

            x_out[halves(c)] = both((1 - x) * half).astype(BF16)
            x_copy(c).start()
            z_out[halves(c)] = both(x * half).astype(BF16)
        elif stage == 3:
            x_copy(c).wait_recv()
            z_out[halves(c)] = (
                z_out[halves(c)].astype(F32) + x_in[halves(c)].astype(F32)
            ).astype(BF16)
            z_copy(c).start()
        elif stage == 4:
            z_copy(c).wait_recv()
            size = CHUNK_ROWS[c] // 4
            at = piece(c, 4, 0, size)
            z_mid[at] = (
                z_out[piece(c, 2, low_z * size, size)].astype(F32) + z_in[at].astype(F32)
            ).astype(BF16)
            zz_copy(c).start()
        elif stage == 5:
            zz_copy(c).wait_recv()
            size = CHUNK_ROWS[c] // 8
            half_ref[own_place(c, low_z, high_z)] = (
                z_mid[piece(c, 4, high_z * size, size)].astype(F32)
                + zz_in[piece(c, 8, 0, size)].astype(F32)
            ).astype(BF16)
            zz_back(c, False).start()
        elif stage == 6:
            zz_back(c, True).wait_recv()
            z_back(c, False).start()
        elif stage == 7:
            z_back(c, True).wait_recv()
            last_copy(c, False).start()
        else:
            last_copy(c, True).wait_recv()
            if c not in (2, 3):
                for hi in range(2):
                    core_copy(c, hi).wait_send()
                y_copy(c).wait_send()
            x_copy(c).wait_send()
            z_copy(c).wait_send()
            zz_copy(c).wait_send()
            zz_back(c, False).wait_send()
            z_back(c, False).wait_send()
            last_copy(c, False).wait_send()

    def steps(*which):
        def run():
            for c, stage in which:
                step(c, stage)

        return run

    live = live_column(layout_ref, dp * 4 + rep, span)
    inverse = inverse_count(areas_ref, span)

    def stats(sums_ref):
        center = sums_ref[0:1, :] * inverse
        return center, lax.rsqrt(sums_ref[1:2, :] * inverse - center * center + EPS)

    def norm_move(to, slot):
        at = heads_norm_ref.at[slot]
        return send_to("rep", to, at, at, norm_send.at[to], norm_recv.at[slot])

    def local_sums(blocks, value, unit, at):
        masked = live * value
        blocks[0, 0:1, at] = jnp.sum(masked * unit, 0, keepdims=True)
        blocks[0, 1:2, at] = jnp.sum(masked, 0, keepdims=True)

    def everywhere(number, blocks, rep_slots, dp_slots, meanwhile, later):
        if number == 0:
            pl.semaphore_wait(barrier, 10)
            heads_norm_ref[rep] = head_norm_ref[...]
            for k in range(1, 4):
                norm_move(lax.rem(rep + k, 4), rep).start()
        blocks[1] = total_along(
            "rep", 4, blocks.at[0], rep_slots, rep_send.at[number], rep_recv.at[number], meanwhile
        )
        return total_along(
            "dp", 8, blocks.at[1], dp_slots, dp_send.at[number], dp_recv.at[number], later
        )

    def slope(value):
        sigma = jax.nn.sigmoid(value)
        return sigma * (1.0 + value * (1.0 - sigma))

    def spread_back(grad, unit, sums, gain, scaling):
        return (
            live
            * (gain * scaling)
            * (grad - sums[1:2] * inverse - unit * (sums[0:1] * inverse))
        ).astype(BF16)

    center, scaling = stats(sums_three_ref)
    strips = [pl.ds(k, middle) for k in range(0, wide, middle)]

    def unit_at(at):
        return (expanded_ref[:, at] - center[:, at.start : at.start + middle]) * scaling[
            :, at.start : at.start + middle
        ]

    for at in strips:
        unit = unit_at(at)
        pre = unit * gain_wide_ref[:, at] + shift_wide_ref[:, at] + in_ref[:, at].astype(F32)
        grad = grad_ref[:, at].astype(F32) * slope(pre)
        out_ref[:, at] = grad
        local_sums(block_wide, grad, unit, at)

    def gather(number, held, to, slot):
        at = held.at[slot]
        return send_to(
            "rep", to, at, at, gather_send.at[number, to], gather_recv.at[number, slot]
        )

    hidden_all[rep] = hidden_one_ref[...]

    def first_chunk():
        half = middle // 2
        rows = classes_ref.shape[1]
        for q in range(4):
            p_ref[q, half : half + rows, :] = classes_ref[q]
            p_ref[q, half + rows : CHUNK_ROWS[0], :] = jnp.zeros(
                (CHUNK_ROWS[0] - half - rows, middle), BF16
            )
        for k in range(2):
            p_ref[2 * upper + k, :half, :] = gates_ref[k * half : (k + 1) * half, :]
            p_ref[2 * (1 - upper) + k, :half, :] = jnp.zeros((half, middle), BF16)
        step(0, 0)
        for k in range(1, 4):
            gather(0, hidden_all, lax.rem(rep + k, 4), rep).start()
        step(0, 1)

    sums = everywhere(
        0,
        block_wide,
        slots_wide_rep,
        slots_wide_dp,
        first_chunk,
        steps((0, 2)),
    )
    norm_three_ref[...] = sums
    for at in strips:
        cut = slice(at.start, at.start + middle)
        low_wide[:, at] = spread_back(
            out_ref[:, at], unit_at(at), sums[:, cut], gain_wide_ref[:, at], scaling[:, cut]
        )

    center, scaling = stats(sums_two_ref)
    unit = (spatial_ref[...] - center) * scaling
    normed = unit * gain_mid_ref[1:2, :] + shift_mid_ref[1:2, :]
    total_ref[...] = against(low_wide[...], w_expand_ref[...]) * slope(normed)

    def expand_gradient():
        rows = middle // 4
        for k in range(wide // middle):
            tile = inner_rows(
                hidden_two_ref[...], low_wide[:, k * middle : (k + 1) * middle]
            ).astype(BF16)
            for q in range(4):
                at = CHUNK_BASE[1] + k * rows
                p_ref[q, at : at + rows, :] = tile[q * rows : (q + 1) * rows]
        step(1, 0)
        step(1, 1)

    local_sums(block_mid.at[0], total_ref[...], unit, slice(None))
    sums = everywhere(
        1,
        block_mid.at[0],
        slots_mid_rep.at[0],
        slots_mid_dp.at[0],
        expand_gradient,
        steps((0, 3), (1, 2)),
    )
    norm_two_ref[...] = sums
    low_mid = spread_back(total_ref[...], unit, sums, gain_mid_ref[1:2, :], scaling)

    total_ref[...] = jnp.zeros_like(total_ref)
    loads[0].wait()
    for t in range(taps):
        moved_ref[t] = inner_rows(shift_taps_ref[t], low_mid).astype(BF16)

    @pl.loop(0, taps)
    def _(t):
        at = pl.ds(pl.multiple_of(t * middle, middle), middle)
        total_ref[...] += against(moved_ref[t], w_spatial_ref[at, :])

    center, scaling = stats(sums_one_ref)
    unit = (reduced_ref[...] - center) * scaling
    normed = unit * gain_mid_ref[0:1, :] + shift_mid_ref[0:1, :]
    total_ref[...] = total_ref[...] * slope(normed)

    def give_low():
        low_all[rep] = low_mid
        for k in range(1, 4):
            gather(1, low_all, lax.rem(rep + k, 4), rep).start()

    def spatial_gradient():
        large = [layout_ref[dp * 4 + p, 1] == 16 for p in range(4)]
        units = spatial_own.shape[0] // 128
        per_tap = middle // 128

        @pl.loop(0, units)
        def _(i):
            unit = units * rep + i
            tap, cut = unit // per_tap, unit % per_tap

            @pl.when((i == 0) | (cut == 0))
            def _():
                kinds = [shift_in_maps(extent, tap, span, 2) for extent in (16, 8)]
                for p in range(4):
                    picks = jnp.where(large[p], kinds[0], kinds[1])
                    moved_all[p] = inner_rows(picks, low_all[p]).astype(BF16)

            lanes = pl.ds(pl.multiple_of(cut * 128, 128), 128)
            total = 0.0
            for p in range(4):
                total = total + inner_rows(hidden_all[p, :, lanes], moved_all[p])
            spatial_own[pl.ds(pl.multiple_of(i * 128, 128), 128), :] = total

    local_sums(block_mid.at[1], total_ref[...], unit, slice(None))
    sums = everywhere(
        2,
        block_mid.at[1],
        slots_mid_rep.at[1],
        slots_mid_dp.at[1],
        give_low,
        steps((0, 4), (1, 3)),
    )
    norm_one_ref[...] = sums
    low_first = spread_back(total_ref[...], unit, sums, gain_mid_ref[0:1, :], scaling)
    quarter = wide // 4
    for q in range(4):
        p_ref[q, REDUCE_BASE : REDUCE_BASE + quarter, :] = inner_rows(
            in_ref[:, q * quarter : (q + 1) * quarter], low_first
        ).astype(BF16)
    step(4, 0)
    step(5, 0)
    step(1, 4)
    step(0, 5)
    step(4, 1)
    step(5, 1)
    for number, held in enumerate((hidden_all, low_all)):
        for k in range(1, 4):
            other = lax.rem(rep + k, 4)
            gather(number, held, other, other).wait_recv()
            gather(number, held, other, rep).wait_send()
    spatial_gradient()
    step(2, 2)
    step(3, 2)
    loads[1].wait()
    for k in range(0, wide, middle):
        out_ref[:, k : k + middle] += against(low_first, w_reduce_ref[k : k + middle, :])
    for turn in (
        ((4, 2), (1, 5), (0, 6), (2, 3), (5, 2)),
        ((3, 3), (4, 3), (1, 6), (0, 7), (2, 4), (5, 3)),
        ((3, 4), (4, 4), (1, 7), (0, 8), (2, 5), (5, 4)),
        ((3, 5), (4, 5), (1, 8), (2, 6), (5, 5)),
        ((3, 6), (4, 6), (2, 7), (5, 6)),
        ((3, 7), (4, 7), (2, 8), (5, 7)),
        ((3, 8), (4, 8), (5, 8)),
    ):
        for c, stage in turn:
            step(c, stage)
    for k in range(1, 4):
        other = lax.rem(rep + k, 4)
        norm_move(other, other).wait_recv()
        norm_move(other, rep).wait_send()


def trunk_back(
    layout,
    grad,
    expanded,
    inputs,
    reduced,
    spatial,
    sums,
    hidden_one,
    hidden_two,
    shift_taps,
    w_reduce,
    w_spatial,
    w_expand,
    gain_mid,
    shift_mid,
    gain_wide,
    shift_wide,
    gates,
    classes,
    head_norm,
):
    span, wide = inputs.shape
    middle = reduced.shape[1]
    taps = shift_taps.shape[0]
    vmem = pl.BlockSpec(memory_space=pltpu.VMEM)
    dma = pltpu.SemaphoreType.DMA
    shape = jax.ShapeDtypeStruct
    small = (SMALL_ROWS, middle)
    held = (HELD_ROWS, middle)
    every = (4, span, middle)
    half = (SMALL_ROWS // 2, middle)
    chunks = len(CHUNK_ROWS)
    out_shape = [
        shape((span, wide), F32),
        shape((2, middle), F32),
        shape((2, middle), F32),
        shape((2, wide), F32),
        shape(small, BF16),
        shape((4, 2, middle), F32),
    ]
    return pl.pallas_call(
        trunk_back_kernel,
        in_specs=[pl.BlockSpec(memory_space=pltpu.SMEM)]
        + [vmem] * 12
        + [pl.BlockSpec(memory_space=pl.ANY)] * 2
        + [vmem] * 8,
        out_specs=[vmem] * len(out_shape),
        out_shape=out_shape,
        scratch_shapes=[
            pltpu.VMEM((4,) + held, BF16),
            pltpu.VMEM((2,) + held, BF16),
            pltpu.VMEM(held, BF16),
            pltpu.VMEM(held, BF16),
            pltpu.VMEM(half, BF16),
            pltpu.VMEM(half, BF16),
            pltpu.VMEM(half, BF16),
            pltpu.VMEM((SMALL_ROWS // 4, middle), BF16),
            pltpu.VMEM((SMALL_ROWS // 4, middle), BF16),
            pltpu.VMEM((SMALL_ROWS // 8, middle), BF16),
            pltpu.VMEM((span, wide), BF16),
            pltpu.VMEM((taps, span, middle), BF16),
            pltpu.VMEM((span, middle), F32),
            pltpu.VMEM((2, 2, 2, middle), F32),
            pltpu.VMEM((2, 2, wide), F32),
            pltpu.VMEM((2, 4, 2, middle), F32),
            pltpu.VMEM((2, 8, 2, middle), F32),
            pltpu.VMEM((4, 2, wide), F32),
            pltpu.VMEM((8, 2, wide), F32),
            dma((3, 4)),
            dma((3, 4)),
            dma((3, 8)),
            dma((3, 8)),
            dma((chunks, 9)),
            dma((chunks, 9)),
            dma((4,)),
            dma((4,)),
            pltpu.VMEM(w_reduce.shape, BF16),
            pltpu.VMEM(w_spatial.shape, BF16),
            pltpu.VMEM(every, BF16),
            pltpu.VMEM(every, BF16),
            pltpu.VMEM(every, BF16),
            pltpu.VMEM((taps * middle // 4, middle), F32),
            dma((2,)),
            dma((2, 4)),
            dma((2, 4)),
        ],
        compiler_params=pltpu.CompilerParams(
            collective_id=9, has_side_effects=True, vmem_limit_bytes=VMEM_LIMIT
        ),
        name="trunk_back",
    )(
        layout,
        layout,
        grad,
        expanded,
        inputs,
        reduced,
        spatial,
        *sums,
        hidden_one,
        hidden_two,
        shift_taps,
        w_reduce,
        w_spatial,
        w_expand,
        gain_mid,
        shift_mid,
        gain_wide[None, :],
        shift_wide[None, :],
        gates,
        classes,
        head_norm,
    )


def finish_kernel(
    classes,
    sums_ref,
    in_grad_ref,
    depth_in_ref,
    logits_in_ref,
    messages_in_ref,
    one_ref,
    two_ref,
    three_ref,
    heads_norm_ref,
    depth_ref,
    logits_ref,
    out_ref,
    reduce_ref,
    spatial_ref,
    expand_ref,
    gates_ref,
    messages_ref,
    classes_ref,
    gain_mid_ref,
    shift_mid_ref,
    gain_wide_ref,
    shift_wide_ref,
    gain_head_ref,
    shift_head_ref,
):
    middle = sums_ref.shape[1]

    def held(at, size):
        return sums_ref[at : at + size, :].astype(F32)

    depth_ref[...] = depth_in_ref[...]
    logits_ref[...] = logits_in_ref[...].T[:classes, :]
    out_ref[...] = in_grad_ref[...]
    messages_ref[...] = messages_in_ref[...].astype(F32)
    gates = gates_ref.shape[0]
    gates_ref[...] = held(0, gates)
    rows = classes_ref.shape[1] // 4
    held_classes = [held(gates, rows)[:, k * 128 : (k + 1) * 128] for k in range(4)]
    classes_ref[...] = jnp.concatenate(held_classes, 0).T[:classes, :]
    rows = expand_ref.shape[0]
    for k in range(expand_ref.shape[1] // middle):
        expand_ref[:, k * middle : (k + 1) * middle] = held(CHUNK_BASE[1] + k * rows, rows)
    spatial_ref[...] = held(SPATIAL_BASE, spatial_ref.shape[0])
    reduce_ref[...] = held(REDUCE_BASE, reduce_ref.shape[0])
    for at, (gain, shift) in enumerate(((gain_mid_ref, shift_mid_ref),) * 2):
        norm = (one_ref, two_ref)[at]
        gain[at : at + 1, :] = norm[0:1, :]
        shift[at : at + 1, :] = norm[1:2, :]
    gain_wide_ref[...] = three_ref[0:1, :]
    shift_wide_ref[...] = three_ref[1:2, :]
    for k in range(4):
        gain_head_ref[:, k * middle : (k + 1) * middle] = heads_norm_ref[k, 0:1, :]
        shift_head_ref[:, k * middle : (k + 1) * middle] = heads_norm_ref[k, 1:2, :]


def finish(classes, sums, in_grad, depth, logits, messages, one, two, three, heads_norm):
    span, wide = in_grad.shape
    middle = sums.shape[1]
    vmem = pl.BlockSpec(memory_space=pltpu.VMEM)
    shape = jax.ShapeDtypeStruct
    out_shape = [
        shape(depth.shape, F32),
        shape((classes, span), F32),
        shape(in_grad.shape, F32),
        shape((wide // 4, middle), F32),
        shape((SMALL_ROWS - SPATIAL_BASE, middle), F32),
        shape((middle // 4, wide), F32),
        shape((middle // 2, middle), F32),
        shape(messages.shape, F32),
        shape((classes, middle // 4), F32),
        shape((2, middle), F32),
        shape((2, middle), F32),
    ] + [shape((1, wide), F32)] * 4
    every = pl.pallas_call(
        functools.partial(finish_kernel, classes),
        in_specs=[vmem] * 9,
        out_specs=[vmem] * len(out_shape),
        out_shape=out_shape,
        compiler_params=params(),
        name="finish",
    )(sums, in_grad, depth, logits, messages, one, two, three, heads_norm)
    return list(every)


def silu_slope(value_in):
    sigma_of = jax.nn.sigmoid(value_in)
    return sigma_of * (1.0 + value_in * (1.0 - sigma_of))


MESH = pl.DeviceIdType.MESH


def greet(axes):
    barrier = pltpu.get_barrier_semaphore()
    count = 0
    for axis, size in axes:
        me = lax.axis_index(axis)
        for k in range(1, size):
            pl.semaphore_signal(
                barrier, inc=1, device_id={axis: lax.rem(me + k, size)}, device_id_type=MESH
            )
        count += size - 1
    pl.semaphore_wait(barrier, count)


def total_kernel(axes, x_ref, out_ref, *scratch):
    greet(axes)
    block = x_ref
    for number, (axis, size) in enumerate(axes):
        slots, stage, send_sems, recv_sems = scratch[4 * number : 4 * number + 4]
        me = lax.axis_index(axis)
        others = [lax.rem(me + k, size) for k in range(1, size)]
        for other in others:
            pltpu.make_async_remote_copy(
                src_ref=block,
                dst_ref=slots.at[me],
                send_sem=send_sems.at[other],
                recv_sem=recv_sems.at[me],
                device_id={axis: other},
                device_id_type=MESH,
            ).start()
        slots[me] = block[...]
        for other in others:
            copy = pltpu.make_async_remote_copy(
                src_ref=block,
                dst_ref=slots.at[other],
                send_sem=send_sems.at[other],
                recv_sem=recv_sems.at[other],
                device_id={axis: other},
                device_id_type=MESH,
            )
            copy.wait_recv()
            copy.wait_send()
        total = slots[0]
        for k in range(1, size):
            total = total + slots[k]
        if number == len(axes) - 1:
            out_ref[...] = total
        else:
            stage[...] = total
            block = stage


def total_of(left, right, axes):
    width = left.shape[0]
    packed = jnp.concatenate([left, right], 0).reshape(-1, 128)
    sized = tuple((axis, lax.axis_size(axis)) for axis in axes)
    scratch = []
    for _, size in sized:
        scratch += [
            pltpu.VMEM((size,) + packed.shape, F32),
            pltpu.VMEM(packed.shape, F32),
            pltpu.SemaphoreType.DMA((size,)),
            pltpu.SemaphoreType.DMA((size,)),
        ]
    number = 1 + (width != 512) + 2 * (len(axes) == 1)
    summed = pl.pallas_call(
        functools.partial(total_kernel, sized),
        out_shape=jax.ShapeDtypeStruct(packed.shape, F32),
        in_specs=[pl.BlockSpec(memory_space=pltpu.VMEM)],
        out_specs=pl.BlockSpec(memory_space=pltpu.VMEM),
        scratch_shapes=scratch,
        compiler_params=pltpu.CompilerParams(collective_id=number, has_side_effects=True),
        name="total",
    )(packed).reshape(2, width)
    return summed[0], summed[1]


def normalize(raw_value, column_sums, squares, pixel_count, norm_gain, norm_shift):
    center = column_sums / pixel_count
    spread_of = squares / pixel_count - center * center
    scaling = lax.rsqrt(spread_of + EPS)
    unit_value = (raw_value - center) * scaling
    return (unit_value * norm_gain + norm_shift, unit_value, scaling)


def moments(raw_value, living, axes):
    return total_of(
        jnp.sum(living * raw_value, 0), jnp.sum(living * raw_value * raw_value, 0), axes
    )


def norm_back(grad_out, unit_value, scaling, norm_gain, living, pixel_count, axes):
    grad_gain, grad_shift = total_of(
        jnp.sum(living * grad_out * unit_value, 0), jnp.sum(living * grad_out, 0), axes
    )
    grad_raw = (
        living
        * (norm_gain * scaling)
        * (grad_out - grad_shift / pixel_count - unit_value * grad_gain / pixel_count)
    )
    return (grad_raw, grad_gain, grad_shift)


def swap(value, bit):
    return lax.ppermute(value, "rep", [(k, k ^ bit) for k in range(4)])


def scatter_rep(value):
    return lax.psum_scatter(value.astype(BF16), "rep", scatter_dimension=0, tiled=True)


def total_dp(value):
    parts = lax.axis_size("dp")
    rows = value.shape[0]
    padded = -(-rows // (8 * parts)) * 8 * parts
    value = jnp.pad(value, ((0, padded - rows), (0, 0)))
    share = lax.psum_scatter(value, "dp", scatter_dimension=0, tiled=True)
    return lax.all_gather(share, "dp", axis=0, tiled=True)[:rows].astype(F32)


def shards(
    inputs,
    layout,
    labels,
    cot_depth,
    w_reduce,
    w_spatial,
    w_expand,
    w_heads,
    w_gates,
    w_messages,
    w_classes,
    gain_mid,
    shift_mid,
    gain_wide,
    shift_wide,
    gain_head,
    shift_head,
):
    pixels = inputs.shape[0]
    middle = w_reduce.shape[1]
    classes = w_classes.shape[1]
    group = lax.axis_size("rep")
    everyone = ("rep", "dp")
    rep = lax.axis_index("rep")
    parity = rep % 2
    upper = rep // 2
    first_row = lax.axis_index("dp") * group
    own_info = geometry(lax.dynamic_slice_in_dim(layout, first_row + rep, 1, 0), pixels)
    group_info = geometry(lax.dynamic_slice_in_dim(layout, first_row, group, 0), pixels)
    living = own_info[2][0].astype(F32)[:, None]
    group_living = group_info[2].astype(F32)
    living_all = group_living.reshape(group * pixels, 1)
    pixel_count = jnp.sum(
        jnp.minimum(layout[:, 0] * layout[:, 1] * layout[:, 2], pixels)
    ).astype(F32)
    split = lax.axis_size("dp") == 8
    if split:
        side = lax.axis_index("dp") % 2
        columns = [[z_at * 2 + k for z_at in range(4)] for k in range(2)]
    zero = jnp.zeros((1,), jnp.int32)
    first = jnp.reshape(9 * parity, (1,)).astype(jnp.int32)

    (
        reduced,
        sums_one,
        hidden_one,
        spatial,
        sums_two,
        hidden_two,
        expanded,
        sums_three,
        trunk_all,
        headed,
        shifts_own,
        shifts_all,
        *trunk_afar,
    ) = trunk_forward(
        split,
        inputs,
        layout,
        w_reduce,
        w_spatial,
        w_expand,
        w_heads,
        gain_mid,
        shift_mid,
        gain_wide,
        shift_wide,
    )
    upper_is_depth = upper == 0
    headed, late_classes, late_labels = lax.optimization_barrier((headed, w_classes, labels))
    depth, logits, gates_local, classes_local, head_low, head_norm, *rest = message_streams(
        split,
        layout,
        headed,
        shifts_all,
        w_messages,
        w_gates,
        late_classes,
        gain_head,
        shift_head,
        cot_depth,
        late_labels,
        trunk_afar + [trunk_all] if split else [],
    )
    classes_local = classes_local[:, :classes]
    is_depth = upper_is_depth
    if split:
        messages_local = rest[0]
    else:
        heads_all, message_all = rest
        heads_all = heads_all.reshape(4, group * pixels, middle)
        source = jnp.where(
            is_depth,
            jnp.concatenate([heads_all[1], heads_all[2], heads_all[3]], 1),
            jnp.concatenate([heads_all[0], heads_all[1], heads_all[2]], 1),
        )
        _, messages_local = rows_back(
            first, message_all.reshape(4 * pixels, middle), source, w_messages, shifts_all, 2, BF16
        )
        grad_messages = lax.psum_scatter(messages_local, "dp", scatter_dimension=1, tiled=True)
        gates_cut = gates_local.reshape(2, pixels, middle)
        gates_share = lax.dynamic_index_in_dim(gates_cut, parity, 0, keepdims=False).astype(F32)
        gates_share += swap(
            lax.dynamic_index_in_dim(gates_cut, 1 - parity, 0, keepdims=False), 1
        ).astype(F32)
    far_sum, lows, near = heads_back(split, head_low, shifts_all, w_heads)
    if split:
        messages_local, far_sum = lax.optimization_barrier((messages_local, far_sum))
    trunk_grad, *lows = near(far_sum, *lows)
    if split:
        grad_messages = lax.psum_scatter(
            messages_local, "dp", scatter_dimension=0, tiled=True, axis_index_groups=columns
        )
        dp = lax.axis_index("dp")
        beside, along = dp + 1 - 2 * side, dp + 2 - 4 * ((dp // 2) % 2)
        groups = [dp, beside, along, along + 1 - 2 * side]
        units = 9

        lower = dp % 4
        at = jnp.stack(
            [units * lower, units * (lower + 4)] + [group * k for k in groups] + [parity, upper]
        )
        far_x, far_z, mate_x, mate_z, trunk_xz, mate_xz = rest[1:]
        near_x, near_z = trunk_afar
        trunks = [trunk_all, near_x, far_x, mate_x, near_z, far_z, mate_z, trunk_xz, mate_xz]
        heads_local = heads_shard(
            at.astype(jnp.int32), layout, [head_low] + lows, trunks, units, 256
        )
        heads_local, trunk_grad = lax.optimization_barrier((heads_local, trunk_grad))
        grad_heads = lax.psum_scatter(
            heads_local,
            "dp",
            scatter_dimension=0,
            tiled=False,
            axis_index_groups=[[k, k + 4] for k in range(4)],
        )
    else:
        heads_local = heads_weight(
            head_low.reshape(group * pixels, middle),
            trunk_all.reshape(group * pixels, -1),
            shifts_all,
        )
        grad_heads = lax.psum_scatter(heads_local, "dp", scatter_dimension=1, tiled=True)
    if split:
        classes_wide = jnp.pad(classes_local.astype(BF16), ((0, 0), (0, 128 - classes)))
        classes_wide = classes_wide.reshape(4, 4, -1, 128)
        classes_wide = jnp.concatenate([classes_wide[:, k] for k in range(4)], 2)
        (
            input_grad,
            norm_one,
            norm_two,
            norm_three,
            small_sums,
            heads_norm,
        ) = trunk_back(
            layout,
            trunk_grad,
            expanded,
            inputs,
            reduced,
            spatial,
            [sums_one, sums_two, sums_three],
            hidden_one,
            hidden_two,
            shifts_own,
            w_reduce,
            w_spatial,
            w_expand,
            gain_mid,
            shift_mid,
            gain_wide,
            shift_wide,
            gates_local,
            classes_wide,
            head_norm,
        )
        every = finish(
            classes,
            small_sums,
            input_grad,
            depth,
            logits,
            grad_messages,
            norm_one,
            norm_two,
            norm_three,
            heads_norm,
        )
        every[0], grad_heads = lax.optimization_barrier((every[0], grad_heads))
        narrow = (1, 7, 8)
        outs = [each.T if k in narrow else each for k, each in enumerate(every)]
        outs.insert(6, grad_heads.astype(F32))
        return tuple(outs[:12]) + tuple(each[0] for each in outs[12:])
    else:
        logits = logits[:, :classes]
        normed_one, unit_one, scale_one = normalize(
            reduced, sums_one[0], sums_one[1], pixel_count, gain_mid[0], shift_mid[0]
        )
        normed_two, unit_two, scale_two = normalize(
            spatial, sums_two[0], sums_two[1], pixel_count, gain_mid[1], shift_mid[1]
        )
        normed_three, unit_three, scale_three = normalize(
            expanded, sums_three[0], sums_three[1], pixel_count, gain_wide, shift_wide
        )
        pre_act = normed_three + inputs.astype(F32)
        pre_grad = trunk_grad.astype(F32) * silu_slope(pre_act)
        expand_raw, grad_gain_wide, grad_shift_wide = norm_back(
            pre_grad, unit_three, scale_three, gain_wide, living, pixel_count, everyone
        )
        expand_low = expand_raw.astype(BF16)
        expand_local = inner_rows(hidden_two, expand_low).astype(BF16)
        hidden_two_grad = against(expand_low, w_expand)
        spatial_raw, gain_grad_two, shift_grad_two = norm_back(
            hidden_two_grad * silu_slope(normed_two),
            unit_two,
            scale_two,
            gain_mid[1],
            living,
            pixel_count,
            everyone,
        )
        spatial_low = spatial_raw.astype(BF16)
        hidden_one_grad, spatial_local = rows_back(
            zero, spatial_low, hidden_one, w_spatial, shifts_own[:, None], 1, F32
        )
        reduced_raw, gain_grad_one, shift_grad_one = norm_back(
            hidden_one_grad * silu_slope(normed_one),
            unit_one,
            scale_one,
            gain_mid[0],
            living,
            pixel_count,
            everyone,
        )
        reduced_low = reduced_raw.astype(BF16)
        reduce_local = inner_rows(inputs, reduced_low).astype(BF16)
        input_grad = pre_grad + against(reduced_low, w_reduce)
        grad_expand = scatter_rep(expand_local)
        grad_spatial = scatter_rep(spatial_local)
        grad_reduce = scatter_rep(reduce_local)
        grad_classes = scatter_rep(classes_local)
        pieces = [
            gates_share.astype(BF16),
            grad_expand.reshape(-1, middle),
            grad_spatial,
            grad_classes.reshape(-1, middle),
        ]
        early = total_dp(jnp.concatenate(pieces, 0))
        rows = [piece.shape[0] for piece in pieces]
        starts = [sum(rows[:k]) for k in range(4)]
        grad_gates, expand_sum, grad_spatial, classes_sum = [
            early[at : at + size] for at, size in zip(starts, rows)
        ]
        grad_expand = expand_sum.reshape(grad_expand.shape)
        grad_classes = classes_sum.reshape(grad_classes.shape)
        grad_reduce = total_dp(grad_reduce)
        grad_gain_mid = jnp.stack([gain_grad_one, gain_grad_two], 0)
        grad_shift_mid = jnp.stack([shift_grad_one, shift_grad_two], 0)
    head_norms = lax.all_gather(
        head_norm, "rep", axis=1, tiled=True
    )
    return (
        depth,
        logits,
        input_grad,
        grad_reduce,
        grad_spatial,
        grad_expand,
        grad_heads.astype(F32),
        grad_gates,
        grad_messages.astype(F32),
        grad_classes,
        grad_gain_mid,
        grad_shift_mid,
        grad_gain_wide,
        grad_shift_wide,
        head_norms[0],
        head_norms[1],
    )


def solution(mesh):
    in_specs = (
        P(("dp", "rep"), None),
        P(),
        P(("dp", "rep")),
        P(("dp", "rep"), None),
        P(),
        P(),
        P(),
        P("rep", None),
        P(),
        P("rep", None),
        P(),
        P(),
        P(),
        P(),
        P(),
        P(),
        P(),
    )
    out_specs = (
        P(("dp", "rep"), None),
        P(("dp", "rep"), None),
        P(("dp", "rep"), None),
        P("rep", None),
        P("rep", None),
        P("rep", None),
        P("rep", "dp"),
        P("rep", None),
        P("rep", "dp"),
        P("rep", None),
        P(),
        P(),
        P(),
        P(),
        P(),
        P(),
    )
    return jax.shard_map(shards, mesh=mesh, in_specs=in_specs, out_specs=out_specs, check_vma=False)
```

```python
import functools

import jax
import jax.numpy as jnp
from jax import lax
from jax.experimental import pallas as pl
from jax.experimental.pallas import tpu as pltpu
from jax.sharding import PartitionSpec as P

EPS = 1e-05
F32 = jnp.float32
BF16 = jnp.bfloat16
VMEM_LIMIT = 60 * 2**20


def geometry(layout, span):
    position = jnp.arange(span, dtype=jnp.int32)
    height = layout[:, 0:1]
    map_width = layout[:, 1:2]
    images = layout[:, 2:3]
    map_area = height * map_width
    inside = position[None, :] % map_area
    row_of = inside // map_width
    col_of = inside % map_width
    living = position[None, :] < images * map_area
    return (row_of, col_of, living, height, map_width)


def neighbours(shape_info, dilation):
    row_of, col_of, living, height, map_width = shape_info
    span = row_of.shape[1]
    position = jnp.arange(span, dtype=jnp.int32)
    every = []
    for step_row in (-1, 0, 1):
        for step_col in (-1, 0, 1):
            target_row = row_of + dilation * step_row
            target_col = col_of + dilation * step_col
            inside = (
                living
                & (target_row >= 0)
                & (target_row < height)
                & (target_col >= 0)
                & (target_col < map_width)
            )
            neighbour = position[None, :] + dilation * (step_row * map_width + step_col)
            every.append(jnp.where(inside, neighbour, -1))
    return jnp.concatenate(every, 0).T


def shift_matrices(shape_info, dilation):
    devices, span = shape_info[0].shape
    picks = neighbours(shape_info, dilation).T.reshape(9, devices, span, 1)
    return (picks == jnp.arange(span, dtype=jnp.int32)).astype(BF16)


def product(left_side, right_side):
    return jnp.dot(left_side, right_side, preferred_element_type=F32)


def inner_rows(left_side, right_side):
    return lax.dot_general(
        left_side, right_side, (((0,), (0,)), ((), ())), preferred_element_type=F32
    )


def against(left_side, right_side):
    return lax.dot_general(
        left_side, right_side, (((1,), (1,)), ((), ())), preferred_element_type=F32
    )


def params():
    return pltpu.CompilerParams(vmem_limit_bytes=VMEM_LIMIT)


def cost(flops, moved):
    return pl.CostEstimate(flops=flops, bytes_accessed=moved, transcendentals=0)


def shifted(g_ref, s_ref):
    blocks, span = s_ref.shape[1], s_ref.shape[2]
    return jnp.concatenate(
        [
            inner_rows(s_ref[0, k], g_ref[pl.ds(k * span, span), :]).astype(BF16)
            for k in range(blocks)
        ],
        0,
    )


def heads_weight_kernel(g_ref, u_ref, s_ref, out_ref):
    taken = shifted(g_ref, s_ref)
    step = 512
    for c in range(0, u_ref.shape[1], step):
        out_ref[:, c : c + step] = inner_rows(taken, u_ref[:, c : c + step]).astype(out_ref.dtype)


def heads_weight(g, u, shifts):
    rows, outs = g.shape
    wide = u.shape[1]
    taps, blocks, span, _ = shifts.shape
    return pl.pallas_call(
        heads_weight_kernel,
        grid=(taps,),
        in_specs=[
            pl.BlockSpec((rows, outs), lambda t: (0, 0)),
            pl.BlockSpec((rows, wide), lambda t: (0, 0)),
            pl.BlockSpec((1, blocks, span, span), lambda t: (t, 0, 0, 0)),
        ],
        out_specs=pl.BlockSpec((outs, wide), lambda t: (0, t)),
        out_shape=jax.ShapeDtypeStruct((outs, taps * wide), BF16),
        compiler_params=params(),
        cost_estimate=cost(2 * rows * wide * outs * taps, outs * taps * wide * 2),
        name="heads_weight",
    )(g, u, shifts)


def rows_back_kernel(halves, first_ref, g_ref, u_ref, w_ref, s_ref, du_ref, dw_ref, total):
    step = pl.program_id(0)
    taken = shifted(g_ref, s_ref)
    depth = w_ref.shape[0]
    which = (step + first_ref[0]) % halves

    @pl.when(step == 0)
    def _():
        total[...] = jnp.zeros_like(total)

    total[which] += against(taken, w_ref[...])
    dw_ref[...] = inner_rows(u_ref[...], taken).astype(dw_ref.dtype)

    @pl.when(step == pl.num_programs(0) - 1)
    def _():
        for k in range(halves):
            du_ref[:, k * depth : (k + 1) * depth] = total[k].astype(du_ref.dtype)


def rows_back(first, g, u, w, shifts, halves, kind):
    rows, outs = g.shape
    depth = u.shape[1] // halves
    steps = w.shape[0] // depth
    taps, blocks, span, _ = shifts.shape
    return pl.pallas_call(
        functools.partial(rows_back_kernel, halves),
        grid_spec=pltpu.PrefetchScalarGridSpec(
            num_scalar_prefetch=1,
            grid=(steps,),
            in_specs=[
                pl.BlockSpec((rows, outs), lambda b, f: (0, 0)),
                pl.BlockSpec((rows, depth), lambda b, f: (0, (b + f[0]) % halves)),
                pl.BlockSpec((depth, outs), lambda b, f: (b, 0)),
                pl.BlockSpec((1, blocks, span, span), lambda b, f: ((b + f[0]) // halves, 0, 0, 0)),
            ],
            out_specs=[
                pl.BlockSpec((rows, halves * depth), lambda b, f: (0, 0)),
                pl.BlockSpec((depth, outs), lambda b, f: (b, 0)),
            ],
            scratch_shapes=[pltpu.VMEM((halves, rows, depth), F32)],
        ),
        out_shape=[
            jax.ShapeDtypeStruct((rows, halves * depth), kind),
            jax.ShapeDtypeStruct(w.shape, BF16),
        ],
        compiler_params=params(),
        cost_estimate=cost(4 * rows * w.size, w.size * 4),
        name="rows_back",
    )(first, g, u, w, shifts)


def send_to(axis, to, src, dst, send_sem, recv_sem):
    return pltpu.make_async_remote_copy(
        src_ref=src,
        dst_ref=dst,
        send_sem=send_sem,
        recv_sem=recv_sem,
        device_id={axis: to},
        device_id_type=MESH,
    )


def total_along(axis, size, block, slots, send_sems, recv_sems, meanwhile=None):
    me = lax.axis_index(axis)
    others = [lax.rem(me + k, size) for k in range(1, size)]
    for other in others:
        send_to(axis, other, block, slots.at[me], send_sems.at[other], recv_sems.at[me]).start()
    slots[me] = block[...]
    if meanwhile is not None:
        meanwhile()
    for other in others:
        copy = send_to(
            axis, other, block, slots.at[other], send_sems.at[other], recv_sems.at[other]
        )
        copy.wait_recv()
        copy.wait_send()
    total = slots[0]
    for k in range(1, size):
        total = total + slots[k]
    return total


def place_in_map(layout_ref, device, span):
    position = lax.broadcasted_iota(jnp.int32, (span, 1), 0)
    large = layout_ref[device, 1] == 16
    row_of = jnp.where(large, position // 16, (position % 64) // 8)
    col_of = jnp.where(large, position % 16, position % 8)
    return position, row_of, col_of


def live_mask(layout_ref, device, span):
    position = lax.broadcasted_iota(jnp.int32, (span, 1), 0)
    return position < layout_ref[device, 0] * layout_ref[device, 1] * layout_ref[device, 2]


def live_column(layout_ref, device, span):
    return jnp.where(live_mask(layout_ref, device, span), 1.0, 0.0)


def inverse_count(areas_ref, span):
    areas = areas_ref[:, 0:1] * areas_ref[:, 1:2] * areas_ref[:, 2:3]
    return 1.0 / jnp.sum(jnp.minimum(areas, span).astype(F32), 0, keepdims=True)


def shift_block(layout_ref, device, dilation, tap, span):
    position, row_of, col_of = place_in_map(layout_ref, device, span)
    height, map_width = layout_ref[device, 0], layout_ref[device, 1]
    step_row, step_col = dilation * (tap // 3 - 1), dilation * (tap % 3 - 1)
    target_row, target_col = row_of + step_row, col_of + step_col
    inside = (
        live_mask(layout_ref, device, span)
        & (target_row >= 0)
        & (target_row < height)
        & (target_col >= 0)
        & (target_col < map_width)
    )
    neighbour = jnp.where(inside, position + step_row * map_width + step_col, -1)
    lanes = lax.broadcasted_iota(jnp.int32, (span, span), 1)
    return jnp.where(neighbour == lanes, 1.0, 0.0).astype(BF16)


def shift_in_maps(extent, tap, span, dilation=1):
    position = lax.broadcasted_iota(jnp.int32, (span, 1), 0)
    row_of, col_of = (position % (extent * extent)) // extent, position % extent
    step_row, step_col = dilation * (tap // 3 - 1), dilation * (tap % 3 - 1)
    target_row, target_col = row_of + step_row, col_of + step_col
    inside = (
        (target_row >= 0) & (target_row < extent) & (target_col >= 0) & (target_col < extent)
    )
    neighbour = jnp.where(inside, position + step_row * extent + step_col, -1)
    lanes = lax.broadcasted_iota(jnp.int32, (span, span), 1)
    return jnp.where(neighbour == lanes, 1.0, 0.0).astype(BF16)


def trunk_kernel(
    split,
    sizes,
    in_ref,
    layout_ref,
    areas_ref,
    w_reduce_ref,
    w_spatial_hbm,
    w_expand_hbm,
    w_heads_hbm,
    gain_mid_ref,
    shift_mid_ref,
    gain_wide_ref,
    shift_wide_ref,
    reduced_ref,
    sums_one_ref,
    hidden_one_ref,
    spatial_ref,
    sums_two_ref,
    hidden_two_ref,
    expanded_ref,
    sums_three_ref,
    trunk_ref,
    headed_ref,
    own_shift_ref,
    all_shift_ref,
    *rest,
):
    if split:
        trunk_x, trunk_z, *rest = rest
    early_out = (reduced_ref, spatial_ref, expanded_ref, own_shift_ref, all_shift_ref)
    reduced_ref, spatial_ref, expanded_ref, own_shift_ref, all_shift_ref, early_sems, *rest = rest
    trunk_rest(
        early_out,
        early_sems,
        split,
        sizes,
        in_ref,
        layout_ref,
        areas_ref,
        w_reduce_ref,
        w_spatial_hbm,
        w_expand_hbm,
        w_heads_hbm,
        gain_mid_ref,
        shift_mid_ref,
        gain_wide_ref,
        shift_wide_ref,
        reduced_ref,
        sums_one_ref,
        hidden_one_ref,
        spatial_ref,
        sums_two_ref,
        hidden_two_ref,
        expanded_ref,
        sums_three_ref,
        trunk_ref,
        headed_ref,
        own_shift_ref,
        all_shift_ref,
        (trunk_x, trunk_z) if split else (),
        *rest,
    )


def trunk_rest(
    early_out,
    early_sems,
    split,
    sizes,
    in_ref,
    layout_ref,
    areas_ref,
    w_reduce_ref,
    w_spatial_hbm,
    w_expand_hbm,
    w_heads_hbm,
    gain_mid_ref,
    shift_mid_ref,
    gain_wide_ref,
    shift_wide_ref,
    reduced_ref,
    sums_one_ref,
    hidden_one_ref,
    spatial_ref,
    sums_two_ref,
    hidden_two_ref,
    expanded_ref,
    sums_three_ref,
    trunk_ref,
    headed_ref,
    own_shift_ref,
    all_shift_ref,
    afar,
    w_spatial_ref,
    w_expand_ref,
    w_heads_ref,
    block_mid,
    block_wide,
    slots_mid_rep,
    slots_mid_dp,
    slots_wide_rep,
    slots_wide_dp,
    load_sems,
    rep_send,
    rep_recv,
    dp_send,
    dp_recv,
    gather_send,
    gather_recv,
    away_send,
    away_recv,
):
    n_rep, n_dp = sizes
    rep = lax.axis_index("rep")
    par, upper = lax.rem(rep, 2), rep // 2
    mate, far = rep + 1 - 2 * par, rep + 2 - 4 * upper
    span, wide = in_ref.shape
    middle = w_reduce_ref.shape[1]
    taps = own_shift_ref.shape[0]
    loads = [
        pltpu.make_async_copy(w_spatial_hbm, w_spatial_ref, load_sems.at[0]),
        pltpu.make_async_copy(w_expand_hbm, w_expand_ref, load_sems.at[1]),
    ]
    heads_load = pltpu.make_async_copy(w_heads_hbm, w_heads_ref, load_sems.at[2])
    for load in loads:
        load.start()
    heads_load.start()

    barrier = pltpu.get_barrier_semaphore()
    for axis, size in (("rep", n_rep), ("dp", n_dp)):
        me = lax.axis_index(axis)
        for k in range(1, size):
            pl.semaphore_signal(
                barrier, inc=1, device_id={axis: lax.rem(me + k, size)}, device_id_type=MESH
            )
    first_row = lax.axis_index("dp") * n_rep
    live = live_column(layout_ref, first_row + rep, span)
    inverse = inverse_count(areas_ref, span)

    def make_own():
        for t in range(taps):
            own_shift_ref[t] = shift_block(layout_ref, first_row + rep, 2, t, span)

    def make_all(first, last):
        def fill():
            for t in range(first, last):
                for p in range(n_rep):
                    all_shift_ref[t, p] = shift_block(layout_ref, first_row + p, 1, t, span)

        return fill

    def everywhere(number, value_ref, blocks, rep_slots, dp_slots, meanwhile, later):
        masked = live * value_ref[...]
        blocks[0, 0:1, :] = jnp.sum(masked, 0, keepdims=True)
        blocks[0, 1:2, :] = jnp.sum(masked * value_ref[...], 0, keepdims=True)
        if number == 0:
            pl.semaphore_wait(barrier, n_rep + n_dp - 2)
        blocks[1] = total_along(
            "rep", n_rep, blocks.at[0], rep_slots, rep_send.at[number], rep_recv.at[number], meanwhile
        )
        return total_along(
            "dp", n_dp, blocks.at[1], dp_slots, dp_send.at[number], dp_recv.at[number], later
        )

    def normed(value, sums, gain, shift):
        center = sums[0:1] * inverse
        scaling = lax.rsqrt(sums[1:2] * inverse - center * center + EPS)
        return (value - center) * (scaling * gain) + shift

    def silu(value):
        return value * jax.nn.sigmoid(value)

    reduced_ref[...] = product(in_ref[...], w_reduce_ref[...])
    sums = everywhere(
        0, reduced_ref, block_mid.at[0], slots_mid_rep.at[0], slots_mid_dp.at[0], make_own, None
    )
    sums_one_ref[...] = sums
    hidden_one_ref[...] = silu(
        normed(reduced_ref[...], sums, gain_mid_ref[0:1, :], shift_mid_ref[0:1, :])
    ).astype(BF16)
    loads[0].wait()
    spatial_ref[...] = jnp.zeros_like(spatial_ref)

    @pl.loop(0, taps)
    def _(t):
        moved = product(own_shift_ref[t], hidden_one_ref[...]).astype(BF16)
        at = pl.ds(pl.multiple_of(t * middle, middle), middle)
        spatial_ref[...] += product(moved, w_spatial_ref[at, :])

    sums = everywhere(
        1, spatial_ref, block_mid.at[1], slots_mid_rep.at[1], slots_mid_dp.at[1], make_all(0, 5), None
    )
    sums_two_ref[...] = sums
    hidden_two_ref[...] = silu(
        normed(spatial_ref[...], sums, gain_mid_ref[1:2, :], shift_mid_ref[1:2, :])
    ).astype(BF16)
    loads[1].wait()
    expanded_ref[...] = product(hidden_two_ref[...], w_expand_ref[...])
    sums = everywhere(
        2, expanded_ref, block_wide, slots_wide_rep, slots_wide_dp, make_all(5, 9), None
    )
    sums_three_ref[...] = sums

    own_rows = pl.ds(pl.multiple_of(par * span, span), span)
    mate_rows = pl.ds(pl.multiple_of((1 - par) * span, span), span)
    pre = normed(expanded_ref[...], sums, gain_wide_ref[...], shift_wide_ref[...])
    trunk_ref[upper, own_rows, :] = silu(pre + in_ref[...].astype(F32)).astype(BF16)
    parts = 4
    piece = span // parts

    def rows(parity, k):
        return pl.ds(pl.multiple_of(parity * span + k * piece, piece), piece)

    def across(side, k):
        at = trunk_ref.at[side, rows(par, k)]
        return send_to("rep", far, at, at, gather_send.at[k], gather_recv.at[k])

    def own_pass(parity):
        at = trunk_ref.at[upper, pl.ds(pl.multiple_of(parity * span, span), span)]
        return send_to("rep", mate, at, at, gather_send.at[parts], gather_recv.at[parts])

    def far_pass(parity, k):
        at = trunk_ref.at[1 - upper, rows(parity, k)]
        slot = parts + 1 + k
        return send_to("rep", mate, at, at, gather_send.at[slot], gather_recv.at[slot])

    dp = lax.axis_index("dp")
    neighbours = (dp + 1 - 2 * lax.rem(dp, 2), dp + 2 - 4 * lax.rem(dp // 2, 2))

    def away(number):
        return send_to(
            "dp",
            neighbours[number],
            trunk_ref.at[upper, own_rows],
            afar[number],
            away_send.at[number],
            away_recv.at[number],
        )

    for k in range(parts):
        across(upper, k).start()
    own_pass(par).start()
    if split:
        for number in range(2):
            away(number).start()
    leaving = [
        pltpu.make_async_copy(src, dst, early_sems.at[k])
        for k, (src, dst) in enumerate(
            zip((reduced_ref, spatial_ref, expanded_ref, own_shift_ref, all_shift_ref), early_out)
        )
    ]
    for copy in leaving:
        copy.start()
    headed_ref[...] = jnp.zeros_like(headed_ref)
    own_pass(1 - par).wait_recv()
    heads_load.wait()

    def convolve(side):
        @pl.loop(0, taps)
        def _(t):
            at = pl.ds(pl.multiple_of(t * wide, wide), wide)
            y = against(trunk_ref[side], w_heads_ref[:, at]).astype(BF16)
            for k in range(2):
                place = pl.ds(k * span, span)
                headed_ref[side, place, :] += product(
                    all_shift_ref[t, 2 * side + k], y[k * span : (k + 1) * span]
                )

    convolve(upper)
    for k in range(parts):
        across(1 - upper, k).wait_recv()
        far_pass(par, k).start()
    for k in range(parts):
        far_pass(1 - par, k).wait_recv()
    convolve(1 - upper)
    for k in range(parts):
        across(upper, k).wait_send()
        far_pass(par, k).wait_send()
    own_pass(par).wait_send()
    if split:
        for number in range(2):
            away(number).wait_send()
            away(number).wait_recv()
    for copy in leaving:
        copy.wait()


def trunk_forward(
    split,
    inputs,
    layout,
    w_reduce,
    w_spatial,
    w_expand,
    w_heads,
    gain_mid,
    shift_mid,
    gain_wide,
    shift_wide,
):
    span, wide = inputs.shape
    middle = w_reduce.shape[1]
    n_rep, n_dp = lax.axis_size("rep"), lax.axis_size("dp")
    taps = 9
    vmem = pl.BlockSpec(memory_space=pltpu.VMEM)
    hbm = pl.BlockSpec(memory_space=pl.ANY)
    smem = pl.BlockSpec(memory_space=pltpu.SMEM)
    dma = pltpu.SemaphoreType.DMA
    shape = jax.ShapeDtypeStruct
    return pl.pallas_call(
        functools.partial(trunk_kernel, split, (n_rep, n_dp)),
        in_specs=[vmem, smem, vmem, vmem] + [hbm] * 3 + [vmem] * 4,
        out_specs=[hbm if k in (0, 3, 6, 10, 11) else vmem for k in range(12)] + [hbm] * (2 * split),
        out_shape=[
            shape((span, middle), F32),
            shape((2, middle), F32),
            shape((span, middle), BF16),
            shape((span, middle), F32),
            shape((2, middle), F32),
            shape((span, middle), BF16),
            shape((span, wide), F32),
            shape((2, wide), F32),
            shape((2, 2 * span, wide), BF16),
            shape((2, 2 * span, w_heads.shape[0]), F32),
            shape((taps, span, span), BF16),
            shape((taps, n_rep, span, span), BF16),
        ]
        + [shape((span, wide), BF16)] * (2 * split),
        scratch_shapes=[
            pltpu.VMEM((span, middle), F32),
            pltpu.VMEM((span, middle), F32),
            pltpu.VMEM((span, wide), F32),
            pltpu.VMEM((taps, span, span), BF16),
            pltpu.VMEM((taps, n_rep, span, span), BF16),
            dma((5,)),
            pltpu.VMEM(w_spatial.shape, BF16),
            pltpu.VMEM(w_expand.shape, BF16),
            pltpu.VMEM(w_heads.shape, BF16),
            pltpu.VMEM((2, 2, 2, middle), F32),
            pltpu.VMEM((2, 2, wide), F32),
            pltpu.VMEM((2, n_rep, 2, middle), F32),
            pltpu.VMEM((2, n_dp, 2, middle), F32),
            pltpu.VMEM((n_rep, 2, wide), F32),
            pltpu.VMEM((n_dp, 2, wide), F32),
            dma((3,)),
            dma((3, n_rep)),
            dma((3, n_rep)),
            dma((3, n_dp)),
            dma((3, n_dp)),
            dma((9,)),
            dma((9,)),
            dma((2,)),
            dma((2,)),
        ],
        compiler_params=pltpu.CompilerParams(
            collective_id=10, has_side_effects=True, vmem_limit_bytes=VMEM_LIMIT
        ),
        name="trunk_forward",
    )(
        inputs,
        layout,
        layout,
        w_reduce,
        w_spatial,
        w_expand,
        w_heads,
        gain_mid,
        shift_mid,
        gain_wide[None, :],
        shift_wide[None, :],
    )


MOVES = 38


def message_kernel(split, n_dp, classes, *refs):
    refs = list(refs)

    def take(count):
        taken, refs[:count] = refs[:count], []
        return taken

    layout_ref, areas_ref, headed_ref, s_hbm, w_hbm, gates_w_ref, classes_w_ref = take(7)
    gain_ref, shift_ref, cot_ref, labels_ref = take(4)
    if split:
        trunk_x, trunk_z, trunk_hbm = take(3)
    depth_ref, logits_ref, gates_ref, classes_ref, low_ref, norm_ref = take(6)
    if split:
        out_ref, far_x, far_z, mate_x, mate_z, trunk_xz, mate_xz = take(7)
    else:
        heads_ref, gm_ref = take(2)
    w_ref, live_ref, acc_ref, acc_in, stream_ref, direct_ref, cot_in, labels_in = take(8)
    depth_out, logits_out, picked_ref, far_ref, near_ref = take(5)
    core_out, core_in, far_out, far_in, near_out, near_in = take(6)
    sums_ref, slots_ref, load_sem, send, recv, dp_send, dp_recv = take(7)
    s_ref, shift_sem = take(2)
    if split:
        heads_ref, gm_ref, beside_ref, cut_own, cut_out, cut_in, cut_taken = take(7)

    rep = lax.axis_index("rep")
    par, upper = lax.rem(rep, 2), rep // 2
    mate, far = rep + 1 - 2 * par, rep + 2 - 4 * upper
    first_row = lax.axis_index("dp") * 4
    side_x = lax.rem(lax.axis_index("dp"), 2)
    beside = lax.axis_index("dp") + 1 - 2 * side_x
    side_z = lax.rem(lax.axis_index("dp") // 2, 2)
    along = lax.axis_index("dp") + 2 - 4 * side_z
    span = s_ref.shape[2]
    middle = headed_ref.shape[2]
    small = middle // 2
    load = pltpu.make_async_copy(w_hbm, w_ref, load_sem)
    shift_load = pltpu.make_async_copy(s_hbm, s_ref, shift_sem)
    shift_load.start()
    load.start()

    barrier = pltpu.get_barrier_semaphore()
    me_dp = lax.axis_index("dp")
    for to in (mate, far):
        pl.semaphore_signal(barrier, inc=1, device_id={"rep": to}, device_id_type=MESH)
    for k in range(1, n_dp):
        pl.semaphore_signal(
            barrier, inc=1, device_id={"dp": lax.rem(me_dp + k, n_dp)}, device_id_type=MESH
        )

    def move(number, src, dst, to, axis="rep"):
        return send_to(axis, to, src, dst, send.at[number], recv.at[number])

    def block(parity):
        return pl.ds(pl.multiple_of(parity * span, span), span)

    for p in range(4):
        live_ref[p // 2, (p % 2) * span : (p % 2 + 1) * span, :] = live_column(
            layout_ref, first_row + p, span
        )
    inverse = inverse_count(areas_ref, span)

    def add_up(number, left, right):
        sums_ref[number, 0:1, :] = left
        sums_ref[number, 1:2, :] = right
        return total_along(
            "dp", n_dp, sums_ref.at[number], slots_ref.at[number], dp_send.at[number], dp_recv.at[number]
        )

    def column_sum(value):
        return jnp.sum(value, 0, keepdims=True)

    left, right = 0.0, 0.0
    for side in range(2):
        masked = live_ref[side] * headed_ref[side]
        left = left + column_sum(masked)
        right = right + column_sum(masked * headed_ref[side])
    pl.semaphore_wait(barrier, n_dp + 1)
    move(9, cot_ref, cot_in, far).start()
    move(10, labels_ref, labels_in, far).start()
    sums = add_up(0, left, right)
    if split:
        lower_side = 1 - upper
        own_block = trunk_hbm.at[lower_side, block(par)]
        copy_x = move(29, trunk_x, far_x, far)
        copy_z = move(30, own_block, far_z, along, "dp")
        near_xz = move(31, trunk_x, trunk_xz.at[upper], along, "dp")
        far_xz = move(32, far_x, trunk_xz.at[lower_side], along, "dp")
        to_mate = [
            move(33, trunk_x, mate_x.at[upper], mate),
            move(34, trunk_z, mate_z.at[upper], mate),
            move(35, far_x, mate_x.at[lower_side], mate),
            move(36, far_z, mate_z.at[lower_side], mate),
            move(37, trunk_xz, mate_xz, mate),
        ]
        near_xz.start()
        copy_z.start()

    center = sums[0:1] * inverse
    scaling = lax.rsqrt(sums[1:2] * inverse - center * center + EPS)
    own_lanes = pl.ds(pl.multiple_of(rep * middle, middle), middle)
    gain = gain_ref[:, own_lanes]
    shift = shift_ref[:, own_lanes]

    def across(head, part):
        at = heads_ref.at[head, part // 2, pl.ds((part % 2) * span, span)]
        return move(part, at, at, far)

    def relay(head, part):
        at = heads_ref.at[head, part // 2, pl.ds((part % 2) * span, span)]
        return move(5 + part, at, at, mate)

    def own_head(head):
        return move(4, heads_ref.at[head], heads_ref.at[head], mate)

    for side in range(2):
        normed = (headed_ref[side] - center) * (scaling * gain) + shift
        heads_ref[rep, side] = (normed * jax.nn.sigmoid(normed)).astype(BF16)
        for k in range(2):
            across(rep, 2 * side + k).start()
    own_head(rep).start()
    if split:
        x_own = move(24, heads_ref.at[rep], beside_ref.at[rep], beside, "dp")
        x_far = move(25, heads_ref.at[far], beside_ref.at[far], beside, "dp")
        x_own.start()
        copy_x.start()

    def tap_of(i):
        return par * 5 + i

    def row_of(i, head_at):
        return pl.multiple_of(par * (3 * small) + i * (3 * middle) + head_at * middle, small)

    half_row = (1 - par) * (12 * middle)
    full_row = pl.multiple_of(half_row + par * small, small)
    part_row = pl.multiple_of(half_row + (1 - par) * middle, small)
    part_lanes = pl.ds(pl.multiple_of(par * small, small), small)
    local = 2 * upper
    remote = 2 * (1 - upper)
    local_head = 1 + upper
    part_head = 2 - upper
    full_head = 2 * par + 1 - upper

    def wrows(row, depth):
        return w_ref[pl.ds(row, depth), :]

    def gather_taps(tap, side, y):
        y = y.astype(BF16)
        for k in range(2):
            acc_ref[side, k * span : (k + 1) * span, :] += product(
                s_ref[tap, 2 * side + k], y[k * span : (k + 1) * span]
            )

    acc_ref[...] = jnp.zeros_like(acc_ref)
    own_head(mate).wait_recv()
    shift_load.wait()
    load.wait()

    @pl.loop(0, 8)
    def _(n):
        i, side = n // 2, n % 2
        gather_taps(
            tap_of(i), side, product(heads_ref[local_head, side], wrows(row_of(i, local), middle))
        )

    @pl.when(par == upper)
    def _():
        @pl.loop(0, 2)
        def _(side):
            gather_taps(4, side, product(heads_ref[full_head, side], wrows(full_row, middle)))

    for part in range(4):
        across(far, part).wait_recv()
        relay(far, part).start()
    if split:
        x_far.start()
    for part in range(4):
        relay(far + 1 - 2 * par, part).wait_recv()

    @pl.loop(0, 8)
    def _(n):
        i, side = n // 2, n % 2
        y = product(heads_ref[remote, side], wrows(row_of(i, 1 - upper), middle))
        y = y + product(heads_ref[remote + 1, side], wrows(row_of(i, 2 - upper), middle))
        gather_taps(tap_of(i), side, y)

    @pl.loop(0, 2)
    def _(side):
        gather_taps(
            4, side, product(heads_ref[part_head, side, :, part_lanes], wrows(part_row, small))
        )

    @pl.when(par != upper)
    def _():
        @pl.loop(0, 2)
        def _(side):
            gather_taps(4, side, product(heads_ref[full_head, side], wrows(full_row, middle)))

    def acc_move(side):
        return move(11 + side, acc_ref.at[side, block(1 - par)], acc_in.at[side], mate)

    for side in range(2):
        acc_move(side).start()

    own_gates = gates_w_ref[pl.ds(pl.multiple_of(upper * middle, middle), middle), :]
    classes_ref[...] = jnp.zeros_like(classes_ref)
    move(9, cot_ref, cot_in, far).wait_recv()
    move(10, labels_ref, labels_in, far).wait_recv()
    gates_total = 0.0

    def gm_move(side, parity):
        at = gm_ref.at[side, block(parity)]
        return move(13 + side, at, at, mate)

    for side in range(2):
        acc_move(side).wait_recv()
        message = acc_ref[side, block(par), :] + acc_in[side]
        stream = heads_ref[3 * upper, side, block(par), :]
        gate = jax.nn.sigmoid(product(stream, own_gates))
        full = stream.astype(F32) + gate * message
        alive = live_ref[side, block(par), :]

        @pl.when(upper == 0)
        def _():
            cot = (cot_ref if side == 0 else cot_in)[...].astype(F32)
            stream_ref[side] = alive * cot
            (depth_ref if side == 0 else depth_out)[...] = alive * full

        @pl.when(upper == 1)
        def _():
            labels = (labels_in if side == 0 else labels_ref)[...]
            full_low = full.astype(BF16)
            logits = product(full_low, classes_w_ref[...])
            (logits_out if side == 0 else logits_ref)[...] = alive * logits
            lanes = lax.broadcasted_iota(jnp.int32, logits.shape, 1)
            shown = jnp.where(lanes < classes, logits, -1e30)
            grown = jnp.exp(shown - jnp.max(shown, 1, keepdims=True))
            probs = grown / jnp.sum(grown, 1, keepdims=True)
            slope = (alive * (probs - jnp.where(lanes == labels, 1.0, 0.0))).astype(BF16)
            classes_ref[...] += inner_rows(full_low, slope)
            stream_ref[side] = against(slope, classes_w_ref[...])

        grad = stream_ref[side]
        grad_gate = (grad * message * gate * (1.0 - gate)).astype(BF16)
        gm_ref[side, block(par), :] = (grad * gate).astype(BF16)
        gm_move(side, par).start()
        gates_total = gates_total + inner_rows(stream, grad_gate)
        direct_ref[side] = grad + against(grad_gate, own_gates)

    gates_ref[...] = gates_total.astype(BF16)

    @pl.when(upper == 0)
    def _():
        move(15, depth_out, depth_ref, far).start()

    @pl.when(upper == 1)
    def _():
        move(16, logits_out, logits_ref, far).start()

    for side in range(2):
        gm_move(side, 1 - par).wait_recv()
    if split:
        lanes = lax.broadcasted_iota(jnp.int32, (middle, small), 1)
        wanted = (lanes // 64) * 128 + lanes % 64
        source = lax.broadcasted_iota(jnp.int32, (middle, small), 0)
        for cut, which in ((cut_out, 1 - side_x), (cut_own, side_x)):
            pick = jnp.where(source == wanted + 64 * which, 1.0, 0.0).astype(BF16)
            for side in range(2):
                cut[side] = product(gm_ref[side], pick).astype(BF16)
        x_cut = move(28, cut_out, cut_in, beside, "dp")
        x_cut.start()

    @pl.loop(0, 10)
    def _(n):
        i, side = n // 2, n % 2
        tap = jnp.where(i == 4, 4, tap_of(i))
        for k in range(2):
            at = pl.ds(k * span, span)
            picked_ref[i, side, at, :] = inner_rows(
                s_ref[tap, 2 * side + k], gm_ref[side, at, :]
            ).astype(BF16)

    def taps_back(side, head_at):
        total = 0.0
        for i in range(4):
            total = total + against(picked_ref[i, side], wrows(row_of(i, head_at), middle))
        return total

    def core_move(side):
        return move(17 + side, core_out.at[side], core_in.at[side], mate)

    def far_move(part):
        at = pl.ds((part % 2) * span, span)
        return move(19 + part, far_out.at[part // 2, at], far_in.at[part // 2, at], far)

    @pl.loop(0, 2)
    def _(side):
        @pl.loop(0, 2)
        def _(j):
            far_ref[j, side] = taps_back(side, 1 - upper + j)

        far_ref[upper, side, :, part_lanes] += against(picked_ref[4, side], wrows(part_row, small))

        @pl.when(par != upper)
        def _():
            far_ref[2 * par - 1 + upper, side] += against(
                picked_ref[4, side], wrows(full_row, middle)
            )

        core_out[side] = far_ref[1 - par, side].astype(BF16)
        core_move(side).start()

    for side in range(2):
        core_move(side).wait_recv()
        for part in (2 * side, 2 * side + 1):
            at = pl.ds((part % 2) * span, span)
            far_out[side, at, :] = (
                far_ref[par, side, at, :] + core_in[side, at, :].astype(F32)
            ).astype(BF16)
            far_move(part).start()

    if split:
        copy_x.wait_recv()
        far_xz.start()

    @pl.loop(0, 2)
    def _(side):
        near_ref[side] = taps_back(side, local)

    @pl.when(par == upper)
    def _():
        @pl.loop(0, 2)
        def _(side):
            near_ref[side] += against(picked_ref[4, side], wrows(full_row, middle))

        near_out[...] = near_ref[...].astype(BF16)
        for side in range(2):
            near_ref[side, block(par), :] = direct_ref[side]
            near_ref[side, block(1 - par), :] = jnp.zeros((span, middle), F32)

    @pl.when(par != upper)
    def _():
        for side in range(2):
            near_out[side, block(par), :] = direct_ref[side].astype(BF16)
            near_out[side, block(1 - par), :] = jnp.zeros((span, middle), BF16)

    near_move = move(23, near_out, near_in, mate)
    near_move.start()

    if split:
        x_own.wait_recv()
        relay_own = move(26, beside_ref.at[rep], beside_ref.at[rep], mate)
        relay_own.start()
        x_far.wait_recv()
        relay_far = move(27, beside_ref.at[far], beside_ref.at[far], mate)
        relay_far.start()
        copy_z.wait_recv()
        for copy in to_mate[:4]:
            copy.start()
        x_cut.wait_recv()
        move(26, beside_ref.at[mate], beside_ref.at[mate], mate).wait_recv()
        other = far + 1 - 2 * par
        move(27, beside_ref.at[other], beside_ref.at[other], mate).wait_recv()

        def fill(tap):
            for p in range(4):
                at = pl.ds(p * span, span)
                cut_taken[0, :, at] = inner_rows(
                    cut_own[p // 2, pl.ds((p % 2) * span, span), :], s_ref[tap, p]
                ).astype(BF16)
                cut_taken[1, :, at] = inner_rows(
                    cut_in[p // 2, pl.ds((p % 2) * span, span), :],
                    shift_block(layout_ref, beside * 4 + p, 1, tap, span),
                ).astype(BF16)

        def gradient(head, lanes):
            total = 0.0
            for number, held in enumerate((heads_ref, beside_ref)):
                for side in range(2):
                    total = total + product(
                        cut_taken[number, :, side * 2 * span : (side + 1) * 2 * span],
                        held[head, side, :, lanes],
                    )
            return total.astype(BF16)

        @pl.loop(0, 4)
        def _(i):
            fill(tap_of(i))
            for at in range(3):
                for k in range(2):
                    row = pl.multiple_of(row_of(i, at) + k * small, small)
                    out_ref[:, pl.ds(row, small)] = gradient(
                        at + 1 - upper, pl.ds(k * small, small)
                    )

        fill(4)
        for k in range(2):
            row = pl.multiple_of(full_row + k * small, small)
            out_ref[:, pl.ds(row, small)] = gradient(full_head, pl.ds(k * small, small))
        out_ref[:, pl.ds(part_row, small)] = gradient(part_head, part_lanes)

    if split:
        near_xz.wait_recv()
        far_xz.wait_recv()
        to_mate[4].start()

    near_move.wait_recv()
    left, right = 0.0, 0.0

    def backward(side):
        unit = (headed_ref[side] - center) * scaling
        normed = unit * gain + shift
        sigma = jax.nn.sigmoid(normed)
        return unit, sigma * (1.0 + normed * (1.0 - sigma))

    for side in range(2):
        for part in (2 * side, 2 * side + 1):
            far_move(part).wait_recv()
        unit, slope = backward(side)
        grad = near_ref[side] + near_in[side].astype(F32) + far_in[side].astype(F32)
        grad = grad * slope
        near_ref[side] = grad
        masked = live_ref[side] * grad
        left = left + column_sum(masked * unit)
        right = right + column_sum(masked)
    sums = add_up(1, left, right)
    norm_ref[...] = sums
    for side in range(2):
        unit = (headed_ref[side] - center) * scaling
        low_ref[side] = (
            live_ref[side]
            * (gain * scaling)
            * (near_ref[side] - sums[1:2] * inverse - unit * (sums[0:1] * inverse))
        ).astype(BF16)

    for part in range(4):
        across(rep, part).wait_send()
        relay(far, part).wait_send()
        far_move(part).wait_send()
    own_head(rep).wait_send()
    move(9, cot_ref, cot_in, far).wait_send()
    move(10, labels_ref, labels_in, far).wait_send()
    for side in range(2):
        acc_move(side).wait_send()
        gm_move(side, par).wait_send()
    for side in range(2):
        core_move(side).wait_send()
    near_move.wait_send()

    @pl.when(upper == 0)
    def _():
        move(15, depth_out, depth_ref, far).wait_send()
        move(16, logits_out, logits_ref, far).wait_recv()

    @pl.when(upper == 1)
    def _():
        move(16, logits_out, logits_ref, far).wait_send()
        move(15, depth_out, depth_ref, far).wait_recv()

    if split:
        for copy in to_mate:
            copy.wait_recv()
            copy.wait_send()
        for copy in (x_own, x_far, x_cut, relay_own, relay_far, copy_x, copy_z, near_xz, far_xz):
            copy.wait_send()


def message_streams(
    split, layout, headed, shifts, w_messages, w_gates, w_classes, gain, shift, cot, labels, afar
):
    n_dp = lax.axis_size("dp")
    span, middle = cot.shape
    small = middle // 2
    classes = w_classes.shape[1]
    vmem = pl.BlockSpec(memory_space=pltpu.VMEM)
    dma = pltpu.SemaphoreType.DMA
    shape = jax.ShapeDtypeStruct
    halves = (2, 2 * span, middle)
    heads = (4, 2, 2 * span, middle)
    out_shape = [
        shape((span, middle), F32),
        shape((span, 128), F32),
        shape((middle, middle), BF16),
        shape((middle, 128), F32),
        shape(halves, BF16),
        shape((2, middle), F32),
    ]
    if split:
        out_shape += [shape((small, w_messages.shape[0]), BF16)] + [shape(afar[0].shape, BF16)] * 2
        out_shape += [shape((2,) + afar[0].shape, BF16)] * 4
    else:
        out_shape += [shape(heads, BF16), shape(halves, BF16)]
    scratch = [
        pltpu.VMEM(w_messages.shape, BF16),
        pltpu.VMEM((2, 2 * span, 1), F32),
        pltpu.VMEM(halves, F32),
        pltpu.VMEM((2, span, middle), F32),
        pltpu.VMEM((2, span, middle), F32),
        pltpu.VMEM((2, span, middle), F32),
        pltpu.VMEM((span, middle), BF16),
        pltpu.VMEM((span, 128), jnp.int32),
        pltpu.VMEM((span, middle), F32),
        pltpu.VMEM((span, 128), F32),
        pltpu.VMEM((5,) + halves, BF16),
        pltpu.VMEM((2,) + halves, F32),
        pltpu.VMEM(halves, F32),
        pltpu.VMEM(halves, BF16),
        pltpu.VMEM(halves, BF16),
        pltpu.VMEM(halves, BF16),
        pltpu.VMEM(halves, BF16),
        pltpu.VMEM(halves, BF16),
        pltpu.VMEM(halves, BF16),
        pltpu.VMEM((2, 2, middle), F32),
        pltpu.VMEM((2, n_dp, 2, middle), F32),
        dma,
        dma((MOVES,)),
        dma((MOVES,)),
        dma((2, n_dp)),
        dma((2, n_dp)),
        pltpu.VMEM(shifts.shape, BF16),
        dma,
    ]
    if split:
        scratch += [
            pltpu.VMEM(heads, BF16),
            pltpu.VMEM(halves, BF16),
            pltpu.VMEM(heads, BF16),
            pltpu.VMEM((2, 2 * span, small), BF16),
            pltpu.VMEM((2, 2 * span, small), BF16),
            pltpu.VMEM((2, 2 * span, small), BF16),
            pltpu.VMEM((2, small, 4 * span), BF16),
        ]
    return pl.pallas_call(
        functools.partial(message_kernel, split, n_dp, classes),
        in_specs=[pl.BlockSpec(memory_space=pltpu.SMEM)]
        + [vmem] * 2
        + [pl.BlockSpec(memory_space=pl.ANY)] * 2
        + [vmem] * 6
        + [pl.BlockSpec(memory_space=pl.ANY)] * len(afar),
        out_specs=[vmem] * 7 + [pl.BlockSpec(memory_space=pl.ANY) if split else vmem] * (len(out_shape) - 7),
        out_shape=out_shape,
        scratch_shapes=scratch,
        compiler_params=pltpu.CompilerParams(
            collective_id=11, has_side_effects=True, vmem_limit_bytes=VMEM_LIMIT
        ),
        name="message_streams",
    )(
        layout,
        layout,
        headed,
        shifts,
        w_messages,
        w_gates,
        jnp.pad(w_classes, ((0, 0), (0, 128 - classes))),
        gain[None, :],
        shift[None, :],
        cot,
        jnp.broadcast_to(labels[:, None], (span, 128)),
        *afar,
    )


def heads_taps(t_ref, low_ref, taken_ref, side):
    span = t_ref.shape[2]

    @pl.loop(0, taken_ref.shape[0])
    def _(t):
        for k in range(2):
            at = pl.ds(k * span, span)
            taken_ref[t, at, :] = inner_rows(t_ref[t, 2 * side + k], low_ref[side, at, :]).astype(
                BF16
            )


def heads_tile(c, taken_ref, w_ref, tile_ref):
    taps, _, _ = taken_ref.shape
    wide = w_ref.shape[1] // taps
    step = tile_ref.shape[1]
    total = 0.0
    for t in range(taps):
        at = pl.ds(pl.multiple_of(t * wide + c * step, step), step)
        total = total + product(taken_ref[t], w_ref[:, at])
    tile_ref[...] = total


def heads_loads(w_hbm, w_ref, sems):
    taps = sems.shape[0]
    wide = w_ref.shape[1] // taps
    spans = [pl.ds(t * wide, wide) for t in range(taps)]
    return [
        pltpu.make_async_copy(w_hbm.at[:, at], w_ref.at[:, at], sems.at[t])
        for t, at in enumerate(spans)
    ]


def meet(partners):
    barrier = pltpu.get_barrier_semaphore()
    for partner in partners:
        pl.semaphore_signal(barrier, inc=1, device_id=partner, device_id_type=MESH)
    pl.semaphore_wait(barrier, len(partners))


def heads_far_kernel(split, low_ref, s_ref, w_hbm, *refs):
    sum_ref, *refs = refs
    if split:
        low_x, low_z, *refs = refs
    w_ref, taken_ref, tile_ref, kept, core_out, core_in, load_sems, send, recv = refs
    rep, dp = lax.axis_index("rep"), lax.axis_index("dp")
    par, upper = lax.rem(rep, 2), rep // 2
    mate = rep + 1 - 2 * par
    beside, along = dp + 1 - 2 * lax.rem(dp, 2), dp + 2 - 4 * lax.rem(dp // 2, 2)
    span = s_ref.shape[2]
    tiles = sum_ref.shape[0]
    loads = heads_loads(w_hbm, w_ref, load_sems)
    for load in loads:
        load.start()
    meet([{"rep": mate}] + ([{"dp": beside}, {"dp": along}] if split else []))

    def block(parity):
        return pl.ds(pl.multiple_of(parity * span, span), span)

    if split:
        copy_x = send_to("dp", beside, low_ref, low_x, send.at[tiles], recv.at[tiles])
        copy_z = send_to("dp", along, low_ref, low_z, send.at[tiles + 1], recv.at[tiles + 1])
        copy_z.start()
        copy_x.start()

    def core_move(c):
        return send_to("rep", mate, core_out.at[c], core_in.at[c], send.at[c], recv.at[c])

    heads_taps(s_ref, low_ref, taken_ref, 1 - upper)
    for load in loads:
        load.wait()

    @pl.loop(0, tiles)
    def _(c):
        heads_tile(c, taken_ref, w_ref, tile_ref)
        core_out[c] = tile_ref[block(1 - par), :].astype(BF16)
        core_move(c).start()
        kept[c] = tile_ref[block(par), :]

    for c in range(tiles):
        core_move(c).wait_recv()
        sum_ref[c] = (kept[c] + core_in[c].astype(F32)).astype(BF16)
        core_move(c).wait_send()
    if split:
        for copy in (copy_x, copy_z):
            copy.wait_recv()
            copy.wait_send()


def heads_near_kernel(split, low_ref, s_ref, w_hbm, sum_ref, *refs):
    if split:
        low_z, *refs = refs
    out_ref, *refs = refs
    if split:
        low_xz, *refs = refs
    w_ref, taken_ref, tile_ref, kept, far_in, near_out, near_in, load_sems, send, recv = refs
    rep, dp = lax.axis_index("rep"), lax.axis_index("dp")
    par, upper = lax.rem(rep, 2), rep // 2
    mate, far = rep + 1 - 2 * par, rep + 2 - 4 * upper
    beside = dp + 1 - 2 * lax.rem(dp, 2)
    span = s_ref.shape[2]
    tiles = sum_ref.shape[0]
    step = tile_ref.shape[1]
    loads = heads_loads(w_hbm, w_ref, load_sems)
    for load in loads:
        load.start()
    meet([{"rep": mate}, {"rep": far}] + ([{"dp": beside}] if split else []))

    def block(parity):
        return pl.ds(pl.multiple_of(parity * span, span), span)

    def far_move(c):
        return send_to("rep", far, sum_ref.at[c], far_in.at[c], send.at[c], recv.at[c])

    def near_move(c):
        return send_to(
            "rep", mate, near_out.at[c], near_in.at[c], send.at[tiles + c], recv.at[tiles + c]
        )

    for c in range(tiles):
        far_move(c).start()
    if split:
        copy_xz = send_to("dp", beside, low_z, low_xz, send.at[2 * tiles], recv.at[2 * tiles])
        copy_xz.start()
    heads_taps(s_ref, low_ref, taken_ref, upper)
    for load in loads:
        load.wait()

    @pl.loop(0, tiles)
    def _(c):
        heads_tile(c, taken_ref, w_ref, tile_ref)
        near_out[c] = tile_ref[block(1 - par), :].astype(BF16)
        near_move(c).start()
        kept[c] = tile_ref[block(par), :]

    for c in range(tiles):
        near_move(c).wait_recv()
        far_move(c).wait_recv()
        out_ref[:, c * step : (c + 1) * step] = (
            kept[c] + near_in[c].astype(F32) + far_in[c].astype(F32)
        ).astype(BF16)
        near_move(c).wait_send()
        far_move(c).wait_send()
    if split:
        copy_xz.wait_recv()
        copy_xz.wait_send()


def heads_back(split, low, shifts, w_heads):
    taps, _, span, _ = shifts.shape
    wide = w_heads.shape[1] // taps
    tiles = wide // 512
    vmem = pl.BlockSpec(memory_space=pltpu.VMEM)
    hbm = pl.BlockSpec(memory_space=pl.ANY)
    dma = pltpu.SemaphoreType.DMA
    shape = jax.ShapeDtypeStruct
    cut = (tiles, span, 512)
    scratch = [
        pltpu.VMEM(w_heads.shape, BF16),
        pltpu.VMEM((taps, 2 * span, low.shape[2]), BF16),
        pltpu.VMEM((2 * span, 512), F32),
        pltpu.VMEM(cut, F32),
    ]

    def of(number):
        return pltpu.CompilerParams(
            collective_id=number, has_side_effects=True, vmem_limit_bytes=VMEM_LIMIT
        )

    lows = [shape(low.shape, BF16)] * (2 * split)
    far_sum, *lows = pl.pallas_call(
        functools.partial(heads_far_kernel, split),
        in_specs=[vmem, vmem, hbm],
        out_specs=[vmem] * (1 + len(lows)),
        out_shape=[shape(cut, BF16)] + lows,
        scratch_shapes=scratch
        + [pltpu.VMEM(cut, BF16)] * 2
        + [dma((taps,)), dma((tiles + 2,)), dma((tiles + 2,))],
        compiler_params=of(12),
        name="heads_far",
    )(low, shifts, w_heads)

    def near(far_sum, *lows):
        last = lows[1:]
        grad, *more = pl.pallas_call(
            functools.partial(heads_near_kernel, split),
            in_specs=[vmem, vmem, hbm, vmem] + [vmem] * len(last),
            out_specs=[vmem] * (1 + len(last)),
            out_shape=[shape((span, wide), BF16)] + [shape(low.shape, BF16)] * len(last),
            scratch_shapes=scratch
            + [pltpu.VMEM(cut, BF16)] * 3
            + [dma((taps,)), dma((2 * tiles + 1,)), dma((2 * tiles + 1,))],
            compiler_params=of(13),
            name="heads_near",
        )(low, shifts, w_heads, far_sum, *last)
        return [grad] + list(lows) + more

    return far_sum, lows, near


def heads_shard_kernel(per_tap, at_ref, layout_ref, *refs):
    lows, trunks = refs[:4], refs[4:13]
    out_ref, taken, turned, kinds = refs[13:]
    unit = pl.program_id(1)
    at = at_ref[pl.program_id(0)] + unit
    tap, chunk = at // per_tap, at % per_tap
    rows = lows[0].shape[1]
    span = rows // 2
    par, upper = at_ref[6], at_ref[7]

    places = [(0, side, k) for side in range(2) for k in range(2)]
    for number in (1, 2):
        places += [(number, side, par) for side in (upper, 1 - upper)]
        places += [(number, side, 1 - par) for side in range(2)]
    places += [(3, side, k) for k in (par, 1 - par) for side in range(2)]

    @pl.when((pl.program_id(0) == 0) & (unit == 0))
    def _():
        for number, low in enumerate(lows):
            for side in range(2):
                for k in range(2):
                    turned[number, side, k] = low[side, k * span : (k + 1) * span, :].T

    @pl.when((unit == 0) | (chunk == 0))
    def _():
        for kind, extent in enumerate((16, 8)):
            kinds[kind] = shift_in_maps(extent, tap, span)
        for slot, (number, side, k) in enumerate(places):
            large = layout_ref[at_ref[2 + number] + 2 * side + k, 1] == 16
            picks = kinds[jnp.where(large, 0, 1)]
            taken[:, slot * span : (slot + 1) * span] = product(
                turned[number, side, k], picks
            ).astype(BF16)

    total = 0.0
    slot = 0
    for trunk in trunks:
        strip = trunk[...].reshape(-1, trunk.shape[-1])
        depth = strip.shape[0]
        total = total + product(taken[:, slot : slot + depth], strip)
        slot += depth
    out_ref[0] = total.astype(BF16)


def heads_shard(at, layout, lows, trunks, units, lanes):
    _, rows, outs = lows[0].shape
    wide = trunks[0].shape[2]
    per_tap = wide // lanes
    whole = pl.BlockSpec(lows[0].shape, lambda i, j, f, g: (0, 0, 0))

    def strip_of(trunk):
        lead = trunk.shape[:-1]
        return pl.BlockSpec(
            lead + (lanes,), lambda i, j, f, g: (0,) * len(lead) + ((f[i] + j) % per_tap,)
        )

    strips = [strip_of(trunk) for trunk in trunks]
    return pl.pallas_call(
        functools.partial(heads_shard_kernel, per_tap),
        grid_spec=pltpu.PrefetchScalarGridSpec(
            num_scalar_prefetch=2,
            grid=(2, units),
            in_specs=[whole] * 4 + strips,
            out_specs=pl.BlockSpec((1, outs, lanes), lambda i, j, f, g: (i, 0, j)),
            scratch_shapes=[
                pltpu.VMEM((outs, 8 * rows), BF16),
                pltpu.VMEM((4, 2, 2, outs, rows // 2), BF16),
                pltpu.VMEM((2, rows // 2, rows // 2), BF16),
            ],
        ),
        out_shape=jax.ShapeDtypeStruct((2, outs, units * lanes), BF16),
        compiler_params=params(),
        cost_estimate=cost(32 * rows * outs * units * lanes, 32 * rows * units * lanes),
        name="heads_shard",
    )(at, layout, *lows, *trunks)


CHUNK_ROWS = (384, 512, 384, 384, 384, 256, 256)
CHUNK_BASE = (0, 384, 1408, 1792, 2176, 896, 1152)
SMALL_ROWS = 2560
HELD_ROWS = 1408
SPATIAL_BASE = 1408
REDUCE_BASE = 896


def trunk_back_kernel(*refs):
    refs = list(refs)

    def take(count):
        taken, refs[:count] = refs[:count], []
        return taken

    layout_ref, areas_ref, grad_ref, expanded_ref, in_ref = take(5)
    reduced_ref, spatial_ref, sums_one_ref, sums_two_ref, sums_three_ref = take(5)
    hidden_one_ref, hidden_two_ref, shift_taps_ref = take(3)
    w_reduce_hbm, w_spatial_hbm, w_expand_ref = take(3)
    gain_mid_ref, shift_mid_ref, gain_wide_ref, shift_wide_ref = take(4)
    gates_ref, classes_ref, head_norm_ref = take(3)
    out_ref, norm_one_ref, norm_two_ref, norm_three_ref, half_ref, heads_norm_ref = take(6)
    p_ref, core_in, core_out, y_in, x_out, x_in, z_out, z_in = take(8)
    z_mid, zz_in = take(2)
    low_wide, moved_ref, total_ref, block_mid, block_wide = take(5)
    slots_mid_rep, slots_mid_dp, slots_wide_rep, slots_wide_dp = take(4)
    rep_send, rep_recv, dp_send, dp_recv, send, recv, norm_send, norm_recv = take(8)
    w_reduce_ref, w_spatial_ref, hidden_all, low_all, moved_all, spatial_own = take(6)
    load_sems, gather_send, gather_recv = take(3)

    rep, dp = lax.axis_index("rep"), lax.axis_index("dp")
    par, upper = lax.rem(rep, 2), rep // 2
    x, z = lax.rem(dp, 2), dp // 2
    mate, far, beside = rep + 1 - 2 * par, rep + 2 - 4 * upper, dp + 1 - 2 * x
    low_z, high_z = lax.rem(z, 2), z // 2
    along, over = dp + 2 - 4 * low_z, dp + 4 - 8 * high_z
    span, wide = in_ref.shape
    middle = reduced_ref.shape[1]
    taps = shift_taps_ref.shape[0]
    loads = [
        pltpu.make_async_copy(w_spatial_hbm, w_spatial_ref, load_sems.at[0]),
        pltpu.make_async_copy(w_reduce_hbm, w_reduce_ref, load_sems.at[1]),
    ]
    for load in loads:
        load.start()
    barrier = pltpu.get_barrier_semaphore()
    for axis, size in (("rep", 4), ("dp", 8)):
        me = lax.axis_index(axis)
        for k in range(1, size):
            pl.semaphore_signal(
                barrier, inc=1, device_id={axis: lax.rem(me + k, size)}, device_id_type=MESH
            )

    def remote(src, dst, c, slot, to):
        return pltpu.make_async_remote_copy(
            src_ref=src,
            dst_ref=dst,
            send_sem=send.at[c, slot],
            recv_sem=recv.at[c, slot],
            device_id=to,
            device_id_type=MESH,
        )

    def whole(c, at=0, size=None):
        size = CHUNK_ROWS[c] if size is None else size
        return pl.ds(pl.multiple_of(CHUNK_BASE[c] + at, 16), size)

    def halves(c):
        return pl.ds(CHUNK_BASE[c] // 2, CHUNK_ROWS[c] // 2)

    def core_copy(c, hi):
        return remote(
            p_ref.at[2 * hi + 1 - par, whole(c)], core_in.at[hi, whole(c)], c, hi, {"rep": mate}
        )

    def y_copy(c):
        return remote(core_out.at[whole(c)], y_in.at[whole(c)], c, 2, {"rep": far})

    def x_copy(c):
        return remote(x_out.at[halves(c)], x_in.at[halves(c)], c, 3, {"dp": beside})

    def piece(c, base, at, size):
        return pl.ds(pl.multiple_of(CHUNK_BASE[c] // base + at, 16), size)

    def z_copy(c):
        size = CHUNK_ROWS[c] // 4
        return remote(
            z_out.at[piece(c, 2, (1 - low_z) * size, size)],
            z_in.at[piece(c, 4, 0, size)],
            c,
            4,
            {"dp": along},
        )

    def zz_copy(c):
        size = CHUNK_ROWS[c] // 8
        return remote(
            z_mid.at[piece(c, 4, (1 - high_z) * size, size)],
            zz_in.at[piece(c, 8, 0, size)],
            c,
            5,
            {"dp": over},
        )

    def own_place(c, low, high=None):
        size = CHUNK_ROWS[c] // 4
        at = x * 2 * size + low * size
        if high is None:
            return whole(c, at, size)
        return whole(c, at + high * (size // 2), size // 2)

    def zz_back(c, incoming):
        place = own_place(c, low_z, 1 - high_z if incoming else high_z)
        return remote(half_ref.at[place], half_ref.at[place], c, 6, {"dp": over})

    def z_back(c, incoming):
        place = own_place(c, 1 - low_z if incoming else low_z)
        return remote(half_ref.at[place], half_ref.at[place], c, 7, {"dp": along})

    def last_copy(c, incoming):
        half = CHUNK_ROWS[c] // 2
        place = whole(c, (1 - x if incoming else x) * half, half)
        return remote(half_ref.at[place], half_ref.at[place], c, 8, {"dp": beside})

    def step(c, stage):
        if stage == 0:
            for hi in range(2):
                core_copy(c, hi).start()
        elif stage == 1:
            for hi in range(2):
                core_copy(c, hi).wait_recv()
            core_out[whole(c)] = (
                p_ref[2 * (1 - upper) + par, whole(c)].astype(F32)
                + core_in[1 - upper, whole(c)].astype(F32)
            ).astype(BF16)
            y_copy(c).start()
        elif stage == 2 and c in (2, 3, 4):
            half = CHUNK_ROWS[c] // 2
            at = CHUNK_BASE[c] - SPATIAL_BASE

            def own(k):
                return spatial_own[pl.ds(pl.multiple_of(at + k * half, 16), half)]

            x_out[halves(c)] = own(1 - x).astype(BF16)
            x_copy(c).start()
            z_out[halves(c)] = own(x).astype(BF16)
        elif stage == 2:
            y_copy(c).wait_recv()
            half = CHUNK_ROWS[c] // 2

            def both(at):
                place = whole(c, at, half)
                return (
                    p_ref[rep, place].astype(F32)
                    + core_in[upper, place].astype(F32)
                    + y_in[place].astype(F32)
                )

            x_out[halves(c)] = both((1 - x) * half).astype(BF16)
            x_copy(c).start()
            z_out[halves(c)] = both(x * half).astype(BF16)
        elif stage == 3:
            x_copy(c).wait_recv()
            z_out[halves(c)] = (
                z_out[halves(c)].astype(F32) + x_in[halves(c)].astype(F32)
            ).astype(BF16)
            z_copy(c).start()
        elif stage == 4:
            z_copy(c).wait_recv()
            size = CHUNK_ROWS[c] // 4
            at = piece(c, 4, 0, size)
            z_mid[at] = (
                z_out[piece(c, 2, low_z * size, size)].astype(F32) + z_in[at].astype(F32)
            ).astype(BF16)
            zz_copy(c).start()
        elif stage == 5:
            zz_copy(c).wait_recv()
            size = CHUNK_ROWS[c] // 8
            half_ref[own_place(c, low_z, high_z)] = (
                z_mid[piece(c, 4, high_z * size, size)].astype(F32)
                + zz_in[piece(c, 8, 0, size)].astype(F32)
            ).astype(BF16)
            zz_back(c, False).start()
        elif stage == 6:
            zz_back(c, True).wait_recv()
            z_back(c, False).start()
        elif stage == 7:
            z_back(c, True).wait_recv()
            last_copy(c, False).start()
        else:
            last_copy(c, True).wait_recv()
            if c not in (2, 3, 4):
                for hi in range(2):
                    core_copy(c, hi).wait_send()
                y_copy(c).wait_send()
            x_copy(c).wait_send()
            z_copy(c).wait_send()
            zz_copy(c).wait_send()
            zz_back(c, False).wait_send()
            z_back(c, False).wait_send()
            last_copy(c, False).wait_send()

    def steps(*which):
        def run():
            for c, stage in which:
                step(c, stage)

        return run

    live = live_column(layout_ref, dp * 4 + rep, span)
    inverse = inverse_count(areas_ref, span)

    def stats(sums_ref):
        center = sums_ref[0:1, :] * inverse
        return center, lax.rsqrt(sums_ref[1:2, :] * inverse - center * center + EPS)

    def norm_move(to, slot):
        at = heads_norm_ref.at[slot]
        return send_to("rep", to, at, at, norm_send.at[to], norm_recv.at[slot])

    def local_sums(blocks, value, unit, at):
        masked = live * value
        blocks[0, 0:1, at] = jnp.sum(masked * unit, 0, keepdims=True)
        blocks[0, 1:2, at] = jnp.sum(masked, 0, keepdims=True)

    def everywhere(number, blocks, rep_slots, dp_slots, meanwhile, later):
        if number == 0:
            pl.semaphore_wait(barrier, 10)
            heads_norm_ref[rep] = head_norm_ref[...]
            for k in range(1, 4):
                norm_move(lax.rem(rep + k, 4), rep).start()
        blocks[1] = total_along(
            "rep", 4, blocks.at[0], rep_slots, rep_send.at[number], rep_recv.at[number], meanwhile
        )
        return total_along(
            "dp", 8, blocks.at[1], dp_slots, dp_send.at[number], dp_recv.at[number], later
        )

    def slope(value):
        sigma = jax.nn.sigmoid(value)
        return sigma * (1.0 + value * (1.0 - sigma))

    def spread_back(grad, unit, sums, gain, scaling):
        return (
            live
            * (gain * scaling)
            * (grad - sums[1:2] * inverse - unit * (sums[0:1] * inverse))
        ).astype(BF16)

    center, scaling = stats(sums_three_ref)
    strips = [pl.ds(k, middle) for k in range(0, wide, middle)]

    def unit_at(at):
        return (expanded_ref[:, at] - center[:, at.start : at.start + middle]) * scaling[
            :, at.start : at.start + middle
        ]

    for at in strips:
        unit = unit_at(at)
        pre = unit * gain_wide_ref[:, at] + shift_wide_ref[:, at] + in_ref[:, at].astype(F32)
        grad = grad_ref[:, at].astype(F32) * slope(pre)
        out_ref[:, at] = grad
        local_sums(block_wide, grad, unit, at)

    def gather(number, held, to, slot):
        at = held.at[slot]
        return send_to(
            "rep", to, at, at, gather_send.at[number, to], gather_recv.at[number, slot]
        )

    hidden_all[rep] = hidden_one_ref[...]

    def first_chunk():
        half = middle // 2
        rows = classes_ref.shape[1]
        for q in range(4):
            p_ref[q, half : half + rows, :] = classes_ref[q]
            p_ref[q, half + rows : CHUNK_ROWS[0], :] = jnp.zeros(
                (CHUNK_ROWS[0] - half - rows, middle), BF16
            )
        for k in range(2):
            p_ref[2 * upper + k, :half, :] = gates_ref[k * half : (k + 1) * half, :]
            p_ref[2 * (1 - upper) + k, :half, :] = jnp.zeros((half, middle), BF16)
        step(0, 0)
        for k in range(1, 4):
            gather(0, hidden_all, lax.rem(rep + k, 4), rep).start()
        step(0, 1)

    sums = everywhere(
        0,
        block_wide,
        slots_wide_rep,
        slots_wide_dp,
        first_chunk,
        steps((0, 2)),
    )
    norm_three_ref[...] = sums
    for at in strips:
        cut = slice(at.start, at.start + middle)
        low_wide[:, at] = spread_back(
            out_ref[:, at], unit_at(at), sums[:, cut], gain_wide_ref[:, at], scaling[:, cut]
        )

    center, scaling = stats(sums_two_ref)
    unit = (spatial_ref[...] - center) * scaling
    normed = unit * gain_mid_ref[1:2, :] + shift_mid_ref[1:2, :]
    total_ref[...] = against(low_wide[...], w_expand_ref[...]) * slope(normed)

    def expand_gradient():
        rows = middle // 4
        for k in range(wide // middle):
            tile = inner_rows(
                hidden_two_ref[...], low_wide[:, k * middle : (k + 1) * middle]
            ).astype(BF16)
            for q in range(4):
                at = CHUNK_BASE[1] + k * rows
                p_ref[q, at : at + rows, :] = tile[q * rows : (q + 1) * rows]
        step(1, 0)
        step(1, 1)

    local_sums(block_mid.at[0], total_ref[...], unit, slice(None))
    sums = everywhere(
        1,
        block_mid.at[0],
        slots_mid_rep.at[0],
        slots_mid_dp.at[0],
        expand_gradient,
        steps((0, 3), (1, 2)),
    )
    norm_two_ref[...] = sums
    low_mid = spread_back(total_ref[...], unit, sums, gain_mid_ref[1:2, :], scaling)

    total_ref[...] = jnp.zeros_like(total_ref)
    loads[0].wait()
    for t in range(taps):
        moved_ref[t] = inner_rows(shift_taps_ref[t], low_mid).astype(BF16)

    @pl.loop(0, taps)
    def _(t):
        at = pl.ds(pl.multiple_of(t * middle, middle), middle)
        total_ref[...] += against(moved_ref[t], w_spatial_ref[at, :])

    center, scaling = stats(sums_one_ref)
    unit = (reduced_ref[...] - center) * scaling
    normed = unit * gain_mid_ref[0:1, :] + shift_mid_ref[0:1, :]
    total_ref[...] = total_ref[...] * slope(normed)

    def give_low():
        low_all[rep] = low_mid
        for k in range(1, 4):
            gather(1, low_all, lax.rem(rep + k, 4), rep).start()

    def spatial_gradient():
        large = [layout_ref[dp * 4 + p, 1] == 16 for p in range(4)]
        units = spatial_own.shape[0] // 128
        per_tap = middle // 128

        @pl.loop(0, units)
        def _(i):
            unit = units * rep + i
            tap, cut = unit // per_tap, unit % per_tap

            @pl.when((i == 0) | (cut == 0))
            def _():
                kinds = [shift_in_maps(extent, tap, span, 2) for extent in (16, 8)]
                for p in range(4):
                    picks = jnp.where(large[p], kinds[0], kinds[1])
                    moved_all[p] = inner_rows(picks, low_all[p]).astype(BF16)

            lanes = pl.ds(pl.multiple_of(cut * 128, 128), 128)
            total = 0.0
            for p in range(4):
                total = total + inner_rows(hidden_all[p, :, lanes], moved_all[p])
            spatial_own[pl.ds(pl.multiple_of(i * 128, 128), 128), :] = total

    local_sums(block_mid.at[1], total_ref[...], unit, slice(None))
    sums = everywhere(
        2,
        block_mid.at[1],
        slots_mid_rep.at[1],
        slots_mid_dp.at[1],
        give_low,
        steps((0, 4), (1, 3)),
    )
    norm_one_ref[...] = sums
    low_first = spread_back(total_ref[...], unit, sums, gain_mid_ref[0:1, :], scaling)
    quarter = wide // 4
    for q in range(4):
        p_ref[q, REDUCE_BASE : REDUCE_BASE + quarter, :] = inner_rows(
            in_ref[:, q * quarter : (q + 1) * quarter], low_first
        ).astype(BF16)
    step(5, 0)
    step(6, 0)
    step(0, 5)
    step(5, 1)
    step(1, 4)
    step(6, 1)
    for number, held in enumerate((hidden_all, low_all)):
        for k in range(1, 4):
            other = lax.rem(rep + k, 4)
            gather(number, held, other, other).wait_recv()
            gather(number, held, other, rep).wait_send()
    spatial_gradient()
    step(2, 2)
    step(4, 2)
    step(3, 2)
    loads[1].wait()
    for k in range(0, wide, middle):
        out_ref[:, k : k + middle] += against(low_first, w_reduce_ref[k : k + middle, :])
    for turn in (
        ((5, 2), (0, 6), (1, 5), (2, 3), (6, 2), (4, 3), (3, 3), (2, 4)),
        ((1, 6), (0, 7), (5, 3), (4, 4), (6, 3), (2, 5), (3, 4), (0, 8)),
        ((4, 5), (1, 7), (2, 6), (5, 4), (3, 5), (1, 8), (6, 4), (4, 6)),
        ((2, 7), (5, 5), (2, 8), (3, 6), (4, 7), (6, 5), (5, 6), (3, 7)),
        ((4, 8), (6, 6), (5, 7), (6, 7), (3, 8), (5, 8), (6, 8)),
    ):
        for c, stage in turn:
            step(c, stage)
    for k in range(1, 4):
        other = lax.rem(rep + k, 4)
        norm_move(other, other).wait_recv()
        norm_move(other, rep).wait_send()


def trunk_back(
    layout,
    grad,
    expanded,
    inputs,
    reduced,
    spatial,
    sums,
    hidden_one,
    hidden_two,
    shift_taps,
    w_reduce,
    w_spatial,
    w_expand,
    gain_mid,
    shift_mid,
    gain_wide,
    shift_wide,
    gates,
    classes,
    head_norm,
):
    span, wide = inputs.shape
    middle = reduced.shape[1]
    taps = shift_taps.shape[0]
    vmem = pl.BlockSpec(memory_space=pltpu.VMEM)
    dma = pltpu.SemaphoreType.DMA
    shape = jax.ShapeDtypeStruct
    small = (SMALL_ROWS, middle)
    held = (HELD_ROWS, middle)
    every = (4, span, middle)
    half = (SMALL_ROWS // 2, middle)
    chunks = len(CHUNK_ROWS)
    out_shape = [
        shape((span, wide), F32),
        shape((2, middle), F32),
        shape((2, middle), F32),
        shape((2, wide), F32),
        shape(small, BF16),
        shape((4, 2, middle), F32),
    ]
    return pl.pallas_call(
        trunk_back_kernel,
        in_specs=[pl.BlockSpec(memory_space=pltpu.SMEM)]
        + [vmem] * 12
        + [pl.BlockSpec(memory_space=pl.ANY)] * 2
        + [vmem] * 8,
        out_specs=[vmem] * len(out_shape),
        out_shape=out_shape,
        scratch_shapes=[
            pltpu.VMEM((4,) + held, BF16),
            pltpu.VMEM((2,) + held, BF16),
            pltpu.VMEM(held, BF16),
            pltpu.VMEM(held, BF16),
            pltpu.VMEM(half, BF16),
            pltpu.VMEM(half, BF16),
            pltpu.VMEM(half, BF16),
            pltpu.VMEM((SMALL_ROWS // 4, middle), BF16),
            pltpu.VMEM((SMALL_ROWS // 4, middle), BF16),
            pltpu.VMEM((SMALL_ROWS // 8, middle), BF16),
            pltpu.VMEM((span, wide), BF16),
            pltpu.VMEM((taps, span, middle), BF16),
            pltpu.VMEM((span, middle), F32),
            pltpu.VMEM((2, 2, 2, middle), F32),
            pltpu.VMEM((2, 2, wide), F32),
            pltpu.VMEM((2, 4, 2, middle), F32),
            pltpu.VMEM((2, 8, 2, middle), F32),
            pltpu.VMEM((4, 2, wide), F32),
            pltpu.VMEM((8, 2, wide), F32),
            dma((3, 4)),
            dma((3, 4)),
            dma((3, 8)),
            dma((3, 8)),
            dma((chunks, 9)),
            dma((chunks, 9)),
            dma((4,)),
            dma((4,)),
            pltpu.VMEM(w_reduce.shape, BF16),
            pltpu.VMEM(w_spatial.shape, BF16),
            pltpu.VMEM(every, BF16),
            pltpu.VMEM(every, BF16),
            pltpu.VMEM(every, BF16),
            pltpu.VMEM((taps * middle // 4, middle), F32),
            dma((2,)),
            dma((2, 4)),
            dma((2, 4)),
        ],
        compiler_params=pltpu.CompilerParams(
            collective_id=9, has_side_effects=True, vmem_limit_bytes=VMEM_LIMIT
        ),
        name="trunk_back",
    )(
        layout,
        layout,
        grad,
        expanded,
        inputs,
        reduced,
        spatial,
        *sums,
        hidden_one,
        hidden_two,
        shift_taps,
        w_reduce,
        w_spatial,
        w_expand,
        gain_mid,
        shift_mid,
        gain_wide[None, :],
        shift_wide[None, :],
        gates,
        classes,
        head_norm,
    )


def finish_kernel(
    classes,
    sums_ref,
    in_grad_ref,
    depth_in_ref,
    logits_in_ref,
    messages_in_ref,
    one_ref,
    two_ref,
    three_ref,
    heads_norm_ref,
    depth_ref,
    logits_ref,
    out_ref,
    reduce_ref,
    spatial_ref,
    expand_ref,
    gates_ref,
    messages_ref,
    classes_ref,
    gain_mid_ref,
    shift_mid_ref,
    gain_wide_ref,
    shift_wide_ref,
    gain_head_ref,
    shift_head_ref,
):
    middle = sums_ref.shape[1]

    def held(at, size):
        return sums_ref[at : at + size, :].astype(F32)

    depth_ref[...] = depth_in_ref[...]
    logits_ref[...] = logits_in_ref[...].T[:classes, :]
    out_ref[...] = in_grad_ref[...]
    messages_ref[...] = messages_in_ref[...].astype(F32)
    gates = gates_ref.shape[0]
    gates_ref[...] = held(0, gates)
    rows = classes_ref.shape[1] // 4
    held_classes = [held(gates, rows)[:, k * 128 : (k + 1) * 128] for k in range(4)]
    classes_ref[...] = jnp.concatenate(held_classes, 0).T[:classes, :]
    rows = expand_ref.shape[0]
    for k in range(expand_ref.shape[1] // middle):
        expand_ref[:, k * middle : (k + 1) * middle] = held(CHUNK_BASE[1] + k * rows, rows)
    spatial_ref[...] = held(SPATIAL_BASE, spatial_ref.shape[0])
    reduce_ref[...] = held(REDUCE_BASE, reduce_ref.shape[0])
    for at, (gain, shift) in enumerate(((gain_mid_ref, shift_mid_ref),) * 2):
        norm = (one_ref, two_ref)[at]
        gain[at : at + 1, :] = norm[0:1, :]
        shift[at : at + 1, :] = norm[1:2, :]
    gain_wide_ref[...] = three_ref[0:1, :]
    shift_wide_ref[...] = three_ref[1:2, :]
    for k in range(4):
        gain_head_ref[:, k * middle : (k + 1) * middle] = heads_norm_ref[k, 0:1, :]
        shift_head_ref[:, k * middle : (k + 1) * middle] = heads_norm_ref[k, 1:2, :]


def finish(classes, sums, in_grad, depth, logits, messages, one, two, three, heads_norm):
    span, wide = in_grad.shape
    middle = sums.shape[1]
    vmem = pl.BlockSpec(memory_space=pltpu.VMEM)
    shape = jax.ShapeDtypeStruct
    out_shape = [
        shape(depth.shape, F32),
        shape((classes, span), F32),
        shape(in_grad.shape, F32),
        shape((wide // 4, middle), F32),
        shape((SMALL_ROWS - SPATIAL_BASE, middle), F32),
        shape((middle // 4, wide), F32),
        shape((middle // 2, middle), F32),
        shape(messages.shape, F32),
        shape((classes, middle // 4), F32),
        shape((2, middle), F32),
        shape((2, middle), F32),
    ] + [shape((1, wide), F32)] * 4
    every = pl.pallas_call(
        functools.partial(finish_kernel, classes),
        in_specs=[vmem] * 9,
        out_specs=[vmem] * len(out_shape),
        out_shape=out_shape,
        compiler_params=params(),
        name="finish",
    )(sums, in_grad, depth, logits, messages, one, two, three, heads_norm)
    return list(every)


def silu_slope(value_in):
    sigma_of = jax.nn.sigmoid(value_in)
    return sigma_of * (1.0 + value_in * (1.0 - sigma_of))


MESH = pl.DeviceIdType.MESH


def greet(axes):
    barrier = pltpu.get_barrier_semaphore()
    count = 0
    for axis, size in axes:
        me = lax.axis_index(axis)
        for k in range(1, size):
            pl.semaphore_signal(
                barrier, inc=1, device_id={axis: lax.rem(me + k, size)}, device_id_type=MESH
            )
        count += size - 1
    pl.semaphore_wait(barrier, count)


def total_kernel(axes, x_ref, out_ref, *scratch):
    greet(axes)
    block = x_ref
    for number, (axis, size) in enumerate(axes):
        slots, stage, send_sems, recv_sems = scratch[4 * number : 4 * number + 4]
        me = lax.axis_index(axis)
        others = [lax.rem(me + k, size) for k in range(1, size)]
        for other in others:
            pltpu.make_async_remote_copy(
                src_ref=block,
                dst_ref=slots.at[me],
                send_sem=send_sems.at[other],
                recv_sem=recv_sems.at[me],
                device_id={axis: other},
                device_id_type=MESH,
            ).start()
        slots[me] = block[...]
        for other in others:
            copy = pltpu.make_async_remote_copy(
                src_ref=block,
                dst_ref=slots.at[other],
                send_sem=send_sems.at[other],
                recv_sem=recv_sems.at[other],
                device_id={axis: other},
                device_id_type=MESH,
            )
            copy.wait_recv()
            copy.wait_send()
        total = slots[0]
        for k in range(1, size):
            total = total + slots[k]
        if number == len(axes) - 1:
            out_ref[...] = total
        else:
            stage[...] = total
            block = stage


def total_of(left, right, axes):
    width = left.shape[0]
    packed = jnp.concatenate([left, right], 0).reshape(-1, 128)
    sized = tuple((axis, lax.axis_size(axis)) for axis in axes)
    scratch = []
    for _, size in sized:
        scratch += [
            pltpu.VMEM((size,) + packed.shape, F32),
            pltpu.VMEM(packed.shape, F32),
            pltpu.SemaphoreType.DMA((size,)),
            pltpu.SemaphoreType.DMA((size,)),
        ]
    number = 1 + (width != 512) + 2 * (len(axes) == 1)
    summed = pl.pallas_call(
        functools.partial(total_kernel, sized),
        out_shape=jax.ShapeDtypeStruct(packed.shape, F32),
        in_specs=[pl.BlockSpec(memory_space=pltpu.VMEM)],
        out_specs=pl.BlockSpec(memory_space=pltpu.VMEM),
        scratch_shapes=scratch,
        compiler_params=pltpu.CompilerParams(collective_id=number, has_side_effects=True),
        name="total",
    )(packed).reshape(2, width)
    return summed[0], summed[1]


def normalize(raw_value, column_sums, squares, pixel_count, norm_gain, norm_shift):
    center = column_sums / pixel_count
    spread_of = squares / pixel_count - center * center
    scaling = lax.rsqrt(spread_of + EPS)
    unit_value = (raw_value - center) * scaling
    return (unit_value * norm_gain + norm_shift, unit_value, scaling)


def moments(raw_value, living, axes):
    return total_of(
        jnp.sum(living * raw_value, 0), jnp.sum(living * raw_value * raw_value, 0), axes
    )


def norm_back(grad_out, unit_value, scaling, norm_gain, living, pixel_count, axes):
    grad_gain, grad_shift = total_of(
        jnp.sum(living * grad_out * unit_value, 0), jnp.sum(living * grad_out, 0), axes
    )
    grad_raw = (
        living
        * (norm_gain * scaling)
        * (grad_out - grad_shift / pixel_count - unit_value * grad_gain / pixel_count)
    )
    return (grad_raw, grad_gain, grad_shift)


def swap(value, bit):
    return lax.ppermute(value, "rep", [(k, k ^ bit) for k in range(4)])


def scatter_rep(value):
    return lax.psum_scatter(value.astype(BF16), "rep", scatter_dimension=0, tiled=True)


def total_dp(value):
    parts = lax.axis_size("dp")
    rows = value.shape[0]
    padded = -(-rows // (8 * parts)) * 8 * parts
    value = jnp.pad(value, ((0, padded - rows), (0, 0)))
    share = lax.psum_scatter(value, "dp", scatter_dimension=0, tiled=True)
    return lax.all_gather(share, "dp", axis=0, tiled=True)[:rows].astype(F32)


def shards(
    inputs,
    layout,
    labels,
    cot_depth,
    w_reduce,
    w_spatial,
    w_expand,
    w_heads,
    w_gates,
    w_messages,
    w_classes,
    gain_mid,
    shift_mid,
    gain_wide,
    shift_wide,
    gain_head,
    shift_head,
):
    pixels = inputs.shape[0]
    middle = w_reduce.shape[1]
    classes = w_classes.shape[1]
    group = lax.axis_size("rep")
    everyone = ("rep", "dp")
    rep = lax.axis_index("rep")
    parity = rep % 2
    upper = rep // 2
    first_row = lax.axis_index("dp") * group
    own_info = geometry(lax.dynamic_slice_in_dim(layout, first_row + rep, 1, 0), pixels)
    group_info = geometry(lax.dynamic_slice_in_dim(layout, first_row, group, 0), pixels)
    living = own_info[2][0].astype(F32)[:, None]
    group_living = group_info[2].astype(F32)
    living_all = group_living.reshape(group * pixels, 1)
    pixel_count = jnp.sum(
        jnp.minimum(layout[:, 0] * layout[:, 1] * layout[:, 2], pixels)
    ).astype(F32)
    split = lax.axis_size("dp") == 8
    if split:
        side = lax.axis_index("dp") % 2
        columns = [[z_at * 2 + k for z_at in range(4)] for k in range(2)]
    zero = jnp.zeros((1,), jnp.int32)
    first = jnp.reshape(9 * parity, (1,)).astype(jnp.int32)

    (
        reduced,
        sums_one,
        hidden_one,
        spatial,
        sums_two,
        hidden_two,
        expanded,
        sums_three,
        trunk_all,
        headed,
        shifts_own,
        shifts_all,
        *trunk_afar,
    ) = trunk_forward(
        split,
        inputs,
        layout,
        w_reduce,
        w_spatial,
        w_expand,
        w_heads,
        gain_mid,
        shift_mid,
        gain_wide,
        shift_wide,
    )
    upper_is_depth = upper == 0
    headed, late_classes, late_labels = lax.optimization_barrier((headed, w_classes, labels))
    depth, logits, gates_local, classes_local, head_low, head_norm, *rest = message_streams(
        split,
        layout,
        headed,
        shifts_all,
        w_messages,
        w_gates,
        late_classes,
        gain_head,
        shift_head,
        cot_depth,
        late_labels,
        trunk_afar + [trunk_all] if split else [],
    )
    classes_local = classes_local[:, :classes]
    is_depth = upper_is_depth
    if split:
        messages_local = rest[0]
    else:
        heads_all, message_all = rest
        heads_all = heads_all.reshape(4, group * pixels, middle)
        source = jnp.where(
            is_depth,
            jnp.concatenate([heads_all[1], heads_all[2], heads_all[3]], 1),
            jnp.concatenate([heads_all[0], heads_all[1], heads_all[2]], 1),
        )
        _, messages_local = rows_back(
            first, message_all.reshape(4 * pixels, middle), source, w_messages, shifts_all, 2, BF16
        )
        grad_messages = lax.psum_scatter(messages_local, "dp", scatter_dimension=1, tiled=True)
        gates_cut = gates_local.reshape(2, pixels, middle)
        gates_share = lax.dynamic_index_in_dim(gates_cut, parity, 0, keepdims=False).astype(F32)
        gates_share += swap(
            lax.dynamic_index_in_dim(gates_cut, 1 - parity, 0, keepdims=False), 1
        ).astype(F32)
    far_sum, lows, near = heads_back(split, head_low, shifts_all, w_heads)
    if split:
        messages_local, far_sum = lax.optimization_barrier((messages_local, far_sum))
    trunk_grad, *lows = near(far_sum, *lows)
    if split:
        grad_messages = lax.psum_scatter(
            messages_local, "dp", scatter_dimension=0, tiled=True, axis_index_groups=columns
        )
        dp = lax.axis_index("dp")
        beside, along = dp + 1 - 2 * side, dp + 2 - 4 * ((dp // 2) % 2)
        groups = [dp, beside, along, along + 1 - 2 * side]
        units = 9

        lower = dp % 4
        at = jnp.stack(
            [units * lower, units * (lower + 4)] + [group * k for k in groups] + [parity, upper]
        )
        far_x, far_z, mate_x, mate_z, trunk_xz, mate_xz = rest[1:]
        near_x, near_z = trunk_afar
        trunks = [trunk_all, near_x, far_x, mate_x, near_z, far_z, mate_z, trunk_xz, mate_xz]
        heads_local = heads_shard(
            at.astype(jnp.int32), layout, [head_low] + lows, trunks, units, 256
        )
        heads_local, trunk_grad = lax.optimization_barrier((heads_local, trunk_grad))
        grad_heads = lax.psum_scatter(
            heads_local,
            "dp",
            scatter_dimension=0,
            tiled=False,
            axis_index_groups=[[k, k + 4] for k in range(4)],
        )
    else:
        heads_local = heads_weight(
            head_low.reshape(group * pixels, middle),
            trunk_all.reshape(group * pixels, -1),
            shifts_all,
        )
        grad_heads = lax.psum_scatter(heads_local, "dp", scatter_dimension=1, tiled=True)
    if split:
        classes_wide = jnp.pad(classes_local.astype(BF16), ((0, 0), (0, 128 - classes)))
        classes_wide = classes_wide.reshape(4, 4, -1, 128)
        classes_wide = jnp.concatenate([classes_wide[:, k] for k in range(4)], 2)
        (
            input_grad,
            norm_one,
            norm_two,
            norm_three,
            small_sums,
            heads_norm,
        ) = trunk_back(
            layout,
            trunk_grad,
            expanded,
            inputs,
            reduced,
            spatial,
            [sums_one, sums_two, sums_three],
            hidden_one,
            hidden_two,
            shifts_own,
            w_reduce,
            w_spatial,
            w_expand,
            gain_mid,
            shift_mid,
            gain_wide,
            shift_wide,
            gates_local,
            classes_wide,
            head_norm,
        )
        every = finish(
            classes,
            small_sums,
            input_grad,
            depth,
            logits,
            grad_messages,
            norm_one,
            norm_two,
            norm_three,
            heads_norm,
        )
        every[0], grad_heads = lax.optimization_barrier((every[0], grad_heads))
        narrow = (1, 7, 8)
        outs = [each.T if k in narrow else each for k, each in enumerate(every)]
        outs.insert(6, grad_heads.astype(F32))
        return tuple(outs[:12]) + tuple(each[0] for each in outs[12:])
    else:
        logits = logits[:, :classes]
        normed_one, unit_one, scale_one = normalize(
            reduced, sums_one[0], sums_one[1], pixel_count, gain_mid[0], shift_mid[0]
        )
        normed_two, unit_two, scale_two = normalize(
            spatial, sums_two[0], sums_two[1], pixel_count, gain_mid[1], shift_mid[1]
        )
        normed_three, unit_three, scale_three = normalize(
            expanded, sums_three[0], sums_three[1], pixel_count, gain_wide, shift_wide
        )
        pre_act = normed_three + inputs.astype(F32)
        pre_grad = trunk_grad.astype(F32) * silu_slope(pre_act)
        expand_raw, grad_gain_wide, grad_shift_wide = norm_back(
            pre_grad, unit_three, scale_three, gain_wide, living, pixel_count, everyone
        )
        expand_low = expand_raw.astype(BF16)
        expand_local = inner_rows(hidden_two, expand_low).astype(BF16)
        hidden_two_grad = against(expand_low, w_expand)
        spatial_raw, gain_grad_two, shift_grad_two = norm_back(
            hidden_two_grad * silu_slope(normed_two),
            unit_two,
            scale_two,
            gain_mid[1],
            living,
            pixel_count,
            everyone,
        )
        spatial_low = spatial_raw.astype(BF16)
        hidden_one_grad, spatial_local = rows_back(
            zero, spatial_low, hidden_one, w_spatial, shifts_own[:, None], 1, F32
        )
        reduced_raw, gain_grad_one, shift_grad_one = norm_back(
            hidden_one_grad * silu_slope(normed_one),
            unit_one,
            scale_one,
            gain_mid[0],
            living,
            pixel_count,
            everyone,
        )
        reduced_low = reduced_raw.astype(BF16)
        reduce_local = inner_rows(inputs, reduced_low).astype(BF16)
        input_grad = pre_grad + against(reduced_low, w_reduce)
        grad_expand = scatter_rep(expand_local)
        grad_spatial = scatter_rep(spatial_local)
        grad_reduce = scatter_rep(reduce_local)
        grad_classes = scatter_rep(classes_local)
        pieces = [
            gates_share.astype(BF16),
            grad_expand.reshape(-1, middle),
            grad_spatial,
            grad_classes.reshape(-1, middle),
        ]
        early = total_dp(jnp.concatenate(pieces, 0))
        rows = [piece.shape[0] for piece in pieces]
        starts = [sum(rows[:k]) for k in range(4)]
        grad_gates, expand_sum, grad_spatial, classes_sum = [
            early[at : at + size] for at, size in zip(starts, rows)
        ]
        grad_expand = expand_sum.reshape(grad_expand.shape)
        grad_classes = classes_sum.reshape(grad_classes.shape)
        grad_reduce = total_dp(grad_reduce)
        grad_gain_mid = jnp.stack([gain_grad_one, gain_grad_two], 0)
        grad_shift_mid = jnp.stack([shift_grad_one, shift_grad_two], 0)
    head_norms = lax.all_gather(
        head_norm, "rep", axis=1, tiled=True
    )
    return (
        depth,
        logits,
        input_grad,
        grad_reduce,
        grad_spatial,
        grad_expand,
        grad_heads.astype(F32),
        grad_gates,
        grad_messages.astype(F32),
        grad_classes,
        grad_gain_mid,
        grad_shift_mid,
        grad_gain_wide,
        grad_shift_wide,
        head_norms[0],
        head_norms[1],
    )


def solution(mesh):
    in_specs = (
        P(("dp", "rep"), None),
        P(),
        P(("dp", "rep")),
        P(("dp", "rep"), None),
        P(),
        P(),
        P(),
        P("rep", None),
        P(),
        P("rep", None),
        P(),
        P(),
        P(),
        P(),
        P(),
        P(),
        P(),
    )
    out_specs = (
        P(("dp", "rep"), None),
        P(("dp", "rep"), None),
        P(("dp", "rep"), None),
        P("rep", None),
        P("rep", None),
        P("rep", None),
        P("rep", "dp"),
        P("rep", None),
        P("rep", "dp"),
        P("rep", None),
        P(),
        P(),
        P(),
        P(),
        P(),
        P(),
    )
    return jax.shard_map(shards, mesh=mesh, in_specs=in_specs, out_specs=out_specs, check_vma=False)
```

```python
import functools

import jax
import jax.numpy as jnp
from jax import lax
from jax.experimental import pallas as pl
from jax.experimental.pallas import tpu as pltpu
from jax.sharding import PartitionSpec as P

EPS = 1e-05
F32 = jnp.float32
BF16 = jnp.bfloat16
VMEM_LIMIT = 60 * 2**20


def geometry(layout, span):
    position = jnp.arange(span, dtype=jnp.int32)
    height = layout[:, 0:1]
    map_width = layout[:, 1:2]
    images = layout[:, 2:3]
    map_area = height * map_width
    inside = position[None, :] % map_area
    row_of = inside // map_width
    col_of = inside % map_width
    living = position[None, :] < images * map_area
    return (row_of, col_of, living, height, map_width)


def neighbours(shape_info, dilation):
    row_of, col_of, living, height, map_width = shape_info
    span = row_of.shape[1]
    position = jnp.arange(span, dtype=jnp.int32)
    every = []
    for step_row in (-1, 0, 1):
        for step_col in (-1, 0, 1):
            target_row = row_of + dilation * step_row
            target_col = col_of + dilation * step_col
            inside = (
                living
                & (target_row >= 0)
                & (target_row < height)
                & (target_col >= 0)
                & (target_col < map_width)
            )
            neighbour = position[None, :] + dilation * (step_row * map_width + step_col)
            every.append(jnp.where(inside, neighbour, -1))
    return jnp.concatenate(every, 0).T


def shift_matrices(shape_info, dilation):
    devices, span = shape_info[0].shape
    picks = neighbours(shape_info, dilation).T.reshape(9, devices, span, 1)
    return (picks == jnp.arange(span, dtype=jnp.int32)).astype(BF16)


def product(left_side, right_side):
    return jnp.dot(left_side, right_side, preferred_element_type=F32)


def inner_rows(left_side, right_side):
    return lax.dot_general(
        left_side, right_side, (((0,), (0,)), ((), ())), preferred_element_type=F32
    )


def against(left_side, right_side):
    return lax.dot_general(
        left_side, right_side, (((1,), (1,)), ((), ())), preferred_element_type=F32
    )


def params():
    return pltpu.CompilerParams(vmem_limit_bytes=VMEM_LIMIT)


def cost(flops, moved):
    return pl.CostEstimate(flops=flops, bytes_accessed=moved, transcendentals=0)


def shifted(g_ref, s_ref):
    blocks, span = s_ref.shape[1], s_ref.shape[2]
    return jnp.concatenate(
        [
            inner_rows(s_ref[0, k], g_ref[pl.ds(k * span, span), :]).astype(BF16)
            for k in range(blocks)
        ],
        0,
    )


def heads_weight_kernel(g_ref, u_ref, s_ref, out_ref):
    taken = shifted(g_ref, s_ref)
    step = 512
    for c in range(0, u_ref.shape[1], step):
        out_ref[:, c : c + step] = inner_rows(taken, u_ref[:, c : c + step]).astype(out_ref.dtype)


def heads_weight(g, u, shifts):
    rows, outs = g.shape
    wide = u.shape[1]
    taps, blocks, span, _ = shifts.shape
    return pl.pallas_call(
        heads_weight_kernel,
        grid=(taps,),
        in_specs=[
            pl.BlockSpec((rows, outs), lambda t: (0, 0)),
            pl.BlockSpec((rows, wide), lambda t: (0, 0)),
            pl.BlockSpec((1, blocks, span, span), lambda t: (t, 0, 0, 0)),
        ],
        out_specs=pl.BlockSpec((outs, wide), lambda t: (0, t)),
        out_shape=jax.ShapeDtypeStruct((outs, taps * wide), BF16),
        compiler_params=params(),
        cost_estimate=cost(2 * rows * wide * outs * taps, outs * taps * wide * 2),
        name="heads_weight",
    )(g, u, shifts)


def rows_back_kernel(halves, first_ref, g_ref, u_ref, w_ref, s_ref, du_ref, dw_ref, total):
    step = pl.program_id(0)
    taken = shifted(g_ref, s_ref)
    depth = w_ref.shape[0]
    which = (step + first_ref[0]) % halves

    @pl.when(step == 0)
    def _():
        total[...] = jnp.zeros_like(total)

    total[which] += against(taken, w_ref[...])
    dw_ref[...] = inner_rows(u_ref[...], taken).astype(dw_ref.dtype)

    @pl.when(step == pl.num_programs(0) - 1)
    def _():
        for k in range(halves):
            du_ref[:, k * depth : (k + 1) * depth] = total[k].astype(du_ref.dtype)


def rows_back(first, g, u, w, shifts, halves, kind):
    rows, outs = g.shape
    depth = u.shape[1] // halves
    steps = w.shape[0] // depth
    taps, blocks, span, _ = shifts.shape
    return pl.pallas_call(
        functools.partial(rows_back_kernel, halves),
        grid_spec=pltpu.PrefetchScalarGridSpec(
            num_scalar_prefetch=1,
            grid=(steps,),
            in_specs=[
                pl.BlockSpec((rows, outs), lambda b, f: (0, 0)),
                pl.BlockSpec((rows, depth), lambda b, f: (0, (b + f[0]) % halves)),
                pl.BlockSpec((depth, outs), lambda b, f: (b, 0)),
                pl.BlockSpec((1, blocks, span, span), lambda b, f: ((b + f[0]) // halves, 0, 0, 0)),
            ],
            out_specs=[
                pl.BlockSpec((rows, halves * depth), lambda b, f: (0, 0)),
                pl.BlockSpec((depth, outs), lambda b, f: (b, 0)),
            ],
            scratch_shapes=[pltpu.VMEM((halves, rows, depth), F32)],
        ),
        out_shape=[
            jax.ShapeDtypeStruct((rows, halves * depth), kind),
            jax.ShapeDtypeStruct(w.shape, BF16),
        ],
        compiler_params=params(),
        cost_estimate=cost(4 * rows * w.size, w.size * 4),
        name="rows_back",
    )(first, g, u, w, shifts)


def send_to(axis, to, src, dst, send_sem, recv_sem):
    return pltpu.make_async_remote_copy(
        src_ref=src,
        dst_ref=dst,
        send_sem=send_sem,
        recv_sem=recv_sem,
        device_id={axis: to},
        device_id_type=MESH,
    )


def total_along(axis, size, block, slots, send_sems, recv_sems, meanwhile=None):
    me = lax.axis_index(axis)
    others = [lax.rem(me + k, size) for k in range(1, size)]
    for other in others:
        send_to(axis, other, block, slots.at[me], send_sems.at[other], recv_sems.at[me]).start()
    slots[me] = block[...]
    if meanwhile is not None:
        meanwhile()
    for other in others:
        copy = send_to(
            axis, other, block, slots.at[other], send_sems.at[other], recv_sems.at[other]
        )
        copy.wait_recv()
        copy.wait_send()
    total = slots[0]
    for k in range(1, size):
        total = total + slots[k]
    return total


def place_in_map(layout_ref, device, span):
    position = lax.broadcasted_iota(jnp.int32, (span, 1), 0)
    large = layout_ref[device, 1] == 16
    row_of = jnp.where(large, position // 16, (position % 64) // 8)
    col_of = jnp.where(large, position % 16, position % 8)
    return position, row_of, col_of


def live_mask(layout_ref, device, span):
    position = lax.broadcasted_iota(jnp.int32, (span, 1), 0)
    return position < layout_ref[device, 0] * layout_ref[device, 1] * layout_ref[device, 2]


def live_column(layout_ref, device, span):
    return jnp.where(live_mask(layout_ref, device, span), 1.0, 0.0)


def inverse_count(areas_ref, span):
    areas = areas_ref[:, 0:1] * areas_ref[:, 1:2] * areas_ref[:, 2:3]
    return 1.0 / jnp.sum(jnp.minimum(areas, span).astype(F32), 0, keepdims=True)


def shift_block(layout_ref, device, dilation, tap, span):
    position, row_of, col_of = place_in_map(layout_ref, device, span)
    height, map_width = layout_ref[device, 0], layout_ref[device, 1]
    step_row, step_col = dilation * (tap // 3 - 1), dilation * (tap % 3 - 1)
    target_row, target_col = row_of + step_row, col_of + step_col
    inside = (
        live_mask(layout_ref, device, span)
        & (target_row >= 0)
        & (target_row < height)
        & (target_col >= 0)
        & (target_col < map_width)
    )
    neighbour = jnp.where(inside, position + step_row * map_width + step_col, -1)
    lanes = lax.broadcasted_iota(jnp.int32, (span, span), 1)
    return jnp.where(neighbour == lanes, 1.0, 0.0).astype(BF16)


def shift_in_maps(extent, tap, span, dilation=1):
    position = lax.broadcasted_iota(jnp.int32, (span, 1), 0)
    row_of, col_of = (position % (extent * extent)) // extent, position % extent
    step_row, step_col = dilation * (tap // 3 - 1), dilation * (tap % 3 - 1)
    target_row, target_col = row_of + step_row, col_of + step_col
    inside = (
        (target_row >= 0) & (target_row < extent) & (target_col >= 0) & (target_col < extent)
    )
    neighbour = jnp.where(inside, position + step_row * extent + step_col, -1)
    lanes = lax.broadcasted_iota(jnp.int32, (span, span), 1)
    return jnp.where(neighbour == lanes, 1.0, 0.0).astype(BF16)


def trunk_kernel(
    split,
    sizes,
    in_ref,
    layout_ref,
    areas_ref,
    w_reduce_ref,
    w_spatial_hbm,
    w_expand_hbm,
    w_heads_hbm,
    gain_mid_ref,
    shift_mid_ref,
    gain_wide_ref,
    shift_wide_ref,
    reduced_ref,
    sums_one_ref,
    hidden_one_ref,
    spatial_ref,
    sums_two_ref,
    hidden_two_ref,
    expanded_ref,
    sums_three_ref,
    trunk_ref,
    headed_ref,
    own_shift_ref,
    all_shift_ref,
    *rest,
):
    if split:
        trunk_x, trunk_z, *rest = rest
    early_out = (reduced_ref, spatial_ref, expanded_ref, own_shift_ref, all_shift_ref)
    reduced_ref, spatial_ref, expanded_ref, own_shift_ref, all_shift_ref, early_sems, *rest = rest
    trunk_rest(
        early_out,
        early_sems,
        split,
        sizes,
        in_ref,
        layout_ref,
        areas_ref,
        w_reduce_ref,
        w_spatial_hbm,
        w_expand_hbm,
        w_heads_hbm,
        gain_mid_ref,
        shift_mid_ref,
        gain_wide_ref,
        shift_wide_ref,
        reduced_ref,
        sums_one_ref,
        hidden_one_ref,
        spatial_ref,
        sums_two_ref,
        hidden_two_ref,
        expanded_ref,
        sums_three_ref,
        trunk_ref,
        headed_ref,
        own_shift_ref,
        all_shift_ref,
        (trunk_x, trunk_z) if split else (),
        *rest,
    )


def trunk_rest(
    early_out,
    early_sems,
    split,
    sizes,
    in_ref,
    layout_ref,
    areas_ref,
    w_reduce_ref,
    w_spatial_hbm,
    w_expand_hbm,
    w_heads_hbm,
    gain_mid_ref,
    shift_mid_ref,
    gain_wide_ref,
    shift_wide_ref,
    reduced_ref,
    sums_one_ref,
    hidden_one_ref,
    spatial_ref,
    sums_two_ref,
    hidden_two_ref,
    expanded_ref,
    sums_three_ref,
    trunk_ref,
    headed_ref,
    own_shift_ref,
    all_shift_ref,
    afar,
    w_spatial_ref,
    w_expand_ref,
    w_heads_ref,
    block_mid,
    block_wide,
    slots_mid_rep,
    slots_mid_dp,
    slots_wide_rep,
    slots_wide_dp,
    load_sems,
    rep_send,
    rep_recv,
    dp_send,
    dp_recv,
    gather_send,
    gather_recv,
    away_send,
    away_recv,
):
    n_rep, n_dp = sizes
    rep = lax.axis_index("rep")
    par, upper = lax.rem(rep, 2), rep // 2
    mate, far = rep + 1 - 2 * par, rep + 2 - 4 * upper
    span, wide = in_ref.shape
    middle = w_reduce_ref.shape[1]
    taps = own_shift_ref.shape[0]
    loads = [
        pltpu.make_async_copy(w_spatial_hbm, w_spatial_ref, load_sems.at[0]),
        pltpu.make_async_copy(w_expand_hbm, w_expand_ref, load_sems.at[1]),
    ]
    heads_load = pltpu.make_async_copy(w_heads_hbm, w_heads_ref, load_sems.at[2])
    for load in loads:
        load.start()
    heads_load.start()

    barrier = pltpu.get_barrier_semaphore()
    for axis, size in (("rep", n_rep), ("dp", n_dp)):
        me = lax.axis_index(axis)
        for k in range(1, size):
            pl.semaphore_signal(
                barrier, inc=1, device_id={axis: lax.rem(me + k, size)}, device_id_type=MESH
            )
    first_row = lax.axis_index("dp") * n_rep
    live = live_column(layout_ref, first_row + rep, span)
    inverse = inverse_count(areas_ref, span)

    def make_own():
        for t in range(taps):
            own_shift_ref[t] = shift_block(layout_ref, first_row + rep, 2, t, span)

    def make_all(first, last):
        def fill():
            for t in range(first, last):
                for p in range(n_rep):
                    all_shift_ref[t, p] = shift_block(layout_ref, first_row + p, 1, t, span)

        return fill

    def everywhere(number, value_ref, blocks, rep_slots, dp_slots, meanwhile, later):
        masked = live * value_ref[...]
        blocks[0, 0:1, :] = jnp.sum(masked, 0, keepdims=True)
        blocks[0, 1:2, :] = jnp.sum(masked * value_ref[...], 0, keepdims=True)
        if number == 0:
            pl.semaphore_wait(barrier, n_rep + n_dp - 2)
        blocks[1] = total_along(
            "rep", n_rep, blocks.at[0], rep_slots, rep_send.at[number], rep_recv.at[number], meanwhile
        )
        return total_along(
            "dp", n_dp, blocks.at[1], dp_slots, dp_send.at[number], dp_recv.at[number], later
        )

    def normed(value, sums, gain, shift):
        center = sums[0:1] * inverse
        scaling = lax.rsqrt(sums[1:2] * inverse - center * center + EPS)
        return (value - center) * (scaling * gain) + shift

    def silu(value):
        return value * jax.nn.sigmoid(value)

    reduced_ref[...] = product(in_ref[...], w_reduce_ref[...])
    sums = everywhere(
        0, reduced_ref, block_mid.at[0], slots_mid_rep.at[0], slots_mid_dp.at[0], make_own, None
    )
    sums_one_ref[...] = sums
    hidden_one_ref[...] = silu(
        normed(reduced_ref[...], sums, gain_mid_ref[0:1, :], shift_mid_ref[0:1, :])
    ).astype(BF16)
    loads[0].wait()
    spatial_ref[...] = jnp.zeros_like(spatial_ref)

    @pl.loop(0, taps)
    def _(t):
        moved = product(own_shift_ref[t], hidden_one_ref[...]).astype(BF16)
        at = pl.ds(pl.multiple_of(t * middle, middle), middle)
        spatial_ref[...] += product(moved, w_spatial_ref[at, :])

    sums = everywhere(
        1, spatial_ref, block_mid.at[1], slots_mid_rep.at[1], slots_mid_dp.at[1], make_all(0, 5), None
    )
    sums_two_ref[...] = sums
    hidden_two_ref[...] = silu(
        normed(spatial_ref[...], sums, gain_mid_ref[1:2, :], shift_mid_ref[1:2, :])
    ).astype(BF16)
    loads[1].wait()
    expanded_ref[...] = product(hidden_two_ref[...], w_expand_ref[...])
    sums = everywhere(
        2, expanded_ref, block_wide, slots_wide_rep, slots_wide_dp, make_all(5, 9), None
    )
    sums_three_ref[...] = sums

    own_rows = pl.ds(pl.multiple_of(par * span, span), span)
    mate_rows = pl.ds(pl.multiple_of((1 - par) * span, span), span)
    pre = normed(expanded_ref[...], sums, gain_wide_ref[...], shift_wide_ref[...])
    trunk_ref[upper, own_rows, :] = silu(pre + in_ref[...].astype(F32)).astype(BF16)
    parts = 4
    piece = span // parts

    def rows(parity, k):
        return pl.ds(pl.multiple_of(parity * span + k * piece, piece), piece)

    def across(side, k):
        at = trunk_ref.at[side, rows(par, k)]
        return send_to("rep", far, at, at, gather_send.at[k], gather_recv.at[k])

    def own_pass(parity):
        at = trunk_ref.at[upper, pl.ds(pl.multiple_of(parity * span, span), span)]
        return send_to("rep", mate, at, at, gather_send.at[parts], gather_recv.at[parts])

    def far_pass(parity, k):
        at = trunk_ref.at[1 - upper, rows(parity, k)]
        slot = parts + 1 + k
        return send_to("rep", mate, at, at, gather_send.at[slot], gather_recv.at[slot])

    dp = lax.axis_index("dp")
    neighbours = (dp + 1 - 2 * lax.rem(dp, 2), dp + 2 - 4 * lax.rem(dp // 2, 2))

    def away(number):
        return send_to(
            "dp",
            neighbours[number],
            trunk_ref.at[upper, own_rows],
            afar[number],
            away_send.at[number],
            away_recv.at[number],
        )

    for k in range(parts):
        across(upper, k).start()
    own_pass(par).start()
    if split:
        for number in range(2):
            away(number).start()
    leaving = [
        pltpu.make_async_copy(src, dst, early_sems.at[k])
        for k, (src, dst) in enumerate(
            zip((reduced_ref, spatial_ref, expanded_ref, own_shift_ref, all_shift_ref), early_out)
        )
    ]
    for copy in leaving:
        copy.start()
    headed_ref[...] = jnp.zeros_like(headed_ref)
    own_pass(1 - par).wait_recv()
    heads_load.wait()

    def convolve(side):
        @pl.loop(0, taps)
        def _(t):
            at = pl.ds(pl.multiple_of(t * wide, wide), wide)
            y = against(trunk_ref[side], w_heads_ref[:, at]).astype(BF16)
            for k in range(2):
                place = pl.ds(k * span, span)
                headed_ref[side, place, :] += product(
                    all_shift_ref[t, 2 * side + k], y[k * span : (k + 1) * span]
                )

    convolve(upper)
    for k in range(parts):
        across(1 - upper, k).wait_recv()
        far_pass(par, k).start()
    for k in range(parts):
        far_pass(1 - par, k).wait_recv()
    convolve(1 - upper)
    for k in range(parts):
        across(upper, k).wait_send()
        far_pass(par, k).wait_send()
    own_pass(par).wait_send()
    if split:
        for number in range(2):
            away(number).wait_send()
            away(number).wait_recv()
    for copy in leaving:
        copy.wait()


def trunk_forward(
    split,
    inputs,
    layout,
    w_reduce,
    w_spatial,
    w_expand,
    w_heads,
    gain_mid,
    shift_mid,
    gain_wide,
    shift_wide,
):
    span, wide = inputs.shape
    middle = w_reduce.shape[1]
    n_rep, n_dp = lax.axis_size("rep"), lax.axis_size("dp")
    taps = 9
    vmem = pl.BlockSpec(memory_space=pltpu.VMEM)
    hbm = pl.BlockSpec(memory_space=pl.ANY)
    smem = pl.BlockSpec(memory_space=pltpu.SMEM)
    dma = pltpu.SemaphoreType.DMA
    shape = jax.ShapeDtypeStruct
    return pl.pallas_call(
        functools.partial(trunk_kernel, split, (n_rep, n_dp)),
        in_specs=[vmem, smem, vmem, vmem] + [hbm] * 3 + [vmem] * 4,
        out_specs=[hbm if k in (0, 3, 6, 10, 11) else vmem for k in range(12)] + [hbm] * (2 * split),
        out_shape=[
            shape((span, middle), F32),
            shape((2, middle), F32),
            shape((span, middle), BF16),
            shape((span, middle), F32),
            shape((2, middle), F32),
            shape((span, middle), BF16),
            shape((span, wide), F32),
            shape((2, wide), F32),
            shape((2, 2 * span, wide), BF16),
            shape((2, 2 * span, w_heads.shape[0]), F32),
            shape((taps, span, span), BF16),
            shape((taps, n_rep, span, span), BF16),
        ]
        + [shape((span, wide), BF16)] * (2 * split),
        scratch_shapes=[
            pltpu.VMEM((span, middle), F32),
            pltpu.VMEM((span, middle), F32),
            pltpu.VMEM((span, wide), F32),
            pltpu.VMEM((taps, span, span), BF16),
            pltpu.VMEM((taps, n_rep, span, span), BF16),
            dma((5,)),
            pltpu.VMEM(w_spatial.shape, BF16),
            pltpu.VMEM(w_expand.shape, BF16),
            pltpu.VMEM(w_heads.shape, BF16),
            pltpu.VMEM((2, 2, 2, middle), F32),
            pltpu.VMEM((2, 2, wide), F32),
            pltpu.VMEM((2, n_rep, 2, middle), F32),
            pltpu.VMEM((2, n_dp, 2, middle), F32),
            pltpu.VMEM((n_rep, 2, wide), F32),
            pltpu.VMEM((n_dp, 2, wide), F32),
            dma((3,)),
            dma((3, n_rep)),
            dma((3, n_rep)),
            dma((3, n_dp)),
            dma((3, n_dp)),
            dma((9,)),
            dma((9,)),
            dma((2,)),
            dma((2,)),
        ],
        compiler_params=pltpu.CompilerParams(
            collective_id=10, has_side_effects=True, vmem_limit_bytes=VMEM_LIMIT
        ),
        name="trunk_forward",
    )(
        inputs,
        layout,
        layout,
        w_reduce,
        w_spatial,
        w_expand,
        w_heads,
        gain_mid,
        shift_mid,
        gain_wide[None, :],
        shift_wide[None, :],
    )


MOVES = 38


def message_kernel(split, n_dp, classes, *refs):
    refs = list(refs)

    def take(count):
        taken, refs[:count] = refs[:count], []
        return taken

    layout_ref, areas_ref, headed_ref, s_hbm, w_hbm, gates_w_ref, classes_w_ref = take(7)
    gain_ref, shift_ref, cot_ref, labels_ref = take(4)
    if split:
        trunk_x, trunk_z, trunk_hbm = take(3)
    depth_ref, logits_ref, gates_ref, classes_ref, low_ref, norm_ref = take(6)
    if split:
        out_ref, far_x, far_z, mate_x, mate_z, trunk_xz, mate_xz = take(7)
    else:
        heads_ref, gm_ref = take(2)
    w_ref, live_ref, acc_ref, acc_in, stream_ref, direct_ref, cot_in, labels_in = take(8)
    depth_out, logits_out, picked_ref, far_ref, near_ref = take(5)
    core_out, core_in, far_out, far_in, near_out, near_in = take(6)
    sums_ref, slots_ref, load_sem, send, recv, dp_send, dp_recv = take(7)
    s_ref, shift_sem = take(2)
    if split:
        heads_ref, gm_ref, beside_ref, cut_own, cut_out, cut_in, cut_taken = take(7)

    rep = lax.axis_index("rep")
    par, upper = lax.rem(rep, 2), rep // 2
    mate, far = rep + 1 - 2 * par, rep + 2 - 4 * upper
    first_row = lax.axis_index("dp") * 4
    side_x = lax.rem(lax.axis_index("dp"), 2)
    beside = lax.axis_index("dp") + 1 - 2 * side_x
    side_z = lax.rem(lax.axis_index("dp") // 2, 2)
    along = lax.axis_index("dp") + 2 - 4 * side_z
    span = s_ref.shape[2]
    middle = headed_ref.shape[2]
    small = middle // 2
    load = pltpu.make_async_copy(w_hbm, w_ref, load_sem)
    shift_load = pltpu.make_async_copy(s_hbm, s_ref, shift_sem)
    shift_load.start()
    load.start()

    barrier = pltpu.get_barrier_semaphore()
    me_dp = lax.axis_index("dp")
    for to in (mate, far):
        pl.semaphore_signal(barrier, inc=1, device_id={"rep": to}, device_id_type=MESH)
    for k in range(1, n_dp):
        pl.semaphore_signal(
            barrier, inc=1, device_id={"dp": lax.rem(me_dp + k, n_dp)}, device_id_type=MESH
        )

    def move(number, src, dst, to, axis="rep"):
        return send_to(axis, to, src, dst, send.at[number], recv.at[number])

    def block(parity):
        return pl.ds(pl.multiple_of(parity * span, span), span)

    for p in range(4):
        live_ref[p // 2, (p % 2) * span : (p % 2 + 1) * span, :] = live_column(
            layout_ref, first_row + p, span
        )
    inverse = inverse_count(areas_ref, span)

    def add_up(number, left, right):
        sums_ref[number, 0:1, :] = left
        sums_ref[number, 1:2, :] = right
        return total_along(
            "dp", n_dp, sums_ref.at[number], slots_ref.at[number], dp_send.at[number], dp_recv.at[number]
        )

    def column_sum(value):
        return jnp.sum(value, 0, keepdims=True)

    left, right = 0.0, 0.0
    for side in range(2):
        masked = live_ref[side] * headed_ref[side]
        left = left + column_sum(masked)
        right = right + column_sum(masked * headed_ref[side])
    pl.semaphore_wait(barrier, n_dp + 1)
    move(9, cot_ref, cot_in, far).start()
    move(10, labels_ref, labels_in, far).start()
    sums = add_up(0, left, right)
    if split:
        lower_side = 1 - upper
        own_block = trunk_hbm.at[lower_side, block(par)]
        copy_x = move(29, trunk_x, far_x, far)
        copy_z = move(30, own_block, far_z, along, "dp")
        near_xz = move(31, trunk_x, trunk_xz.at[upper], along, "dp")
        far_xz = move(32, far_x, trunk_xz.at[lower_side], along, "dp")
        to_mate = [
            move(33, trunk_x, mate_x.at[upper], mate),
            move(34, trunk_z, mate_z.at[upper], mate),
            move(35, far_x, mate_x.at[lower_side], mate),
            move(36, far_z, mate_z.at[lower_side], mate),
            move(37, trunk_xz, mate_xz, mate),
        ]
        near_xz.start()
        copy_z.start()

    center = sums[0:1] * inverse
    scaling = lax.rsqrt(sums[1:2] * inverse - center * center + EPS)
    own_lanes = pl.ds(pl.multiple_of(rep * middle, middle), middle)
    gain = gain_ref[:, own_lanes]
    shift = shift_ref[:, own_lanes]

    def across(head, part):
        at = heads_ref.at[head, part // 2, pl.ds((part % 2) * span, span)]
        return move(part, at, at, far)

    def relay(head, part):
        at = heads_ref.at[head, part // 2, pl.ds((part % 2) * span, span)]
        return move(5 + part, at, at, mate)

    def own_head(head):
        return move(4, heads_ref.at[head], heads_ref.at[head], mate)

    for side in range(2):
        normed = (headed_ref[side] - center) * (scaling * gain) + shift
        heads_ref[rep, side] = (normed * jax.nn.sigmoid(normed)).astype(BF16)
        for k in range(2):
            across(rep, 2 * side + k).start()
    own_head(rep).start()
    if split:
        x_own = move(24, heads_ref.at[rep], beside_ref.at[rep], beside, "dp")
        x_far = move(25, heads_ref.at[far], beside_ref.at[far], beside, "dp")
        x_own.start()
        copy_x.start()

    def tap_of(i):
        return par * 5 + i

    def row_of(i, head_at):
        return pl.multiple_of(par * (3 * small) + i * (3 * middle) + head_at * middle, small)

    half_row = (1 - par) * (12 * middle)
    full_row = pl.multiple_of(half_row + par * small, small)
    part_row = pl.multiple_of(half_row + (1 - par) * middle, small)
    part_lanes = pl.ds(pl.multiple_of(par * small, small), small)
    local = 2 * upper
    remote = 2 * (1 - upper)
    local_head = 1 + upper
    part_head = 2 - upper
    full_head = 2 * par + 1 - upper

    def wrows(row, depth):
        return w_ref[pl.ds(row, depth), :]

    def gather_taps(tap, side, y):
        y = y.astype(BF16)
        for k in range(2):
            acc_ref[side, k * span : (k + 1) * span, :] += product(
                s_ref[tap, 2 * side + k], y[k * span : (k + 1) * span]
            )

    acc_ref[...] = jnp.zeros_like(acc_ref)
    own_head(mate).wait_recv()
    shift_load.wait()
    load.wait()

    @pl.loop(0, 8)
    def _(n):
        i, side = n // 2, n % 2
        gather_taps(
            tap_of(i), side, product(heads_ref[local_head, side], wrows(row_of(i, local), middle))
        )

    @pl.when(par == upper)
    def _():
        @pl.loop(0, 2)
        def _(side):
            gather_taps(4, side, product(heads_ref[full_head, side], wrows(full_row, middle)))

    for part in range(4):
        across(far, part).wait_recv()
        relay(far, part).start()
    if split:
        x_far.start()
    for part in range(4):
        relay(far + 1 - 2 * par, part).wait_recv()

    @pl.loop(0, 8)
    def _(n):
        i, side = n // 2, n % 2
        y = product(heads_ref[remote, side], wrows(row_of(i, 1 - upper), middle))
        y = y + product(heads_ref[remote + 1, side], wrows(row_of(i, 2 - upper), middle))
        gather_taps(tap_of(i), side, y)

    @pl.loop(0, 2)
    def _(side):
        gather_taps(
            4, side, product(heads_ref[part_head, side, :, part_lanes], wrows(part_row, small))
        )

    @pl.when(par != upper)
    def _():
        @pl.loop(0, 2)
        def _(side):
            gather_taps(4, side, product(heads_ref[full_head, side], wrows(full_row, middle)))

    def acc_move(side):
        return move(11 + side, acc_ref.at[side, block(1 - par)], acc_in.at[side], mate)

    for side in range(2):
        acc_move(side).start()

    own_gates = gates_w_ref[pl.ds(pl.multiple_of(upper * middle, middle), middle), :]
    classes_ref[...] = jnp.zeros_like(classes_ref)
    move(9, cot_ref, cot_in, far).wait_recv()
    move(10, labels_ref, labels_in, far).wait_recv()
    gates_total = 0.0

    def gm_move(side, parity):
        at = gm_ref.at[side, block(parity)]
        return move(13 + side, at, at, mate)

    for side in range(2):
        acc_move(side).wait_recv()
        message = acc_ref[side, block(par), :] + acc_in[side]
        stream = heads_ref[3 * upper, side, block(par), :]
        gate = jax.nn.sigmoid(product(stream, own_gates))
        full = stream.astype(F32) + gate * message
        alive = live_ref[side, block(par), :]

        @pl.when(upper == 0)
        def _():
            cot = (cot_ref if side == 0 else cot_in)[...].astype(F32)
            stream_ref[side] = alive * cot
            (depth_ref if side == 0 else depth_out)[...] = alive * full

        @pl.when(upper == 1)
        def _():
            labels = (labels_in if side == 0 else labels_ref)[...]
            full_low = full.astype(BF16)
            logits = product(full_low, classes_w_ref[...])
            (logits_out if side == 0 else logits_ref)[...] = alive * logits
            lanes = lax.broadcasted_iota(jnp.int32, logits.shape, 1)
            shown = jnp.where(lanes < classes, logits, -1e30)
            grown = jnp.exp(shown - jnp.max(shown, 1, keepdims=True))
            probs = grown / jnp.sum(grown, 1, keepdims=True)
            slope = (alive * (probs - jnp.where(lanes == labels, 1.0, 0.0))).astype(BF16)
            classes_ref[...] += inner_rows(full_low, slope)
            stream_ref[side] = against(slope, classes_w_ref[...])

        grad = stream_ref[side]
        grad_gate = (grad * message * gate * (1.0 - gate)).astype(BF16)
        gm_ref[side, block(par), :] = (grad * gate).astype(BF16)
        gm_move(side, par).start()
        gates_total = gates_total + inner_rows(stream, grad_gate)
        direct_ref[side] = grad + against(grad_gate, own_gates)

    gates_ref[...] = gates_total.astype(BF16)

    @pl.when(upper == 0)
    def _():
        move(15, depth_out, depth_ref, far).start()

    @pl.when(upper == 1)
    def _():
        move(16, logits_out, logits_ref, far).start()

    for side in range(2):
        gm_move(side, 1 - par).wait_recv()
    if split:
        lanes = lax.broadcasted_iota(jnp.int32, (middle, small), 1)
        wanted = (lanes // 64) * 128 + lanes % 64
        source = lax.broadcasted_iota(jnp.int32, (middle, small), 0)
        for cut, which in ((cut_out, 1 - side_x), (cut_own, side_x)):
            pick = jnp.where(source == wanted + 64 * which, 1.0, 0.0).astype(BF16)
            for side in range(2):
                cut[side] = product(gm_ref[side], pick).astype(BF16)
        x_cut = move(28, cut_out, cut_in, beside, "dp")
        x_cut.start()

    @pl.loop(0, 10)
    def _(n):
        i, side = n // 2, n % 2
        tap = jnp.where(i == 4, 4, tap_of(i))
        for k in range(2):
            at = pl.ds(k * span, span)
            picked_ref[i, side, at, :] = inner_rows(
                s_ref[tap, 2 * side + k], gm_ref[side, at, :]
            ).astype(BF16)

    def taps_back(side, head_at):
        total = 0.0
        for i in range(4):
            total = total + against(picked_ref[i, side], wrows(row_of(i, head_at), middle))
        return total

    def core_move(side):
        return move(17 + side, core_out.at[side], core_in.at[side], mate)

    def far_move(part):
        at = pl.ds((part % 2) * span, span)
        return move(19 + part, far_out.at[part // 2, at], far_in.at[part // 2, at], far)

    @pl.loop(0, 2)
    def _(side):
        @pl.loop(0, 2)
        def _(j):
            far_ref[j, side] = taps_back(side, 1 - upper + j)

        far_ref[upper, side, :, part_lanes] += against(picked_ref[4, side], wrows(part_row, small))

        @pl.when(par != upper)
        def _():
            far_ref[2 * par - 1 + upper, side] += against(
                picked_ref[4, side], wrows(full_row, middle)
            )

        core_out[side] = far_ref[1 - par, side].astype(BF16)
        core_move(side).start()

    for side in range(2):
        core_move(side).wait_recv()
        for part in (2 * side, 2 * side + 1):
            at = pl.ds((part % 2) * span, span)
            far_out[side, at, :] = (
                far_ref[par, side, at, :] + core_in[side, at, :].astype(F32)
            ).astype(BF16)
            far_move(part).start()

    if split:
        copy_x.wait_recv()
        far_xz.start()

    @pl.loop(0, 2)
    def _(side):
        near_ref[side] = taps_back(side, local)

    @pl.when(par == upper)
    def _():
        @pl.loop(0, 2)
        def _(side):
            near_ref[side] += against(picked_ref[4, side], wrows(full_row, middle))

        near_out[...] = near_ref[...].astype(BF16)
        for side in range(2):
            near_ref[side, block(par), :] = direct_ref[side]
            near_ref[side, block(1 - par), :] = jnp.zeros((span, middle), F32)

    @pl.when(par != upper)
    def _():
        for side in range(2):
            near_out[side, block(par), :] = direct_ref[side].astype(BF16)
            near_out[side, block(1 - par), :] = jnp.zeros((span, middle), BF16)

    near_move = move(23, near_out, near_in, mate)
    near_move.start()

    if split:
        x_own.wait_recv()
        relay_own = move(26, beside_ref.at[rep], beside_ref.at[rep], mate)
        relay_own.start()
        x_far.wait_recv()
        relay_far = move(27, beside_ref.at[far], beside_ref.at[far], mate)
        relay_far.start()
        copy_z.wait_recv()
        for copy in to_mate[:4]:
            copy.start()
        x_cut.wait_recv()
        move(26, beside_ref.at[mate], beside_ref.at[mate], mate).wait_recv()
        other = far + 1 - 2 * par
        move(27, beside_ref.at[other], beside_ref.at[other], mate).wait_recv()

        def fill(tap):
            for p in range(4):
                at = pl.ds(p * span, span)
                cut_taken[0, :, at] = inner_rows(
                    cut_own[p // 2, pl.ds((p % 2) * span, span), :], s_ref[tap, p]
                ).astype(BF16)
                cut_taken[1, :, at] = inner_rows(
                    cut_in[p // 2, pl.ds((p % 2) * span, span), :],
                    shift_block(layout_ref, beside * 4 + p, 1, tap, span),
                ).astype(BF16)

        def gradient(head, lanes):
            total = 0.0
            for number, held in enumerate((heads_ref, beside_ref)):
                for side in range(2):
                    total = total + product(
                        cut_taken[number, :, side * 2 * span : (side + 1) * 2 * span],
                        held[head, side, :, lanes],
                    )
            return total.astype(BF16)

        @pl.loop(0, 4)
        def _(i):
            fill(tap_of(i))
            for at in range(3):
                for k in range(2):
                    row = pl.multiple_of(row_of(i, at) + k * small, small)
                    out_ref[:, pl.ds(row, small)] = gradient(
                        at + 1 - upper, pl.ds(k * small, small)
                    )

        fill(4)
        for k in range(2):
            row = pl.multiple_of(full_row + k * small, small)
            out_ref[:, pl.ds(row, small)] = gradient(full_head, pl.ds(k * small, small))
        out_ref[:, pl.ds(part_row, small)] = gradient(part_head, part_lanes)

    if split:
        near_xz.wait_recv()
        far_xz.wait_recv()
        to_mate[4].start()

    near_move.wait_recv()
    left, right = 0.0, 0.0

    def backward(side):
        unit = (headed_ref[side] - center) * scaling
        normed = unit * gain + shift
        sigma = jax.nn.sigmoid(normed)
        return unit, sigma * (1.0 + normed * (1.0 - sigma))

    for side in range(2):
        for part in (2 * side, 2 * side + 1):
            far_move(part).wait_recv()
        unit, slope = backward(side)
        grad = near_ref[side] + near_in[side].astype(F32) + far_in[side].astype(F32)
        grad = grad * slope
        near_ref[side] = grad
        masked = live_ref[side] * grad
        left = left + column_sum(masked * unit)
        right = right + column_sum(masked)
    sums = add_up(1, left, right)
    norm_ref[...] = sums
    for side in range(2):
        unit = (headed_ref[side] - center) * scaling
        low_ref[side] = (
            live_ref[side]
            * (gain * scaling)
            * (near_ref[side] - sums[1:2] * inverse - unit * (sums[0:1] * inverse))
        ).astype(BF16)

    for part in range(4):
        across(rep, part).wait_send()
        relay(far, part).wait_send()
        far_move(part).wait_send()
    own_head(rep).wait_send()
    move(9, cot_ref, cot_in, far).wait_send()
    move(10, labels_ref, labels_in, far).wait_send()
    for side in range(2):
        acc_move(side).wait_send()
        gm_move(side, par).wait_send()
    for side in range(2):
        core_move(side).wait_send()
    near_move.wait_send()

    @pl.when(upper == 0)
    def _():
        move(15, depth_out, depth_ref, far).wait_send()
        move(16, logits_out, logits_ref, far).wait_recv()

    @pl.when(upper == 1)
    def _():
        move(16, logits_out, logits_ref, far).wait_send()
        move(15, depth_out, depth_ref, far).wait_recv()

    if split:
        for copy in to_mate:
            copy.wait_recv()
            copy.wait_send()
        for copy in (x_own, x_far, x_cut, relay_own, relay_far, copy_x, copy_z, near_xz, far_xz):
            copy.wait_send()


def message_streams(
    split, layout, headed, shifts, w_messages, w_gates, w_classes, gain, shift, cot, labels, afar
):
    n_dp = lax.axis_size("dp")
    span, middle = cot.shape
    small = middle // 2
    classes = w_classes.shape[1]
    vmem = pl.BlockSpec(memory_space=pltpu.VMEM)
    dma = pltpu.SemaphoreType.DMA
    shape = jax.ShapeDtypeStruct
    halves = (2, 2 * span, middle)
    heads = (4, 2, 2 * span, middle)
    out_shape = [
        shape((span, middle), F32),
        shape((span, 128), F32),
        shape((middle, middle), BF16),
        shape((middle, 128), F32),
        shape(halves, BF16),
        shape((2, middle), F32),
    ]
    if split:
        out_shape += [shape((small, w_messages.shape[0]), BF16)] + [shape(afar[0].shape, BF16)] * 2
        out_shape += [shape((2,) + afar[0].shape, BF16)] * 4
    else:
        out_shape += [shape(heads, BF16), shape(halves, BF16)]
    scratch = [
        pltpu.VMEM(w_messages.shape, BF16),
        pltpu.VMEM((2, 2 * span, 1), F32),
        pltpu.VMEM(halves, F32),
        pltpu.VMEM((2, span, middle), F32),
        pltpu.VMEM((2, span, middle), F32),
        pltpu.VMEM((2, span, middle), F32),
        pltpu.VMEM((span, middle), BF16),
        pltpu.VMEM((span, 128), jnp.int32),
        pltpu.VMEM((span, middle), F32),
        pltpu.VMEM((span, 128), F32),
        pltpu.VMEM((5,) + halves, BF16),
        pltpu.VMEM((2,) + halves, F32),
        pltpu.VMEM(halves, F32),
        pltpu.VMEM(halves, BF16),
        pltpu.VMEM(halves, BF16),
        pltpu.VMEM(halves, BF16),
        pltpu.VMEM(halves, BF16),
        pltpu.VMEM(halves, BF16),
        pltpu.VMEM(halves, BF16),
        pltpu.VMEM((2, 2, middle), F32),
        pltpu.VMEM((2, n_dp, 2, middle), F32),
        dma,
        dma((MOVES,)),
        dma((MOVES,)),
        dma((2, n_dp)),
        dma((2, n_dp)),
        pltpu.VMEM(shifts.shape, BF16),
        dma,
    ]
    if split:
        scratch += [
            pltpu.VMEM(heads, BF16),
            pltpu.VMEM(halves, BF16),
            pltpu.VMEM(heads, BF16),
            pltpu.VMEM((2, 2 * span, small), BF16),
            pltpu.VMEM((2, 2 * span, small), BF16),
            pltpu.VMEM((2, 2 * span, small), BF16),
            pltpu.VMEM((2, small, 4 * span), BF16),
        ]
    return pl.pallas_call(
        functools.partial(message_kernel, split, n_dp, classes),
        in_specs=[pl.BlockSpec(memory_space=pltpu.SMEM)]
        + [vmem] * 2
        + [pl.BlockSpec(memory_space=pl.ANY)] * 2
        + [vmem] * 6
        + [pl.BlockSpec(memory_space=pl.ANY)] * len(afar),
        out_specs=[vmem] * 7 + [pl.BlockSpec(memory_space=pl.ANY) if split else vmem] * (len(out_shape) - 7),
        out_shape=out_shape,
        scratch_shapes=scratch,
        compiler_params=pltpu.CompilerParams(
            collective_id=11, has_side_effects=True, vmem_limit_bytes=VMEM_LIMIT
        ),
        name="message_streams",
    )(
        layout,
        layout,
        headed,
        shifts,
        w_messages,
        w_gates,
        jnp.pad(w_classes, ((0, 0), (0, 128 - classes))),
        gain[None, :],
        shift[None, :],
        cot,
        jnp.broadcast_to(labels[:, None], (span, 128)),
        *afar,
    )


def heads_taps(t_ref, low_ref, taken_ref, side):
    span = t_ref.shape[2]

    @pl.loop(0, taken_ref.shape[0])
    def _(t):
        for k in range(2):
            at = pl.ds(k * span, span)
            taken_ref[t, at, :] = inner_rows(t_ref[t, 2 * side + k], low_ref[side, at, :]).astype(
                BF16
            )


def heads_tile(c, taken_ref, w_ref, tile_ref):
    taps, _, _ = taken_ref.shape
    wide = w_ref.shape[1] // taps
    step = tile_ref.shape[1]
    total = 0.0
    for t in range(taps):
        at = pl.ds(pl.multiple_of(t * wide + c * step, step), step)
        total = total + product(taken_ref[t], w_ref[:, at])
    tile_ref[...] = total


def heads_loads(w_hbm, w_ref, sems):
    taps = sems.shape[0]
    wide = w_ref.shape[1] // taps
    spans = [pl.ds(t * wide, wide) for t in range(taps)]
    return [
        pltpu.make_async_copy(w_hbm.at[:, at], w_ref.at[:, at], sems.at[t])
        for t, at in enumerate(spans)
    ]


def meet(partners):
    barrier = pltpu.get_barrier_semaphore()
    for partner in partners:
        pl.semaphore_signal(barrier, inc=1, device_id=partner, device_id_type=MESH)
    pl.semaphore_wait(barrier, len(partners))


def heads_far_kernel(split, low_ref, s_ref, w_hbm, *refs):
    sum_ref, *refs = refs
    if split:
        low_x, low_z, *refs = refs
    w_ref, taken_ref, tile_ref, kept, core_out, core_in, load_sems, send, recv = refs
    rep, dp = lax.axis_index("rep"), lax.axis_index("dp")
    par, upper = lax.rem(rep, 2), rep // 2
    mate = rep + 1 - 2 * par
    beside, along = dp + 1 - 2 * lax.rem(dp, 2), dp + 2 - 4 * lax.rem(dp // 2, 2)
    span = s_ref.shape[2]
    tiles = sum_ref.shape[0]
    loads = heads_loads(w_hbm, w_ref, load_sems)
    for load in loads:
        load.start()
    meet([{"rep": mate}] + ([{"dp": beside}, {"dp": along}] if split else []))

    def block(parity):
        return pl.ds(pl.multiple_of(parity * span, span), span)

    if split:
        copy_x = send_to("dp", beside, low_ref, low_x, send.at[tiles], recv.at[tiles])
        copy_z = send_to("dp", along, low_ref, low_z, send.at[tiles + 1], recv.at[tiles + 1])
        copy_z.start()
        copy_x.start()

    def core_move(c):
        return send_to("rep", mate, core_out.at[c], core_in.at[c], send.at[c], recv.at[c])

    heads_taps(s_ref, low_ref, taken_ref, 1 - upper)
    for load in loads:
        load.wait()

    @pl.loop(0, tiles)
    def _(c):
        heads_tile(c, taken_ref, w_ref, tile_ref)
        core_out[c] = tile_ref[block(1 - par), :].astype(BF16)
        core_move(c).start()
        kept[c] = tile_ref[block(par), :]

    for c in range(tiles):
        core_move(c).wait_recv()
        sum_ref[c] = (kept[c] + core_in[c].astype(F32)).astype(BF16)
        core_move(c).wait_send()
    if split:
        for copy in (copy_x, copy_z):
            copy.wait_recv()
            copy.wait_send()


def heads_near_kernel(split, low_ref, s_ref, w_hbm, sum_ref, *refs):
    if split:
        low_z, *refs = refs
    out_ref, *refs = refs
    if split:
        low_xz, *refs = refs
    w_ref, taken_ref, tile_ref, kept, far_in, near_out, near_in, load_sems, send, recv = refs
    rep, dp = lax.axis_index("rep"), lax.axis_index("dp")
    par, upper = lax.rem(rep, 2), rep // 2
    mate, far = rep + 1 - 2 * par, rep + 2 - 4 * upper
    beside = dp + 1 - 2 * lax.rem(dp, 2)
    span = s_ref.shape[2]
    tiles = sum_ref.shape[0]
    step = tile_ref.shape[1]
    loads = heads_loads(w_hbm, w_ref, load_sems)
    for load in loads:
        load.start()
    meet([{"rep": mate}, {"rep": far}] + ([{"dp": beside}] if split else []))

    def block(parity):
        return pl.ds(pl.multiple_of(parity * span, span), span)

    def far_move(c):
        return send_to("rep", far, sum_ref.at[c], far_in.at[c], send.at[c], recv.at[c])

    def near_move(c):
        return send_to(
            "rep", mate, near_out.at[c], near_in.at[c], send.at[tiles + c], recv.at[tiles + c]
        )

    for c in range(tiles):
        far_move(c).start()
    if split:
        copy_xz = send_to("dp", beside, low_z, low_xz, send.at[2 * tiles], recv.at[2 * tiles])
        copy_xz.start()
    heads_taps(s_ref, low_ref, taken_ref, upper)
    for load in loads:
        load.wait()

    @pl.loop(0, tiles)
    def _(c):
        heads_tile(c, taken_ref, w_ref, tile_ref)
        near_out[c] = tile_ref[block(1 - par), :].astype(BF16)
        near_move(c).start()
        kept[c] = tile_ref[block(par), :]

    for c in range(tiles):
        near_move(c).wait_recv()
        far_move(c).wait_recv()
        out_ref[:, c * step : (c + 1) * step] = (
            kept[c] + near_in[c].astype(F32) + far_in[c].astype(F32)
        ).astype(BF16)
        near_move(c).wait_send()
        far_move(c).wait_send()
    if split:
        copy_xz.wait_recv()
        copy_xz.wait_send()


def heads_back(split, low, shifts, w_heads):
    taps, _, span, _ = shifts.shape
    wide = w_heads.shape[1] // taps
    tiles = wide // 512
    vmem = pl.BlockSpec(memory_space=pltpu.VMEM)
    hbm = pl.BlockSpec(memory_space=pl.ANY)
    dma = pltpu.SemaphoreType.DMA
    shape = jax.ShapeDtypeStruct
    cut = (tiles, span, 512)
    scratch = [
        pltpu.VMEM(w_heads.shape, BF16),
        pltpu.VMEM((taps, 2 * span, low.shape[2]), BF16),
        pltpu.VMEM((2 * span, 512), F32),
        pltpu.VMEM(cut, F32),
    ]

    def of(number):
        return pltpu.CompilerParams(
            collective_id=number, has_side_effects=True, vmem_limit_bytes=VMEM_LIMIT
        )

    lows = [shape(low.shape, BF16)] * (2 * split)
    far_sum, *lows = pl.pallas_call(
        functools.partial(heads_far_kernel, split),
        in_specs=[vmem, vmem, hbm],
        out_specs=[vmem] * (1 + len(lows)),
        out_shape=[shape(cut, BF16)] + lows,
        scratch_shapes=scratch
        + [pltpu.VMEM(cut, BF16)] * 2
        + [dma((taps,)), dma((tiles + 2,)), dma((tiles + 2,))],
        compiler_params=of(12),
        name="heads_far",
    )(low, shifts, w_heads)

    def near(far_sum, *lows):
        last = lows[1:]
        grad, *more = pl.pallas_call(
            functools.partial(heads_near_kernel, split),
            in_specs=[vmem, vmem, hbm, vmem] + [vmem] * len(last),
            out_specs=[vmem] * (1 + len(last)),
            out_shape=[shape((span, wide), BF16)] + [shape(low.shape, BF16)] * len(last),
            scratch_shapes=scratch
            + [pltpu.VMEM(cut, BF16)] * 3
            + [dma((taps,)), dma((2 * tiles + 1,)), dma((2 * tiles + 1,))],
            compiler_params=of(13),
            name="heads_near",
        )(low, shifts, w_heads, far_sum, *last)
        return [grad] + list(lows) + more

    return far_sum, lows, near


def heads_shard_kernel(per_tap, at_ref, layout_ref, *refs):
    lows, trunks = refs[:4], refs[4:13]
    out_ref, taken, turned, kinds = refs[13:]
    unit = pl.program_id(1)
    at = at_ref[pl.program_id(0)] + unit
    tap, chunk = at // per_tap, at % per_tap
    rows = lows[0].shape[1]
    span = rows // 2
    par, upper = at_ref[6], at_ref[7]

    places = [(0, side, k) for side in range(2) for k in range(2)]
    for number in (1, 2):
        places += [(number, side, par) for side in (upper, 1 - upper)]
        places += [(number, side, 1 - par) for side in range(2)]
    places += [(3, side, k) for k in (par, 1 - par) for side in range(2)]

    @pl.when((pl.program_id(0) == 0) & (unit == 0))
    def _():
        for number, low in enumerate(lows):
            for side in range(2):
                for k in range(2):
                    turned[number, side, k] = low[side, k * span : (k + 1) * span, :].T

    @pl.when((unit == 0) | (chunk == 0))
    def _():
        for kind, extent in enumerate((16, 8)):
            kinds[kind] = shift_in_maps(extent, tap, span)
        for slot, (number, side, k) in enumerate(places):
            large = layout_ref[at_ref[2 + number] + 2 * side + k, 1] == 16
            picks = kinds[jnp.where(large, 0, 1)]
            taken[:, slot * span : (slot + 1) * span] = product(
                turned[number, side, k], picks
            ).astype(BF16)

    total = 0.0
    slot = 0
    for trunk in trunks:
        strip = trunk[...].reshape(-1, trunk.shape[-1])
        depth = strip.shape[0]
        total = total + product(taken[:, slot : slot + depth], strip)
        slot += depth
    out_ref[0] = total.astype(BF16)


def heads_shard(at, layout, lows, trunks, units, lanes):
    _, rows, outs = lows[0].shape
    wide = trunks[0].shape[2]
    per_tap = wide // lanes
    whole = pl.BlockSpec(lows[0].shape, lambda i, j, f, g: (0, 0, 0))

    def strip_of(trunk):
        lead = trunk.shape[:-1]
        return pl.BlockSpec(
            lead + (lanes,), lambda i, j, f, g: (0,) * len(lead) + ((f[i] + j) % per_tap,)
        )

    strips = [strip_of(trunk) for trunk in trunks]
    return pl.pallas_call(
        functools.partial(heads_shard_kernel, per_tap),
        grid_spec=pltpu.PrefetchScalarGridSpec(
            num_scalar_prefetch=2,
            grid=(2, units),
            in_specs=[whole] * 4 + strips,
            out_specs=pl.BlockSpec((1, outs, lanes), lambda i, j, f, g: (i, 0, j)),
            scratch_shapes=[
                pltpu.VMEM((outs, 8 * rows), BF16),
                pltpu.VMEM((4, 2, 2, outs, rows // 2), BF16),
                pltpu.VMEM((2, rows // 2, rows // 2), BF16),
            ],
        ),
        out_shape=jax.ShapeDtypeStruct((2, outs, units * lanes), BF16),
        compiler_params=params(),
        cost_estimate=cost(32 * rows * outs * units * lanes, 32 * rows * units * lanes),
        name="heads_shard",
    )(at, layout, *lows, *trunks)


CHUNK_ROWS = (384, 512, 384, 384, 384, 256, 256)
CHUNK_BASE = (0, 384, 1408, 1792, 2176, 896, 1152)
SMALL_ROWS = 2560
HELD_ROWS = 1408
SPATIAL_BASE = 1408
REDUCE_BASE = 896


def trunk_back_kernel(*refs):
    refs = list(refs)

    def take(count):
        taken, refs[:count] = refs[:count], []
        return taken

    layout_ref, areas_ref, grad_ref, expanded_ref, in_ref = take(5)
    reduced_ref, spatial_ref, sums_one_ref, sums_two_ref, sums_three_ref = take(5)
    hidden_one_ref, hidden_two_ref, shift_taps_ref = take(3)
    w_reduce_hbm, w_spatial_hbm, w_expand_ref = take(3)
    gain_mid_ref, shift_mid_ref, gain_wide_ref, shift_wide_ref = take(4)
    gates_ref, classes_ref, head_norm_ref = take(3)
    out_ref, norm_one_ref, norm_two_ref, norm_three_ref, half_ref, heads_norm_ref = take(6)
    p_ref, core_in, core_out, y_in, x_out, x_in, z_out, z_in = take(8)
    z_mid, zz_in = take(2)
    low_wide, moved_ref, total_ref, block_mid, block_wide = take(5)
    slots_mid_rep, slots_mid_dp, slots_wide_rep, slots_wide_dp = take(4)
    rep_send, rep_recv, dp_send, dp_recv, send, recv, norm_send, norm_recv = take(8)
    w_reduce_ref, w_spatial_ref, hidden_all, low_all, moved_all, spatial_own = take(6)
    load_sems, gather_send, gather_recv = take(3)

    rep, dp = lax.axis_index("rep"), lax.axis_index("dp")
    par, upper = lax.rem(rep, 2), rep // 2
    x, z = lax.rem(dp, 2), dp // 2
    mate, far, beside = rep + 1 - 2 * par, rep + 2 - 4 * upper, dp + 1 - 2 * x
    low_z, high_z = lax.rem(z, 2), z // 2
    along, over = dp + 2 - 4 * low_z, dp + 4 - 8 * high_z
    span, wide = in_ref.shape
    middle = reduced_ref.shape[1]
    taps = shift_taps_ref.shape[0]
    loads = [
        pltpu.make_async_copy(w_spatial_hbm, w_spatial_ref, load_sems.at[0]),
        pltpu.make_async_copy(w_reduce_hbm, w_reduce_ref, load_sems.at[1]),
    ]
    for load in loads:
        load.start()
    barrier = pltpu.get_barrier_semaphore()
    for axis, size in (("rep", 4), ("dp", 8)):
        me = lax.axis_index(axis)
        for k in range(1, size):
            pl.semaphore_signal(
                barrier, inc=1, device_id={axis: lax.rem(me + k, size)}, device_id_type=MESH
            )

    def remote(src, dst, c, slot, to):
        return pltpu.make_async_remote_copy(
            src_ref=src,
            dst_ref=dst,
            send_sem=send.at[c, slot],
            recv_sem=recv.at[c, slot],
            device_id=to,
            device_id_type=MESH,
        )

    def whole(c, at=0, size=None):
        size = CHUNK_ROWS[c] if size is None else size
        return pl.ds(pl.multiple_of(CHUNK_BASE[c] + at, 16), size)

    def halves(c):
        return pl.ds(CHUNK_BASE[c] // 2, CHUNK_ROWS[c] // 2)

    def core_copy(c, hi):
        return remote(
            p_ref.at[2 * hi + 1 - par, whole(c)], core_in.at[hi, whole(c)], c, hi, {"rep": mate}
        )

    def y_copy(c):
        return remote(core_out.at[whole(c)], y_in.at[whole(c)], c, 2, {"rep": far})

    def x_copy(c):
        return remote(x_out.at[halves(c)], x_in.at[halves(c)], c, 3, {"dp": beside})

    def piece(c, base, at, size):
        return pl.ds(pl.multiple_of(CHUNK_BASE[c] // base + at, 16), size)

    def z_copy(c):
        size = CHUNK_ROWS[c] // 4
        return remote(
            z_out.at[piece(c, 2, (1 - low_z) * size, size)],
            z_in.at[piece(c, 4, 0, size)],
            c,
            4,
            {"dp": along},
        )

    def zz_copy(c):
        at = piece(c, 4, 0, CHUNK_ROWS[c] // 4)
        return remote(z_mid.at[at], zz_in.at[at], c, 5, {"dp": over})

    def own_place(c, low):
        size = CHUNK_ROWS[c] // 4
        return whole(c, x * 2 * size + low * size, size)

    def z_back(c, incoming):
        place = own_place(c, 1 - low_z if incoming else low_z)
        return remote(half_ref.at[place], half_ref.at[place], c, 6, {"dp": along})

    def last_copy(c, incoming):
        half = CHUNK_ROWS[c] // 2
        place = whole(c, (1 - x if incoming else x) * half, half)
        return remote(half_ref.at[place], half_ref.at[place], c, 7, {"dp": beside})

    def step(c, stage):
        if stage == 0:
            for hi in range(2):
                core_copy(c, hi).start()
        elif stage == 1:
            for hi in range(2):
                core_copy(c, hi).wait_recv()
            core_out[whole(c)] = (
                p_ref[2 * (1 - upper) + par, whole(c)].astype(F32)
                + core_in[1 - upper, whole(c)].astype(F32)
            ).astype(BF16)
            y_copy(c).start()
        elif stage == 2 and c in (2, 3, 4):
            half = CHUNK_ROWS[c] // 2
            at = CHUNK_BASE[c] - SPATIAL_BASE

            def own(k):
                return spatial_own[pl.ds(pl.multiple_of(at + k * half, 16), half)]

            x_out[halves(c)] = own(1 - x).astype(BF16)
            x_copy(c).start()
            z_out[halves(c)] = own(x).astype(BF16)
        elif stage == 2:
            y_copy(c).wait_recv()
            half = CHUNK_ROWS[c] // 2

            def both(at):
                place = whole(c, at, half)
                return (
                    p_ref[rep, place].astype(F32)
                    + core_in[upper, place].astype(F32)
                    + y_in[place].astype(F32)
                )

            x_out[halves(c)] = both((1 - x) * half).astype(BF16)
            x_copy(c).start()
            z_out[halves(c)] = both(x * half).astype(BF16)
        elif stage == 3:
            x_copy(c).wait_recv()
            z_out[halves(c)] = (
                z_out[halves(c)].astype(F32) + x_in[halves(c)].astype(F32)
            ).astype(BF16)
            z_copy(c).start()
        elif stage == 4:
            z_copy(c).wait_recv()
            size = CHUNK_ROWS[c] // 4
            at = piece(c, 4, 0, size)
            z_mid[at] = (
                z_out[piece(c, 2, low_z * size, size)].astype(F32) + z_in[at].astype(F32)
            ).astype(BF16)
            zz_copy(c).start()
        elif stage == 5:
            zz_copy(c).wait_recv()
            at = piece(c, 4, 0, CHUNK_ROWS[c] // 4)
            half_ref[own_place(c, low_z)] = (
                z_mid[at].astype(F32) + zz_in[at].astype(F32)
            ).astype(BF16)
            z_back(c, False).start()
        elif stage == 6:
            z_back(c, True).wait_recv()
            last_copy(c, False).start()
        else:
            last_copy(c, True).wait_recv()
            if c not in (2, 3, 4):
                for hi in range(2):
                    core_copy(c, hi).wait_send()
                y_copy(c).wait_send()
            x_copy(c).wait_send()
            z_copy(c).wait_send()
            zz_copy(c).wait_send()
            z_back(c, False).wait_send()
            last_copy(c, False).wait_send()

    def steps(*which):
        def run():
            for c, stage in which:
                step(c, stage)

        return run

    live = live_column(layout_ref, dp * 4 + rep, span)
    inverse = inverse_count(areas_ref, span)

    def stats(sums_ref):
        center = sums_ref[0:1, :] * inverse
        return center, lax.rsqrt(sums_ref[1:2, :] * inverse - center * center + EPS)

    def norm_move(to, slot):
        at = heads_norm_ref.at[slot]
        return send_to("rep", to, at, at, norm_send.at[to], norm_recv.at[slot])

    def local_sums(blocks, value, unit, at):
        masked = live * value
        blocks[0, 0:1, at] = jnp.sum(masked * unit, 0, keepdims=True)
        blocks[0, 1:2, at] = jnp.sum(masked, 0, keepdims=True)

    def everywhere(number, blocks, rep_slots, dp_slots, meanwhile, later):
        if number == 0:
            pl.semaphore_wait(barrier, 10)
            heads_norm_ref[rep] = head_norm_ref[...]
            for k in range(1, 4):
                norm_move(lax.rem(rep + k, 4), rep).start()
        blocks[1] = total_along(
            "rep", 4, blocks.at[0], rep_slots, rep_send.at[number], rep_recv.at[number], meanwhile
        )
        return total_along(
            "dp", 8, blocks.at[1], dp_slots, dp_send.at[number], dp_recv.at[number], later
        )

    def slope(value):
        sigma = jax.nn.sigmoid(value)
        return sigma * (1.0 + value * (1.0 - sigma))

    def spread_back(grad, unit, sums, gain, scaling):
        return (
            live
            * (gain * scaling)
            * (grad - sums[1:2] * inverse - unit * (sums[0:1] * inverse))
        ).astype(BF16)

    center, scaling = stats(sums_three_ref)
    strips = [pl.ds(k, middle) for k in range(0, wide, middle)]

    def unit_at(at):
        return (expanded_ref[:, at] - center[:, at.start : at.start + middle]) * scaling[
            :, at.start : at.start + middle
        ]

    for at in strips:
        unit = unit_at(at)
        pre = unit * gain_wide_ref[:, at] + shift_wide_ref[:, at] + in_ref[:, at].astype(F32)
        grad = grad_ref[:, at].astype(F32) * slope(pre)
        out_ref[:, at] = grad
        local_sums(block_wide, grad, unit, at)

    def gather(number, held, to, slot):
        at = held.at[slot]
        return send_to(
            "rep", to, at, at, gather_send.at[number, to], gather_recv.at[number, slot]
        )

    hidden_all[rep] = hidden_one_ref[...]

    def first_chunk():
        half = middle // 2
        rows = classes_ref.shape[1]
        for q in range(4):
            p_ref[q, half : half + rows, :] = classes_ref[q]
            p_ref[q, half + rows : CHUNK_ROWS[0], :] = jnp.zeros(
                (CHUNK_ROWS[0] - half - rows, middle), BF16
            )
        for k in range(2):
            p_ref[2 * upper + k, :half, :] = gates_ref[k * half : (k + 1) * half, :]
            p_ref[2 * (1 - upper) + k, :half, :] = jnp.zeros((half, middle), BF16)
        step(0, 0)
        for k in range(1, 4):
            gather(0, hidden_all, lax.rem(rep + k, 4), rep).start()
        step(0, 1)

    sums = everywhere(
        0,
        block_wide,
        slots_wide_rep,
        slots_wide_dp,
        first_chunk,
        steps((0, 2)),
    )
    norm_three_ref[...] = sums
    for at in strips:
        cut = slice(at.start, at.start + middle)
        low_wide[:, at] = spread_back(
            out_ref[:, at], unit_at(at), sums[:, cut], gain_wide_ref[:, at], scaling[:, cut]
        )

    center, scaling = stats(sums_two_ref)
    unit = (spatial_ref[...] - center) * scaling
    normed = unit * gain_mid_ref[1:2, :] + shift_mid_ref[1:2, :]
    total_ref[...] = against(low_wide[...], w_expand_ref[...]) * slope(normed)

    def expand_gradient():
        rows = middle // 4
        for k in range(wide // middle):
            tile = inner_rows(
                hidden_two_ref[...], low_wide[:, k * middle : (k + 1) * middle]
            ).astype(BF16)
            for q in range(4):
                at = CHUNK_BASE[1] + k * rows
                p_ref[q, at : at + rows, :] = tile[q * rows : (q + 1) * rows]
        step(1, 0)
        step(1, 1)

    local_sums(block_mid.at[0], total_ref[...], unit, slice(None))
    sums = everywhere(
        1,
        block_mid.at[0],
        slots_mid_rep.at[0],
        slots_mid_dp.at[0],
        expand_gradient,
        steps((0, 3), (1, 2)),
    )
    norm_two_ref[...] = sums
    low_mid = spread_back(total_ref[...], unit, sums, gain_mid_ref[1:2, :], scaling)

    total_ref[...] = jnp.zeros_like(total_ref)
    loads[0].wait()
    for t in range(taps):
        moved_ref[t] = inner_rows(shift_taps_ref[t], low_mid).astype(BF16)

    @pl.loop(0, taps)
    def _(t):
        at = pl.ds(pl.multiple_of(t * middle, middle), middle)
        total_ref[...] += against(moved_ref[t], w_spatial_ref[at, :])

    center, scaling = stats(sums_one_ref)
    unit = (reduced_ref[...] - center) * scaling
    normed = unit * gain_mid_ref[0:1, :] + shift_mid_ref[0:1, :]
    total_ref[...] = total_ref[...] * slope(normed)

    def give_low():
        low_all[rep] = low_mid
        for k in range(1, 4):
            gather(1, low_all, lax.rem(rep + k, 4), rep).start()

    def spatial_gradient():
        large = [layout_ref[dp * 4 + p, 1] == 16 for p in range(4)]
        units = spatial_own.shape[0] // 128
        per_tap = middle // 128

        @pl.loop(0, units)
        def _(i):
            unit = units * rep + i
            tap, cut = unit // per_tap, unit % per_tap

            @pl.when((i == 0) | (cut == 0))
            def _():
                kinds = [shift_in_maps(extent, tap, span, 2) for extent in (16, 8)]
                for p in range(4):
                    picks = jnp.where(large[p], kinds[0], kinds[1])
                    moved_all[p] = inner_rows(picks, low_all[p]).astype(BF16)

            lanes = pl.ds(pl.multiple_of(cut * 128, 128), 128)
            total = 0.0
            for p in range(4):
                total = total + inner_rows(hidden_all[p, :, lanes], moved_all[p])
            spatial_own[pl.ds(pl.multiple_of(i * 128, 128), 128), :] = total

    local_sums(block_mid.at[1], total_ref[...], unit, slice(None))
    sums = everywhere(
        2,
        block_mid.at[1],
        slots_mid_rep.at[1],
        slots_mid_dp.at[1],
        give_low,
        steps((0, 4), (1, 3)),
    )
    norm_one_ref[...] = sums
    low_first = spread_back(total_ref[...], unit, sums, gain_mid_ref[0:1, :], scaling)
    quarter = wide // 4
    for q in range(4):
        p_ref[q, REDUCE_BASE : REDUCE_BASE + quarter, :] = inner_rows(
            in_ref[:, q * quarter : (q + 1) * quarter], low_first
        ).astype(BF16)
    step(5, 0)
    step(6, 0)
    step(0, 5)
    step(5, 1)
    step(1, 4)
    step(6, 1)
    for number, held in enumerate((hidden_all, low_all)):
        for k in range(1, 4):
            other = lax.rem(rep + k, 4)
            gather(number, held, other, other).wait_recv()
            gather(number, held, other, rep).wait_send()
    spatial_gradient()
    step(2, 2)
    step(4, 2)
    step(3, 2)
    loads[1].wait()
    for k in range(0, wide, middle):
        out_ref[:, k : k + middle] += against(low_first, w_reduce_ref[k : k + middle, :])
    for turn in (
        ((5, 2), (1, 5), (2, 3), (6, 2), (4, 3), (3, 3), (2, 4), (0, 6)),
        ((5, 3), (4, 4), (6, 3), (2, 5), (3, 4), (0, 7), (4, 5), (1, 6)),
        ((5, 4), (3, 5), (1, 7), (6, 4), (2, 6), (5, 5), (2, 7), (4, 6)),
        ((6, 5), (3, 6), (4, 7), (5, 6), (6, 6), (3, 7), (5, 7), (6, 7)),
    ):
        for c, stage in turn:
            step(c, stage)
    for k in range(1, 4):
        other = lax.rem(rep + k, 4)
        norm_move(other, other).wait_recv()
        norm_move(other, rep).wait_send()


def trunk_back(
    layout,
    grad,
    expanded,
    inputs,
    reduced,
    spatial,
    sums,
    hidden_one,
    hidden_two,
    shift_taps,
    w_reduce,
    w_spatial,
    w_expand,
    gain_mid,
    shift_mid,
    gain_wide,
    shift_wide,
    gates,
    classes,
    head_norm,
):
    span, wide = inputs.shape
    middle = reduced.shape[1]
    taps = shift_taps.shape[0]
    vmem = pl.BlockSpec(memory_space=pltpu.VMEM)
    dma = pltpu.SemaphoreType.DMA
    shape = jax.ShapeDtypeStruct
    small = (SMALL_ROWS, middle)
    held = (HELD_ROWS, middle)
    every = (4, span, middle)
    half = (SMALL_ROWS // 2, middle)
    chunks = len(CHUNK_ROWS)
    out_shape = [
        shape((span, wide), F32),
        shape((2, middle), F32),
        shape((2, middle), F32),
        shape((2, wide), F32),
        shape(small, BF16),
        shape((4, 2, middle), F32),
    ]
    return pl.pallas_call(
        trunk_back_kernel,
        in_specs=[pl.BlockSpec(memory_space=pltpu.SMEM)]
        + [vmem] * 12
        + [pl.BlockSpec(memory_space=pl.ANY)] * 2
        + [vmem] * 8,
        out_specs=[vmem] * len(out_shape),
        out_shape=out_shape,
        scratch_shapes=[
            pltpu.VMEM((4,) + held, BF16),
            pltpu.VMEM((2,) + held, BF16),
            pltpu.VMEM(held, BF16),
            pltpu.VMEM(held, BF16),
            pltpu.VMEM(half, BF16),
            pltpu.VMEM(half, BF16),
            pltpu.VMEM(half, BF16),
            pltpu.VMEM((SMALL_ROWS // 4, middle), BF16),
            pltpu.VMEM((SMALL_ROWS // 4, middle), BF16),
            pltpu.VMEM((SMALL_ROWS // 4, middle), BF16),
            pltpu.VMEM((span, wide), BF16),
            pltpu.VMEM((taps, span, middle), BF16),
            pltpu.VMEM((span, middle), F32),
            pltpu.VMEM((2, 2, 2, middle), F32),
            pltpu.VMEM((2, 2, wide), F32),
            pltpu.VMEM((2, 4, 2, middle), F32),
            pltpu.VMEM((2, 8, 2, middle), F32),
            pltpu.VMEM((4, 2, wide), F32),
            pltpu.VMEM((8, 2, wide), F32),
            dma((3, 4)),
            dma((3, 4)),
            dma((3, 8)),
            dma((3, 8)),
            dma((chunks, 8)),
            dma((chunks, 8)),
            dma((4,)),
            dma((4,)),
            pltpu.VMEM(w_reduce.shape, BF16),
            pltpu.VMEM(w_spatial.shape, BF16),
            pltpu.VMEM(every, BF16),
            pltpu.VMEM(every, BF16),
            pltpu.VMEM(every, BF16),
            pltpu.VMEM((taps * middle // 4, middle), F32),
            dma((2,)),
            dma((2, 4)),
            dma((2, 4)),
        ],
        compiler_params=pltpu.CompilerParams(
            collective_id=9, has_side_effects=True, vmem_limit_bytes=VMEM_LIMIT
        ),
        name="trunk_back",
    )(
        layout,
        layout,
        grad,
        expanded,
        inputs,
        reduced,
        spatial,
        *sums,
        hidden_one,
        hidden_two,
        shift_taps,
        w_reduce,
        w_spatial,
        w_expand,
        gain_mid,
        shift_mid,
        gain_wide[None, :],
        shift_wide[None, :],
        gates,
        classes,
        head_norm,
    )


FINISH_STEPS = 4


def finish_kernel(
    classes,
    sums_ref,
    in_grad_ref,
    depth_in_ref,
    logits_in_ref,
    heads_in_ref,
    messages_in_ref,
    one_ref,
    two_ref,
    three_ref,
    heads_norm_ref,
    depth_ref,
    logits_ref,
    out_ref,
    reduce_ref,
    spatial_ref,
    expand_ref,
    heads_ref,
    gates_ref,
    messages_ref,
    classes_ref,
    gain_mid_ref,
    shift_mid_ref,
    gain_wide_ref,
    shift_wide_ref,
    gain_head_ref,
    shift_head_ref,
):
    middle = sums_ref.shape[1]
    now = pl.program_id(0)

    def held(base, size, at=0):
        return sums_ref[pl.ds(pl.multiple_of(base + at, 16), size), :].astype(F32)

    depth_ref[...] = depth_in_ref[...]
    out_ref[...] = in_grad_ref[...]
    heads_ref[...] = heads_in_ref[...].astype(F32)
    messages_ref[...] = messages_in_ref[...].astype(F32)
    gates = gates_ref.shape[0]
    gates_ref[...] = held(0, gates, now * gates)
    rows = expand_ref.shape[0]
    for k in range(expand_ref.shape[1] // middle):
        expand_ref[:, k * middle : (k + 1) * middle] = held(
            CHUNK_BASE[1] + k * rows * FINISH_STEPS, rows, now * rows
        )
    rows = spatial_ref.shape[0]
    spatial_ref[...] = held(SPATIAL_BASE, rows, now * rows)
    rows = reduce_ref.shape[0]
    reduce_ref[...] = held(REDUCE_BASE, rows, now * rows)

    @pl.when(now == 0)
    def _():
        logits_ref[...] = logits_in_ref[...].T[:classes, :]
        rows = classes_ref.shape[1] // 4
        tail = sums_ref[middle // 2 : middle // 2 + rows, :].astype(F32)
        held_classes = [tail[:, k * 128 : (k + 1) * 128] for k in range(4)]
        classes_ref[...] = jnp.concatenate(held_classes, 0).T[:classes, :]
        for at, norm in enumerate((one_ref, two_ref)):
            gain_mid_ref[at : at + 1, :] = norm[0:1, :]
            shift_mid_ref[at : at + 1, :] = norm[1:2, :]
        gain_wide_ref[...] = three_ref[0:1, :]
        shift_wide_ref[...] = three_ref[1:2, :]
        for k in range(4):
            gain_head_ref[:, k * middle : (k + 1) * middle] = heads_norm_ref[k, 0:1, :]
            shift_head_ref[:, k * middle : (k + 1) * middle] = heads_norm_ref[k, 1:2, :]


def finish(classes, sums, in_grad, depth, logits, heads, messages, one, two, three, heads_norm):
    span, wide = in_grad.shape
    middle = sums.shape[1]
    shape = jax.ShapeDtypeStruct
    out_shape = [
        shape(depth.shape, F32),
        shape((classes, span), F32),
        shape(in_grad.shape, F32),
        shape((wide // 4, middle), F32),
        shape((SMALL_ROWS - SPATIAL_BASE, middle), F32),
        shape((middle // 4, wide), F32),
        shape(heads.shape, F32),
        shape((middle // 2, middle), F32),
        shape(messages.shape, F32),
        shape((classes, middle // 4), F32),
        shape((2, middle), F32),
        shape((2, middle), F32),
    ] + [shape((1, wide), F32)] * 4

    def whole(array):
        zeros = (0,) * len(array.shape)
        return pl.BlockSpec(array.shape, lambda i: zeros)

    def by_rows(array):
        return pl.BlockSpec((array.shape[0] // FINISH_STEPS, array.shape[1]), lambda i: (i, 0))

    cut_in = (1, 2, 4, 5)
    cut_out = (0, 2, 3, 4, 5, 6, 7, 8)
    operands = (sums, in_grad, depth, logits, heads, messages, one, two, three, heads_norm)
    return pl.pallas_call(
        functools.partial(finish_kernel, classes),
        grid=(FINISH_STEPS,),
        in_specs=[by_rows(v) if k in cut_in else whole(v) for k, v in enumerate(operands)],
        out_specs=[by_rows(v) if k in cut_out else whole(v) for k, v in enumerate(out_shape)],
        out_shape=out_shape,
        compiler_params=params(),
        name="finish",
    )(*operands)


def silu_slope(value_in):
    sigma_of = jax.nn.sigmoid(value_in)
    return sigma_of * (1.0 + value_in * (1.0 - sigma_of))


MESH = pl.DeviceIdType.MESH


def greet(axes):
    barrier = pltpu.get_barrier_semaphore()
    count = 0
    for axis, size in axes:
        me = lax.axis_index(axis)
        for k in range(1, size):
            pl.semaphore_signal(
                barrier, inc=1, device_id={axis: lax.rem(me + k, size)}, device_id_type=MESH
            )
        count += size - 1
    pl.semaphore_wait(barrier, count)


def total_kernel(axes, x_ref, out_ref, *scratch):
    greet(axes)
    block = x_ref
    for number, (axis, size) in enumerate(axes):
        slots, stage, send_sems, recv_sems = scratch[4 * number : 4 * number + 4]
        me = lax.axis_index(axis)
        others = [lax.rem(me + k, size) for k in range(1, size)]
        for other in others:
            pltpu.make_async_remote_copy(
                src_ref=block,
                dst_ref=slots.at[me],
                send_sem=send_sems.at[other],
                recv_sem=recv_sems.at[me],
                device_id={axis: other},
                device_id_type=MESH,
            ).start()
        slots[me] = block[...]
        for other in others:
            copy = pltpu.make_async_remote_copy(
                src_ref=block,
                dst_ref=slots.at[other],
                send_sem=send_sems.at[other],
                recv_sem=recv_sems.at[other],
                device_id={axis: other},
                device_id_type=MESH,
            )
            copy.wait_recv()
            copy.wait_send()
        total = slots[0]
        for k in range(1, size):
            total = total + slots[k]
        if number == len(axes) - 1:
            out_ref[...] = total
        else:
            stage[...] = total
            block = stage


def total_of(left, right, axes):
    width = left.shape[0]
    packed = jnp.concatenate([left, right], 0).reshape(-1, 128)
    sized = tuple((axis, lax.axis_size(axis)) for axis in axes)
    scratch = []
    for _, size in sized:
        scratch += [
            pltpu.VMEM((size,) + packed.shape, F32),
            pltpu.VMEM(packed.shape, F32),
            pltpu.SemaphoreType.DMA((size,)),
            pltpu.SemaphoreType.DMA((size,)),
        ]
    number = 1 + (width != 512) + 2 * (len(axes) == 1)
    summed = pl.pallas_call(
        functools.partial(total_kernel, sized),
        out_shape=jax.ShapeDtypeStruct(packed.shape, F32),
        in_specs=[pl.BlockSpec(memory_space=pltpu.VMEM)],
        out_specs=pl.BlockSpec(memory_space=pltpu.VMEM),
        scratch_shapes=scratch,
        compiler_params=pltpu.CompilerParams(collective_id=number, has_side_effects=True),
        name="total",
    )(packed).reshape(2, width)
    return summed[0], summed[1]


def normalize(raw_value, column_sums, squares, pixel_count, norm_gain, norm_shift):
    center = column_sums / pixel_count
    spread_of = squares / pixel_count - center * center
    scaling = lax.rsqrt(spread_of + EPS)
    unit_value = (raw_value - center) * scaling
    return (unit_value * norm_gain + norm_shift, unit_value, scaling)


def moments(raw_value, living, axes):
    return total_of(
        jnp.sum(living * raw_value, 0), jnp.sum(living * raw_value * raw_value, 0), axes
    )


def norm_back(grad_out, unit_value, scaling, norm_gain, living, pixel_count, axes):
    grad_gain, grad_shift = total_of(
        jnp.sum(living * grad_out * unit_value, 0), jnp.sum(living * grad_out, 0), axes
    )
    grad_raw = (
        living
        * (norm_gain * scaling)
        * (grad_out - grad_shift / pixel_count - unit_value * grad_gain / pixel_count)
    )
    return (grad_raw, grad_gain, grad_shift)


def swap(value, bit):
    return lax.ppermute(value, "rep", [(k, k ^ bit) for k in range(4)])


def scatter_rep(value):
    return lax.psum_scatter(value.astype(BF16), "rep", scatter_dimension=0, tiled=True)


def total_dp(value):
    parts = lax.axis_size("dp")
    rows = value.shape[0]
    padded = -(-rows // (8 * parts)) * 8 * parts
    value = jnp.pad(value, ((0, padded - rows), (0, 0)))
    share = lax.psum_scatter(value, "dp", scatter_dimension=0, tiled=True)
    return lax.all_gather(share, "dp", axis=0, tiled=True)[:rows].astype(F32)


def shards(
    inputs,
    layout,
    labels,
    cot_depth,
    w_reduce,
    w_spatial,
    w_expand,
    w_heads,
    w_gates,
    w_messages,
    w_classes,
    gain_mid,
    shift_mid,
    gain_wide,
    shift_wide,
    gain_head,
    shift_head,
):
    pixels = inputs.shape[0]
    middle = w_reduce.shape[1]
    classes = w_classes.shape[1]
    group = lax.axis_size("rep")
    everyone = ("rep", "dp")
    rep = lax.axis_index("rep")
    parity = rep % 2
    upper = rep // 2
    first_row = lax.axis_index("dp") * group
    own_info = geometry(lax.dynamic_slice_in_dim(layout, first_row + rep, 1, 0), pixels)
    group_info = geometry(lax.dynamic_slice_in_dim(layout, first_row, group, 0), pixels)
    living = own_info[2][0].astype(F32)[:, None]
    group_living = group_info[2].astype(F32)
    living_all = group_living.reshape(group * pixels, 1)
    pixel_count = jnp.sum(
        jnp.minimum(layout[:, 0] * layout[:, 1] * layout[:, 2], pixels)
    ).astype(F32)
    split = lax.axis_size("dp") == 8
    if split:
        side = lax.axis_index("dp") % 2
        columns = [[z_at * 2 + k for z_at in range(4)] for k in range(2)]
    zero = jnp.zeros((1,), jnp.int32)
    first = jnp.reshape(9 * parity, (1,)).astype(jnp.int32)

    (
        reduced,
        sums_one,
        hidden_one,
        spatial,
        sums_two,
        hidden_two,
        expanded,
        sums_three,
        trunk_all,
        headed,
        shifts_own,
        shifts_all,
        *trunk_afar,
    ) = trunk_forward(
        split,
        inputs,
        layout,
        w_reduce,
        w_spatial,
        w_expand,
        w_heads,
        gain_mid,
        shift_mid,
        gain_wide,
        shift_wide,
    )
    upper_is_depth = upper == 0
    headed, late_classes, late_labels = lax.optimization_barrier((headed, w_classes, labels))
    depth, logits, gates_local, classes_local, head_low, head_norm, *rest = message_streams(
        split,
        layout,
        headed,
        shifts_all,
        w_messages,
        w_gates,
        late_classes,
        gain_head,
        shift_head,
        cot_depth,
        late_labels,
        trunk_afar + [trunk_all] if split else [],
    )
    classes_local = classes_local[:, :classes]
    is_depth = upper_is_depth
    if split:
        messages_local = rest[0]
    else:
        heads_all, message_all = rest
        heads_all = heads_all.reshape(4, group * pixels, middle)
        source = jnp.where(
            is_depth,
            jnp.concatenate([heads_all[1], heads_all[2], heads_all[3]], 1),
            jnp.concatenate([heads_all[0], heads_all[1], heads_all[2]], 1),
        )
        _, messages_local = rows_back(
            first, message_all.reshape(4 * pixels, middle), source, w_messages, shifts_all, 2, BF16
        )
        grad_messages = lax.psum_scatter(messages_local, "dp", scatter_dimension=1, tiled=True)
        gates_cut = gates_local.reshape(2, pixels, middle)
        gates_share = lax.dynamic_index_in_dim(gates_cut, parity, 0, keepdims=False).astype(F32)
        gates_share += swap(
            lax.dynamic_index_in_dim(gates_cut, 1 - parity, 0, keepdims=False), 1
        ).astype(F32)
    far_sum, lows, near = heads_back(split, head_low, shifts_all, w_heads)
    if split:
        messages_local, far_sum = lax.optimization_barrier((messages_local, far_sum))
    trunk_grad, *lows = near(far_sum, *lows)
    if split:
        grad_messages = lax.psum_scatter(
            messages_local, "dp", scatter_dimension=0, tiled=True, axis_index_groups=columns
        )
        dp = lax.axis_index("dp")
        beside, along = dp + 1 - 2 * side, dp + 2 - 4 * ((dp // 2) % 2)
        groups = [dp, beside, along, along + 1 - 2 * side]
        units = 9

        lower = dp % 4
        at = jnp.stack(
            [units * lower, units * (lower + 4)] + [group * k for k in groups] + [parity, upper]
        )
        far_x, far_z, mate_x, mate_z, trunk_xz, mate_xz = rest[1:]
        near_x, near_z = trunk_afar
        trunks = [trunk_all, near_x, far_x, mate_x, near_z, far_z, mate_z, trunk_xz, mate_xz]
        heads_local = heads_shard(
            at.astype(jnp.int32), layout, [head_low] + lows, trunks, units, 256
        )
        heads_local, trunk_grad = lax.optimization_barrier((heads_local, trunk_grad))
        grad_heads = lax.psum_scatter(
            heads_local,
            "dp",
            scatter_dimension=0,
            tiled=False,
            axis_index_groups=[[k, k + 4] for k in range(4)],
        )
    else:
        heads_local = heads_weight(
            head_low.reshape(group * pixels, middle),
            trunk_all.reshape(group * pixels, -1),
            shifts_all,
        )
        grad_heads = lax.psum_scatter(heads_local, "dp", scatter_dimension=1, tiled=True)
    if split:
        classes_wide = jnp.pad(classes_local.astype(BF16), ((0, 0), (0, 128 - classes)))
        classes_wide = classes_wide.reshape(4, 4, -1, 128)
        classes_wide = jnp.concatenate([classes_wide[:, k] for k in range(4)], 2)
        (
            input_grad,
            norm_one,
            norm_two,
            norm_three,
            small_sums,
            heads_norm,
        ) = trunk_back(
            layout,
            trunk_grad,
            expanded,
            inputs,
            reduced,
            spatial,
            [sums_one, sums_two, sums_three],
            hidden_one,
            hidden_two,
            shifts_own,
            w_reduce,
            w_spatial,
            w_expand,
            gain_mid,
            shift_mid,
            gain_wide,
            shift_wide,
            gates_local,
            classes_wide,
            head_norm,
        )
        every = finish(
            classes,
            small_sums,
            input_grad,
            depth,
            logits,
            grad_heads,
            grad_messages,
            norm_one,
            norm_two,
            norm_three,
            heads_norm,
        )
        narrow = (1, 8, 9)
        outs = [each.T if k in narrow else each for k, each in enumerate(every)]
        return tuple(outs[:12]) + tuple(each[0] for each in outs[12:])
    else:
        logits = logits[:, :classes]
        normed_one, unit_one, scale_one = normalize(
            reduced, sums_one[0], sums_one[1], pixel_count, gain_mid[0], shift_mid[0]
        )
        normed_two, unit_two, scale_two = normalize(
            spatial, sums_two[0], sums_two[1], pixel_count, gain_mid[1], shift_mid[1]
        )
        normed_three, unit_three, scale_three = normalize(
            expanded, sums_three[0], sums_three[1], pixel_count, gain_wide, shift_wide
        )
        pre_act = normed_three + inputs.astype(F32)
        pre_grad = trunk_grad.astype(F32) * silu_slope(pre_act)
        expand_raw, grad_gain_wide, grad_shift_wide = norm_back(
            pre_grad, unit_three, scale_three, gain_wide, living, pixel_count, everyone
        )
        expand_low = expand_raw.astype(BF16)
        expand_local = inner_rows(hidden_two, expand_low).astype(BF16)
        hidden_two_grad = against(expand_low, w_expand)
        spatial_raw, gain_grad_two, shift_grad_two = norm_back(
            hidden_two_grad * silu_slope(normed_two),
            unit_two,
            scale_two,
            gain_mid[1],
            living,
            pixel_count,
            everyone,
        )
        spatial_low = spatial_raw.astype(BF16)
        hidden_one_grad, spatial_local = rows_back(
            zero, spatial_low, hidden_one, w_spatial, shifts_own[:, None], 1, F32
        )
        reduced_raw, gain_grad_one, shift_grad_one = norm_back(
            hidden_one_grad * silu_slope(normed_one),
            unit_one,
            scale_one,
            gain_mid[0],
            living,
            pixel_count,
            everyone,
        )
        reduced_low = reduced_raw.astype(BF16)
        reduce_local = inner_rows(inputs, reduced_low).astype(BF16)
        input_grad = pre_grad + against(reduced_low, w_reduce)
        grad_expand = scatter_rep(expand_local)
        grad_spatial = scatter_rep(spatial_local)
        grad_reduce = scatter_rep(reduce_local)
        grad_classes = scatter_rep(classes_local)
        pieces = [
            gates_share.astype(BF16),
            grad_expand.reshape(-1, middle),
            grad_spatial,
            grad_classes.reshape(-1, middle),
        ]
        early = total_dp(jnp.concatenate(pieces, 0))
        rows = [piece.shape[0] for piece in pieces]
        starts = [sum(rows[:k]) for k in range(4)]
        grad_gates, expand_sum, grad_spatial, classes_sum = [
            early[at : at + size] for at, size in zip(starts, rows)
        ]
        grad_expand = expand_sum.reshape(grad_expand.shape)
        grad_classes = classes_sum.reshape(grad_classes.shape)
        grad_reduce = total_dp(grad_reduce)
        grad_gain_mid = jnp.stack([gain_grad_one, gain_grad_two], 0)
        grad_shift_mid = jnp.stack([shift_grad_one, shift_grad_two], 0)
    head_norms = lax.all_gather(
        head_norm, "rep", axis=1, tiled=True
    )
    return (
        depth,
        logits,
        input_grad,
        grad_reduce,
        grad_spatial,
        grad_expand,
        grad_heads.astype(F32),
        grad_gates,
        grad_messages.astype(F32),
        grad_classes,
        grad_gain_mid,
        grad_shift_mid,
        grad_gain_wide,
        grad_shift_wide,
        head_norms[0],
        head_norms[1],
    )


def solution(mesh):
    in_specs = (
        P(("dp", "rep"), None),
        P(),
        P(("dp", "rep")),
        P(("dp", "rep"), None),
        P(),
        P(),
        P(),
        P("rep", None),
        P(),
        P("rep", None),
        P(),
        P(),
        P(),
        P(),
        P(),
        P(),
        P(),
    )
    out_specs = (
        P(("dp", "rep"), None),
        P(("dp", "rep"), None),
        P(("dp", "rep"), None),
        P("rep", None),
        P("rep", None),
        P("rep", None),
        P("rep", "dp"),
        P("rep", None),
        P("rep", "dp"),
        P("rep", None),
        P(),
        P(),
        P(),
        P(),
        P(),
        P(),
    )
    return jax.shard_map(shards, mesh=mesh, in_specs=in_specs, out_specs=out_specs, check_vma=False)
```

```python
import functools

import jax
import jax.numpy as jnp
from jax import lax
from jax.experimental import pallas as pl
from jax.experimental.pallas import tpu as pltpu
from jax.sharding import PartitionSpec as P

EPS = 1e-05
F32 = jnp.float32
BF16 = jnp.bfloat16
VMEM_LIMIT = 60 * 2**20


def geometry(layout, span):
    position = jnp.arange(span, dtype=jnp.int32)
    height = layout[:, 0:1]
    map_width = layout[:, 1:2]
    images = layout[:, 2:3]
    map_area = height * map_width
    inside = position[None, :] % map_area
    row_of = inside // map_width
    col_of = inside % map_width
    living = position[None, :] < images * map_area
    return (row_of, col_of, living, height, map_width)


def neighbours(shape_info, dilation):
    row_of, col_of, living, height, map_width = shape_info
    span = row_of.shape[1]
    position = jnp.arange(span, dtype=jnp.int32)
    every = []
    for step_row in (-1, 0, 1):
        for step_col in (-1, 0, 1):
            target_row = row_of + dilation * step_row
            target_col = col_of + dilation * step_col
            inside = (
                living
                & (target_row >= 0)
                & (target_row < height)
                & (target_col >= 0)
                & (target_col < map_width)
            )
            neighbour = position[None, :] + dilation * (step_row * map_width + step_col)
            every.append(jnp.where(inside, neighbour, -1))
    return jnp.concatenate(every, 0).T


def shift_matrices(shape_info, dilation):
    devices, span = shape_info[0].shape
    picks = neighbours(shape_info, dilation).T.reshape(9, devices, span, 1)
    return (picks == jnp.arange(span, dtype=jnp.int32)).astype(BF16)


def product(left_side, right_side):
    return jnp.dot(left_side, right_side, preferred_element_type=F32)


def inner_rows(left_side, right_side):
    return lax.dot_general(
        left_side, right_side, (((0,), (0,)), ((), ())), preferred_element_type=F32
    )


def against(left_side, right_side):
    return lax.dot_general(
        left_side, right_side, (((1,), (1,)), ((), ())), preferred_element_type=F32
    )


def params():
    return pltpu.CompilerParams(vmem_limit_bytes=VMEM_LIMIT)


def cost(flops, moved):
    return pl.CostEstimate(flops=flops, bytes_accessed=moved, transcendentals=0)


def shifted(g_ref, s_ref):
    blocks, span = s_ref.shape[1], s_ref.shape[2]
    return jnp.concatenate(
        [
            inner_rows(s_ref[0, k], g_ref[pl.ds(k * span, span), :]).astype(BF16)
            for k in range(blocks)
        ],
        0,
    )


def heads_weight_kernel(g_ref, u_ref, s_ref, out_ref):
    taken = shifted(g_ref, s_ref)
    step = 512
    for c in range(0, u_ref.shape[1], step):
        out_ref[:, c : c + step] = inner_rows(taken, u_ref[:, c : c + step]).astype(out_ref.dtype)


def heads_weight(g, u, shifts):
    rows, outs = g.shape
    wide = u.shape[1]
    taps, blocks, span, _ = shifts.shape
    return pl.pallas_call(
        heads_weight_kernel,
        grid=(taps,),
        in_specs=[
            pl.BlockSpec((rows, outs), lambda t: (0, 0)),
            pl.BlockSpec((rows, wide), lambda t: (0, 0)),
            pl.BlockSpec((1, blocks, span, span), lambda t: (t, 0, 0, 0)),
        ],
        out_specs=pl.BlockSpec((outs, wide), lambda t: (0, t)),
        out_shape=jax.ShapeDtypeStruct((outs, taps * wide), BF16),
        compiler_params=params(),
        cost_estimate=cost(2 * rows * wide * outs * taps, outs * taps * wide * 2),
        name="heads_weight",
    )(g, u, shifts)


def rows_back_kernel(halves, first_ref, g_ref, u_ref, w_ref, s_ref, du_ref, dw_ref, total):
    step = pl.program_id(0)
    taken = shifted(g_ref, s_ref)
    depth = w_ref.shape[0]
    which = (step + first_ref[0]) % halves

    @pl.when(step == 0)
    def _():
        total[...] = jnp.zeros_like(total)

    total[which] += against(taken, w_ref[...])
    dw_ref[...] = inner_rows(u_ref[...], taken).astype(dw_ref.dtype)

    @pl.when(step == pl.num_programs(0) - 1)
    def _():
        for k in range(halves):
            du_ref[:, k * depth : (k + 1) * depth] = total[k].astype(du_ref.dtype)


def rows_back(first, g, u, w, shifts, halves, kind):
    rows, outs = g.shape
    depth = u.shape[1] // halves
    steps = w.shape[0] // depth
    taps, blocks, span, _ = shifts.shape
    return pl.pallas_call(
        functools.partial(rows_back_kernel, halves),
        grid_spec=pltpu.PrefetchScalarGridSpec(
            num_scalar_prefetch=1,
            grid=(steps,),
            in_specs=[
                pl.BlockSpec((rows, outs), lambda b, f: (0, 0)),
                pl.BlockSpec((rows, depth), lambda b, f: (0, (b + f[0]) % halves)),
                pl.BlockSpec((depth, outs), lambda b, f: (b, 0)),
                pl.BlockSpec((1, blocks, span, span), lambda b, f: ((b + f[0]) // halves, 0, 0, 0)),
            ],
            out_specs=[
                pl.BlockSpec((rows, halves * depth), lambda b, f: (0, 0)),
                pl.BlockSpec((depth, outs), lambda b, f: (b, 0)),
            ],
            scratch_shapes=[pltpu.VMEM((halves, rows, depth), F32)],
        ),
        out_shape=[
            jax.ShapeDtypeStruct((rows, halves * depth), kind),
            jax.ShapeDtypeStruct(w.shape, BF16),
        ],
        compiler_params=params(),
        cost_estimate=cost(4 * rows * w.size, w.size * 4),
        name="rows_back",
    )(first, g, u, w, shifts)


def send_to(axis, to, src, dst, send_sem, recv_sem):
    return pltpu.make_async_remote_copy(
        src_ref=src,
        dst_ref=dst,
        send_sem=send_sem,
        recv_sem=recv_sem,
        device_id={axis: to},
        device_id_type=MESH,
    )


def total_along(axis, size, block, slots, send_sems, recv_sems, meanwhile=None):
    me = lax.axis_index(axis)
    others = [lax.rem(me + k, size) for k in range(1, size)]
    for other in others:
        send_to(axis, other, block, slots.at[me], send_sems.at[other], recv_sems.at[me]).start()
    slots[me] = block[...]
    if meanwhile is not None:
        meanwhile()
    for other in others:
        copy = send_to(
            axis, other, block, slots.at[other], send_sems.at[other], recv_sems.at[other]
        )
        copy.wait_recv()
        copy.wait_send()
    total = slots[0]
    for k in range(1, size):
        total = total + slots[k]
    return total


def place_in_map(layout_ref, device, span):
    position = lax.broadcasted_iota(jnp.int32, (span, 1), 0)
    large = layout_ref[device, 1] == 16
    row_of = jnp.where(large, position // 16, (position % 64) // 8)
    col_of = jnp.where(large, position % 16, position % 8)
    return position, row_of, col_of


def live_mask(layout_ref, device, span):
    position = lax.broadcasted_iota(jnp.int32, (span, 1), 0)
    return position < layout_ref[device, 0] * layout_ref[device, 1] * layout_ref[device, 2]


def live_column(layout_ref, device, span):
    return jnp.where(live_mask(layout_ref, device, span), 1.0, 0.0)


def inverse_count(areas_ref, span):
    areas = areas_ref[:, 0:1] * areas_ref[:, 1:2] * areas_ref[:, 2:3]
    return 1.0 / jnp.sum(jnp.minimum(areas, span).astype(F32), 0, keepdims=True)


def shift_block(layout_ref, device, dilation, tap, span):
    position, row_of, col_of = place_in_map(layout_ref, device, span)
    height, map_width = layout_ref[device, 0], layout_ref[device, 1]
    step_row, step_col = dilation * (tap // 3 - 1), dilation * (tap % 3 - 1)
    target_row, target_col = row_of + step_row, col_of + step_col
    inside = (
        live_mask(layout_ref, device, span)
        & (target_row >= 0)
        & (target_row < height)
        & (target_col >= 0)
        & (target_col < map_width)
    )
    neighbour = jnp.where(inside, position + step_row * map_width + step_col, -1)
    lanes = lax.broadcasted_iota(jnp.int32, (span, span), 1)
    return jnp.where(neighbour == lanes, 1.0, 0.0).astype(BF16)


def shift_in_maps(extent, tap, span, dilation=1):
    position = lax.broadcasted_iota(jnp.int32, (span, 1), 0)
    row_of, col_of = (position % (extent * extent)) // extent, position % extent
    step_row, step_col = dilation * (tap // 3 - 1), dilation * (tap % 3 - 1)
    target_row, target_col = row_of + step_row, col_of + step_col
    inside = (
        (target_row >= 0) & (target_row < extent) & (target_col >= 0) & (target_col < extent)
    )
    neighbour = jnp.where(inside, position + step_row * extent + step_col, -1)
    lanes = lax.broadcasted_iota(jnp.int32, (span, span), 1)
    return jnp.where(neighbour == lanes, 1.0, 0.0).astype(BF16)


def trunk_kernel(
    split,
    sizes,
    in_ref,
    layout_ref,
    areas_ref,
    w_reduce_ref,
    w_spatial_hbm,
    w_expand_hbm,
    w_heads_hbm,
    gain_mid_ref,
    shift_mid_ref,
    gain_wide_ref,
    shift_wide_ref,
    reduced_ref,
    sums_one_ref,
    hidden_one_ref,
    spatial_ref,
    sums_two_ref,
    hidden_two_ref,
    expanded_ref,
    sums_three_ref,
    trunk_ref,
    headed_ref,
    own_shift_ref,
    all_shift_ref,
    *rest,
):
    if split:
        trunk_x, trunk_z, *rest = rest
    early_out = (reduced_ref, spatial_ref, expanded_ref, own_shift_ref, all_shift_ref)
    reduced_ref, spatial_ref, expanded_ref, own_shift_ref, all_shift_ref, early_sems, *rest = rest
    trunk_rest(
        early_out,
        early_sems,
        split,
        sizes,
        in_ref,
        layout_ref,
        areas_ref,
        w_reduce_ref,
        w_spatial_hbm,
        w_expand_hbm,
        w_heads_hbm,
        gain_mid_ref,
        shift_mid_ref,
        gain_wide_ref,
        shift_wide_ref,
        reduced_ref,
        sums_one_ref,
        hidden_one_ref,
        spatial_ref,
        sums_two_ref,
        hidden_two_ref,
        expanded_ref,
        sums_three_ref,
        trunk_ref,
        headed_ref,
        own_shift_ref,
        all_shift_ref,
        (trunk_x, trunk_z) if split else (),
        *rest,
    )


def trunk_rest(
    early_out,
    early_sems,
    split,
    sizes,
    in_ref,
    layout_ref,
    areas_ref,
    w_reduce_ref,
    w_spatial_hbm,
    w_expand_hbm,
    w_heads_hbm,
    gain_mid_ref,
    shift_mid_ref,
    gain_wide_ref,
    shift_wide_ref,
    reduced_ref,
    sums_one_ref,
    hidden_one_ref,
    spatial_ref,
    sums_two_ref,
    hidden_two_ref,
    expanded_ref,
    sums_three_ref,
    trunk_ref,
    headed_ref,
    own_shift_ref,
    all_shift_ref,
    afar,
    w_spatial_ref,
    w_expand_ref,
    w_heads_ref,
    block_mid,
    block_wide,
    slots_mid_rep,
    slots_mid_dp,
    slots_wide_rep,
    slots_wide_dp,
    load_sems,
    rep_send,
    rep_recv,
    dp_send,
    dp_recv,
    gather_send,
    gather_recv,
    away_send,
    away_recv,
):
    n_rep, n_dp = sizes
    rep = lax.axis_index("rep")
    par, upper = lax.rem(rep, 2), rep // 2
    mate, far = rep + 1 - 2 * par, rep + 2 - 4 * upper
    span, wide = in_ref.shape
    middle = w_reduce_ref.shape[1]
    taps = own_shift_ref.shape[0]
    loads = [
        pltpu.make_async_copy(w_spatial_hbm, w_spatial_ref, load_sems.at[0]),
        pltpu.make_async_copy(w_expand_hbm, w_expand_ref, load_sems.at[1]),
    ]
    heads_load = pltpu.make_async_copy(w_heads_hbm, w_heads_ref, load_sems.at[2])
    for load in loads:
        load.start()
    heads_load.start()

    barrier = pltpu.get_barrier_semaphore()
    for axis, size in (("rep", n_rep), ("dp", n_dp)):
        me = lax.axis_index(axis)
        for k in range(1, size):
            pl.semaphore_signal(
                barrier, inc=1, device_id={axis: lax.rem(me + k, size)}, device_id_type=MESH
            )
    first_row = lax.axis_index("dp") * n_rep
    live = live_column(layout_ref, first_row + rep, span)
    inverse = inverse_count(areas_ref, span)

    def make_own():
        for t in range(taps):
            own_shift_ref[t] = shift_block(layout_ref, first_row + rep, 2, t, span)

    def make_all(first, last):
        def fill():
            for t in range(first, last):
                for p in range(n_rep):
                    all_shift_ref[t, p] = shift_block(layout_ref, first_row + p, 1, t, span)

        return fill

    def everywhere(number, value_ref, blocks, rep_slots, dp_slots, meanwhile, later):
        masked = live * value_ref[...]
        blocks[0, 0:1, :] = jnp.sum(masked, 0, keepdims=True)
        blocks[0, 1:2, :] = jnp.sum(masked * value_ref[...], 0, keepdims=True)
        if number == 0:
            pl.semaphore_wait(barrier, n_rep + n_dp - 2)
        blocks[1] = total_along(
            "rep", n_rep, blocks.at[0], rep_slots, rep_send.at[number], rep_recv.at[number], meanwhile
        )
        return total_along(
            "dp", n_dp, blocks.at[1], dp_slots, dp_send.at[number], dp_recv.at[number], later
        )

    def normed(value, sums, gain, shift):
        center = sums[0:1] * inverse
        scaling = lax.rsqrt(sums[1:2] * inverse - center * center + EPS)
        return (value - center) * (scaling * gain) + shift

    def silu(value):
        return value * jax.nn.sigmoid(value)

    reduced_ref[...] = product(in_ref[...], w_reduce_ref[...])
    sums = everywhere(
        0, reduced_ref, block_mid.at[0], slots_mid_rep.at[0], slots_mid_dp.at[0], make_own, None
    )
    sums_one_ref[...] = sums
    hidden_one_ref[...] = silu(
        normed(reduced_ref[...], sums, gain_mid_ref[0:1, :], shift_mid_ref[0:1, :])
    ).astype(BF16)
    loads[0].wait()
    spatial_ref[...] = jnp.zeros_like(spatial_ref)

    @pl.loop(0, taps)
    def _(t):
        moved = product(own_shift_ref[t], hidden_one_ref[...]).astype(BF16)
        at = pl.ds(pl.multiple_of(t * middle, middle), middle)
        spatial_ref[...] += product(moved, w_spatial_ref[at, :])

    sums = everywhere(
        1, spatial_ref, block_mid.at[1], slots_mid_rep.at[1], slots_mid_dp.at[1], make_all(0, 5), None
    )
    sums_two_ref[...] = sums
    hidden_two_ref[...] = silu(
        normed(spatial_ref[...], sums, gain_mid_ref[1:2, :], shift_mid_ref[1:2, :])
    ).astype(BF16)
    loads[1].wait()
    expanded_ref[...] = product(hidden_two_ref[...], w_expand_ref[...])
    sums = everywhere(
        2, expanded_ref, block_wide, slots_wide_rep, slots_wide_dp, make_all(5, 9), None
    )
    sums_three_ref[...] = sums

    own_rows = pl.ds(pl.multiple_of(par * span, span), span)
    mate_rows = pl.ds(pl.multiple_of((1 - par) * span, span), span)
    pre = normed(expanded_ref[...], sums, gain_wide_ref[...], shift_wide_ref[...])
    trunk_ref[upper, own_rows, :] = silu(pre + in_ref[...].astype(F32)).astype(BF16)
    parts = 4
    piece = span // parts

    def rows(parity, k):
        return pl.ds(pl.multiple_of(parity * span + k * piece, piece), piece)

    def across(side, k):
        at = trunk_ref.at[side, rows(par, k)]
        return send_to("rep", far, at, at, gather_send.at[k], gather_recv.at[k])

    def own_pass(parity):
        at = trunk_ref.at[upper, pl.ds(pl.multiple_of(parity * span, span), span)]
        return send_to("rep", mate, at, at, gather_send.at[parts], gather_recv.at[parts])

    def far_pass(parity, k):
        at = trunk_ref.at[1 - upper, rows(parity, k)]
        slot = parts + 1 + k
        return send_to("rep", mate, at, at, gather_send.at[slot], gather_recv.at[slot])

    dp = lax.axis_index("dp")
    neighbours = (dp + 1 - 2 * lax.rem(dp, 2), dp + 2 - 4 * lax.rem(dp // 2, 2))

    def away(number):
        return send_to(
            "dp",
            neighbours[number],
            trunk_ref.at[upper, own_rows],
            afar[number],
            away_send.at[number],
            away_recv.at[number],
        )

    for k in range(parts):
        across(upper, k).start()
    own_pass(par).start()
    if split:
        for number in range(2):
            away(number).start()
    leaving = [
        pltpu.make_async_copy(src, dst, early_sems.at[k])
        for k, (src, dst) in enumerate(
            zip((reduced_ref, spatial_ref, expanded_ref, own_shift_ref, all_shift_ref), early_out)
        )
    ]
    for copy in leaving:
        copy.start()
    headed_ref[...] = jnp.zeros_like(headed_ref)
    own_pass(1 - par).wait_recv()
    heads_load.wait()

    def convolve(side):
        @pl.loop(0, taps)
        def _(t):
            at = pl.ds(pl.multiple_of(t * wide, wide), wide)
            y = against(trunk_ref[side], w_heads_ref[:, at]).astype(BF16)
            for k in range(2):
                place = pl.ds(k * span, span)
                headed_ref[side, place, :] += product(
                    all_shift_ref[t, 2 * side + k], y[k * span : (k + 1) * span]
                )

    convolve(upper)
    for k in range(parts):
        across(1 - upper, k).wait_recv()
        far_pass(par, k).start()
    for k in range(parts):
        far_pass(1 - par, k).wait_recv()
    convolve(1 - upper)
    for k in range(parts):
        across(upper, k).wait_send()
        far_pass(par, k).wait_send()
    own_pass(par).wait_send()
    if split:
        for number in range(2):
            away(number).wait_send()
            away(number).wait_recv()
    for copy in leaving:
        copy.wait()


def trunk_forward(
    split,
    inputs,
    layout,
    w_reduce,
    w_spatial,
    w_expand,
    w_heads,
    gain_mid,
    shift_mid,
    gain_wide,
    shift_wide,
):
    span, wide = inputs.shape
    middle = w_reduce.shape[1]
    n_rep, n_dp = lax.axis_size("rep"), lax.axis_size("dp")
    taps = 9
    vmem = pl.BlockSpec(memory_space=pltpu.VMEM)
    hbm = pl.BlockSpec(memory_space=pl.ANY)
    smem = pl.BlockSpec(memory_space=pltpu.SMEM)
    dma = pltpu.SemaphoreType.DMA
    shape = jax.ShapeDtypeStruct
    return pl.pallas_call(
        functools.partial(trunk_kernel, split, (n_rep, n_dp)),
        in_specs=[vmem, smem, vmem, vmem] + [hbm] * 3 + [vmem] * 4,
        out_specs=[hbm if k in (0, 3, 6, 10, 11) else vmem for k in range(12)] + [hbm] * (2 * split),
        out_shape=[
            shape((span, middle), F32),
            shape((2, middle), F32),
            shape((span, middle), BF16),
            shape((span, middle), F32),
            shape((2, middle), F32),
            shape((span, middle), BF16),
            shape((span, wide), F32),
            shape((2, wide), F32),
            shape((2, 2 * span, wide), BF16),
            shape((2, 2 * span, w_heads.shape[0]), F32),
            shape((taps, span, span), BF16),
            shape((taps, n_rep, span, span), BF16),
        ]
        + [shape((span, wide), BF16)] * (2 * split),
        scratch_shapes=[
            pltpu.VMEM((span, middle), F32),
            pltpu.VMEM((span, middle), F32),
            pltpu.VMEM((span, wide), F32),
            pltpu.VMEM((taps, span, span), BF16),
            pltpu.VMEM((taps, n_rep, span, span), BF16),
            dma((5,)),
            pltpu.VMEM(w_spatial.shape, BF16),
            pltpu.VMEM(w_expand.shape, BF16),
            pltpu.VMEM(w_heads.shape, BF16),
            pltpu.VMEM((2, 2, 2, middle), F32),
            pltpu.VMEM((2, 2, wide), F32),
            pltpu.VMEM((2, n_rep, 2, middle), F32),
            pltpu.VMEM((2, n_dp, 2, middle), F32),
            pltpu.VMEM((n_rep, 2, wide), F32),
            pltpu.VMEM((n_dp, 2, wide), F32),
            dma((3,)),
            dma((3, n_rep)),
            dma((3, n_rep)),
            dma((3, n_dp)),
            dma((3, n_dp)),
            dma((9,)),
            dma((9,)),
            dma((2,)),
            dma((2,)),
        ],
        compiler_params=pltpu.CompilerParams(
            collective_id=10, has_side_effects=True, vmem_limit_bytes=VMEM_LIMIT
        ),
        name="trunk_forward",
    )(
        inputs,
        layout,
        layout,
        w_reduce,
        w_spatial,
        w_expand,
        w_heads,
        gain_mid,
        shift_mid,
        gain_wide[None, :],
        shift_wide[None, :],
    )


MOVES = 38


def message_kernel(split, n_dp, classes, *refs):
    refs = list(refs)

    def take(count):
        taken, refs[:count] = refs[:count], []
        return taken

    layout_ref, areas_ref, headed_ref, s_hbm, w_hbm, gates_w_ref, classes_w_ref = take(7)
    gain_ref, shift_ref, cot_ref, labels_ref = take(4)
    if split:
        trunk_x, trunk_z, trunk_hbm = take(3)
    depth_ref, logits_ref, gates_ref, classes_ref, low_ref, norm_ref = take(6)
    if split:
        out_ref, far_x, far_z, mate_x, mate_z, trunk_xz, mate_xz = take(7)
    else:
        heads_ref, gm_ref = take(2)
    w_ref, live_ref, acc_ref, acc_in, stream_ref, direct_ref, cot_in, labels_in = take(8)
    depth_out, logits_out, picked_ref, far_ref, near_ref = take(5)
    core_out, core_in, far_out, far_in, near_out, near_in = take(6)
    sums_ref, slots_ref, load_sem, send, recv, dp_send, dp_recv = take(7)
    s_ref, shift_sem = take(2)
    if split:
        heads_ref, gm_ref, beside_ref, cut_own, cut_out, cut_in, cut_taken = take(7)

    rep = lax.axis_index("rep")
    par, upper = lax.rem(rep, 2), rep // 2
    mate, far = rep + 1 - 2 * par, rep + 2 - 4 * upper
    first_row = lax.axis_index("dp") * 4
    side_x = lax.rem(lax.axis_index("dp"), 2)
    beside = lax.axis_index("dp") + 1 - 2 * side_x
    side_z = lax.rem(lax.axis_index("dp") // 2, 2)
    along = lax.axis_index("dp") + 2 - 4 * side_z
    span = s_ref.shape[2]
    middle = headed_ref.shape[2]
    small = middle // 2
    load = pltpu.make_async_copy(w_hbm, w_ref, load_sem)
    shift_load = pltpu.make_async_copy(s_hbm, s_ref, shift_sem)
    shift_load.start()
    load.start()

    barrier = pltpu.get_barrier_semaphore()
    me_dp = lax.axis_index("dp")
    for to in (mate, far):
        pl.semaphore_signal(barrier, inc=1, device_id={"rep": to}, device_id_type=MESH)
    for k in range(1, n_dp):
        pl.semaphore_signal(
            barrier, inc=1, device_id={"dp": lax.rem(me_dp + k, n_dp)}, device_id_type=MESH
        )

    def move(number, src, dst, to, axis="rep"):
        return send_to(axis, to, src, dst, send.at[number], recv.at[number])

    def block(parity):
        return pl.ds(pl.multiple_of(parity * span, span), span)

    for p in range(4):
        live_ref[p // 2, (p % 2) * span : (p % 2 + 1) * span, :] = live_column(
            layout_ref, first_row + p, span
        )
    inverse = inverse_count(areas_ref, span)

    def add_up(number, left, right):
        sums_ref[number, 0:1, :] = left
        sums_ref[number, 1:2, :] = right
        return total_along(
            "dp", n_dp, sums_ref.at[number], slots_ref.at[number], dp_send.at[number], dp_recv.at[number]
        )

    def column_sum(value):
        return jnp.sum(value, 0, keepdims=True)

    left, right = 0.0, 0.0
    for side in range(2):
        masked = live_ref[side] * headed_ref[side]
        left = left + column_sum(masked)
        right = right + column_sum(masked * headed_ref[side])
    pl.semaphore_wait(barrier, n_dp + 1)
    move(9, cot_ref, cot_in, far).start()
    move(10, labels_ref, labels_in, far).start()
    sums = add_up(0, left, right)
    if split:
        lower_side = 1 - upper
        own_block = trunk_hbm.at[lower_side, block(par)]
        copy_x = move(29, trunk_x, far_x, far)
        copy_z = move(30, own_block, far_z, along, "dp")
        near_xz = move(31, trunk_x, trunk_xz.at[upper], along, "dp")
        far_xz = move(32, far_x, trunk_xz.at[lower_side], along, "dp")
        to_mate = [
            move(33, trunk_x, mate_x.at[upper], mate),
            move(34, trunk_z, mate_z.at[upper], mate),
            move(35, far_x, mate_x.at[lower_side], mate),
            move(36, far_z, mate_z.at[lower_side], mate),
            move(37, trunk_xz, mate_xz, mate),
        ]
        near_xz.start()
        copy_z.start()

    center = sums[0:1] * inverse
    scaling = lax.rsqrt(sums[1:2] * inverse - center * center + EPS)
    own_lanes = pl.ds(pl.multiple_of(rep * middle, middle), middle)
    gain = gain_ref[:, own_lanes]
    shift = shift_ref[:, own_lanes]

    def across(head, part):
        at = heads_ref.at[head, part // 2, pl.ds((part % 2) * span, span)]
        return move(part, at, at, far)

    def relay(head, part):
        at = heads_ref.at[head, part // 2, pl.ds((part % 2) * span, span)]
        return move(5 + part, at, at, mate)

    def own_head(head):
        return move(4, heads_ref.at[head], heads_ref.at[head], mate)

    for side in range(2):
        normed = (headed_ref[side] - center) * (scaling * gain) + shift
        heads_ref[rep, side] = (normed * jax.nn.sigmoid(normed)).astype(BF16)
        for k in range(2):
            across(rep, 2 * side + k).start()
    own_head(rep).start()
    if split:
        x_own = move(24, heads_ref.at[rep], beside_ref.at[rep], beside, "dp")
        x_far = move(25, heads_ref.at[far], beside_ref.at[far], beside, "dp")
        x_own.start()
        copy_x.start()

    def tap_of(i):
        return par * 5 + i

    def row_of(i, head_at):
        return pl.multiple_of(par * (3 * small) + i * (3 * middle) + head_at * middle, small)

    half_row = (1 - par) * (12 * middle)
    full_row = pl.multiple_of(half_row + par * small, small)
    part_row = pl.multiple_of(half_row + (1 - par) * middle, small)
    part_lanes = pl.ds(pl.multiple_of(par * small, small), small)
    local = 2 * upper
    remote = 2 * (1 - upper)
    local_head = 1 + upper
    part_head = 2 - upper
    full_head = 2 * par + 1 - upper

    def wrows(row, depth):
        return w_ref[pl.ds(row, depth), :]

    def gather_taps(tap, side, y):
        y = y.astype(BF16)
        for k in range(2):
            acc_ref[side, k * span : (k + 1) * span, :] += product(
                s_ref[tap, 2 * side + k], y[k * span : (k + 1) * span]
            )

    acc_ref[...] = jnp.zeros_like(acc_ref)
    own_head(mate).wait_recv()
    shift_load.wait()
    load.wait()

    @pl.loop(0, 8)
    def _(n):
        i, side = n // 2, n % 2
        gather_taps(
            tap_of(i), side, product(heads_ref[local_head, side], wrows(row_of(i, local), middle))
        )

    @pl.when(par == upper)
    def _():
        @pl.loop(0, 2)
        def _(side):
            gather_taps(4, side, product(heads_ref[full_head, side], wrows(full_row, middle)))

    for part in range(4):
        across(far, part).wait_recv()
        relay(far, part).start()
    if split:
        x_far.start()
    for part in range(4):
        relay(far + 1 - 2 * par, part).wait_recv()

    @pl.loop(0, 8)
    def _(n):
        i, side = n // 2, n % 2
        y = product(heads_ref[remote, side], wrows(row_of(i, 1 - upper), middle))
        y = y + product(heads_ref[remote + 1, side], wrows(row_of(i, 2 - upper), middle))
        gather_taps(tap_of(i), side, y)

    @pl.loop(0, 2)
    def _(side):
        gather_taps(
            4, side, product(heads_ref[part_head, side, :, part_lanes], wrows(part_row, small))
        )

    @pl.when(par != upper)
    def _():
        @pl.loop(0, 2)
        def _(side):
            gather_taps(4, side, product(heads_ref[full_head, side], wrows(full_row, middle)))

    def acc_move(side):
        return move(11 + side, acc_ref.at[side, block(1 - par)], acc_in.at[side], mate)

    for side in range(2):
        acc_move(side).start()

    own_gates = gates_w_ref[pl.ds(pl.multiple_of(upper * middle, middle), middle), :]
    classes_ref[...] = jnp.zeros_like(classes_ref)
    move(9, cot_ref, cot_in, far).wait_recv()
    move(10, labels_ref, labels_in, far).wait_recv()
    gates_total = 0.0

    def gm_move(side, parity):
        at = gm_ref.at[side, block(parity)]
        return move(13 + side, at, at, mate)

    for side in range(2):
        acc_move(side).wait_recv()
        message = acc_ref[side, block(par), :] + acc_in[side]
        stream = heads_ref[3 * upper, side, block(par), :]
        gate = jax.nn.sigmoid(product(stream, own_gates))
        full = stream.astype(F32) + gate * message
        alive = live_ref[side, block(par), :]

        @pl.when(upper == 0)
        def _():
            cot = (cot_ref if side == 0 else cot_in)[...].astype(F32)
            stream_ref[side] = alive * cot
            (depth_ref if side == 0 else depth_out)[...] = alive * full

        @pl.when(upper == 1)
        def _():
            labels = (labels_in if side == 0 else labels_ref)[...]
            full_low = full.astype(BF16)
            logits = product(full_low, classes_w_ref[...])
            (logits_out if side == 0 else logits_ref)[...] = alive * logits
            lanes = lax.broadcasted_iota(jnp.int32, logits.shape, 1)
            shown = jnp.where(lanes < classes, logits, -1e30)
            grown = jnp.exp(shown - jnp.max(shown, 1, keepdims=True))
            probs = grown / jnp.sum(grown, 1, keepdims=True)
            slope = (alive * (probs - jnp.where(lanes == labels, 1.0, 0.0))).astype(BF16)
            classes_ref[...] += inner_rows(full_low, slope)
            stream_ref[side] = against(slope, classes_w_ref[...])

        grad = stream_ref[side]
        grad_gate = (grad * message * gate * (1.0 - gate)).astype(BF16)
        gm_ref[side, block(par), :] = (grad * gate).astype(BF16)
        gm_move(side, par).start()
        gates_total = gates_total + inner_rows(stream, grad_gate)
        direct_ref[side] = grad + against(grad_gate, own_gates)

    gates_ref[...] = gates_total.astype(BF16)

    @pl.when(upper == 0)
    def _():
        move(15, depth_out, depth_ref, far).start()

    @pl.when(upper == 1)
    def _():
        move(16, logits_out, logits_ref, far).start()

    for side in range(2):
        gm_move(side, 1 - par).wait_recv()
    if split:
        lanes = lax.broadcasted_iota(jnp.int32, (middle, small), 1)
        wanted = (lanes // 64) * 128 + lanes % 64
        source = lax.broadcasted_iota(jnp.int32, (middle, small), 0)
        for cut, which in ((cut_out, 1 - side_x), (cut_own, side_x)):
            pick = jnp.where(source == wanted + 64 * which, 1.0, 0.0).astype(BF16)
            for side in range(2):
                cut[side] = product(gm_ref[side], pick).astype(BF16)
        x_cut = move(28, cut_out, cut_in, beside, "dp")
        x_cut.start()

    @pl.loop(0, 10)
    def _(n):
        i, side = n // 2, n % 2
        tap = jnp.where(i == 4, 4, tap_of(i))
        for k in range(2):
            at = pl.ds(k * span, span)
            picked_ref[i, side, at, :] = inner_rows(
                s_ref[tap, 2 * side + k], gm_ref[side, at, :]
            ).astype(BF16)

    def taps_back(side, head_at):
        total = 0.0
        for i in range(4):
            total = total + against(picked_ref[i, side], wrows(row_of(i, head_at), middle))
        return total

    def core_move(side):
        return move(17 + side, core_out.at[side], core_in.at[side], mate)

    def far_move(part):
        at = pl.ds((part % 2) * span, span)
        return move(19 + part, far_out.at[part // 2, at], far_in.at[part // 2, at], far)

    @pl.loop(0, 2)
    def _(side):
        @pl.loop(0, 2)
        def _(j):
            far_ref[j, side] = taps_back(side, 1 - upper + j)

        far_ref[upper, side, :, part_lanes] += against(picked_ref[4, side], wrows(part_row, small))

        @pl.when(par != upper)
        def _():
            far_ref[2 * par - 1 + upper, side] += against(
                picked_ref[4, side], wrows(full_row, middle)
            )

        core_out[side] = far_ref[1 - par, side].astype(BF16)
        core_move(side).start()

    for side in range(2):
        core_move(side).wait_recv()
        for part in (2 * side, 2 * side + 1):
            at = pl.ds((part % 2) * span, span)
            far_out[side, at, :] = (
                far_ref[par, side, at, :] + core_in[side, at, :].astype(F32)
            ).astype(BF16)
            far_move(part).start()

    if split:
        copy_x.wait_recv()
        far_xz.start()

    @pl.loop(0, 2)
    def _(side):
        near_ref[side] = taps_back(side, local)

    @pl.when(par == upper)
    def _():
        @pl.loop(0, 2)
        def _(side):
            near_ref[side] += against(picked_ref[4, side], wrows(full_row, middle))

        near_out[...] = near_ref[...].astype(BF16)
        for side in range(2):
            near_ref[side, block(par), :] = direct_ref[side]
            near_ref[side, block(1 - par), :] = jnp.zeros((span, middle), F32)

    @pl.when(par != upper)
    def _():
        for side in range(2):
            near_out[side, block(par), :] = direct_ref[side].astype(BF16)
            near_out[side, block(1 - par), :] = jnp.zeros((span, middle), BF16)

    near_move = move(23, near_out, near_in, mate)
    near_move.start()

    if split:
        x_own.wait_recv()
        relay_own = move(26, beside_ref.at[rep], beside_ref.at[rep], mate)
        relay_own.start()
        x_far.wait_recv()
        relay_far = move(27, beside_ref.at[far], beside_ref.at[far], mate)
        relay_far.start()
        copy_z.wait_recv()
        for copy in to_mate[:4]:
            copy.start()
        x_cut.wait_recv()
        move(26, beside_ref.at[mate], beside_ref.at[mate], mate).wait_recv()
        other = far + 1 - 2 * par
        move(27, beside_ref.at[other], beside_ref.at[other], mate).wait_recv()

        def fill(tap):
            for p in range(4):
                at = pl.ds(p * span, span)
                cut_taken[0, :, at] = inner_rows(
                    cut_own[p // 2, pl.ds((p % 2) * span, span), :], s_ref[tap, p]
                ).astype(BF16)
                cut_taken[1, :, at] = inner_rows(
                    cut_in[p // 2, pl.ds((p % 2) * span, span), :],
                    shift_block(layout_ref, beside * 4 + p, 1, tap, span),
                ).astype(BF16)

        def gradient(head, lanes):
            total = 0.0
            for number, held in enumerate((heads_ref, beside_ref)):
                for side in range(2):
                    total = total + product(
                        cut_taken[number, :, side * 2 * span : (side + 1) * 2 * span],
                        held[head, side, :, lanes],
                    )
            return total.astype(BF16)

        @pl.loop(0, 4)
        def _(i):
            fill(tap_of(i))
            for at in range(3):
                for k in range(2):
                    row = pl.multiple_of(row_of(i, at) + k * small, small)
                    out_ref[:, pl.ds(row, small)] = gradient(
                        at + 1 - upper, pl.ds(k * small, small)
                    )

        fill(4)
        for k in range(2):
            row = pl.multiple_of(full_row + k * small, small)
            out_ref[:, pl.ds(row, small)] = gradient(full_head, pl.ds(k * small, small))
        out_ref[:, pl.ds(part_row, small)] = gradient(part_head, part_lanes)

    if split:
        near_xz.wait_recv()
        far_xz.wait_recv()
        to_mate[4].start()

    near_move.wait_recv()
    left, right = 0.0, 0.0

    def backward(side):
        unit = (headed_ref[side] - center) * scaling
        normed = unit * gain + shift
        sigma = jax.nn.sigmoid(normed)
        return unit, sigma * (1.0 + normed * (1.0 - sigma))

    for side in range(2):
        for part in (2 * side, 2 * side + 1):
            far_move(part).wait_recv()
        unit, slope = backward(side)
        grad = near_ref[side] + near_in[side].astype(F32) + far_in[side].astype(F32)
        grad = grad * slope
        near_ref[side] = grad
        masked = live_ref[side] * grad
        left = left + column_sum(masked * unit)
        right = right + column_sum(masked)
    sums = add_up(1, left, right)
    norm_ref[...] = sums
    for side in range(2):
        unit = (headed_ref[side] - center) * scaling
        low_ref[side] = (
            live_ref[side]
            * (gain * scaling)
            * (near_ref[side] - sums[1:2] * inverse - unit * (sums[0:1] * inverse))
        ).astype(BF16)

    for part in range(4):
        across(rep, part).wait_send()
        relay(far, part).wait_send()
        far_move(part).wait_send()
    own_head(rep).wait_send()
    move(9, cot_ref, cot_in, far).wait_send()
    move(10, labels_ref, labels_in, far).wait_send()
    for side in range(2):
        acc_move(side).wait_send()
        gm_move(side, par).wait_send()
    for side in range(2):
        core_move(side).wait_send()
    near_move.wait_send()

    @pl.when(upper == 0)
    def _():
        move(15, depth_out, depth_ref, far).wait_send()
        move(16, logits_out, logits_ref, far).wait_recv()

    @pl.when(upper == 1)
    def _():
        move(16, logits_out, logits_ref, far).wait_send()
        move(15, depth_out, depth_ref, far).wait_recv()

    if split:
        for copy in to_mate:
            copy.wait_recv()
            copy.wait_send()
        for copy in (x_own, x_far, x_cut, relay_own, relay_far, copy_x, copy_z, near_xz, far_xz):
            copy.wait_send()


def message_streams(
    split, layout, headed, shifts, w_messages, w_gates, w_classes, gain, shift, cot, labels, afar
):
    n_dp = lax.axis_size("dp")
    span, middle = cot.shape
    small = middle // 2
    classes = w_classes.shape[1]
    vmem = pl.BlockSpec(memory_space=pltpu.VMEM)
    dma = pltpu.SemaphoreType.DMA
    shape = jax.ShapeDtypeStruct
    halves = (2, 2 * span, middle)
    heads = (4, 2, 2 * span, middle)
    out_shape = [
        shape((span, middle), F32),
        shape((span, 128), F32),
        shape((middle, middle), BF16),
        shape((middle, 128), F32),
        shape(halves, BF16),
        shape((2, middle), F32),
    ]
    if split:
        out_shape += [shape((small, w_messages.shape[0]), BF16)] + [shape(afar[0].shape, BF16)] * 2
        out_shape += [shape((2,) + afar[0].shape, BF16)] * 4
    else:
        out_shape += [shape(heads, BF16), shape(halves, BF16)]
    scratch = [
        pltpu.VMEM(w_messages.shape, BF16),
        pltpu.VMEM((2, 2 * span, 1), F32),
        pltpu.VMEM(halves, F32),
        pltpu.VMEM((2, span, middle), F32),
        pltpu.VMEM((2, span, middle), F32),
        pltpu.VMEM((2, span, middle), F32),
        pltpu.VMEM((span, middle), BF16),
        pltpu.VMEM((span, 128), jnp.int32),
        pltpu.VMEM((span, middle), F32),
        pltpu.VMEM((span, 128), F32),
        pltpu.VMEM((5,) + halves, BF16),
        pltpu.VMEM((2,) + halves, F32),
        pltpu.VMEM(halves, F32),
        pltpu.VMEM(halves, BF16),
        pltpu.VMEM(halves, BF16),
        pltpu.VMEM(halves, BF16),
        pltpu.VMEM(halves, BF16),
        pltpu.VMEM(halves, BF16),
        pltpu.VMEM(halves, BF16),
        pltpu.VMEM((2, 2, middle), F32),
        pltpu.VMEM((2, n_dp, 2, middle), F32),
        dma,
        dma((MOVES,)),
        dma((MOVES,)),
        dma((2, n_dp)),
        dma((2, n_dp)),
        pltpu.VMEM(shifts.shape, BF16),
        dma,
    ]
    if split:
        scratch += [
            pltpu.VMEM(heads, BF16),
            pltpu.VMEM(halves, BF16),
            pltpu.VMEM(heads, BF16),
            pltpu.VMEM((2, 2 * span, small), BF16),
            pltpu.VMEM((2, 2 * span, small), BF16),
            pltpu.VMEM((2, 2 * span, small), BF16),
            pltpu.VMEM((2, small, 4 * span), BF16),
        ]
    return pl.pallas_call(
        functools.partial(message_kernel, split, n_dp, classes),
        in_specs=[pl.BlockSpec(memory_space=pltpu.SMEM)]
        + [vmem] * 2
        + [pl.BlockSpec(memory_space=pl.ANY)] * 2
        + [vmem] * 6
        + [pl.BlockSpec(memory_space=pl.ANY)] * len(afar),
        out_specs=[vmem] * 7 + [pl.BlockSpec(memory_space=pl.ANY) if split else vmem] * (len(out_shape) - 7),
        out_shape=out_shape,
        scratch_shapes=scratch,
        compiler_params=pltpu.CompilerParams(
            collective_id=11, has_side_effects=True, vmem_limit_bytes=VMEM_LIMIT
        ),
        name="message_streams",
    )(
        layout,
        layout,
        headed,
        shifts,
        w_messages,
        w_gates,
        jnp.pad(w_classes, ((0, 0), (0, 128 - classes))),
        gain[None, :],
        shift[None, :],
        cot,
        jnp.broadcast_to(labels[:, None], (span, 128)),
        *afar,
    )


def heads_taps(t_ref, low_ref, taken_ref, side):
    span = t_ref.shape[2]

    @pl.loop(0, taken_ref.shape[0])
    def _(t):
        for k in range(2):
            at = pl.ds(k * span, span)
            taken_ref[t, at, :] = inner_rows(t_ref[t, k], low_ref[side, at, :]).astype(
                BF16
            )


def heads_tile(c, taken_ref, w_ref, tile_ref):
    taps, _, _ = taken_ref.shape
    wide = w_ref.shape[1] // taps
    step = tile_ref.shape[1]
    total = 0.0
    for t in range(taps):
        at = pl.ds(pl.multiple_of(t * wide + c * step, step), step)
        total = total + product(taken_ref[t], w_ref[:, at])
    tile_ref[...] = total


def heads_load(w_hbm, w_ref, sems, t, c, step):
    wide = w_ref.shape[1] // sems.shape[0]
    at = pl.ds(pl.multiple_of(t * wide + c * step, step), step)
    return pltpu.make_async_copy(w_hbm.at[:, at], w_ref.at[:, at], sems.at[t, c])


def meet(partners):
    barrier = pltpu.get_barrier_semaphore()
    for partner in partners:
        pl.semaphore_signal(barrier, inc=1, device_id=partner, device_id_type=MESH)
    pl.semaphore_wait(barrier, len(partners))


def heads_far_kernel(split, low_ref, s_hbm, w_hbm, *refs):
    sum_ref, *refs = refs
    if split:
        low_x, low_z, *refs = refs
    w_ref, taken_ref, tile_ref, kept, s_ref, s_sem, *refs = refs
    core_out, core_in, load_sems, send, recv = refs
    rep, dp = lax.axis_index("rep"), lax.axis_index("dp")
    par, upper = lax.rem(rep, 2), rep // 2
    mate = rep + 1 - 2 * par
    beside, along = dp + 1 - 2 * lax.rem(dp, 2), dp + 2 - 4 * lax.rem(dp // 2, 2)
    span = s_ref.shape[2]
    tiles = sum_ref.shape[0]
    step = tile_ref.shape[1]
    taps = load_sems.shape[0]
    s_load = pltpu.make_async_copy(s_hbm.at[:, pl.ds(2 * (1 - upper), 2)], s_ref, s_sem)
    s_load.start()

    def load(t, c):
        return heads_load(w_hbm, w_ref, load_sems, t, c, step)

    for t in range(taps):
        load(t, 0).start()
    meet([{"rep": mate}] + ([{"dp": beside}, {"dp": along}] if split else []))

    def block(parity):
        return pl.ds(pl.multiple_of(parity * span, span), span)

    if split:
        copy_x = send_to("dp", beside, low_ref, low_x, send.at[tiles], recv.at[tiles])
        copy_z = send_to("dp", along, low_ref, low_z, send.at[tiles + 1], recv.at[tiles + 1])
        copy_z.start()
        copy_x.start()

    def core_move(c):
        return send_to("rep", mate, core_out.at[c], core_in.at[c], send.at[c], recv.at[c])

    for c in range(1, tiles):
        for t in range(taps):
            load(t, c).start()
    s_load.wait()
    heads_taps(s_ref, low_ref, taken_ref, 1 - upper)

    @pl.loop(0, tiles)
    def _(c):
        for t in range(taps):
            load(t, c).wait()
        heads_tile(c, taken_ref, w_ref, tile_ref)
        core_out[c] = tile_ref[block(1 - par), :].astype(BF16)
        core_move(c).start()
        kept[c] = tile_ref[block(par), :]

    for c in range(tiles):
        core_move(c).wait_recv()
        sum_ref[c] = (kept[c] + core_in[c].astype(F32)).astype(BF16)
        core_move(c).wait_send()
    if split:
        for copy in (copy_x, copy_z):
            copy.wait_recv()
            copy.wait_send()


def heads_near_kernel(split, low_ref, s_hbm, w_hbm, sum_ref, *refs):
    if split:
        low_z, *refs = refs
    out_ref, *refs = refs
    if split:
        low_xz, *refs = refs
    w_ref, taken_ref, tile_ref, kept, s_ref, s_sem, *refs = refs
    far_in, near_out, near_in, load_sems, send, recv = refs
    rep, dp = lax.axis_index("rep"), lax.axis_index("dp")
    par, upper = lax.rem(rep, 2), rep // 2
    mate, far = rep + 1 - 2 * par, rep + 2 - 4 * upper
    beside = dp + 1 - 2 * lax.rem(dp, 2)
    span = s_ref.shape[2]
    tiles = sum_ref.shape[0]
    step = tile_ref.shape[1]
    step = tile_ref.shape[1]
    taps = load_sems.shape[0]
    s_load = pltpu.make_async_copy(s_hbm.at[:, pl.ds(2 * (upper), 2)], s_ref, s_sem)
    s_load.start()

    def load(t, c):
        return heads_load(w_hbm, w_ref, load_sems, t, c, step)

    for t in range(taps):
        load(t, 0).start()
    meet([{"rep": mate}, {"rep": far}] + ([{"dp": beside}] if split else []))

    def block(parity):
        return pl.ds(pl.multiple_of(parity * span, span), span)

    def far_move(c):
        return send_to("rep", far, sum_ref.at[c], far_in.at[c], send.at[c], recv.at[c])

    def near_move(c):
        return send_to(
            "rep", mate, near_out.at[c], near_in.at[c], send.at[tiles + c], recv.at[tiles + c]
        )

    for c in range(tiles):
        far_move(c).start()
    if split:
        copy_xz = send_to("dp", beside, low_z, low_xz, send.at[2 * tiles], recv.at[2 * tiles])
        copy_xz.start()
    for c in range(1, tiles):
        for t in range(taps):
            load(t, c).start()
    s_load.wait()
    heads_taps(s_ref, low_ref, taken_ref, upper)

    @pl.loop(0, tiles)
    def _(c):
        for t in range(taps):
            load(t, c).wait()
        heads_tile(c, taken_ref, w_ref, tile_ref)
        near_out[c] = tile_ref[block(1 - par), :].astype(BF16)
        near_move(c).start()
        kept[c] = tile_ref[block(par), :]

    for c in range(tiles):
        near_move(c).wait_recv()
        far_move(c).wait_recv()
        out_ref[:, c * step : (c + 1) * step] = (
            kept[c] + near_in[c].astype(F32) + far_in[c].astype(F32)
        ).astype(BF16)
        near_move(c).wait_send()
        far_move(c).wait_send()
    if split:
        copy_xz.wait_recv()
        copy_xz.wait_send()


def heads_back(split, low, shifts, w_heads):
    taps, _, span, _ = shifts.shape
    wide = w_heads.shape[1] // taps
    tiles = wide // 512
    vmem = pl.BlockSpec(memory_space=pltpu.VMEM)
    hbm = pl.BlockSpec(memory_space=pl.ANY)
    dma = pltpu.SemaphoreType.DMA
    shape = jax.ShapeDtypeStruct
    cut = (tiles, span, 512)
    scratch = [
        pltpu.VMEM(w_heads.shape, BF16),
        pltpu.VMEM((taps, 2 * span, low.shape[2]), BF16),
        pltpu.VMEM((2 * span, 512), F32),
        pltpu.VMEM(cut, F32),
        pltpu.VMEM((taps, 2, span, span), BF16),
        dma,
    ]

    def of(number):
        return pltpu.CompilerParams(
            collective_id=number, has_side_effects=True, vmem_limit_bytes=VMEM_LIMIT
        )

    lows = [shape(low.shape, BF16)] * (2 * split)
    far_sum, *lows = pl.pallas_call(
        functools.partial(heads_far_kernel, split),
        in_specs=[vmem, hbm, hbm],
        out_specs=[vmem] * (1 + len(lows)),
        out_shape=[shape(cut, BF16)] + lows,
        scratch_shapes=scratch
        + [pltpu.VMEM(cut, BF16)] * 2
        + [dma((taps, tiles)), dma((tiles + 2,)), dma((tiles + 2,))],
        compiler_params=of(12),
        name="heads_far",
    )(low, shifts, w_heads)

    def near(far_sum, *lows):
        last = lows[1:]
        grad, *more = pl.pallas_call(
            functools.partial(heads_near_kernel, split),
            in_specs=[vmem, hbm, hbm, vmem] + [vmem] * len(last),
            out_specs=[vmem] * (1 + len(last)),
            out_shape=[shape((span, wide), BF16)] + [shape(low.shape, BF16)] * len(last),
            scratch_shapes=scratch
            + [pltpu.VMEM(cut, BF16)] * 3
            + [dma((taps, tiles)), dma((2 * tiles + 1,)), dma((2 * tiles + 1,))],
            compiler_params=of(13),
            name="heads_near",
        )(low, shifts, w_heads, far_sum, *last)
        return [grad] + list(lows) + more

    return far_sum, lows, near


def heads_shard_kernel(per_tap, at_ref, layout_ref, *refs):
    lows, trunks = refs[:4], refs[4:13]
    out_ref, taken, turned, kinds = refs[13:]
    unit = pl.program_id(1)
    at = at_ref[pl.program_id(0)] + unit
    tap, chunk = at // per_tap, at % per_tap
    rows = lows[0].shape[1]
    span = rows // 2
    par, upper = at_ref[6], at_ref[7]

    places = [(0, side, k) for side in range(2) for k in range(2)]
    for number in (1, 2):
        places += [(number, side, par) for side in (upper, 1 - upper)]
        places += [(number, side, 1 - par) for side in range(2)]
    places += [(3, side, k) for k in (par, 1 - par) for side in range(2)]

    @pl.when((pl.program_id(0) == 0) & (unit == 0))
    def _():
        for number, low in enumerate(lows):
            for side in range(2):
                for k in range(2):
                    turned[number, side, k] = low[side, k * span : (k + 1) * span, :].T

    @pl.when((unit == 0) | (chunk == 0))
    def _():
        for kind, extent in enumerate((16, 8)):
            kinds[kind] = shift_in_maps(extent, tap, span)
        for slot, (number, side, k) in enumerate(places):
            large = layout_ref[at_ref[2 + number] + 2 * side + k, 1] == 16
            picks = kinds[jnp.where(large, 0, 1)]
            taken[:, slot * span : (slot + 1) * span] = product(
                turned[number, side, k], picks
            ).astype(BF16)

    total = 0.0
    slot = 0
    for trunk in trunks:
        strip = trunk[...].reshape(-1, trunk.shape[-1])
        depth = strip.shape[0]
        total = total + product(taken[:, slot : slot + depth], strip)
        slot += depth
    out_ref[0] = total.astype(BF16)


def heads_shard(at, layout, lows, trunks, units, lanes):
    _, rows, outs = lows[0].shape
    wide = trunks[0].shape[2]
    per_tap = wide // lanes
    whole = pl.BlockSpec(lows[0].shape, lambda i, j, f, g: (0, 0, 0))

    def strip_of(trunk):
        lead = trunk.shape[:-1]
        return pl.BlockSpec(
            lead + (lanes,), lambda i, j, f, g: (0,) * len(lead) + ((f[i] + j) % per_tap,)
        )

    strips = [strip_of(trunk) for trunk in trunks]
    return pl.pallas_call(
        functools.partial(heads_shard_kernel, per_tap),
        grid_spec=pltpu.PrefetchScalarGridSpec(
            num_scalar_prefetch=2,
            grid=(2, units),
            in_specs=[whole] * 4 + strips,
            out_specs=pl.BlockSpec((1, outs, lanes), lambda i, j, f, g: (i, 0, j)),
            scratch_shapes=[
                pltpu.VMEM((outs, 8 * rows), BF16),
                pltpu.VMEM((4, 2, 2, outs, rows // 2), BF16),
                pltpu.VMEM((2, rows // 2, rows // 2), BF16),
            ],
        ),
        out_shape=jax.ShapeDtypeStruct((2, outs, units * lanes), BF16),
        compiler_params=params(),
        cost_estimate=cost(32 * rows * outs * units * lanes, 32 * rows * units * lanes),
        name="heads_shard",
    )(at, layout, *lows, *trunks)


CHUNK_ROWS = (384, 512, 384, 384, 384, 256, 256)
CHUNK_BASE = (0, 384, 1408, 1792, 2176, 896, 1152)
SMALL_ROWS = 2560
HELD_ROWS = 1408
SPATIAL_BASE = 1408
REDUCE_BASE = 896


def trunk_back_kernel(*refs):
    refs = list(refs)

    def take(count):
        taken, refs[:count] = refs[:count], []
        return taken

    layout_ref, areas_ref, grad_ref, expanded_ref, in_ref = take(5)
    reduced_ref, spatial_ref, sums_one_ref, sums_two_ref, sums_three_ref = take(5)
    hidden_one_ref, hidden_two_ref, shift_taps_ref = take(3)
    w_reduce_hbm, w_spatial_hbm, w_expand_ref = take(3)
    gain_mid_ref, shift_mid_ref, gain_wide_ref, shift_wide_ref = take(4)
    gates_ref, classes_ref, head_norm_ref = take(3)
    out_ref, norm_one_ref, norm_two_ref, norm_three_ref, half_ref, heads_norm_ref = take(6)
    p_ref, core_in, core_out, y_in, x_out, x_in, z_out, z_in = take(8)
    z_mid, zz_in = take(2)
    low_wide, moved_ref, total_ref, block_mid, block_wide = take(5)
    slots_mid_rep, slots_mid_dp, slots_wide_rep, slots_wide_dp = take(4)
    rep_send, rep_recv, dp_send, dp_recv, send, recv, norm_send, norm_recv = take(8)
    w_reduce_ref, w_spatial_ref, hidden_all, low_all, moved_all, spatial_own = take(6)
    load_sems, gather_send, gather_recv = take(3)

    rep, dp = lax.axis_index("rep"), lax.axis_index("dp")
    par, upper = lax.rem(rep, 2), rep // 2
    x, z = lax.rem(dp, 2), dp // 2
    mate, far, beside = rep + 1 - 2 * par, rep + 2 - 4 * upper, dp + 1 - 2 * x
    low_z, high_z = lax.rem(z, 2), z // 2
    along, over = dp + 2 - 4 * low_z, dp + 4 - 8 * high_z
    span, wide = in_ref.shape
    middle = reduced_ref.shape[1]
    taps = shift_taps_ref.shape[0]
    loads = [
        pltpu.make_async_copy(w_spatial_hbm, w_spatial_ref, load_sems.at[0]),
        pltpu.make_async_copy(w_reduce_hbm, w_reduce_ref, load_sems.at[1]),
    ]
    for load in loads:
        load.start()
    barrier = pltpu.get_barrier_semaphore()
    for axis, size in (("rep", 4), ("dp", 8)):
        me = lax.axis_index(axis)
        for k in range(1, size):
            pl.semaphore_signal(
                barrier, inc=1, device_id={axis: lax.rem(me + k, size)}, device_id_type=MESH
            )

    def remote(src, dst, c, slot, to):
        return pltpu.make_async_remote_copy(
            src_ref=src,
            dst_ref=dst,
            send_sem=send.at[c, slot],
            recv_sem=recv.at[c, slot],
            device_id=to,
            device_id_type=MESH,
        )

    def whole(c, at=0, size=None):
        size = CHUNK_ROWS[c] if size is None else size
        return pl.ds(pl.multiple_of(CHUNK_BASE[c] + at, 16), size)

    def halves(c):
        return pl.ds(CHUNK_BASE[c] // 2, CHUNK_ROWS[c] // 2)

    def core_copy(c, hi):
        return remote(
            p_ref.at[2 * hi + 1 - par, whole(c)], core_in.at[hi, whole(c)], c, hi, {"rep": mate}
        )

    def y_copy(c):
        return remote(core_out.at[whole(c)], y_in.at[whole(c)], c, 2, {"rep": far})

    def x_copy(c):
        return remote(x_out.at[halves(c)], x_in.at[halves(c)], c, 3, {"dp": beside})

    def piece(c, base, at, size):
        return pl.ds(pl.multiple_of(CHUNK_BASE[c] // base + at, 16), size)

    def z_copy(c):
        size = CHUNK_ROWS[c] // 4
        return remote(
            z_out.at[piece(c, 2, (1 - low_z) * size, size)],
            z_in.at[piece(c, 4, 0, size)],
            c,
            4,
            {"dp": along},
        )

    def zz_copy(c):
        at = piece(c, 4, 0, CHUNK_ROWS[c] // 4)
        return remote(z_mid.at[at], zz_in.at[at], c, 5, {"dp": over})

    def own_place(c, low):
        size = CHUNK_ROWS[c] // 4
        return whole(c, x * 2 * size + low * size, size)

    def z_back(c, incoming):
        place = own_place(c, 1 - low_z if incoming else low_z)
        return remote(half_ref.at[place], half_ref.at[place], c, 6, {"dp": along})

    def last_copy(c, incoming):
        half = CHUNK_ROWS[c] // 2
        place = whole(c, (1 - x if incoming else x) * half, half)
        return remote(half_ref.at[place], half_ref.at[place], c, 7, {"dp": beside})

    def step(c, stage):
        if stage == 0:
            for hi in range(2):
                core_copy(c, hi).start()
        elif stage == 1:
            for hi in range(2):
                core_copy(c, hi).wait_recv()
            core_out[whole(c)] = (
                p_ref[2 * (1 - upper) + par, whole(c)].astype(F32)
                + core_in[1 - upper, whole(c)].astype(F32)
            ).astype(BF16)
            y_copy(c).start()
        elif stage == 2 and c in (2, 3, 4):
            half = CHUNK_ROWS[c] // 2
            at = CHUNK_BASE[c] - SPATIAL_BASE

            def own(k):
                return spatial_own[pl.ds(pl.multiple_of(at + k * half, 16), half)]

            x_out[halves(c)] = own(1 - x).astype(BF16)
            x_copy(c).start()
            z_out[halves(c)] = own(x).astype(BF16)
        elif stage == 2:
            y_copy(c).wait_recv()
            half = CHUNK_ROWS[c] // 2

            def both(at):
                place = whole(c, at, half)
                return (
                    p_ref[rep, place].astype(F32)
                    + core_in[upper, place].astype(F32)
                    + y_in[place].astype(F32)
                )

            x_out[halves(c)] = both((1 - x) * half).astype(BF16)
            x_copy(c).start()
            z_out[halves(c)] = both(x * half).astype(BF16)
        elif stage == 3:
            x_copy(c).wait_recv()
            z_out[halves(c)] = (
                z_out[halves(c)].astype(F32) + x_in[halves(c)].astype(F32)
            ).astype(BF16)
            z_copy(c).start()
        elif stage == 4:
            z_copy(c).wait_recv()
            size = CHUNK_ROWS[c] // 4
            at = piece(c, 4, 0, size)
            z_mid[at] = (
                z_out[piece(c, 2, low_z * size, size)].astype(F32) + z_in[at].astype(F32)
            ).astype(BF16)
            zz_copy(c).start()
        elif stage == 5:
            zz_copy(c).wait_recv()
            at = piece(c, 4, 0, CHUNK_ROWS[c] // 4)
            half_ref[own_place(c, low_z)] = (
                z_mid[at].astype(F32) + zz_in[at].astype(F32)
            ).astype(BF16)
            z_back(c, False).start()
        elif stage == 6:
            z_back(c, True).wait_recv()
            last_copy(c, False).start()
        else:
            last_copy(c, True).wait_recv()
            if c not in (2, 3, 4):
                for hi in range(2):
                    core_copy(c, hi).wait_send()
                y_copy(c).wait_send()
            x_copy(c).wait_send()
            z_copy(c).wait_send()
            zz_copy(c).wait_send()
            z_back(c, False).wait_send()
            last_copy(c, False).wait_send()

    def steps(*which):
        def run():
            for c, stage in which:
                step(c, stage)

        return run

    live = live_column(layout_ref, dp * 4 + rep, span)
    inverse = inverse_count(areas_ref, span)

    def stats(sums_ref):
        center = sums_ref[0:1, :] * inverse
        return center, lax.rsqrt(sums_ref[1:2, :] * inverse - center * center + EPS)

    def norm_move(to, slot):
        at = heads_norm_ref.at[slot]
        return send_to("rep", to, at, at, norm_send.at[to], norm_recv.at[slot])

    def local_sums(blocks, value, unit, at):
        masked = live * value
        blocks[0, 0:1, at] = jnp.sum(masked * unit, 0, keepdims=True)
        blocks[0, 1:2, at] = jnp.sum(masked, 0, keepdims=True)

    def everywhere(number, blocks, rep_slots, dp_slots, meanwhile, later):
        if number == 0:
            pl.semaphore_wait(barrier, 10)
            heads_norm_ref[rep] = head_norm_ref[...]
            for k in range(1, 4):
                norm_move(lax.rem(rep + k, 4), rep).start()
        blocks[1] = total_along(
            "rep", 4, blocks.at[0], rep_slots, rep_send.at[number], rep_recv.at[number], meanwhile
        )
        return total_along(
            "dp", 8, blocks.at[1], dp_slots, dp_send.at[number], dp_recv.at[number], later
        )

    def slope(value):
        sigma = jax.nn.sigmoid(value)
        return sigma * (1.0 + value * (1.0 - sigma))

    def spread_back(grad, unit, sums, gain, scaling):
        return (
            live
            * (gain * scaling)
            * (grad - sums[1:2] * inverse - unit * (sums[0:1] * inverse))
        ).astype(BF16)

    center, scaling = stats(sums_three_ref)
    strips = [pl.ds(k, middle) for k in range(0, wide, middle)]

    def unit_at(at):
        return (expanded_ref[:, at] - center[:, at.start : at.start + middle]) * scaling[
            :, at.start : at.start + middle
        ]

    for at in strips:
        unit = unit_at(at)
        pre = unit * gain_wide_ref[:, at] + shift_wide_ref[:, at] + in_ref[:, at].astype(F32)
        grad = grad_ref[:, at].astype(F32) * slope(pre)
        out_ref[:, at] = grad
        local_sums(block_wide, grad, unit, at)

    def gather(number, held, to, slot):
        at = held.at[slot]
        return send_to(
            "rep", to, at, at, gather_send.at[number, to], gather_recv.at[number, slot]
        )

    hidden_all[rep] = hidden_one_ref[...]

    def first_chunk():
        half = middle // 2
        rows = classes_ref.shape[1]
        for q in range(4):
            p_ref[q, half : half + rows, :] = classes_ref[q]
            p_ref[q, half + rows : CHUNK_ROWS[0], :] = jnp.zeros(
                (CHUNK_ROWS[0] - half - rows, middle), BF16
            )
        for k in range(2):
            p_ref[2 * upper + k, :half, :] = gates_ref[k * half : (k + 1) * half, :]
            p_ref[2 * (1 - upper) + k, :half, :] = jnp.zeros((half, middle), BF16)
        step(0, 0)
        for k in range(1, 4):
            gather(0, hidden_all, lax.rem(rep + k, 4), rep).start()
        step(0, 1)

    sums = everywhere(
        0,
        block_wide,
        slots_wide_rep,
        slots_wide_dp,
        first_chunk,
        steps((0, 2)),
    )
    norm_three_ref[...] = sums
    for at in strips:
        cut = slice(at.start, at.start + middle)
        low_wide[:, at] = spread_back(
            out_ref[:, at], unit_at(at), sums[:, cut], gain_wide_ref[:, at], scaling[:, cut]
        )

    center, scaling = stats(sums_two_ref)
    unit = (spatial_ref[...] - center) * scaling
    normed = unit * gain_mid_ref[1:2, :] + shift_mid_ref[1:2, :]
    total_ref[...] = against(low_wide[...], w_expand_ref[...]) * slope(normed)

    def expand_gradient():
        rows = middle // 4
        for k in range(wide // middle):
            tile = inner_rows(
                hidden_two_ref[...], low_wide[:, k * middle : (k + 1) * middle]
            ).astype(BF16)
            for q in range(4):
                at = CHUNK_BASE[1] + k * rows
                p_ref[q, at : at + rows, :] = tile[q * rows : (q + 1) * rows]
        step(1, 0)
        step(1, 1)

    local_sums(block_mid.at[0], total_ref[...], unit, slice(None))
    sums = everywhere(
        1,
        block_mid.at[0],
        slots_mid_rep.at[0],
        slots_mid_dp.at[0],
        expand_gradient,
        steps((0, 3), (1, 2)),
    )
    norm_two_ref[...] = sums
    low_mid = spread_back(total_ref[...], unit, sums, gain_mid_ref[1:2, :], scaling)

    total_ref[...] = jnp.zeros_like(total_ref)
    loads[0].wait()
    for t in range(taps):
        moved_ref[t] = inner_rows(shift_taps_ref[t], low_mid).astype(BF16)

    @pl.loop(0, taps)
    def _(t):
        at = pl.ds(pl.multiple_of(t * middle, middle), middle)
        total_ref[...] += against(moved_ref[t], w_spatial_ref[at, :])

    center, scaling = stats(sums_one_ref)
    unit = (reduced_ref[...] - center) * scaling
    normed = unit * gain_mid_ref[0:1, :] + shift_mid_ref[0:1, :]
    total_ref[...] = total_ref[...] * slope(normed)

    def give_low():
        low_all[rep] = low_mid
        for k in range(1, 4):
            gather(1, low_all, lax.rem(rep + k, 4), rep).start()

    def spatial_gradient():
        large = [layout_ref[dp * 4 + p, 1] == 16 for p in range(4)]
        units = spatial_own.shape[0] // 128
        per_tap = middle // 128

        @pl.loop(0, units)
        def _(i):
            unit = units * rep + i
            tap, cut = unit // per_tap, unit % per_tap

            @pl.when((i == 0) | (cut == 0))
            def _():
                kinds = [shift_in_maps(extent, tap, span, 2) for extent in (16, 8)]
                for p in range(4):
                    picks = jnp.where(large[p], kinds[0], kinds[1])
                    moved_all[p] = inner_rows(picks, low_all[p]).astype(BF16)

            lanes = pl.ds(pl.multiple_of(cut * 128, 128), 128)
            total = 0.0
            for p in range(4):
                total = total + inner_rows(hidden_all[p, :, lanes], moved_all[p])
            spatial_own[pl.ds(pl.multiple_of(i * 128, 128), 128), :] = total

    local_sums(block_mid.at[1], total_ref[...], unit, slice(None))
    sums = everywhere(
        2,
        block_mid.at[1],
        slots_mid_rep.at[1],
        slots_mid_dp.at[1],
        give_low,
        steps((0, 4), (1, 3)),
    )
    norm_one_ref[...] = sums
    low_first = spread_back(total_ref[...], unit, sums, gain_mid_ref[0:1, :], scaling)
    quarter = wide // 4
    for q in range(4):
        p_ref[q, REDUCE_BASE : REDUCE_BASE + quarter, :] = inner_rows(
            in_ref[:, q * quarter : (q + 1) * quarter], low_first
        ).astype(BF16)
    step(5, 0)
    step(6, 0)
    step(0, 5)
    step(5, 1)
    step(1, 4)
    step(6, 1)
    for number, held in enumerate((hidden_all, low_all)):
        for k in range(1, 4):
            other = lax.rem(rep + k, 4)
            gather(number, held, other, other).wait_recv()
            gather(number, held, other, rep).wait_send()
    spatial_gradient()
    step(2, 2)
    step(4, 2)
    step(3, 2)
    loads[1].wait()
    for k in range(0, wide, middle):
        out_ref[:, k : k + middle] += against(low_first, w_reduce_ref[k : k + middle, :])
    for turn in (
        ((5, 2), (1, 5), (2, 3), (6, 2), (4, 3), (3, 3), (2, 4), (0, 6)),
        ((5, 3), (4, 4), (6, 3), (2, 5), (3, 4), (0, 7), (4, 5), (1, 6)),
        ((5, 4), (3, 5), (1, 7), (6, 4), (2, 6), (5, 5), (2, 7), (4, 6)),
        ((6, 5), (3, 6), (4, 7), (5, 6), (6, 6), (3, 7), (5, 7), (6, 7)),
    ):
        for c, stage in turn:
            step(c, stage)
    for k in range(1, 4):
        other = lax.rem(rep + k, 4)
        norm_move(other, other).wait_recv()
        norm_move(other, rep).wait_send()


def trunk_back(
    layout,
    grad,
    expanded,
    inputs,
    reduced,
    spatial,
    sums,
    hidden_one,
    hidden_two,
    shift_taps,
    w_reduce,
    w_spatial,
    w_expand,
    gain_mid,
    shift_mid,
    gain_wide,
    shift_wide,
    gates,
    classes,
    head_norm,
):
    span, wide = inputs.shape
    middle = reduced.shape[1]
    taps = shift_taps.shape[0]
    vmem = pl.BlockSpec(memory_space=pltpu.VMEM)
    dma = pltpu.SemaphoreType.DMA
    shape = jax.ShapeDtypeStruct
    small = (SMALL_ROWS, middle)
    held = (HELD_ROWS, middle)
    every = (4, span, middle)
    half = (SMALL_ROWS // 2, middle)
    chunks = len(CHUNK_ROWS)
    out_shape = [
        shape((span, wide), F32),
        shape((2, middle), F32),
        shape((2, middle), F32),
        shape((2, wide), F32),
        shape(small, BF16),
        shape((4, 2, middle), F32),
    ]
    return pl.pallas_call(
        trunk_back_kernel,
        in_specs=[pl.BlockSpec(memory_space=pltpu.SMEM)]
        + [vmem] * 12
        + [pl.BlockSpec(memory_space=pl.ANY)] * 2
        + [vmem] * 8,
        out_specs=[vmem] * len(out_shape),
        out_shape=out_shape,
        scratch_shapes=[
            pltpu.VMEM((4,) + held, BF16),
            pltpu.VMEM((2,) + held, BF16),
            pltpu.VMEM(held, BF16),
            pltpu.VMEM(held, BF16),
            pltpu.VMEM(half, BF16),
            pltpu.VMEM(half, BF16),
            pltpu.VMEM(half, BF16),
            pltpu.VMEM((SMALL_ROWS // 4, middle), BF16),
            pltpu.VMEM((SMALL_ROWS // 4, middle), BF16),
            pltpu.VMEM((SMALL_ROWS // 4, middle), BF16),
            pltpu.VMEM((span, wide), BF16),
            pltpu.VMEM((taps, span, middle), BF16),
            pltpu.VMEM((span, middle), F32),
            pltpu.VMEM((2, 2, 2, middle), F32),
            pltpu.VMEM((2, 2, wide), F32),
            pltpu.VMEM((2, 4, 2, middle), F32),
            pltpu.VMEM((2, 8, 2, middle), F32),
            pltpu.VMEM((4, 2, wide), F32),
            pltpu.VMEM((8, 2, wide), F32),
            dma((3, 4)),
            dma((3, 4)),
            dma((3, 8)),
            dma((3, 8)),
            dma((chunks, 8)),
            dma((chunks, 8)),
            dma((4,)),
            dma((4,)),
            pltpu.VMEM(w_reduce.shape, BF16),
            pltpu.VMEM(w_spatial.shape, BF16),
            pltpu.VMEM(every, BF16),
            pltpu.VMEM(every, BF16),
            pltpu.VMEM(every, BF16),
            pltpu.VMEM((taps * middle // 4, middle), F32),
            dma((2,)),
            dma((2, 4)),
            dma((2, 4)),
        ],
        compiler_params=pltpu.CompilerParams(
            collective_id=9, has_side_effects=True, vmem_limit_bytes=VMEM_LIMIT
        ),
        name="trunk_back",
    )(
        layout,
        layout,
        grad,
        expanded,
        inputs,
        reduced,
        spatial,
        *sums,
        hidden_one,
        hidden_two,
        shift_taps,
        w_reduce,
        w_spatial,
        w_expand,
        gain_mid,
        shift_mid,
        gain_wide[None, :],
        shift_wide[None, :],
        gates,
        classes,
        head_norm,
    )


FINISH_STEPS = 4


def finish_kernel(
    classes,
    sums_ref,
    in_grad_ref,
    depth_in_ref,
    logits_in_ref,
    heads_in_ref,
    messages_in_ref,
    one_ref,
    two_ref,
    three_ref,
    heads_norm_ref,
    depth_ref,
    logits_ref,
    out_ref,
    reduce_ref,
    spatial_ref,
    expand_ref,
    heads_ref,
    gates_ref,
    messages_ref,
    classes_ref,
    gain_mid_ref,
    shift_mid_ref,
    gain_wide_ref,
    shift_wide_ref,
    gain_head_ref,
    shift_head_ref,
):
    middle = sums_ref.shape[1]
    now = pl.program_id(0)

    def held(base, size, at=0):
        return sums_ref[pl.ds(pl.multiple_of(base + at, 16), size), :].astype(F32)

    depth_ref[...] = depth_in_ref[...]
    out_ref[...] = in_grad_ref[...]
    heads_ref[...] = heads_in_ref[...].astype(F32)
    messages_ref[...] = messages_in_ref[...].astype(F32)
    gates = gates_ref.shape[0]
    gates_ref[...] = held(0, gates, now * gates)
    rows = expand_ref.shape[0]
    for k in range(expand_ref.shape[1] // middle):
        expand_ref[:, k * middle : (k + 1) * middle] = held(
            CHUNK_BASE[1] + k * rows * FINISH_STEPS, rows, now * rows
        )
    rows = spatial_ref.shape[0]
    spatial_ref[...] = held(SPATIAL_BASE, rows, now * rows)
    rows = reduce_ref.shape[0]
    reduce_ref[...] = held(REDUCE_BASE, rows, now * rows)

    @pl.when(now == 0)
    def _():
        logits_ref[...] = logits_in_ref[...].T[:classes, :]
        rows = classes_ref.shape[1] // 4
        tail = sums_ref[middle // 2 : middle // 2 + rows, :].astype(F32)
        held_classes = [tail[:, k * 128 : (k + 1) * 128] for k in range(4)]
        classes_ref[...] = jnp.concatenate(held_classes, 0).T[:classes, :]
        for at, norm in enumerate((one_ref, two_ref)):
            gain_mid_ref[at : at + 1, :] = norm[0:1, :]
            shift_mid_ref[at : at + 1, :] = norm[1:2, :]
        gain_wide_ref[...] = three_ref[0:1, :]
        shift_wide_ref[...] = three_ref[1:2, :]
        for k in range(4):
            gain_head_ref[:, k * middle : (k + 1) * middle] = heads_norm_ref[k, 0:1, :]
            shift_head_ref[:, k * middle : (k + 1) * middle] = heads_norm_ref[k, 1:2, :]


def finish(classes, sums, in_grad, depth, logits, heads, messages, one, two, three, heads_norm):
    span, wide = in_grad.shape
    middle = sums.shape[1]
    shape = jax.ShapeDtypeStruct
    out_shape = [
        shape(depth.shape, F32),
        shape((classes, span), F32),
        shape(in_grad.shape, F32),
        shape((wide // 4, middle), F32),
        shape((SMALL_ROWS - SPATIAL_BASE, middle), F32),
        shape((middle // 4, wide), F32),
        shape(heads.shape, F32),
        shape((middle // 2, middle), F32),
        shape(messages.shape, F32),
        shape((classes, middle // 4), F32),
        shape((2, middle), F32),
        shape((2, middle), F32),
    ] + [shape((1, wide), F32)] * 4

    def whole(array):
        zeros = (0,) * len(array.shape)
        return pl.BlockSpec(array.shape, lambda i: zeros)

    def by_rows(array):
        return pl.BlockSpec((array.shape[0] // FINISH_STEPS, array.shape[1]), lambda i: (i, 0))

    cut_in = (1, 2, 4, 5)
    cut_out = (0, 2, 3, 4, 5, 6, 7, 8)
    operands = (sums, in_grad, depth, logits, heads, messages, one, two, three, heads_norm)
    return pl.pallas_call(
        functools.partial(finish_kernel, classes),
        grid=(FINISH_STEPS,),
        in_specs=[by_rows(v) if k in cut_in else whole(v) for k, v in enumerate(operands)],
        out_specs=[by_rows(v) if k in cut_out else whole(v) for k, v in enumerate(out_shape)],
        out_shape=out_shape,
        compiler_params=params(),
        name="finish",
    )(*operands)


def silu_slope(value_in):
    sigma_of = jax.nn.sigmoid(value_in)
    return sigma_of * (1.0 + value_in * (1.0 - sigma_of))


MESH = pl.DeviceIdType.MESH


def greet(axes):
    barrier = pltpu.get_barrier_semaphore()
    count = 0
    for axis, size in axes:
        me = lax.axis_index(axis)
        for k in range(1, size):
            pl.semaphore_signal(
                barrier, inc=1, device_id={axis: lax.rem(me + k, size)}, device_id_type=MESH
            )
        count += size - 1
    pl.semaphore_wait(barrier, count)


def total_kernel(axes, x_ref, out_ref, *scratch):
    greet(axes)
    block = x_ref
    for number, (axis, size) in enumerate(axes):
        slots, stage, send_sems, recv_sems = scratch[4 * number : 4 * number + 4]
        me = lax.axis_index(axis)
        others = [lax.rem(me + k, size) for k in range(1, size)]
        for other in others:
            pltpu.make_async_remote_copy(
                src_ref=block,
                dst_ref=slots.at[me],
                send_sem=send_sems.at[other],
                recv_sem=recv_sems.at[me],
                device_id={axis: other},
                device_id_type=MESH,
            ).start()
        slots[me] = block[...]
        for other in others:
            copy = pltpu.make_async_remote_copy(
                src_ref=block,
                dst_ref=slots.at[other],
                send_sem=send_sems.at[other],
                recv_sem=recv_sems.at[other],
                device_id={axis: other},
                device_id_type=MESH,
            )
            copy.wait_recv()
            copy.wait_send()
        total = slots[0]
        for k in range(1, size):
            total = total + slots[k]
        if number == len(axes) - 1:
            out_ref[...] = total
        else:
            stage[...] = total
            block = stage


def total_of(left, right, axes):
    width = left.shape[0]
    packed = jnp.concatenate([left, right], 0).reshape(-1, 128)
    sized = tuple((axis, lax.axis_size(axis)) for axis in axes)
    scratch = []
    for _, size in sized:
        scratch += [
            pltpu.VMEM((size,) + packed.shape, F32),
            pltpu.VMEM(packed.shape, F32),
            pltpu.SemaphoreType.DMA((size,)),
            pltpu.SemaphoreType.DMA((size,)),
        ]
    number = 1 + (width != 512) + 2 * (len(axes) == 1)
    summed = pl.pallas_call(
        functools.partial(total_kernel, sized),
        out_shape=jax.ShapeDtypeStruct(packed.shape, F32),
        in_specs=[pl.BlockSpec(memory_space=pltpu.VMEM)],
        out_specs=pl.BlockSpec(memory_space=pltpu.VMEM),
        scratch_shapes=scratch,
        compiler_params=pltpu.CompilerParams(collective_id=number, has_side_effects=True),
        name="total",
    )(packed).reshape(2, width)
    return summed[0], summed[1]


def normalize(raw_value, column_sums, squares, pixel_count, norm_gain, norm_shift):
    center = column_sums / pixel_count
    spread_of = squares / pixel_count - center * center
    scaling = lax.rsqrt(spread_of + EPS)
    unit_value = (raw_value - center) * scaling
    return (unit_value * norm_gain + norm_shift, unit_value, scaling)


def moments(raw_value, living, axes):
    return total_of(
        jnp.sum(living * raw_value, 0), jnp.sum(living * raw_value * raw_value, 0), axes
    )


def norm_back(grad_out, unit_value, scaling, norm_gain, living, pixel_count, axes):
    grad_gain, grad_shift = total_of(
        jnp.sum(living * grad_out * unit_value, 0), jnp.sum(living * grad_out, 0), axes
    )
    grad_raw = (
        living
        * (norm_gain * scaling)
        * (grad_out - grad_shift / pixel_count - unit_value * grad_gain / pixel_count)
    )
    return (grad_raw, grad_gain, grad_shift)


def swap(value, bit):
    return lax.ppermute(value, "rep", [(k, k ^ bit) for k in range(4)])


def scatter_rep(value):
    return lax.psum_scatter(value.astype(BF16), "rep", scatter_dimension=0, tiled=True)


def total_dp(value):
    parts = lax.axis_size("dp")
    rows = value.shape[0]
    padded = -(-rows // (8 * parts)) * 8 * parts
    value = jnp.pad(value, ((0, padded - rows), (0, 0)))
    share = lax.psum_scatter(value, "dp", scatter_dimension=0, tiled=True)
    return lax.all_gather(share, "dp", axis=0, tiled=True)[:rows].astype(F32)


def shards(
    inputs,
    layout,
    labels,
    cot_depth,
    w_reduce,
    w_spatial,
    w_expand,
    w_heads,
    w_gates,
    w_messages,
    w_classes,
    gain_mid,
    shift_mid,
    gain_wide,
    shift_wide,
    gain_head,
    shift_head,
):
    pixels = inputs.shape[0]
    middle = w_reduce.shape[1]
    classes = w_classes.shape[1]
    group = lax.axis_size("rep")
    everyone = ("rep", "dp")
    rep = lax.axis_index("rep")
    parity = rep % 2
    upper = rep // 2
    first_row = lax.axis_index("dp") * group
    own_info = geometry(lax.dynamic_slice_in_dim(layout, first_row + rep, 1, 0), pixels)
    group_info = geometry(lax.dynamic_slice_in_dim(layout, first_row, group, 0), pixels)
    living = own_info[2][0].astype(F32)[:, None]
    group_living = group_info[2].astype(F32)
    living_all = group_living.reshape(group * pixels, 1)
    pixel_count = jnp.sum(
        jnp.minimum(layout[:, 0] * layout[:, 1] * layout[:, 2], pixels)
    ).astype(F32)
    split = lax.axis_size("dp") == 8
    if split:
        side = lax.axis_index("dp") % 2
        columns = [[z_at * 2 + k for z_at in range(4)] for k in range(2)]
    zero = jnp.zeros((1,), jnp.int32)
    first = jnp.reshape(9 * parity, (1,)).astype(jnp.int32)

    (
        reduced,
        sums_one,
        hidden_one,
        spatial,
        sums_two,
        hidden_two,
        expanded,
        sums_three,
        trunk_all,
        headed,
        shifts_own,
        shifts_all,
        *trunk_afar,
    ) = trunk_forward(
        split,
        inputs,
        layout,
        w_reduce,
        w_spatial,
        w_expand,
        w_heads,
        gain_mid,
        shift_mid,
        gain_wide,
        shift_wide,
    )
    upper_is_depth = upper == 0
    headed, late_classes, late_labels = lax.optimization_barrier((headed, w_classes, labels))
    depth, logits, gates_local, classes_local, head_low, head_norm, *rest = message_streams(
        split,
        layout,
        headed,
        shifts_all,
        w_messages,
        w_gates,
        late_classes,
        gain_head,
        shift_head,
        cot_depth,
        late_labels,
        trunk_afar + [trunk_all] if split else [],
    )
    classes_local = classes_local[:, :classes]
    is_depth = upper_is_depth
    if split:
        messages_local = rest[0]
    else:
        heads_all, message_all = rest
        heads_all = heads_all.reshape(4, group * pixels, middle)
        source = jnp.where(
            is_depth,
            jnp.concatenate([heads_all[1], heads_all[2], heads_all[3]], 1),
            jnp.concatenate([heads_all[0], heads_all[1], heads_all[2]], 1),
        )
        _, messages_local = rows_back(
            first, message_all.reshape(4 * pixels, middle), source, w_messages, shifts_all, 2, BF16
        )
        grad_messages = lax.psum_scatter(messages_local, "dp", scatter_dimension=1, tiled=True)
        gates_cut = gates_local.reshape(2, pixels, middle)
        gates_share = lax.dynamic_index_in_dim(gates_cut, parity, 0, keepdims=False).astype(F32)
        gates_share += swap(
            lax.dynamic_index_in_dim(gates_cut, 1 - parity, 0, keepdims=False), 1
        ).astype(F32)
    far_sum, lows, near = heads_back(split, head_low, shifts_all, w_heads)
    if split:
        messages_local, far_sum = lax.optimization_barrier((messages_local, far_sum))
    trunk_grad, *lows = near(far_sum, *lows)
    if split:
        grad_messages = lax.psum_scatter(
            messages_local, "dp", scatter_dimension=0, tiled=True, axis_index_groups=columns
        )
        dp = lax.axis_index("dp")
        beside, along = dp + 1 - 2 * side, dp + 2 - 4 * ((dp // 2) % 2)
        groups = [dp, beside, along, along + 1 - 2 * side]
        units = 9

        lower = dp % 4
        at = jnp.stack(
            [units * lower, units * (lower + 4)] + [group * k for k in groups] + [parity, upper]
        )
        far_x, far_z, mate_x, mate_z, trunk_xz, mate_xz = rest[1:]
        near_x, near_z = trunk_afar
        trunks = [trunk_all, near_x, far_x, mate_x, near_z, far_z, mate_z, trunk_xz, mate_xz]
        heads_local = heads_shard(
            at.astype(jnp.int32), layout, [head_low] + lows, trunks, units, 256
        )
        heads_local, trunk_grad = lax.optimization_barrier((heads_local, trunk_grad))
        grad_heads = lax.psum_scatter(
            heads_local,
            "dp",
            scatter_dimension=0,
            tiled=False,
            axis_index_groups=[[k, k + 4] for k in range(4)],
        )
    else:
        heads_local = heads_weight(
            head_low.reshape(group * pixels, middle),
            trunk_all.reshape(group * pixels, -1),
            shifts_all,
        )
        grad_heads = lax.psum_scatter(heads_local, "dp", scatter_dimension=1, tiled=True)
    if split:
        classes_wide = jnp.pad(classes_local.astype(BF16), ((0, 0), (0, 128 - classes)))
        classes_wide = classes_wide.reshape(4, 4, -1, 128)
        classes_wide = jnp.concatenate([classes_wide[:, k] for k in range(4)], 2)
        (
            input_grad,
            norm_one,
            norm_two,
            norm_three,
            small_sums,
            heads_norm,
        ) = trunk_back(
            layout,
            trunk_grad,
            expanded,
            inputs,
            reduced,
            spatial,
            [sums_one, sums_two, sums_three],
            hidden_one,
            hidden_two,
            shifts_own,
            w_reduce,
            w_spatial,
            w_expand,
            gain_mid,
            shift_mid,
            gain_wide,
            shift_wide,
            gates_local,
            classes_wide,
            head_norm,
        )
        every = finish(
            classes,
            small_sums,
            input_grad,
            depth,
            logits,
            grad_heads,
            grad_messages,
            norm_one,
            norm_two,
            norm_three,
            heads_norm,
        )
        narrow = (1, 8, 9)
        outs = [each.T if k in narrow else each for k, each in enumerate(every)]
        return tuple(outs[:12]) + tuple(each[0] for each in outs[12:])
    else:
        logits = logits[:, :classes]
        normed_one, unit_one, scale_one = normalize(
            reduced, sums_one[0], sums_one[1], pixel_count, gain_mid[0], shift_mid[0]
        )
        normed_two, unit_two, scale_two = normalize(
            spatial, sums_two[0], sums_two[1], pixel_count, gain_mid[1], shift_mid[1]
        )
        normed_three, unit_three, scale_three = normalize(
            expanded, sums_three[0], sums_three[1], pixel_count, gain_wide, shift_wide
        )
        pre_act = normed_three + inputs.astype(F32)
        pre_grad = trunk_grad.astype(F32) * silu_slope(pre_act)
        expand_raw, grad_gain_wide, grad_shift_wide = norm_back(
            pre_grad, unit_three, scale_three, gain_wide, living, pixel_count, everyone
        )
        expand_low = expand_raw.astype(BF16)
        expand_local = inner_rows(hidden_two, expand_low).astype(BF16)
        hidden_two_grad = against(expand_low, w_expand)
        spatial_raw, gain_grad_two, shift_grad_two = norm_back(
            hidden_two_grad * silu_slope(normed_two),
            unit_two,
            scale_two,
            gain_mid[1],
            living,
            pixel_count,
            everyone,
        )
        spatial_low = spatial_raw.astype(BF16)
        hidden_one_grad, spatial_local = rows_back(
            zero, spatial_low, hidden_one, w_spatial, shifts_own[:, None], 1, F32
        )
        reduced_raw, gain_grad_one, shift_grad_one = norm_back(
            hidden_one_grad * silu_slope(normed_one),
            unit_one,
            scale_one,
            gain_mid[0],
            living,
            pixel_count,
            everyone,
        )
        reduced_low = reduced_raw.astype(BF16)
        reduce_local = inner_rows(inputs, reduced_low).astype(BF16)
        input_grad = pre_grad + against(reduced_low, w_reduce)
        grad_expand = scatter_rep(expand_local)
        grad_spatial = scatter_rep(spatial_local)
        grad_reduce = scatter_rep(reduce_local)
        grad_classes = scatter_rep(classes_local)
        pieces = [
            gates_share.astype(BF16),
            grad_expand.reshape(-1, middle),
            grad_spatial,
            grad_classes.reshape(-1, middle),
        ]
        early = total_dp(jnp.concatenate(pieces, 0))
        rows = [piece.shape[0] for piece in pieces]
        starts = [sum(rows[:k]) for k in range(4)]
        grad_gates, expand_sum, grad_spatial, classes_sum = [
            early[at : at + size] for at, size in zip(starts, rows)
        ]
        grad_expand = expand_sum.reshape(grad_expand.shape)
        grad_classes = classes_sum.reshape(grad_classes.shape)
        grad_reduce = total_dp(grad_reduce)
        grad_gain_mid = jnp.stack([gain_grad_one, gain_grad_two], 0)
        grad_shift_mid = jnp.stack([shift_grad_one, shift_grad_two], 0)
    head_norms = lax.all_gather(
        head_norm, "rep", axis=1, tiled=True
    )
    return (
        depth,
        logits,
        input_grad,
        grad_reduce,
        grad_spatial,
        grad_expand,
        grad_heads.astype(F32),
        grad_gates,
        grad_messages.astype(F32),
        grad_classes,
        grad_gain_mid,
        grad_shift_mid,
        grad_gain_wide,
        grad_shift_wide,
        head_norms[0],
        head_norms[1],
    )


def solution(mesh):
    in_specs = (
        P(("dp", "rep"), None),
        P(),
        P(("dp", "rep")),
        P(("dp", "rep"), None),
        P(),
        P(),
        P(),
        P("rep", None),
        P(),
        P("rep", None),
        P(),
        P(),
        P(),
        P(),
        P(),
        P(),
        P(),
    )
    out_specs = (
        P(("dp", "rep"), None),
        P(("dp", "rep"), None),
        P(("dp", "rep"), None),
        P("rep", None),
        P("rep", None),
        P("rep", None),
        P("rep", "dp"),
        P("rep", None),
        P("rep", "dp"),
        P("rep", None),
        P(),
        P(),
        P(),
        P(),
        P(),
        P(),
    )
    return jax.shard_map(shards, mesh=mesh, in_specs=in_specs, out_specs=out_specs, check_vma=False)
```
